32 devices in a mesh: dp: 4 (over y, core), vocab: 8 (over z, x).
Axes of the slice: x: 2, y: 2, z: 4, core: 2. Of those that a mesh axis runs over, the one named last changes fastest.
Arguments:
- token_ids: int32 [32, 512], P(('dp', 'vocab')), may hold values from 0 to 7679, as said below
- lengths: int32 [32], P(('dp', 'vocab')), may hold values from 16 to 512, as said below
- type_ids: int32 [32, 512], P(('dp', 'vocab')), may hold values from 0 to 1
- word_table: bfloat16 [7680, 768], P('vocab'), may hold values from -6 to 6
- pos_table: bfloat16 [512, 768], replicated, may hold values from -3 to 3
- type_table: bfloat16 [2, 768], replicated, may hold values from -3 to 3
- gains: bfloat16 [5, 768], replicated, may hold values from 0.25 to 1.75
- shifts: bfloat16 [13, 768], replicated, may hold values from -2 to 2
- w_qkv: bfloat16 [2, 768, 2304], replicated, may hold values from -0.21875 to 0.21875
- w_out: bfloat16 [2, 768, 768], replicated, may hold values from -0.625 to 0.625
- b_ff1: bfloat16 [2, 3072], replicated, may hold values from -2 to 2
- w_ff1: bfloat16 [2, 768, 3072], replicated, may hold values from -0.21875 to 0.21875
- w_ff2: bfloat16 [2, 3072, 768], replicated, may hold values from -0.109375 to 0.109375
- cotangent: bfloat16 [32, 512, 768], P(('dp', 'vocab')), may hold values from -6 to 6
Outputs:
- hidden_out: bfloat16 [32, 512, 768], P(('dp', 'vocab'))
- table_grad: float32 [7680, 768], P('vocab')
- pos_grad: float32 [512, 768], P('vocab')
- type_grad: float32 [2, 768], P(None, 'vocab')
- gains_grad: float32 [5, 768], P(None, 'vocab')
- shifts_grad: float32 [13, 768], P(None, 'vocab')
- w_qkv_grad: float32 [2, 768, 2304], P(None, 'vocab')
- w_out_grad: float32 [2, 768, 768], P(None, 'vocab')
- b_ff1_grad: float32 [2, 3072], P(None, 'vocab')
- w_ff1_grad: float32 [2, 768, 3072], P(None, 'vocab')
- w_ff2_grad: float32 [2, 3072, 768], P(None, 'vocab')
The draws below stay inside these ranges and needn't reach their ends.
Inputs may be any that keep to these rules, and one draw needn't show every extreme that they name: `token_ids`: among the tokens of one device at most 128 ids lie in the 960 rows held by any one index of vocab, and in exactly 128 for one of them. `lengths`: the first sequence has 512 tokens; slots of a sequence beyond its length are padding that no query attends to.
All inputs are finite; a program needn't handle non-finite values.
Results may differ from the reference program's by a relative error of at most 0.02.
Values may be sent and summed in bfloat16 or wider, within the bound.
No kernel may reach another device: no remote copies, remote signals or barrier semaphores. Data moves between devices by JAX's collectives and lax.ppermute only.
A program may use at most 256 MiB of HBM per device.

```python
import math
import jax
import jax.numpy as jnp
from jax import lax

D = 768
HEADS = 12
HEAD_DIM = 64
FF = 3072
ROWS_DEV = 960
L = 512
NL = 2
SEQ_DEV = 1
VOCAB = 7680
SEQS = 32
CAP = 128


def draw_token_ids(key, part):
    key = jax.random.fold_in(key, 11)
    subkeys = jax.random.split(key, 5)
    owners = VOCAB // ROWS_DEV
    blocks = SEQS // SEQ_DEV
    token_count = SEQ_DEV * L
    hot_owner = jax.random.randint(subkeys[0], (blocks, 1), 0, owners)
    position = jnp.arange(token_count, dtype=jnp.int32)[None, :]
    stripe = (position - CAP) % (owners - 1)
    jitter = jax.random.randint(subkeys[1], (blocks, token_count), 0, 2)
    other_owner = (hot_owner + 1 + (stripe + jitter) % (owners - 1)) % owners
    owner_of = jnp.where(position < CAP, hot_owner, other_owner)
    first_pick = jax.random.randint(subkeys[2], (blocks, token_count), 0, ROWS_DEV)
    second_pick = jax.random.randint(subkeys[3], (blocks, token_count), 0, ROWS_DEV)
    row_in = first_pick * second_pick // ROWS_DEV
    order_keys = jax.random.randint(subkeys[4], (blocks, token_count), 0, 65536) * token_count + position
    shuffle = jnp.argsort(order_keys, axis=1)
    placed = jnp.take_along_axis(owner_of * ROWS_DEV + row_in, shuffle, axis=1)
    return placed.reshape(SEQS, L).astype(jnp.int32)


def draw_lengths(key, part):
    key = jax.random.fold_in(key, 7)
    drawn = jax.random.randint(key, (SEQS,), L // 32, L + 1)
    return drawn.at[0].set(L).astype(jnp.int32)


def touch_ends(values, rng, low, largest):
    longest = values.shape.index(max(values.shape))
    spots = []
    for shift in (0, 1):
        where = [jax.random.randint(jax.random.fold_in(rng, axis), (), 0, length) for axis, length in enumerate(values.shape)]
        where[longest] = (where[longest] + shift) % values.shape[longest]
        spots.append(tuple(where))
    return values.at[spots[0]].set(low).at[spots[1]].set(largest)


def steps_of(rng, extent, cuts, low, high):
    def one(axis_at, blocks):
        draws = jax.random.uniform(jax.random.fold_in(jax.random.fold_in(rng, 6), axis_at), (blocks,), jnp.float32, low / len(cuts), high / len(cuts))
        return jnp.repeat(jnp.exp(draws), extent[axis_at] // blocks).reshape((-1,) + (1,) * (len(extent) - axis_at - 1))

    factor_of = one(*cuts[0])
    for cut in cuts[1:]:
        factor_of = factor_of * one(*cut)
    return factor_of


def centred(rng, extent, deviation, most, cuts=(), kind=jnp.bfloat16):
    array = jax.random.normal(rng, extent, jnp.float32) * deviation
    if len(cuts) > 0:
        array = steps_of(rng, extent, cuts, -0.22, 0.18) * array
    return jnp.clip(array, min=-most, max=most).astype(kind)


def setup_inputs(seed: int = 0) -> dict:
    seeds = jax.random.split(jax.random.key(seed), 15)
    return {
        "token_ids": draw_token_ids(jax.random.fold_in(seeds[14], 71), 0),
        "lengths": draw_lengths(jax.random.fold_in(seeds[14], 71), 0),
        "type_ids": touch_ends(jax.random.randint(seeds[2], (SEQS, L), 0, 2), jax.random.fold_in(seeds[2], 1), 0, 1).astype(jnp.int32),
        "word_table": centred(seeds[3], (VOCAB, D), 1.0, 6.0, ((0, 8),)),
        "pos_table": centred(seeds[4], (L, D), 0.5, 3.0),
        "type_table": centred(seeds[5], (2, D), 0.5, 3.0),
        "gains": jnp.clip(1.0 + 0.15 * jax.random.normal(seeds[6], (2 * NL + 1, D), jnp.float32), 0.25, 1.75).astype(jnp.bfloat16),
        "shifts": centred(seeds[7], (6 * NL + 1, D), 0.3, 2.0),
        "w_qkv": centred(seeds[8], (NL, D, 3 * D), D ** -0.5, 0.21875),
        "w_out": centred(seeds[9], (NL, D, D), (D // 8) ** -0.5, 0.625),
        "b_ff1": centred(seeds[10], (NL, FF), 0.3, 2.0),
        "w_ff1": centred(seeds[11], (NL, D, FF), D ** -0.5, 0.21875),
        "w_ff2": centred(seeds[12], (NL, FF, D), FF ** -0.5, 0.109375),
        "cotangent": centred(seeds[13], (SEQS, L, D), 1.0, 6.0, ((0, 32),)),
    }


norm_eps = 1e-12

@jax.custom_vjp
def low(v):
    return lax.optimization_barrier(v.astype(jnp.bfloat16)).astype(jnp.float32)

@jax.custom_vjp
def low_back(v):
    return v

def low_keep(v):
    return (low(v), None)

def low_pass(kept, grad):
    return (grad,)

def back_keep(v):
    return (v, None)

def back_low(kept, grad):
    return (low(grad),)
low.defvjp(low_keep, low_pass)
low_back.defvjp(back_keep, back_low)

def normalize(inputs, gain_row, shift_row):
    centered = inputs - lax.optimization_barrier(jnp.mean(inputs, axis=-1, keepdims=True))
    spread = lax.rsqrt(lax.optimization_barrier(jnp.mean(centered * centered, axis=-1, keepdims=True)) + norm_eps)
    return centered * spread * gain_row + shift_row

def product(left_op, right_op):
    return jnp.dot(left_op, right_op, precision=lax.Precision.HIGHEST, preferred_element_type=jnp.float32)

def split_heads(matrix):
    return matrix.reshape(matrix.shape[0], HEADS, HEAD_DIM)

def attend_one(queries, keys_in, values, length):
    scores = jnp.einsum('qhd,khd->hqk', split_heads(queries), split_heads(keys_in), precision=lax.Precision.HIGHEST) * HEAD_DIM ** (-0.5)
    scores = low_back(scores)
    visible = jnp.arange(L)[None, None, :] < length
    scores = jnp.where(visible, scores, -1e+30)
    top_score = lax.optimization_barrier(jnp.max(scores, axis=-1, keepdims=True))
    weights = jnp.exp(scores - top_score)
    softened = low(weights / lax.optimization_barrier(jnp.sum(weights, axis=-1, keepdims=True)))
    context = jnp.einsum('hqk,khd->qhd', softened, split_heads(values), precision=lax.Precision.HIGHEST)
    return context.reshape(L, D)

def activate(inputs):
    return jax.nn.gelu(inputs, approximate=False)

def encoder_layer(states, group_lengths, params, layer_num):
    word, position_tab, type_tab, gain_vals, shift_vals, qkv_w, out_w, ffn_bias, first_w, second_w = params
    shift_base = 1 + 6 * layer_num
    group_size = group_lengths.shape[0]
    mixed_qkv = low_back(product(low(states), qkv_w[layer_num]))
    queries = low(mixed_qkv[:, :D] + shift_vals[shift_base])
    keys_in = low(mixed_qkv[:, D:2 * D])
    values = low(mixed_qkv[:, 2 * D:] + shift_vals[shift_base + 1])
    context = jax.vmap(attend_one)(queries.reshape(group_size, L, D), keys_in.reshape(group_size, L, D), values.reshape(group_size, L, D), group_lengths)
    context = low(low_back(context.reshape(-1, D)))
    attended = low_back(product(context, out_w[layer_num])) + shift_vals[shift_base + 2]
    middle = normalize(states + attended, gain_vals[1 + 2 * layer_num], shift_vals[shift_base + 3])
    hidden_pre = low_back(product(low(middle), first_w[layer_num])) + ffn_bias[layer_num]
    active = low(activate(hidden_pre))
    ffn_out = low_back(product(active, second_w[layer_num])) + shift_vals[shift_base + 4]
    return normalize(middle + ffn_out, gain_vals[2 + 2 * layer_num], shift_vals[shift_base + 5])

def group_forward(params, group_ids, group_types, group_lengths):
    word, position_tab, type_tab, gain_vals, shift_vals = (params[0], params[1], params[2], params[3], params[4])
    embedded = word[group_ids] + position_tab[None, :, :] + type_tab[group_types]
    states = normalize(embedded, gain_vals[0], shift_vals[0]).reshape(-1, D)
    for layer_num in range(NL):
        states = encoder_layer(states, group_lengths, params, layer_num)
    return states.reshape(group_ids.shape[0], L, D)

def reference(token_ids, lengths, type_ids, word_table, pos_table, type_table, gains, shifts, w_qkv, w_out, b_ff1, w_ff1, w_ff2, cotangent):
    params = (word_table.astype(jnp.float32), pos_table.astype(jnp.float32), type_table.astype(jnp.float32), gains.astype(jnp.float32), shifts.astype(jnp.float32), w_qkv.astype(jnp.float32), w_out.astype(jnp.float32), b_ff1.astype(jnp.float32), w_ff1.astype(jnp.float32), w_ff2.astype(jnp.float32))
    group_size = math.gcd(SEQS, max(1, 4096 // L))
    grouped = (token_ids.reshape(-1, group_size, L), type_ids.reshape(-1, group_size, L), lengths.reshape(-1, group_size))

    def forward(weights):

        def one_group(blocks):
            return group_forward(weights, blocks[0], blocks[1], blocks[2])
        return lax.map(jax.checkpoint(one_group), grouped).reshape(SEQS, L, D)
    outputs, pullback = jax.vjp(forward, params)
    gradients = pullback(cotangent.astype(jnp.float32))[0]
    return (outputs.astype(jnp.bfloat16), gradients[0], gradients[1], gradients[2], gradients[3], gradients[4], gradients[5], gradients[6], gradients[7], gradients[8], gradients[9])
```

```python
import jax
import jax.numpy as jnp
from jax import lax
from jax.sharding import PartitionSpec as P

HEADS = 12
HEAD_DIM = 64
NL = 2

norm_eps = 1e-12
AXES = ("dp", "vocab")


def normalize(inputs):
    centered = inputs - jnp.mean(inputs, axis=-1, keepdims=True)
    spread = lax.rsqrt(jnp.mean(centered * centered, axis=-1, keepdims=True) + norm_eps)
    return (centered * spread, spread)


def norm_back(grad_out, normed, spread, gain_row):
    scaled = grad_out * gain_row
    return spread * (
        scaled
        - jnp.mean(scaled, axis=-1, keepdims=True)
        - normed * jnp.mean(scaled * normed, axis=-1, keepdims=True)
    )


def contract_rows(left_op, right_op):
    return lax.dot_general(
        left_op, right_op, (((0,), (0,)), ((), ())), preferred_element_type=jnp.float32
    )


def contract_cols(left_op, right_op):
    return lax.dot_general(
        left_op, right_op, (((1,), (1,)), ((), ())), preferred_element_type=jnp.float32
    )


def split_heads(matrix):
    return matrix.reshape(matrix.shape[0], HEADS, HEAD_DIM)


def activate(inputs):
    return jax.nn.gelu(inputs, approximate=False)


def score_block(queries, keys_in, length):
    scores = jnp.einsum(
        "qhd,khd->hqk",
        split_heads(queries),
        split_heads(keys_in),
        preferred_element_type=jnp.float32,
    ) * HEAD_DIM ** (-0.5)
    visible = jnp.arange(keys_in.shape[0])[None, None, :] < length
    return jnp.where(visible, scores, -1e30)


def attend(queries, keys_in, values, length):
    scores = score_block(queries, keys_in, length)
    top_score = jnp.max(scores, axis=-1, keepdims=True)
    weights = jnp.exp(scores - top_score)
    row_total = jnp.sum(weights, axis=-1, keepdims=True)
    softened = (weights / row_total).astype(jnp.bfloat16)
    context = jnp.einsum(
        "hqk,khd->qhd", softened, split_heads(values), preferred_element_type=jnp.float32
    )
    return (
        context.reshape(queries.shape).astype(jnp.bfloat16),
        top_score[..., 0] + jnp.log(row_total[..., 0]),
    )


def attend_back(queries, keys_in, values, length, total_log, grad_context):
    scores = score_block(queries, keys_in, length)
    softened = jnp.exp(scores - total_log[..., None])
    grad_split = split_heads(grad_context)
    grad_probs = jnp.einsum(
        "qhd,khd->hqk", grad_split, split_heads(values), preferred_element_type=jnp.float32
    )
    grad_values = jnp.einsum(
        "hqk,qhd->khd",
        softened.astype(jnp.bfloat16),
        grad_split,
        preferred_element_type=jnp.float32,
    )
    weighted = jnp.sum(softened * grad_probs, axis=-1, keepdims=True)
    grad_scores = (softened * (grad_probs - weighted)).astype(jnp.bfloat16)
    score_scale = HEAD_DIM ** (-0.5)
    grad_queries = (
        jnp.einsum(
            "hqk,khd->qhd", grad_scores, split_heads(keys_in), preferred_element_type=jnp.float32
        )
        * score_scale
    )
    grad_keys = (
        jnp.einsum(
            "hqk,qhd->khd", grad_scores, split_heads(queries), preferred_element_type=jnp.float32
        )
        * score_scale
    )
    return (
        grad_queries.reshape(queries.shape),
        grad_keys.reshape(queries.shape),
        grad_values.reshape(queries.shape),
    )


class Cube:
    def __init__(self, dp_size, vocab_size):
        self.dp_size = dp_size
        self.vocab_size = vocab_size
        self.dp_bits = dp_size.bit_length() - 1
        self.vocab_bits = vocab_size.bit_length() - 1
        assert 1 << self.dp_bits == dp_size and 1 << self.vocab_bits == vocab_size
        self.vocab_masks = [6 if bit == 2 else 1 << bit for bit in range(self.vocab_bits)]

    def permute(self, value, dp_mask, vocab_mask):
        count = self.vocab_size
        pairs = [
            (d * count + v, (d ^ dp_mask) * count + (v ^ vocab_mask))
            for d in range(self.dp_size)
            for v in range(count)
        ]
        return lax.ppermute(value, AXES, pairs)

    def core(self, value):
        return self.permute(value, 1, 0)

    def my_bit(self, bit):
        place = lax.axis_index("vocab")
        value = (place >> bit) & 1
        if bit == 1 and self.vocab_bits > 2:
            value = value ^ ((place >> 2) & 1)
        return value

    def to_blocks(self, matrix):
        rows, cols = matrix.shape
        part = rows // self.vocab_size
        if self.vocab_bits > 2:
            wide = matrix.reshape(self.vocab_size // 8, 2, 2, 2 * part, cols)
            wide = jnp.stack([wide[:, 0], wide[:, 1, ::-1]], axis=1)
        else:
            wide = matrix
        return wide.reshape((2,) * self.vocab_bits + (part, cols))

    def reduce(self, blocks, order):
        left = list(reversed(range(self.vocab_bits)))
        halved = False
        for dim in order:
            if dim == "y" and len(left) > 0 and self.dp_bits == 2:
                halved = True
                shape = blocks.shape
                rows = shape[-2] // 2
                blocks = blocks.reshape(shape[:-2] + (2, rows, shape[-1]))
                axis = len(shape) - 2
                mine = (lax.axis_index("dp") >> 1) & 1
                keep = lax.dynamic_index_in_dim(blocks, mine, axis, keepdims=False)
                send = lax.dynamic_index_in_dim(blocks, 1 - mine, axis, keepdims=False)
                blocks = self.add(keep, self.permute(send, 2, 0))
            elif dim == "y":
                for bit in range(1, self.dp_bits):
                    blocks = self.add(blocks, self.permute(blocks, 1 << bit, 0))
            else:
                axis = left.index(dim)
                left.pop(axis)
                mine = self.my_bit(dim)
                keep = lax.dynamic_index_in_dim(blocks, mine, axis, keepdims=False)
                send = lax.dynamic_index_in_dim(blocks, 1 - mine, axis, keepdims=False)
                blocks = self.add(keep, self.permute(send, 0, self.vocab_masks[dim]))
        if halved:
            other = self.permute(blocks, 2, 0)
            mine = ((lax.axis_index("dp") >> 1) & 1) == 0
            blocks = jnp.concatenate(
                [jnp.where(mine, blocks, other), jnp.where(mine, other, blocks)], axis=0
            )
        return blocks

    def add(self, left_op, right_op):
        return (left_op.astype(jnp.float32) + right_op.astype(jnp.float32)).astype(jnp.bfloat16)

    def halves(self, matrix):
        mine = lax.axis_index("dp") & 1
        width = matrix.shape[1] // 2
        keep = lax.dynamic_slice_in_dim(matrix, mine * width, width, 1)
        send = lax.dynamic_slice_in_dim(matrix, (1 - mine) * width, width, 1)
        return keep, send

    def join_core(self, share):
        other = self.core(share)
        mine = (lax.axis_index("dp") & 1) == 0
        return jnp.concatenate(
            [jnp.where(mine, share, other), jnp.where(mine, other, share)], axis=-1
        ).astype(jnp.float32)


def both(own, other):
    return jnp.concatenate([own, other], axis=0)


def on_device(
    cube,
    token_ids,
    lengths,
    type_ids,
    word_table,
    pos_table,
    type_table,
    gains,
    shifts,
    w_qkv,
    w_out,
    b_ff1,
    w_ff1,
    w_ff2,
    cotangent,
):
    owners = cube.vocab_size
    local_rows, model_width = word_table.shape
    assert token_ids.shape[0] == 1
    token_count = token_ids.shape[1]
    slot_count = 2 * token_count // owners
    slots = owners * slot_count
    gain_vals = gains.astype(jnp.float32)
    shift_vals = shifts.astype(jnp.float32)
    ffn_bias = b_ff1.astype(jnp.float32)
    flat_ids = token_ids.reshape(token_count)
    me = lax.axis_index("vocab")

    all_ids = lax.all_to_all(
        jnp.broadcast_to(flat_ids[None, :], (owners, token_count)),
        "vocab",
        split_axis=0,
        concat_axis=0,
        tiled=True,
    )
    local = all_ids - me * local_rows
    here = (local >= 0) & (local < local_rows)
    rank = jnp.cumsum(here.astype(jnp.int32), axis=1) - 1
    slot_hit = (
        jnp.where(here, rank, -1)[:, None, :]
        == jnp.arange(slot_count, dtype=jnp.int32)[None, :, None]
    )
    asked = jnp.sum(jnp.where(slot_hit, local[:, None, :] + 1, 0), axis=2).reshape(slots) - 1
    row_hit = (asked[:, None] == jnp.arange(local_rows, dtype=jnp.int32)[None, :]).astype(
        jnp.bfloat16
    )
    found_rows = jnp.dot(row_hit, word_table, preferred_element_type=jnp.float32).astype(
        jnp.bfloat16
    )
    replies = lax.all_to_all(
        found_rows.reshape(owners, slot_count, model_width),
        "vocab",
        split_axis=0,
        concat_axis=0,
        tiled=True,
    ).reshape(slots, model_width)
    owner_of = flat_ids // local_rows
    chosen = (owner_of[:, None] == jnp.arange(owners, dtype=jnp.int32)[None, :]).astype(jnp.int32)
    before = jnp.cumsum(chosen, axis=0) - chosen
    slot_of = owner_of * slot_count + jnp.sum(before * chosen, axis=1)
    dispatch = (slot_of[:, None] == jnp.arange(slots, dtype=jnp.int32)[None, :]).astype(
        jnp.bfloat16
    )
    word_rows = jnp.dot(dispatch, replies, preferred_element_type=jnp.float32)
    type_flat = type_ids.reshape(token_count)
    type_rows = jnp.where(
        type_flat[:, None] == 1,
        type_table[1].astype(jnp.float32)[None, :],
        type_table[0].astype(jnp.float32)[None, :],
    )
    embedded = word_rows + pos_table.astype(jnp.float32) + type_rows
    normed_emb, spread_emb = normalize(embedded)
    states = normed_emb * gain_vals[0] + shift_vals[0]
    saved_acts = []
    length = lengths[0]
    for layer_num in range(NL):
        shift_base = 1 + 6 * layer_num
        states_low = states.astype(jnp.bfloat16)
        states_other = cube.core(states_low)
        mixed_qkv = jnp.dot(states_low, w_qkv[layer_num], preferred_element_type=jnp.float32)
        queries = (mixed_qkv[:, :model_width] + shift_vals[shift_base]).astype(jnp.bfloat16)
        keys_in = mixed_qkv[:, model_width : 2 * model_width].astype(jnp.bfloat16)
        values = (mixed_qkv[:, 2 * model_width :] + shift_vals[shift_base + 1]).astype(jnp.bfloat16)
        context, total_log = attend(queries, keys_in, values, length)
        context_other = cube.core(context)
        attended = (
            jnp.dot(context, w_out[layer_num], preferred_element_type=jnp.float32)
            + shift_vals[shift_base + 2]
        )
        normed_one, spread_one = normalize(states + attended)
        middle = normed_one * gain_vals[1 + 2 * layer_num] + shift_vals[shift_base + 3]
        middle_low = middle.astype(jnp.bfloat16)
        middle_other = cube.core(middle_low)
        hidden_pre = (
            jnp.dot(middle_low, w_ff1[layer_num], preferred_element_type=jnp.float32)
            + ffn_bias[layer_num]
        )
        active = activate(hidden_pre).astype(jnp.bfloat16)
        active_other = cube.core(active)
        ffn_out = (
            jnp.dot(active, w_ff2[layer_num], preferred_element_type=jnp.float32)
            + shift_vals[shift_base + 4]
        )
        normed_two, spread_two = normalize(middle + ffn_out)
        saved_acts.append(
            (
                (states_low, states_other),
                (queries, keys_in, values),
                total_log,
                (context, context_other),
                normed_one,
                spread_one,
                (middle_low, middle_other),
                hidden_pre,
                (active, active_other),
                normed_two,
                spread_two,
            )
        )
        states = normed_two * gain_vals[2 + 2 * layer_num] + shift_vals[shift_base + 5]
    hidden_out = states.reshape(1, token_count, model_width).astype(jnp.bfloat16)
    grad_states = cotangent.reshape(token_count, model_width).astype(jnp.float32)
    gain_grads = [None] * (2 * NL + 1)
    shift_grads = [None] * (6 * NL + 1)
    bias_grads = [None] * NL
    layer_grads = [None] * NL
    bits = list(range(cube.vocab_bits))
    turn = lambda n: bits[n % len(bits) :] + bits[: n % len(bits)]
    for layer_num in reversed(range(NL)):
        (
            states_both,
            (queries, keys_in, values),
            total_log,
            context_both,
            normed_one,
            spread_one,
            middle_both,
            hidden_pre,
            active_both,
            normed_two,
            spread_two,
        ) = saved_acts[layer_num]
        shift_base = 1 + 6 * layer_num
        gain_grads[2 + 2 * layer_num] = jnp.sum(grad_states * normed_two, axis=0)
        shift_grads[shift_base + 5] = jnp.sum(grad_states, axis=0)
        grad_second = norm_back(grad_states, normed_two, spread_two, gain_vals[2 + 2 * layer_num])
        shift_grads[shift_base + 4] = jnp.sum(grad_second, axis=0)
        second_low = grad_second.astype(jnp.bfloat16)
        keep, send = cube.halves(second_low)
        grad_w_two = contract_rows(both(*active_both), both(keep, cube.core(send)))
        share_two = cube.reduce(
            cube.to_blocks(grad_w_two.astype(jnp.bfloat16)), ["y"] + turn(0)
        )
        grad_active = contract_cols(second_low, w_ff2[layer_num])
        grad_pre = jax.vjp(activate, hidden_pre)[1](grad_active)[0]
        bias_grads[layer_num] = jnp.sum(grad_pre, axis=0)
        pre_low = grad_pre.astype(jnp.bfloat16)
        keep, send = cube.halves(pre_low)
        grad_w_one = contract_rows(both(*middle_both), both(keep, cube.core(send)))
        share_one = cube.reduce(
            cube.to_blocks(grad_w_one.astype(jnp.bfloat16)), turn(1 + layer_num) + ["y"]
        )
        grad_middle = grad_second + contract_cols(pre_low, w_ff1[layer_num])
        gain_grads[1 + 2 * layer_num] = jnp.sum(grad_middle * normed_one, axis=0)
        shift_grads[shift_base + 3] = jnp.sum(grad_middle, axis=0)
        grad_first = norm_back(grad_middle, normed_one, spread_one, gain_vals[1 + 2 * layer_num])
        shift_grads[shift_base + 2] = jnp.sum(grad_first, axis=0)
        first_low = grad_first.astype(jnp.bfloat16)
        keep, send = cube.halves(first_low)
        grad_w_out = contract_rows(both(*context_both), both(keep, cube.core(send)))
        grad_context = contract_cols(first_low, w_out[layer_num]).astype(jnp.bfloat16)
        grad_queries, grad_keys, grad_values = attend_back(
            queries, keys_in, values, length, total_log, grad_context
        )
        shift_grads[shift_base] = jnp.sum(grad_queries, axis=0)
        shift_grads[shift_base + 1] = jnp.sum(grad_values, axis=0)
        grad_mixed = jnp.concatenate([grad_queries, grad_keys, grad_values], axis=1).astype(
            jnp.bfloat16
        )
        keep, send = cube.halves(grad_mixed)
        grad_w_qkv = contract_rows(both(*states_both), both(keep, cube.core(send)))
        share_mix = cube.reduce(
            cube.to_blocks(
                jnp.concatenate([grad_w_qkv, grad_w_out], axis=1).astype(jnp.bfloat16)
            ),
            turn(2 + 2 * layer_num) + ["y"],
        )
        grad_states = grad_first + contract_cols(grad_mixed, w_qkv[layer_num])
        layer_grads[layer_num] = (share_mix, share_one, share_two)
    gain_grads[0] = jnp.sum(grad_states * normed_emb, axis=0)
    shift_grads[0] = jnp.sum(grad_states, axis=0)
    grad_embedded = norm_back(grad_states, normed_emb, spread_emb, gain_vals[0])

    outgoing = lax.dot_general(
        dispatch,
        grad_embedded.astype(jnp.bfloat16),
        (((0,), (0,)), ((), ())),
        preferred_element_type=jnp.float32,
    ).astype(jnp.bfloat16)
    incoming = lax.all_to_all(
        outgoing.reshape(owners, slot_count, model_width),
        "vocab",
        split_axis=0,
        concat_axis=0,
        tiled=True,
    ).reshape(slots, model_width)
    table_part = contract_rows(row_hit, incoming).astype(jnp.bfloat16)
    keep, send = cube.halves(table_part)
    table_part = cube.add(keep, cube.core(send))
    for bit in range(1, cube.dp_bits):
        table_part = cube.add(table_part, cube.permute(table_part, 1 << bit, 0))
    table_out = cube.join_core(table_part)

    type_zero = jnp.sum(jnp.where(type_flat[:, None] == 0, grad_embedded, 0.0), axis=0)
    type_one = jnp.sum(jnp.where(type_flat[:, None] == 1, grad_embedded, 0.0), axis=0)
    small = jnp.concatenate(
        [
            jnp.stack([type_zero, type_one] + gain_grads + shift_grads).reshape(
                -1, owners, model_width // owners
            ),
            jnp.stack(bias_grads).reshape(NL, owners, -1, model_width // owners)
            .transpose(0, 2, 1, 3)
            .reshape(-1, owners, model_width // owners),
        ],
        axis=0,
    )
    small_rows = small.shape[0]
    small = small.transpose(1, 0, 2).reshape(owners, -1)
    packed_rows = -(-small.shape[1] // model_width)
    small = jnp.pad(small, ((0, 0), (0, packed_rows * model_width - small.shape[1])))
    pos_rows = token_count // owners
    packed = jnp.concatenate(
        [
            grad_embedded.reshape(owners, pos_rows, model_width),
            small.reshape(owners, packed_rows, model_width),
        ],
        axis=1,
    ).astype(jnp.bfloat16)
    keep, send = cube.halves(packed.reshape(-1, model_width))
    packed = cube.add(keep, cube.core(send))
    share_pack = cube.reduce(cube.to_blocks(packed), turn(1) + ["y"])

    mix_out, one_out, two_out = [], [], []
    for share_mix, share_one, share_two in layer_grads:
        wide = 3 * model_width // 2
        mix_out.append((share_mix[:, :wide], share_mix[:, wide:]))
        one_out.append(share_one)
        two_out.append(share_two)
    qkv_out = cube.join_core(jnp.stack([m[0] for m in mix_out]))
    wout_out = cube.join_core(jnp.stack([m[1] for m in mix_out]))
    one_out = cube.join_core(jnp.stack(one_out))
    two_out = cube.join_core(jnp.stack(two_out))
    pack_out = cube.join_core(share_pack)
    pos_out = pack_out[:pos_rows]
    small_out = pack_out[pos_rows:].reshape(-1)[: small_rows * (model_width // owners)].reshape(
        small_rows, model_width // owners
    )
    type_out = small_out[:2]
    gain_out = small_out[2 : 2 + 2 * NL + 1]
    shift_out = small_out[2 + 2 * NL + 1 : 2 + 2 * NL + 1 + 6 * NL + 1]
    bias_out = small_out[2 + 2 * NL + 1 + 6 * NL + 1 :].reshape(NL, -1)
    return (
        hidden_out,
        table_out,
        pos_out,
        type_out,
        gain_out,
        shift_out,
        qkv_out,
        wout_out,
        bias_out,
        one_out,
        two_out,
    )


def solution(mesh):
    cube = Cube(mesh.shape["dp"], mesh.shape["vocab"])
    in_specs = (
        P(("dp", "vocab"), None),
        P(("dp", "vocab")),
        P(("dp", "vocab"), None),
        P("vocab", None),
        P(),
        P(),
        P(),
        P(),
        P(),
        P(),
        P(),
        P(),
        P(),
        P(("dp", "vocab"), None, None),
    )
    out_specs = (
        P(("dp", "vocab"), None, None),
        P("vocab", None),
        P("vocab", None),
        P(None, "vocab"),
        P(None, "vocab"),
        P(None, "vocab"),
        P(None, "vocab", None),
        P(None, "vocab", None),
        P(None, "vocab"),
        P(None, "vocab", None),
        P(None, "vocab", None),
    )

    def run(*args):
        return on_device(cube, *args)

    return jax.shard_map(run, mesh=mesh, in_specs=in_specs, out_specs=out_specs, check_vma=False)
```

```python
import functools
import jax
import jax.numpy as jnp
from jax import lax
from jax.experimental import pallas as pl
from jax.experimental.pallas import tpu as pltpu
from jax.sharding import PartitionSpec as P

HEADS = 12
HEAD_DIM = 64
NL = 2
norm_eps = 1e-12
SCALE = HEAD_DIM ** (-0.5)
ANY = pl.BlockSpec(memory_space=pl.ANY)
VM = pl.BlockSpec(memory_space=pltpu.VMEM)
SM = pl.BlockSpec(memory_space=pltpu.SMEM)
F32, LOW = jnp.float32, jnp.bfloat16


def run(kernel, after, out_shape, in_specs, operands, **options):
    count = len(operands)

    def body(*refs):
        kernel(*refs[:count], *refs[count + len(after) :])

    return pl.pallas_call(
        body,
        out_shape=out_shape,
        in_specs=list(in_specs) + [ANY] * len(after),
        compiler_params=PARAMS,
        **options,
    )(*operands, *after)


PARAMS = pltpu.CompilerParams(vmem_limit_bytes=60 * 1024 * 1024)


def normalize(inputs):
    centered = inputs - jnp.mean(inputs, axis=-1, keepdims=True)
    spread = lax.rsqrt(jnp.mean(centered * centered, axis=-1, keepdims=True) + norm_eps)
    return (centered * spread, spread)


def norm_back(grad_out, normed, spread, gain_row):
    scaled = grad_out * gain_row
    return spread * (
        scaled
        - jnp.mean(scaled, axis=-1, keepdims=True)
        - normed * jnp.mean(scaled * normed, axis=-1, keepdims=True)
    )


def dot(left_op, right_op, dims=((1,), (0,))):
    return lax.dot_general(left_op, right_op, (dims, ((), ())), preferred_element_type=F32)


ROWS = ((0,), (0,))
COLS = ((1,), (1,))


def gelu_pair(inputs):
    size = jnp.abs(inputs)
    bell = jnp.exp2(inputs * inputs * (-0.5 * 1.4426950408889634))
    t = 1.0 / (1.0 + size * (0.3275911 * 0.7071067811865476))
    tail = t * (
        0.5 * 0.254829592
        + t * (0.5 * -0.284496736 + t * (0.5 * 1.421413741 + t * (0.5 * -1.453152027 + t * (0.5 * 1.061405429))))
    )
    tail = tail * bell
    phi = jnp.where(inputs >= 0.0, 1.0 - tail, tail)
    return inputs * phi, phi + inputs * bell * 0.3989422804014327


def forward_kernel(
    layer,
    length_ref, x_ref, rows_ref, qkv_bias_ref, ffn_bias_ref, wqkv_hbm, wout_hbm, w1_hbm, w2_hbm,
    xlow_ref, mixed_ref, lse_ref, ctxt_ref, n1_ref, s1_ref, mlow_ref, gp_ref, act_ref, n2_ref, s2_ref, next_ref,
    wqkv, wout, w1, w2, sems,
    xlow, mixed, ctxt, mlow, gp, act, n1, n2, nxt, middle, acc, osems,
):
    loads = [
        pltpu.make_async_copy(src.at[layer], dst, sems.at[i])
        for i, (src, dst) in enumerate([(wqkv_hbm, wqkv), (wout_hbm, wout), (w1_hbm, w1), (w2_hbm, w2)])
    ]
    for load in loads:
        load.start()
    stores = []

    def emit(src, dst):
        copy = pltpu.make_async_copy(src, dst, osems.at[len(stores)])
        copy.start()
        stores.append(copy)

    tokens, width = x_ref.shape
    xlow[...] = x_ref[...].astype(LOW)
    emit(xlow, xlow_ref)
    loads[0].wait()

    def qkv_step(i, carry):
        cols = pl.ds(pl.multiple_of(i * 256, 256), 256)
        mixed[:, cols] = (dot(xlow[...], wqkv[:, cols]) + qkv_bias_ref[:, cols]).astype(LOW)
        return carry

    lax.fori_loop(0, 3 * width // 256, qkv_step, 0)
    emit(mixed, mixed_ref)

    key_slot = lax.broadcasted_iota(jnp.int32, (tokens, 128), 0)
    visible = jnp.where(key_slot < length_ref[0], 0.0, -1e30)[:, :1]
    lane = lax.broadcasted_iota(jnp.int32, (tokens, 128), 1)

    def pair_step(j, carry):
        at = pl.multiple_of(j * 128, 128)
        q = mixed[:, pl.ds(at, 128)] * jnp.asarray(SCALE, LOW)
        k = mixed[:, pl.ds(pl.multiple_of(width + at, 128), 128)]
        v = mixed[:, pl.ds(pl.multiple_of(2 * width + at, 128), 128)]
        vt = v.T
        for h in range(2):
            kh = jnp.where((lane < 64) == (h == 0), k, jnp.zeros_like(k))
            scores = dot(kh, q, COLS) + visible
            top = jnp.max(scores, axis=0, keepdims=True)
            weights = jnp.exp(scores - top)
            total = jnp.sum(weights, axis=0, keepdims=True)
            out = dot(vt[h * 64 : (h + 1) * 64], weights.astype(LOW)) * (1.0 / total)
            ctxt[pl.ds(pl.multiple_of(at + h * 64, 64), 64), :] = out.astype(LOW)
            lse_ref[pl.ds(2 * j + h, 1), :] = top + jnp.log(total)
        return carry

    lax.fori_loop(0, HEADS // 2, pair_step, 0)
    emit(ctxt, ctxt_ref)
    loads[1].wait()
    attended = dot(ctxt[...], wout[...], ROWS) + rows_ref[0:1]
    normed, spread = normalize(x_ref[...] + attended)
    n1[...] = normed
    emit(n1, n1_ref)
    s1_ref[...] = jnp.broadcast_to(spread, s1_ref.shape)
    middle[...] = normed * rows_ref[1:2] + rows_ref[2:3]
    mlow[...] = middle[...].astype(LOW)
    emit(mlow, mlow_ref)
    loads[2].wait()
    loads[3].wait()
    acc[...] = middle[...] + rows_ref[3:4]
    chunk = 512

    def ffn_step(i, carry):
        cols = pl.ds(pl.multiple_of(i * chunk, chunk), chunk)
        pre = dot(mlow[...], w1[:, cols]) + ffn_bias_ref[:, cols]
        active, slope = gelu_pair(pre)
        gp[:, cols] = slope.astype(LOW)
        active = active.astype(LOW)
        act[:, cols] = active
        acc[...] += dot(active, w2[cols, :])
        return carry

    lax.fori_loop(0, w1.shape[1] // chunk, ffn_step, 0)
    emit(gp, gp_ref)
    emit(act, act_ref)
    normed, spread = normalize(acc[...])
    n2[...] = normed
    emit(n2, n2_ref)
    s2_ref[...] = jnp.broadcast_to(spread, s2_ref.shape)
    nxt[...] = normed * rows_ref[4:5] + rows_ref[5:6]
    emit(nxt, next_ref)
    for store in stores:
        store.wait()


def forward_layer(layer, length, states, rows, qkv_bias, ffn_bias, w_qkv, w_out, w_ff1, w_ff2, after=()):
    tokens, width = states.shape
    ff = w_ff1.shape[2]
    s = jax.ShapeDtypeStruct
    outs = (
        s((tokens, width), LOW), s((tokens, 3 * width), LOW), s((HEADS, tokens), F32), s((width, tokens), LOW),
        s((tokens, width), F32), s((tokens, 128), F32), s((tokens, width), LOW), s((tokens, ff), LOW), s((tokens, ff), LOW),
        s((tokens, width), F32), s((tokens, 128), F32), s((tokens, width), F32),
    )
    ospec = (ANY, ANY, VM, ANY, ANY, VM, ANY, ANY, ANY, ANY, VM, ANY)
    v = pltpu.VMEM
    scratch = [
        v((width, 3 * width), LOW), v((width, width), LOW), v((width, ff), LOW), v((ff, width), LOW), pltpu.SemaphoreType.DMA((4,)),
        v((tokens, width), LOW), v((tokens, 3 * width), LOW), v((width, tokens), LOW), v((tokens, width), LOW),
        v((tokens, ff), LOW), v((tokens, ff), LOW), v((tokens, width), F32), v((tokens, width), F32), v((tokens, width), F32),
        v((tokens, width), F32), v((tokens, width), F32), pltpu.SemaphoreType.DMA((9,)),
    ]
    flops = 2 * tokens * width * (4 * width + 2 * ff) + 8 * tokens * tokens * width
    return run(
        functools.partial(forward_kernel, layer),
        after,
        out_shape=outs,
        in_specs=[SM, VM, VM, VM, VM, ANY, ANY, ANY, ANY],
        operands=(length, states, rows, qkv_bias, ffn_bias, w_qkv, w_out, w_ff1, w_ff2),
        out_specs=ospec,
        scratch_shapes=scratch,
        cost_estimate=pl.CostEstimate(flops=flops, bytes_accessed=30 << 20, transcendentals=0),
        name="forward_layer",
    )


def feed_back_kernel(
    layer,
    core_ref, grad_ref, n2_ref, s2_ref, n1_ref, s1_ref, rows_ref, gp_hbm, wout_hbm, w1_hbm, w2_hbm,
    pre_keep_ref, pre_send_ref, sec_keep_ref, sec_send_ref, first_ref, fst_keep_ref, fst_send_ref, gctx_ref, sums_ref, bias_ref,
    wout, w1, w2, gp, sems, second, grad_mid, keep, send,
):
    loads = [
        pltpu.make_async_copy(src, dst, sems.at[i])
        for i, (src, dst) in enumerate([(w2_hbm.at[layer], w2), (gp_hbm, gp), (w1_hbm.at[layer], w1), (wout_hbm.at[layer], wout)])
    ]
    for load in loads:
        load.start()
    mine = core_ref[0]
    width = second.shape[1]
    half = width // 2
    grad = grad_ref[...].astype(F32)
    n2 = n2_ref[...]
    sums_ref[0:1] = jnp.sum(grad * n2, axis=0, keepdims=True)
    sums_ref[1:2] = jnp.sum(grad, axis=0, keepdims=True)
    e = norm_back(grad, n2, s2_ref[:, :1], rows_ref[4:5])
    sums_ref[2:3] = jnp.sum(e, axis=0, keepdims=True)
    grad_mid[...] = e
    second[...] = e.astype(LOW)

    def part(source, keep_to, send_to):
        @pl.when(mine == 0)
        def _():
            keep_to[...] = source[:, :half]
            send_to[...] = source[:, half:]

        @pl.when(mine == 1)
        def _():
            keep_to[...] = source[:, half:]
            send_to[...] = source[:, :half]

    part(second, sec_keep_ref, sec_send_ref)
    loads[0].wait()
    loads[1].wait()
    loads[2].wait()
    chunk = 512
    steps = w1.shape[1] // chunk

    def step(i, carry):
        cols = pl.ds(pl.multiple_of(i * chunk, chunk), chunk)
        grad_pre = dot(second[...], w2[cols, :], COLS) * gp[:, cols].astype(F32)
        bias_ref[:, cols] = jnp.sum(grad_pre, axis=0, keepdims=True)
        low = grad_pre.astype(LOW)
        there = pl.ds(pl.multiple_of(lax.rem(i, steps // 2) * chunk, chunk), chunk)
        side = (i >= steps // 2).astype(jnp.int32)

        @pl.when(side == mine)
        def _():
            keep[:, there] = low

        @pl.when(side != mine)
        def _():
            send[:, there] = low

        grad_mid[...] += dot(low, w1[:, cols], COLS)
        return carry

    lax.fori_loop(0, steps, step, 0)
    stores = [
        pltpu.make_async_copy(send, pre_send_ref, sems.at[4]),
        pltpu.make_async_copy(keep, pre_keep_ref, sems.at[5]),
    ]
    for store in stores:
        store.start()
    grad = grad_mid[...]
    n1 = n1_ref[...]
    sums_ref[3:4] = jnp.sum(grad * n1, axis=0, keepdims=True)
    sums_ref[4:5] = jnp.sum(grad, axis=0, keepdims=True)
    c = norm_back(grad, n1, s1_ref[:, :1], rows_ref[1:2])
    sums_ref[5:6] = jnp.sum(c, axis=0, keepdims=True)
    first_ref[...] = c
    second[...] = c.astype(LOW)
    part(second, fst_keep_ref, fst_send_ref)
    loads[3].wait()
    gctx_ref[...] = dot(second[...], wout[...], COLS).astype(LOW)
    for store in stores:
        store.wait()


def feed_back(layer, core, grad, n2, s2, n1, s1, rows, gp, w_out, w_ff1, w_ff2, after=()):
    tokens, width = n2.shape
    ff = gp.shape[1]
    s = jax.ShapeDtypeStruct
    v = pltpu.VMEM
    halfs = s((tokens, width // 2), LOW)
    return run(
        functools.partial(feed_back_kernel, layer),
        after,
        out_shape=(
            s((tokens, ff // 2), LOW), s((tokens, ff // 2), LOW), halfs, halfs, s((tokens, width), F32), halfs, halfs,
            s((tokens, width), LOW), s((6, width), F32), s((1, ff), F32),
        ),
        in_specs=[SM, VM, VM, VM, VM, VM, VM, ANY, ANY, ANY, ANY],
        operands=(core, grad, n2, s2, n1, s1, rows, gp, w_out, w_ff1, w_ff2),
        out_specs=(ANY, ANY) + (VM,) * 8,
        scratch_shapes=[
            v((width, width), LOW), v((width, ff), LOW), v((ff, width), LOW), v((tokens, ff), LOW), pltpu.SemaphoreType.DMA((6,)),
            v((tokens, width), LOW), v((tokens, width), F32), v((tokens, ff // 2), LOW), v((tokens, ff // 2), LOW),
        ],
        cost_estimate=pl.CostEstimate(flops=2 * tokens * width * (width + 2 * ff), bytes_accessed=20 << 20, transcendentals=0),
        name="feed_back",
    )


def attend_back_kernel(
    layer,
    core_ref, length_ref, mixed_ref, lse_ref, gctx_ref, first_ref, wqkv_hbm,
    keep_ref, send_ref, next_ref, sums_ref,
    wqkv, dmix, sems,
):
    load = pltpu.make_async_copy(wqkv_hbm.at[layer], wqkv, sems.at[0])
    load.start()
    tokens, width = first_ref.shape
    key_slot = lax.broadcasted_iota(jnp.int32, (tokens, 128), 0)
    visible = jnp.where(key_slot < length_ref[0], 0.0, -1e30)[:, :1]
    lane = lax.broadcasted_iota(jnp.int32, (tokens, 128), 1)

    def pair_step(j, carry):
        at = pl.multiple_of(j * 128, 128)
        qcols = pl.ds(at, 128)
        kcols = pl.ds(pl.multiple_of(width + at, 128), 128)
        vcols = pl.ds(pl.multiple_of(2 * width + at, 128), 128)
        q = mixed_ref[:, qcols] * jnp.asarray(SCALE, LOW)
        k = mixed_ref[:, kcols]
        v = mixed_ref[:, vcols]
        g = gctx_ref[:, qcols]
        kt = k.T
        grad_v, grad_k, grad_qt = [], [], []
        for h in range(2):
            mask = (lane < 64) == (h == 0)
            kh = jnp.where(mask, k, jnp.zeros_like(k))
            vh = jnp.where(mask, v, jnp.zeros_like(v))
            probs = jnp.exp(dot(kh, q, COLS) + visible - lse_ref[pl.ds(2 * j + h, 1), :])
            grad_probs = dot(vh, g, COLS)
            weighted = jnp.sum(probs * grad_probs, axis=0, keepdims=True)
            grad_scores = (probs * (grad_probs - weighted)).astype(LOW)
            grad_v.append(dot(probs.astype(LOW), g))
            grad_k.append(dot(grad_scores, q))
            grad_qt.append(dot(kt[h * 64 : (h + 1) * 64], grad_scores))
        grad_q = jnp.concatenate(grad_qt, axis=0).T * SCALE
        grad_v = jnp.where(lane < 64, grad_v[0], grad_v[1])
        grad_k = jnp.where(lane < 64, grad_k[0], grad_k[1])
        sums_ref[0:1, qcols] = jnp.sum(grad_q, axis=0, keepdims=True)
        sums_ref[1:2, qcols] = jnp.sum(grad_v, axis=0, keepdims=True)
        dmix[:, qcols] = grad_q.astype(LOW)
        dmix[:, kcols] = grad_k.astype(LOW)
        dmix[:, vcols] = grad_v.astype(LOW)
        return carry

    lax.fori_loop(0, HEADS // 2, pair_step, 0)
    half = 3 * width // 2
    mine = core_ref[0]

    @pl.when(mine == 0)
    def _():
        keep_ref[...] = dmix[:, :half]
        send_ref[...] = dmix[:, half:]

    @pl.when(mine == 1)
    def _():
        keep_ref[...] = dmix[:, half:]
        send_ref[...] = dmix[:, :half]

    load.wait()
    next_ref[...] = first_ref[...] + dot(dmix[...], wqkv[...], COLS)


def attend_back(layer, core, length, mixed, lse, gctx, first, w_qkv, after=()):
    tokens, width = first.shape
    s = jax.ShapeDtypeStruct
    v = pltpu.VMEM
    halfs = s((tokens, 3 * width // 2), LOW)
    return run(
        functools.partial(attend_back_kernel, layer),
        after,
        out_shape=(halfs, halfs, s((tokens, width), F32), s((2, width), F32)),
        in_specs=[SM, SM, VM, VM, VM, VM, ANY],
        operands=(core, length, mixed, lse, gctx, first, w_qkv),
        out_specs=(VM,) * 4,
        scratch_shapes=[v((width, 3 * width), LOW), v((tokens, 3 * width), LOW), pltpu.SemaphoreType.DMA((1,))],
        cost_estimate=pl.CostEstimate(
            flops=6 * tokens * width * width + 24 * tokens * tokens * width, bytes_accessed=12 << 20, transcendentals=0
        ),
        name="attend_back",
    )


COORDS = ("core", "x", "a", "b", "y")


def place(coords_ref, dims, result, keep_ref, send_ref):
    count = keep_ref.shape[0]
    for i in range(2 * count):
        block = i
        if dims is not None:
            bit = {}
            for n, dim in enumerate(dims):
                relative = (i >> (len(dims) - 1 - n)) & 1
                whole = dim == "y" and n == len(dims) - 1
                bit[dim] = relative if whole else coords_ref[COORDS.index(dim)] ^ relative
            block = 8 * bit["b"] + 4 * (bit["a"] ^ bit["b"]) + 2 * bit["x"] + bit["y"]
        if i < count:
            keep_ref[i] = result[block]
        else:
            send_ref[i - count] = result[block]


def feed_weights_kernel(
    blocks, dims_one, dims_two, coords_ref, mid_own, mid_oth, pre_own, pre_oth, sec_own, sec_oth, act_own, act_oth,
    one_keep_ref, one_send_ref, two_keep_ref, two_send_ref,
    mid, pre, sec, act, midt, sect, one, two, sems,
):
    tokens = mid_own.shape[0]
    loads = []
    for own, oth, dst in ((mid_own, mid_oth, mid), (pre_own, pre_oth, pre), (sec_own, sec_oth, sec), (act_own, act_oth, act)):
        for n, src in enumerate((own, oth)):
            load = pltpu.make_async_copy(src, dst.at[pl.ds(n * tokens, tokens)], sems.at[len(loads)])
            load.start()
            loads.append(load)
    width = mid.shape[1]
    for load in loads[:4]:
        load.wait()
    midt[...] = mid[...].T
    chunk = 512

    def step_one(i, carry):
        cols = pl.ds(pl.multiple_of(i * chunk, chunk), chunk)
        one[:, :, cols] = dot(midt[...], pre[:, cols]).astype(LOW).reshape(one.shape[:2] + (chunk,))
        return carry

    lax.fori_loop(0, pre.shape[1] // chunk, step_one, 0)
    place(coords_ref, dims_one, one, one_keep_ref, one_send_ref)
    for load in loads[4:]:
        load.wait()
    sect[...] = sec[...].T
    per = one.shape[0] // blocks
    part = act.shape[1] // blocks

    def step_two(i, carry):
        cols = pl.ds(pl.multiple_of(i * part, part), part)
        got = dot(sect[...], act[:, cols]).astype(LOW)
        for n in range(per):
            two[i * per + n] = got[n * two.shape[1] : (n + 1) * two.shape[1]]
        return carry

    lax.fori_loop(0, blocks, step_two, 0)
    place(coords_ref, dims_two, two, two_keep_ref, two_send_ref)


def feed_weights(blocks, dims_one, dims_two, coords, mid, pre, sec, act, after=()):
    tokens, width = mid[0].shape
    s = jax.ShapeDtypeStruct
    v = pltpu.VMEM
    count = 2 * blocks
    one = (count, width // count, pre[0].shape[1])
    two = (count, sec[0].shape[1] * blocks // count, act[0].shape[1] // blocks)
    half = lambda t: s((t[0] // 2,) + t[1:], LOW)
    return run(
        functools.partial(feed_weights_kernel, blocks, dims_one, dims_two),
        after,
        out_shape=(half(one), half(one), half(two), half(two)),
        in_specs=[SM] + [ANY] * 8,
        operands=(coords, *mid, *pre, *sec, *act),
        out_specs=(VM,) * 4,
        scratch_shapes=[
            v((2 * tokens, width), LOW), v((2 * tokens, pre[0].shape[1]), LOW), v((2 * tokens, sec[0].shape[1]), LOW),
            v((2 * tokens, act[0].shape[1]), LOW), v((width, 2 * tokens), LOW), v((sec[0].shape[1], 2 * tokens), LOW),
            v(one, LOW), v(two, LOW), pltpu.SemaphoreType.DMA((8,)),
        ],
        cost_estimate=pl.CostEstimate(
            flops=4 * tokens * (width * pre[0].shape[1] + sec[0].shape[1] * act[0].shape[1]), bytes_accessed=16 << 20, transcendentals=0
        ),
        name="feed_weights",
    )


def attend_weights_kernel(
    dims,
    coords_ref, x_own, x_oth, mix_own, mix_oth, ctx_own, ctx_oth, fst_own, fst_oth,
    keep_ref, send_ref,
    x, mix, ctxt, fst, xt, res, sems,
):
    tokens = x_own.shape[0]
    loads = []
    for own, oth, dst in ((x_own, x_oth, x), (mix_own, mix_oth, mix), (fst_own, fst_oth, fst)):
        for n, src in enumerate((own, oth)):
            loads.append(pltpu.make_async_copy(src, dst.at[pl.ds(n * tokens, tokens)], sems.at[len(loads)]))
    for n, src in enumerate((ctx_own, ctx_oth)):
        loads.append(pltpu.make_async_copy(src, ctxt.at[:, pl.ds(n * tokens, tokens)], sems.at[len(loads)]))
    for load in loads:
        load.start()
    loads[0].wait()
    loads[1].wait()
    xt[...] = x[...].T
    for load in loads[2:]:
        load.wait()
    chunk = fst.shape[1]
    steps = mix.shape[1] // chunk
    shape = res.shape[:2] + (chunk,)
    for i in range(steps):
        res[:, :, i * chunk : (i + 1) * chunk] = dot(xt[...], mix[:, i * chunk : (i + 1) * chunk]).astype(LOW).reshape(shape)
    res[:, :, steps * chunk :] = dot(ctxt[...], fst[...]).astype(LOW).reshape(shape)
    place(coords_ref, dims, res, keep_ref, send_ref)


def attend_weights(blocks, dims, coords, x, mix, ctx, fst, after=()):
    tokens, width = x[0].shape
    s = jax.ShapeDtypeStruct
    v = pltpu.VMEM
    count = 2 * blocks
    cols = mix[0].shape[1] + fst[0].shape[1]
    res = (count, width // count, cols)
    half = s((count // 2,) + res[1:], LOW)
    return run(
        functools.partial(attend_weights_kernel, dims),
        after,
        out_shape=(half, half),
        in_specs=[SM] + [ANY] * 8,
        operands=(coords, *x, *mix, *ctx, *fst),
        out_specs=(VM, VM),
        scratch_shapes=[
            v((2 * tokens, width), LOW), v((2 * tokens, mix[0].shape[1]), LOW), v((width, 2 * tokens), LOW),
            v((2 * tokens, fst[0].shape[1]), LOW), v((width, 2 * tokens), LOW), v(res, LOW), pltpu.SemaphoreType.DMA((8,)),
        ],
        cost_estimate=pl.CostEstimate(flops=4 * tokens * width * cols, bytes_accessed=10 << 20, transcendentals=0),
        name="attend_weights",
    )


AXES = ("dp", "vocab")
VOCAB_MASK = {"x": 1, "a": 2, "b": 6}


def add(left_op, right_op):
    return (left_op.astype(F32) + right_op.astype(F32)).astype(LOW)


class Cube:
    def __init__(self, dp_size, vocab_size):
        self.dp_size = dp_size
        self.vocab_size = vocab_size
        self.dp_bits = dp_size.bit_length() - 1
        self.vocab_bits = vocab_size.bit_length() - 1
        assert 1 << self.dp_bits == dp_size and 1 << self.vocab_bits == vocab_size
        self.small = self.dp_bits == 2 and self.vocab_bits == 3

    def permute(self, value, dp_mask, vocab_mask):
        count = self.vocab_size
        pairs = [
            (d * count + v, (d ^ dp_mask) * count + (v ^ vocab_mask))
            for d in range(self.dp_size)
            for v in range(count)
        ]
        return lax.ppermute(value, AXES, pairs)

    def core(self, value):
        return self.permute(value, 1, 0)

    def along(self, value, dim):
        return self.permute(value, 2, 0) if dim == "y" else self.permute(value, 0, VOCAB_MASK[dim])

    def core_is_first(self):
        return (lax.axis_index("dp") & 1) == 0

    def coords(self):
        dp, vocab = lax.axis_index("dp"), lax.axis_index("vocab")
        b = (vocab >> 2) & 1
        return jnp.stack([dp & 1, vocab & 1, ((vocab >> 1) & 1) ^ b, b, (dp >> 1) & 1])

    def halves(self, matrix):
        mine = lax.axis_index("dp") & 1
        width = matrix.shape[1] // 2
        keep = lax.dynamic_slice_in_dim(matrix, mine * width, width, 1)
        send = lax.dynamic_slice_in_dim(matrix, (1 - mine) * width, width, 1)
        return keep, send

    def ordered(self, first, mine, other, axis):
        return jnp.concatenate(
            [jnp.where(first, mine, other), jnp.where(first, other, mine)], axis=axis
        )

    def join_core(self, share, axis):
        return self.ordered(self.core_is_first(), share, self.core(share), axis).astype(F32)

    def reduce(self, matrix):
        for bit in reversed(range(self.vocab_bits)):
            mine = (lax.axis_index("vocab") >> bit) & 1
            rows = matrix.shape[0] // 2
            keep = lax.dynamic_slice_in_dim(matrix, mine * rows, rows, 0)
            send = lax.dynamic_slice_in_dim(matrix, (1 - mine) * rows, rows, 0)
            matrix = add(keep, self.permute(send, 0, 1 << bit))
        for bit in range(1, self.dp_bits):
            matrix = add(matrix, self.permute(matrix, 1 << bit, 0))
        return matrix


class Chain:
    def __init__(self, cube, dims, keep, send):
        self.cube, self.dims, self.keep, self.send = cube, dims, keep, send
        self.got = []
        for n, dim in enumerate(dims):
            if dim == "y" and n == len(dims) - 1:
                got = cube.along(self.keep, "y")
                self.got.append(got)
                self.keep = add(self.keep, got)
                break
            got = cube.along(self.send, dim)
            self.got.append(got)
            half = self.keep.shape[0] // 2
            last = n == len(dims) - 1 or (n == len(dims) - 2 and dims[-1] == "y")
            if last:
                self.keep = add(self.keep, got)
            else:
                self.keep, self.send = (
                    add(self.keep[:half], got[:half]),
                    add(self.keep[half:], got[half:]),
                )
        if dims[-1] != "y":
            other = cube.along(self.keep, "y")
            first = ((lax.axis_index("dp") >> 1) & 1) == 0
            self.share = cube.ordered(first, self.keep, other, 0)
        else:
            self.share = self.keep
        self.share = self.share.reshape(-1, self.share.shape[-1])


def on_device(
    cube,
    token_ids,
    lengths,
    type_ids,
    word_table,
    pos_table,
    type_table,
    gains,
    shifts,
    w_qkv,
    w_out,
    b_ff1,
    w_ff1,
    w_ff2,
    cotangent,
):
    owners = cube.vocab_size
    local_rows, width = word_table.shape
    assert token_ids.shape[0] == 1
    tokens = token_ids.shape[1]
    slot_count = 2 * tokens // owners
    slots = owners * slot_count
    gain_vals = gains.astype(F32)
    shift_vals = shifts.astype(F32)
    flat_ids = token_ids.reshape(tokens)
    me = lax.axis_index("vocab")
    coords = cube.coords()

    all_ids = lax.all_to_all(
        jnp.broadcast_to(flat_ids[None, :], (owners, tokens)), "vocab", split_axis=0, concat_axis=0, tiled=True
    )
    local = all_ids - me * local_rows
    here = (local >= 0) & (local < local_rows)
    rank = jnp.cumsum(here.astype(jnp.int32), axis=1) - 1
    slot_hit = (
        jnp.where(here, rank, -1)[:, None, :] == jnp.arange(slot_count, dtype=jnp.int32)[None, :, None]
    )
    asked = jnp.sum(jnp.where(slot_hit, local[:, None, :] + 1, 0), axis=2).reshape(slots) - 1
    row_hit = (asked[:, None] == jnp.arange(local_rows, dtype=jnp.int32)[None, :]).astype(LOW)
    found_rows = dot(row_hit, word_table).astype(LOW)
    replies = lax.all_to_all(
        found_rows.reshape(owners, slot_count, width), "vocab", split_axis=0, concat_axis=0, tiled=True
    ).reshape(slots, width)
    owner_of = flat_ids // local_rows
    chosen = (owner_of[:, None] == jnp.arange(owners, dtype=jnp.int32)[None, :]).astype(jnp.int32)
    before = jnp.cumsum(chosen, axis=0) - chosen
    slot_of = owner_of * slot_count + jnp.sum(before * chosen, axis=1)
    dispatch = (slot_of[:, None] == jnp.arange(slots, dtype=jnp.int32)[None, :]).astype(LOW)
    word_rows = dot(dispatch, replies)
    type_flat = type_ids.reshape(tokens)
    type_rows = jnp.where(type_flat[:, None] == 1, type_table[1].astype(F32)[None, :], type_table[0].astype(F32)[None, :])
    embedded = word_rows + pos_table.astype(F32) + type_rows
    normed_emb, spread_emb = normalize(embedded)
    states = normed_emb * gain_vals[0] + shift_vals[0]

    saved, layer_rows = [], []
    for layer in range(NL):
        base = 1 + 6 * layer
        rows = jnp.stack(
            [
                shift_vals[base + 2],
                gain_vals[1 + 2 * layer],
                shift_vals[base + 3],
                shift_vals[base + 4],
                gain_vals[2 + 2 * layer],
                shift_vals[base + 5],
            ]
        )
        qkv_bias = jnp.concatenate([shift_vals[base], jnp.zeros((width,), F32), shift_vals[base + 1]])[None, :]
        ffn_bias = b_ff1[layer].astype(F32)[None, :]
        out = forward_layer(layer, lengths, states, rows, qkv_bias, ffn_bias, w_qkv, w_out, w_ff1, w_ff2)
        xlow, mixed, lse, ctxt, n1, s1, mlow, gp, act, n2, s2, states = out
        saved.append((mixed, lse, n1, s1, gp, n2, s2) + tuple((own, cube.core(own)) for own in (xlow, ctxt, mlow, act)))
        layer_rows.append(rows)
    hidden_out = states.astype(LOW).reshape(1, tokens, width)

    small = cube.small
    blocks = 8
    plans = {1: (("x", "a", "b", "y"), ("a", "b", "x", "y"), ("b", "x", "a", "y")),
             0: (("y", "x", "a", "b"), ("x", "a", "b", "y"), ("a", "b", "x", "y"))}
    gain_grads = [None] * (2 * NL + 1)
    shift_grads = [None] * (6 * NL + 1)
    bias_grads = [None] * NL
    shares = [None] * NL
    grad = cotangent.reshape(tokens, width)
    core = coords[:1]
    for layer in reversed(range(NL)):
        base = 1 + 6 * layer
        mixed, lse, n1, s1, gp, n2, s2, x2, ctx2, mid2, act2 = saved[layer]
        plan = plans[layer] if small else (None, None, None)
        pre_keep, pre_send, sec_keep, sec_send, first, fst_keep, fst_send, gctx, sums, bias = feed_back(
            layer, core, grad, n2, s2, n1, s1, layer_rows[layer], gp, w_out, w_ff1, w_ff2
        )
        gain_grads[2 + 2 * layer] = sums[0]
        shift_grads[base + 5] = sums[1]
        shift_grads[base + 4] = sums[2]
        gain_grads[1 + 2 * layer] = sums[3]
        shift_grads[base + 3] = sums[4]
        shift_grads[base + 2] = sums[5]
        bias_grads[layer] = bias[0]
        pre2 = (pre_keep, cube.core(pre_send))
        sec2 = (sec_keep, cube.core(sec_send))
        fst2 = (fst_keep, cube.core(fst_send))
        mix_keep, mix_send, grad, att_sums = attend_back(layer, core, lengths, mixed, lse, gctx, first, w_qkv)
        shift_grads[base] = att_sums[0]
        shift_grads[base + 1] = att_sums[1]
        mix2 = (mix_keep, cube.core(mix_send))
        one = feed_weights(blocks, plan[0], plan[1], coords, mid2, pre2, sec2, act2, after=())
        mix = attend_weights(blocks, plan[2], coords, x2, mix2, ctx2, fst2, after=one[:1])
        if small:
            chains = [
                Chain(cube, plan[0], one[0], one[1]),
                Chain(cube, plan[1], one[2], one[3]),
                Chain(cube, plan[2], mix[0], mix[1]),
            ]
            share_one, share_two, share_mix = [chain.share for chain in chains]
            if layer == 1:
                grad = lax.optimization_barrier((grad, mix[0]))[0]
        else:
            whole = lambda keep, send: jnp.concatenate([keep, send], axis=0)
            share_one = cube.reduce(whole(one[0], one[1]).reshape(width, -1))
            two = whole(one[2], one[3])
            two = two.reshape(blocks, width // 2, -1).transpose(0, 2, 1).reshape(-1, width // 2)
            share_two = cube.reduce(two).T
            share_mix = cube.reduce(whole(mix[0], mix[1]).reshape(width, -1))
        shares[layer] = (share_one, share_two, share_mix)

    gain_grads[0] = jnp.sum(grad * normed_emb, axis=0)
    shift_grads[0] = jnp.sum(grad, axis=0)
    grad_embedded = norm_back(grad, normed_emb, spread_emb, gain_vals[0])
    emb_low = grad_embedded.astype(LOW)
    outgoing = dot(dispatch, emb_low, ROWS).astype(LOW)
    incoming = lax.all_to_all(
        outgoing.reshape(owners, slot_count, width), "vocab", split_axis=0, concat_axis=0, tiled=True
    ).reshape(slots, width)
    table_part = dot(row_hit, incoming, ROWS).astype(LOW)
    keep, send = cube.halves(table_part)
    table_part = add(keep, cube.core(send))
    for bit in range(1, cube.dp_bits):
        table_part = add(table_part, cube.permute(table_part, 1 << bit, 0))
    table_out = cube.join_core(table_part, -1)

    type_zero = jnp.sum(jnp.where(type_flat[:, None] == 0, grad_embedded, 0.0), axis=0)
    type_one = jnp.sum(jnp.where(type_flat[:, None] == 1, grad_embedded, 0.0), axis=0)
    share_width = width // owners
    small_sums = jnp.concatenate(
        [
            jnp.stack([type_zero, type_one] + gain_grads + shift_grads).reshape(-1, owners, share_width),
            jnp.stack(bias_grads).reshape(NL, owners, -1, share_width).transpose(0, 2, 1, 3).reshape(-1, owners, share_width),
        ],
        axis=0,
    )
    small_rows = small_sums.shape[0]
    small_sums = small_sums.transpose(1, 0, 2).reshape(owners, -1)
    packed_rows = -(-small_sums.shape[1] // width)
    small_sums = jnp.pad(small_sums, ((0, 0), (0, packed_rows * width - small_sums.shape[1])))
    pos_rows = tokens // owners
    packed = jnp.concatenate(
        [grad_embedded.reshape(owners, pos_rows, width), small_sums.reshape(owners, packed_rows, width)], axis=1
    ).astype(LOW)
    keep, send = cube.halves(packed.reshape(-1, width))
    share_pack = cube.reduce(add(keep, cube.core(send)))

    wide = 3 * width // 2
    one_out = cube.join_core(jnp.stack([share[0] for share in shares]), 2)
    two_out = cube.join_core(jnp.stack([share[1] for share in shares]), 1).transpose(0, 2, 1)
    mix = jnp.stack([share[2] for share in shares])
    mix_other = cube.core(mix)
    first = cube.core_is_first()
    qkv_out = cube.ordered(first, mix[..., :wide], mix_other[..., :wide], 2).astype(F32)
    wout_out = cube.ordered(first, mix[..., wide:], mix_other[..., wide:], 2).astype(F32)
    pack_out = cube.join_core(share_pack, 1)
    pos_out = pack_out[:pos_rows]
    small_out = pack_out[pos_rows:].reshape(-1)[: small_rows * share_width].reshape(small_rows, share_width)
    at_gain, at_shift, at_bias = 2, 2 + 2 * NL + 1, 2 + 2 * NL + 1 + 6 * NL + 1
    return (
        hidden_out,
        table_out,
        pos_out,
        small_out[:at_gain],
        small_out[at_gain:at_shift],
        small_out[at_shift:at_bias],
        qkv_out,
        wout_out,
        small_out[at_bias:].reshape(NL, -1),
        one_out,
        two_out,
    )


def solution(mesh):
    cube = Cube(mesh.shape["dp"], mesh.shape["vocab"])
    both = ("dp", "vocab")
    in_specs = (
        P(both, None),
        P(both),
        P(both, None),
        P("vocab", None),
        P(),
        P(),
        P(),
        P(),
        P(),
        P(),
        P(),
        P(),
        P(),
        P(both, None, None),
    )
    out_specs = (
        P(both, None, None),
        P("vocab", None),
        P("vocab", None),
        P(None, "vocab"),
        P(None, "vocab"),
        P(None, "vocab"),
        P(None, "vocab", None),
        P(None, "vocab", None),
        P(None, "vocab"),
        P(None, "vocab", None),
        P(None, "vocab", None),
    )
    return jax.shard_map(
        functools.partial(on_device, cube), mesh=mesh, in_specs=in_specs, out_specs=out_specs, check_vma=False
    )
```

```python
import functools
import jax
import jax.numpy as jnp
from jax import lax
from jax.experimental import pallas as pl
from jax.experimental.pallas import tpu as pltpu
from jax.sharding import PartitionSpec as P

HEADS = 12
HEAD_DIM = 64
NL = 2
norm_eps = 1e-12
SCALE = HEAD_DIM ** (-0.5)
ANY = pl.BlockSpec(memory_space=pl.ANY)
HBM = pl.BlockSpec(memory_space=pltpu.HBM)
VM = pl.BlockSpec(memory_space=pltpu.VMEM)
SM = pl.BlockSpec(memory_space=pltpu.SMEM)
F32, LOW = jnp.float32, jnp.bfloat16

CHEAP = pl.CostEstimate(flops=1, bytes_accessed=1, transcendentals=0)
DEAR = pl.CostEstimate(flops=10**10, bytes_accessed=1, transcendentals=0)
LONG = pl.CostEstimate(flops=10**11, bytes_accessed=1, transcendentals=0)


def run(kernel, after, out_shape, in_specs, operands, vmem, **options):
    count = len(operands)

    def body(*refs):
        kernel(*refs[:count], *refs[count + len(after) :])

    return pl.pallas_call(
        body,
        out_shape=out_shape,
        in_specs=list(in_specs) + [ANY] * len(after),
        compiler_params=pltpu.CompilerParams(vmem_limit_bytes=vmem * 1024 * 1024),
        **options,
    )(*operands, *after)


def normalize(inputs):
    centered = inputs - jnp.mean(inputs, axis=-1, keepdims=True)
    spread = lax.rsqrt(jnp.mean(centered * centered, axis=-1, keepdims=True) + norm_eps)
    return (centered * spread, spread)


def norm_back(grad_out, normed, spread, gain_row):
    scaled = grad_out * gain_row
    return spread * (
        scaled
        - jnp.mean(scaled, axis=-1, keepdims=True)
        - normed * jnp.mean(scaled * normed, axis=-1, keepdims=True)
    )


def dot(left_op, right_op, dims=((1,), (0,))):
    return lax.dot_general(left_op, right_op, (dims, ((), ())), preferred_element_type=F32)


ROWS = ((0,), (0,))
COLS = ((1,), (1,))


def gelu_pair(inputs):
    size = jnp.abs(inputs)
    bell = jnp.exp2(inputs * inputs * (-0.5 * 1.4426950408889634))
    t = 1.0 / (1.0 + size * (0.3275911 * 0.7071067811865476))
    tail = t * (
        0.5 * 0.254829592
        + t * (0.5 * -0.284496736 + t * (0.5 * 1.421413741 + t * (0.5 * -1.453152027 + t * (0.5 * 1.061405429))))
    )
    tail = tail * bell
    phi = jnp.where(inputs >= 0.0, 1.0 - tail, tail)
    return inputs * phi, phi + inputs * bell * 0.3989422804014327


def forward_kernel(
    coords_ref, length_ref, replies_ref, slot_ref, kind_ref, pos_ref, type_ref, gains_ref, shifts_ref, ffn_bias_ref,
    grad_ref, wqkv_hbm, wout_hbm, w1_hbm, w2_hbm,
    *refs,
):
    n0_ref, s0_ref, hidden_ref = refs[:3]
    top = refs[3:8]
    outs = [refs[8 + 11 * layer : 19 + 11 * layer] for layer in range(NL)]
    wqkv, wout, w1, w2, sems, xlow, mixed, ctxt, mlow, gp, act, n0, n1, n2, x, osems = refs[6 + 11 * NL :]
    tokens, width = x.shape
    ff = w1.shape[2]
    loads = []
    for layer in range(NL):
        for i, (src, dst) in enumerate([(wqkv_hbm, wqkv), (wout_hbm, wout), (w1_hbm, w1), (w2_hbm, w2)]):
            loads.append(pltpu.make_async_copy(src.at[layer], dst.at[layer], sems.at[4 * layer + i]))
    for load in loads:
        load.start()
    pending, used = {}, [0]

    def emit(name, src, dst, at=None):
        if at is not None:
            src, dst = src.at[:, at], dst.at[:, at]
        copy = pltpu.make_async_copy(src, dst, osems.at[used[0]])
        used[0] += 1
        copy.start()
        pending.setdefault(name, []).append(copy)

    def reuse(name):
        for copy in pending.pop(name, ()):
            copy.wait()

    gains = gains_ref[...].astype(F32)
    shifts = shifts_ref[...].astype(F32)
    number = lax.broadcasted_iota(jnp.int32, (tokens, replies_ref.shape[0]), 1)
    hit = jnp.where(number == slot_ref[:, :1], 1.0, 0.0).astype(LOW)
    types = type_ref[...].astype(F32)
    embedded = dot(hit, replies_ref[...]) + pos_ref[...].astype(F32)
    embedded = embedded + jnp.where(kind_ref[:, :1] > 0.5, types[1:2], types[0:1])
    normed, spread = normalize(embedded)
    n0[...] = normed
    emit("n0", n0, n0_ref)
    s0_ref[...] = jnp.broadcast_to(spread, s0_ref.shape)
    x[...] = normed * gains[0:1] + shifts[0:1]

    key_slot = lax.broadcasted_iota(jnp.int32, (tokens, 128), 0)
    visible = jnp.where(key_slot < length_ref[0], 0.0, -1e30)[:, :1]
    lane = lax.broadcasted_iota(jnp.int32, (tokens, 128), 1)
    chunk = 512

    for layer in range(NL):
        base = 1 + 6 * layer
        xlow_ref, mixed_ref, lse_ref, ctxt_ref, n1_ref, s1_ref, mlow_ref, gp_ref, act_ref = outs[layer][:9]

        reuse("xlow")
        xlow[...] = x[...].astype(LOW)
        emit("xlow", xlow, xlow_ref)
        loads[4 * layer].wait()
        reuse("mixed")
        for i in range(3):
            cols = slice(i * width, (i + 1) * width)
            got = dot(xlow[...], wqkv[layer, :, cols])
            if i != 1:
                row = base + (0 if i == 0 else 1)
                got = got + shifts[row : row + 1]
            mixed[:, cols] = got.astype(LOW)
        emit("mixed", mixed, mixed_ref)
        reuse("ctxt")

        def pair_step(j, carry):
            at = pl.multiple_of(j * 128, 128)
            q = mixed[:, pl.ds(at, 128)] * jnp.asarray(SCALE, LOW)
            k = mixed[:, pl.ds(pl.multiple_of(width + at, 128), 128)]
            v = mixed[:, pl.ds(pl.multiple_of(2 * width + at, 128), 128)]
            vt = v.T
            for h in range(2):
                kh = jnp.where((lane < 64) == (h == 0), k, jnp.zeros_like(k))
                scores = dot(kh, q, COLS) + visible
                top = jnp.max(scores, axis=0, keepdims=True)
                weights = jnp.exp(scores - top)
                total = jnp.sum(weights, axis=0, keepdims=True)
                out = dot(vt[h * 64 : (h + 1) * 64], weights.astype(LOW)) * (1.0 / total)
                ctxt[pl.ds(pl.multiple_of(at + h * 64, 64), 64), :] = out.astype(LOW)
                lse_ref[pl.ds(2 * j + h, 1), :] = top + jnp.log(total)
            return carry

        lax.fori_loop(0, HEADS // 2, pair_step, 0)
        emit("ctxt", ctxt, ctxt_ref)
        loads[4 * layer + 1].wait()
        attended = dot(ctxt[...], wout[layer], ROWS) + shifts[base + 2 : base + 3]
        normed, spread = normalize(x[...] + attended)
        reuse("n1")
        n1[...] = normed
        emit("n1", n1, n1_ref)
        s1_ref[...] = jnp.broadcast_to(spread, s1_ref.shape)
        x[...] = normed * gains[1 + 2 * layer : 2 + 2 * layer] + shifts[base + 3 : base + 4]
        reuse("mlow")
        mlow[...] = x[...].astype(LOW)
        emit("mlow", mlow, mlow_ref)
        loads[4 * layer + 2].wait()
        reuse("gp")
        reuse("act")
        for i in range(ff // chunk):
            cols = slice(i * chunk, (i + 1) * chunk)
            pre = dot(mlow[...], w1[layer, :, cols]) + ffn_bias_ref[layer : layer + 1, cols]
            active, slope = gelu_pair(pre)
            gp[:, cols] = slope.astype(LOW)
            act[:, cols] = active.astype(LOW)
            emit("gp", gp, gp_ref, pl.ds(i * chunk, chunk))
            emit("act", act, act_ref, pl.ds(i * chunk, chunk))
        loads[4 * layer + 3].wait()
        normed, spread = normalize(x[...] + shifts[base + 4 : base + 5] + dot(act[...], w2[layer]))
        if layer < NL - 1:
            n2_ref, s2_ref = outs[layer][9:11]
            n2[...] = normed
            emit("n2", n2, n2_ref)
            s2_ref[...] = jnp.broadcast_to(spread, s2_ref.shape)
        else:
            gain = gains[2 * NL : 2 * NL + 1]
            norm_end(coords_ref[0], grad_ref[...].astype(F32), normed, spread, gain, *top)
        x[...] = normed * gains[2 + 2 * layer : 3 + 2 * layer] + shifts[base + 5 : base + 6]
    hidden_ref[...] = x[...].astype(LOW)
    for name in list(pending):
        reuse(name)


def forward(
    coords, length, replies, slot_col, kind_col, pos, types, gains, shifts, ffn_bias, cotangent, w_qkv, w_out, w_ff1, w_ff2
):
    tokens, width = pos.shape
    ff = w_ff1.shape[2]
    s = jax.ShapeDtypeStruct
    v = pltpu.VMEM
    spread = s((tokens, 128), F32)
    wide = s((tokens, width), F32)
    low = s((tokens, width), LOW)
    layer_out = (
        low, s((tokens, 3 * width), LOW), s((HEADS, tokens), F32), s((width, tokens), LOW),
        wide, spread, low, s((tokens, ff), LOW), s((tokens, ff), LOW), wide, spread,
    )
    layer_spec = (ANY, ANY, VM, ANY, ANY, VM, ANY, ANY, ANY, ANY, VM)
    chunks = ff // 512
    end = norm_end_shapes(tokens, width)
    outs = run(
        forward_kernel,
        (),
        out_shape=(wide, spread, low) + end + layer_out * (NL - 1) + layer_out[:9],
        in_specs=[SM, SM] + [VM] * 9 + [HBM] * 4,
        operands=(
            coords, length, replies, slot_col, kind_col, pos, types, gains, shifts, ffn_bias, cotangent, w_qkv, w_out, w_ff1, w_ff2
        ),
        out_specs=(ANY, VM, VM) + (VM,) * 5 + layer_spec * (NL - 1) + layer_spec[:9],
        scratch_shapes=[
            v((NL, width, 3 * width), LOW), v((NL, width, width), LOW), v((NL, width, ff), LOW), v((NL, ff, width), LOW),
            pltpu.SemaphoreType.DMA((4 * NL,)),
            v((tokens, width), LOW), v((tokens, 3 * width), LOW), v((width, tokens), LOW), v((tokens, width), LOW),
            v((tokens, ff), LOW), v((tokens, ff), LOW), v((tokens, width), F32), v((tokens, width), F32),
            v((tokens, width), F32), v((tokens, width), F32), pltpu.SemaphoreType.DMA((1 + NL * (6 + 2 * chunks),)),
        ],
        cost_estimate=CHEAP,
        vmem=60,
        name="forward",
    )
    return outs[:3], outs[3:8], [outs[8 + 11 * layer : 19 + 11 * layer] for layer in range(NL)]


def part(mine, source, keep_to, send_to):
    half = source.shape[1] // 2

    @pl.when(mine == 0)
    def _():
        keep_to[...] = source[:, :half]
        send_to[...] = source[:, half:]

    @pl.when(mine == 1)
    def _():
        keep_to[...] = source[:, half:]
        send_to[...] = source[:, :half]


def norm_end(mine, grad, n, s, gain, back_ref, low_ref, keep_ref, send_ref, sums_ref):
    sums_ref[0:1] = jnp.sum(grad * n, axis=0, keepdims=True)
    sums_ref[1:2] = jnp.sum(grad, axis=0, keepdims=True)
    back = norm_back(grad, n, s, gain)
    sums_ref[2:3] = jnp.sum(back, axis=0, keepdims=True)
    back_ref[...] = back
    low_ref[...] = back.astype(LOW)
    if keep_ref is not None:
        part(mine, low_ref, keep_ref, send_ref)


def norm_end_shapes(tokens, width):
    s = jax.ShapeDtypeStruct
    half = s((tokens, width // 2), LOW)
    return (s((tokens, width), F32), s((tokens, width), LOW), half, half, s((3, width), F32))


def feed_back_body(mine, second, gp, w2, ready, bias_ref, keep, send):
    chunk = 512
    steps = gp.shape[1] // chunk
    for i in range(steps):
        ready(i)
        cols = slice(i * chunk, (i + 1) * chunk)
        grad_pre = dot(second[...], w2[cols, :], COLS) * gp[:, cols].astype(F32)
        bias_ref[:, cols] = jnp.sum(grad_pre, axis=0, keepdims=True)
        side, at = divmod(i, steps // 2)
        there = slice(at * chunk, (at + 1) * chunk)
        low = grad_pre.astype(LOW)

        @pl.when(mine == side)
        def _():
            keep[:, there] = low

        @pl.when(mine != side)
        def _():
            send[:, there] = low


def both_halves(mine, keep, send, weight):
    half = keep.shape[1]
    first = jnp.where(mine == 0, keep[...], send[...])
    second = jnp.where(mine == 0, send[...], keep[...])
    return dot(first, weight[:, :half], COLS) + dot(second, weight[:, half:], COLS)


def attend_back_body(length_ref, mixed_ref, lse_ref, gctx_ref, att_ref, dmix):
    tokens, width = gctx_ref.shape
    key_slot = lax.broadcasted_iota(jnp.int32, (tokens, 128), 0)
    visible = jnp.where(key_slot < length_ref[0], 0.0, -1e30)[:, :1]
    lane = lax.broadcasted_iota(jnp.int32, (tokens, 128), 1)

    def pair_step(j, carry):
        at = pl.multiple_of(j * 128, 128)
        qcols = pl.ds(at, 128)
        kcols = pl.ds(pl.multiple_of(width + at, 128), 128)
        vcols = pl.ds(pl.multiple_of(2 * width + at, 128), 128)
        q = mixed_ref[:, qcols] * jnp.asarray(SCALE, LOW)
        k = mixed_ref[:, kcols]
        v = mixed_ref[:, vcols]
        g = gctx_ref[:, qcols]
        kt = k.T
        grad_v, grad_k, grad_qt = [], [], []
        for h in range(2):
            mask = (lane < 64) == (h == 0)
            kh = jnp.where(mask, k, jnp.zeros_like(k))
            vh = jnp.where(mask, v, jnp.zeros_like(v))
            probs = jnp.exp(dot(kh, q, COLS) + visible - lse_ref[pl.ds(2 * j + h, 1), :])
            grad_probs = dot(vh, g, COLS)
            weighted = jnp.sum(probs * grad_probs, axis=0, keepdims=True)
            grad_scores = (probs * (grad_probs - weighted)).astype(LOW)
            grad_v.append(dot(probs.astype(LOW), g))
            grad_k.append(dot(grad_scores, q))
            grad_qt.append(dot(kt[h * 64 : (h + 1) * 64], grad_scores))
        grad_q = jnp.concatenate(grad_qt, axis=0).T * SCALE
        grad_v = jnp.where(lane < 64, grad_v[0], grad_v[1])
        grad_k = jnp.where(lane < 64, grad_k[0], grad_k[1])
        att_ref[0:1, qcols] = jnp.sum(grad_q, axis=0, keepdims=True)
        att_ref[1:2, qcols] = jnp.sum(grad_v, axis=0, keepdims=True)
        dmix[:, qcols] = grad_q.astype(LOW)
        dmix[:, kcols] = grad_k.astype(LOW)
        dmix[:, vcols] = grad_v.astype(LOW)
        return carry

    lax.fori_loop(0, HEADS // 2, pair_step, 0)


def chunk_loads(sems, at, pairs, chunk=512):
    loads = []
    (w2_src, w2), (gp_src, gp) = pairs
    for i in range(gp.shape[1] // chunk):
        there = pl.ds(i * chunk, chunk)
        loads.append(
            (
                pltpu.make_async_copy(w2_src.at[there], w2.at[there], sems.at[at + 2 * i]),
                pltpu.make_async_copy(gp_src.at[:, there], gp.at[:, there], sems.at[at + 2 * i + 1]),
            )
        )
    return loads


def feed_kernel(
    layer, coords_ref, e_ref, second, n1_ref, s1_ref, gains_ref, gp_hbm, wout_hbm, w1_hbm, w2_hbm,
    keep_ref, send_ref, bias_ref, first_ref, low_ref, fst_keep_ref, fst_send_ref, gctx_ref, sums_ref,
    gp, wout, w1, w2, keep, send, sems,
):
    mine = coords_ref[0]
    loads = chunk_loads(sems, 4, ((w2_hbm.at[layer], w2), (gp_hbm, gp)))
    for pair in loads:
        for load in pair:
            load.start()
    late = [
        pltpu.make_async_copy(w1_hbm.at[layer], w1, sems.at[0]),
        pltpu.make_async_copy(wout_hbm.at[layer], wout, sems.at[1]),
    ]
    for load in late:
        load.start()

    def ready(i):
        for load in loads[i]:
            load.wait()

    feed_back_body(mine, second, gp, w2, ready, bias_ref, keep, send)
    stores = [
        pltpu.make_async_copy(send, send_ref, sems.at[2]),
        pltpu.make_async_copy(keep, keep_ref, sems.at[3]),
    ]
    for store in stores:
        store.start()
    late[0].wait()
    grad = e_ref[...] + both_halves(mine, keep, send, w1)
    gain = gains_ref[...].astype(F32)[1 + 2 * layer : 2 + 2 * layer]
    norm_end(mine, grad, n1_ref[...], s1_ref[:, :1], gain, first_ref, low_ref, fst_keep_ref, fst_send_ref, sums_ref)
    late[1].wait()
    gctx_ref[...] = dot(low_ref[...], wout[...], COLS).astype(LOW)
    for store in stores:
        store.wait()


def feed(layer, coords, e, second, n1, s1, gains, gp, w_out, w_ff1, w_ff2, after=()):
    tokens, width = n1.shape
    ff = gp.shape[1]
    s = jax.ShapeDtypeStruct
    v = pltpu.VMEM
    half = s((tokens, ff // 2), LOW)
    end = norm_end_shapes(tokens, width)
    return run(
        functools.partial(feed_kernel, layer),
        after,
        out_shape=(half, half, s((1, ff), F32)) + end[:4] + (s((tokens, width), LOW), end[4]),
        in_specs=[SM] + [VM] * 5 + [HBM] * 4,
        operands=(coords, e, second, n1, s1, gains, gp, w_out, w_ff1, w_ff2),
        out_specs=(ANY, ANY) + (VM,) * 7,
        scratch_shapes=[
            v((tokens, ff), LOW), v((width, width), LOW), v((width, ff), LOW), v((ff, width), LOW),
            v((tokens, ff // 2), LOW), v((tokens, ff // 2), LOW), pltpu.SemaphoreType.DMA((4 + 2 * (ff // 512),)),
        ],
        cost_estimate=CHEAP,
        vmem=52,
        name="feed",
    )


def between_kernel(
    layer, coords_ref, length_ref, mixed_ref, lse_ref, gctx_in, first_in, n2_ref, s2_ref, n1_ref, s1_ref, gains_ref,
    gp_hbm, wqkv_hbm, wout_hbm, w1_hbm, w2_hbm,
    mix_keep_ref, mix_send_ref, pre_keep_ref, pre_send_ref,
    att_ref, sec_keep_ref, sec_send_ref, top_ref, bias_ref, first_ref, low_ref, gctx_ref, sums_ref,
    gp, wqkv, wout, w1, w2, dmix, mix_keep, mix_send, keep, send, e, second, sems,
):
    mine = coords_ref[0]
    below = layer - 1
    early = pltpu.make_async_copy(wqkv_hbm.at[layer], wqkv, sems.at[0])
    early.start()
    loads = chunk_loads(sems, 7, ((w2_hbm.at[below], w2), (gp_hbm, gp)))
    for pair in loads:
        for load in pair:
            load.start()
    late = [
        pltpu.make_async_copy(w1_hbm.at[below], w1, sems.at[1]),
        pltpu.make_async_copy(wout_hbm.at[below], wout, sems.at[2]),
    ]
    for load in late:
        load.start()
    stores = []

    def emit(src, dst):
        stores.append(pltpu.make_async_copy(src, dst, sems.at[3 + len(stores)]))
        stores[-1].start()

    attend_back_body(length_ref, mixed_ref, lse_ref, gctx_in, att_ref, dmix)
    part(mine, dmix, mix_keep, mix_send)
    emit(mix_send, mix_send_ref)
    emit(mix_keep, mix_keep_ref)
    early.wait()
    grad = first_in[...] + dot(dmix[...], wqkv[...], COLS)
    gains = gains_ref[...].astype(F32)
    norm_end(
        mine, grad, n2_ref[...], s2_ref[:, :1], gains[2 * layer : 2 * layer + 1], e, second, sec_keep_ref, sec_send_ref, top_ref
    )

    def ready(i):
        for load in loads[i]:
            load.wait()

    feed_back_body(mine, second, gp, w2, ready, bias_ref, keep, send)
    emit(send, pre_send_ref)
    emit(keep, pre_keep_ref)
    late[0].wait()
    grad = e[...] + both_halves(mine, keep, send, w1)
    norm_end(
        mine, grad, n1_ref[...], s1_ref[:, :1], gains[1 + 2 * below : 2 + 2 * below], first_ref, low_ref, None, None, sums_ref
    )
    late[1].wait()
    gctx_ref[...] = dot(low_ref[...], wout[...], COLS).astype(LOW)
    for store in stores:
        store.wait()


def between(layer, coords, length, mixed, lse, gctx, first, n2, s2, n1, s1, gains, gp, w_qkv, w_out, w_ff1, w_ff2, after=()):
    tokens, width = first.shape
    ff = gp.shape[1]
    s = jax.ShapeDtypeStruct
    v = pltpu.VMEM
    mix = s((tokens, 3 * width // 2), LOW)
    pre = s((tokens, ff // 2), LOW)
    sec = s((tokens, width // 2), LOW)
    low = s((tokens, width), LOW)
    three = s((3, width), F32)
    return run(
        functools.partial(between_kernel, layer),
        after,
        out_shape=(
            mix, mix, pre, pre, s((2, width), F32), sec, sec, three, s((1, ff), F32), s((tokens, width), F32), low, low, three,
        ),
        in_specs=[SM, SM] + [VM] * 9 + [HBM] * 5,
        operands=(coords, length, mixed, lse, gctx, first, n2, s2, n1, s1, gains, gp, w_qkv, w_out, w_ff1, w_ff2),
        out_specs=(ANY,) * 4 + (VM,) * 9,
        scratch_shapes=[
            v((tokens, ff), LOW), v((width, 3 * width), LOW), v((width, width), LOW), v((width, ff), LOW), v((ff, width), LOW),
            v((tokens, 3 * width), LOW), v(mix.shape, LOW), v(mix.shape, LOW), v(pre.shape, LOW), v(pre.shape, LOW),
            v((tokens, width), F32), v((tokens, width), LOW), pltpu.SemaphoreType.DMA((7 + 2 * (ff // 512),)),
        ],
        cost_estimate=CHEAP,
        vmem=58,
        name="between",
    )


COORDS = ("core", "x", "a", "b", "y")


def place(coords_ref, plan, result, *outs):
    count = result.shape[0]
    size = count // len(outs)
    dims = [] if plan is None else [dim for turn in plan for dim in turn]
    for i in range(count):
        block = i
        if plan is not None:
            bit = {}
            for n, dim in enumerate(dims):
                relative = (i >> (len(dims) - 1 - n)) & 1
                whole = plan[-1] == ("y",) and n == len(dims) - 1
                bit[dim] = relative if whole else coords_ref[COORDS.index(dim)] ^ relative
            block = 16 * bit.get("core", 0) + 8 * bit["b"] + 4 * bit["a"] + 2 * bit["x"] + bit["y"]
        out = outs[i // size]
        out[i % size] = result[block].astype(out.dtype)


def parts_of(plan):
    return 2 if plan is None else 2 ** len(plan[0])


def load_both(pairs, sems):
    loads = []
    for own, oth, dst in pairs:
        for n, src in enumerate((own, oth)):
            size = own.shape[0]
            load = pltpu.make_async_copy(src, dst.at[pl.ds(n * size, size)], sems.at[len(loads)])
            load.start()
            loads.append(load)
    return loads


def weights_kernel(plans, blocks, coords_ref, *refs):
    count = 8 if len(plans) == 2 else 16
    sources, refs = refs[:count], refs[count:]
    outs = []
    for plan in plans:
        outs.append(refs[: parts_of(plan)])
        refs = refs[parts_of(plan) :]
    sec, act, mid, pre, sect, midt, two, one = refs[:8]
    rest, sems = refs[8:-1], refs[-1]
    tokens = sources[0].shape[0]
    loads = []
    targets = [sec, act, mid, pre]
    if rest:
        x, mix, ctxt, fst, xt, mixed = rest
        targets += [x, mix, ctxt, fst]
    for n, target in enumerate(targets):
        for side in range(2):
            there = pl.ds(side * tokens, tokens)
            view = target.at[:, there] if rest and n == 6 else target.at[there]
            loads.append(pltpu.make_async_copy(sources[2 * n + side], view, sems.at[2 * n + side]))
            loads[-1].start()

    def ready(n):
        loads[2 * n].wait()
        loads[2 * n + 1].wait()

    ready(0)
    sect[...] = sec[...].T
    ready(1)
    rows = two.shape[1]
    cols = act.shape[1] // blocks

    def step_two(i, carry):
        got = dot(sect[...], act[:, pl.ds(pl.multiple_of(i * cols, cols), cols)]).astype(LOW)
        for y in range(2):
            for n in range(4):
                at = (4 * y + n) * rows
                two[2 * i + y, :, n * cols : (n + 1) * cols] = got[at : at + rows]
        return carry

    lax.fori_loop(0, blocks, step_two, 0)
    place(coords_ref, plans[0], two, *outs[0])
    ready(2)
    midt[...] = mid[...].T
    ready(3)
    chunk = 512

    def step_one(i, carry):
        there = pl.ds(pl.multiple_of(i * chunk, chunk), chunk)
        one[:, :, there] = dot(midt[...], pre[:, there]).astype(LOW).reshape(one.shape[:2] + (chunk,))
        return carry

    lax.fori_loop(0, pre.shape[1] // chunk, step_one, 0)
    place(coords_ref, plans[1], one, *outs[1])
    if rest:
        ready(4)
        xt[...] = x[...].T
        ready(5)
        width = fst.shape[1]
        shape = mixed.shape[:2] + (width,)
        for i in range(mix.shape[1] // width):
            there = slice(i * width, (i + 1) * width)
            mixed[:, :, there] = dot(xt[...], mix[:, there]).astype(LOW).reshape(shape)
        ready(6)
        ready(7)
        mixed[:, :, mix.shape[1] :] = dot(ctxt[...], fst[...]).astype(LOW).reshape(shape)
        place(coords_ref, plans[2], mixed, *outs[2])


def weights(blocks, plans, coords, sec, act, mid, pre, attention=(), after=()):
    tokens, width = mid[0].shape
    s = jax.ShapeDtypeStruct
    v = pltpu.VMEM
    count = 2 * blocks
    block = (count, width // count, 2 * width)
    outs = sum(((s((count // parts_of(plan),) + block[1:], LOW),) * parts_of(plan) for plan in plans), ())
    pairs = (sec, act, mid, pre) + tuple(attention)
    both = lambda pair: v((2 * tokens, pair[0].shape[1]), LOW)
    scratch = [both(pair) for pair in (sec, act, mid, pre)]
    scratch += [v((sec[0].shape[1], 2 * tokens), LOW), v((width, 2 * tokens), LOW), v(block, LOW), v(block, LOW)]
    if attention:
        x, mix, ctx, fst = attention
        scratch += [both(x), both(mix), v((width, 2 * tokens), LOW), both(fst), v((width, 2 * tokens), LOW), v(block, LOW)]
    got = run(
        functools.partial(weights_kernel, plans, blocks),
        after,
        out_shape=outs,
        in_specs=[SM] + [ANY] * (2 * len(pairs)),
        operands=(coords,) + tuple(array for pair in pairs for array in pair),
        out_specs=(VM,) * len(outs),
        scratch_shapes=scratch + [pltpu.SemaphoreType.DMA((2 * len(pairs),))],
        cost_estimate=CHEAP,
        vmem=52 if attention else 34,
        name="weights",
    )
    parts = []
    for plan in plans:
        parts.append(got[: parts_of(plan)])
        got = got[parts_of(plan) :]
    return parts


def combine_kernel(forms, *refs):
    count = sum(sum(form[0]) for form in forms)
    ins, outs = refs[:count], refs[count:]
    for terms_of, parts, axis in forms:
        results, outs = outs[:parts], outs[parts:]
        at = 0
        for terms in terms_of:
            mine, ins = ins[:terms], ins[terms:]
            size = mine[0].shape[0] // parts
            rows = mine[0].shape[1]
            for part in range(parts):
                for i in range(size):
                    total = mine[0][part * size + i].astype(F32)
                    for term in mine[1:]:
                        total = total + term[part * size + i].astype(F32)
                    if axis == 0:
                        results[part][at + i] = total.astype(LOW)
                    else:
                        results[part][i, at : at + rows] = total.astype(LOW)
            at += size if axis == 0 else rows


def combine(items, after=(), cost=CHEAP):
    forms = tuple((tuple(len(terms) for terms in sums), parts, axis) for sums, parts, axis in items)
    shapes = []
    for sums, parts, axis in items:
        shape = list(sums[0][0].shape)
        shape[axis] = sum(terms[0].shape[axis] for terms in sums)
        shape[0] //= parts
        shapes += [jax.ShapeDtypeStruct(tuple(shape), LOW)] * parts
    operands = tuple(array for sums, _, _ in items for terms in sums for array in terms)
    size = sum(array.size for array in operands)
    outs = run(
        functools.partial(combine_kernel, forms),
        after,
        out_shape=tuple(shapes),
        in_specs=[VM] * len(operands),
        operands=operands,
        out_specs=(VM,) * len(shapes),
        cost_estimate=cost,
        vmem=6 + 4 * size // (1 << 20),
        name="combine",
    )
    got = []
    for _, parts, _ in forms:
        got.append(outs[:parts])
        outs = outs[parts:]
    return got


def last_kernel(
    plan, coords_ref, length_ref, mixed_ref, lse_ref, gctx_ref, first_ref, n_ref, s_ref, gains_ref, x_ref, ctxt_ref, low_ref,
    slot_ref, type_ref, top0, top1, low0, low1, att1, bias0, bias1, wqkv_hbm,
    out_ref, keep_ref, send_ref,
    wqkv, dmix, xt, res, back_ref, back_low, att0, emb, small, sems,
):
    tokens, width = back_ref.shape
    load = pltpu.make_async_copy(wqkv_hbm.at[0], wqkv, sems.at[0])
    load.start()
    attend_back_body(length_ref, mixed_ref, lse_ref, gctx_ref, att0, dmix)
    load.wait()
    grad = first_ref[...] + dot(dmix[...], wqkv[...], COLS)
    gain = gains_ref[...].astype(F32)[0:1]
    norm_end(coords_ref[0], grad, n_ref[...], s_ref[:, :1], gain, back_ref, back_low, None, None, emb)
    slots = out_ref.shape[0]
    chunk = 256

    def step(i, carry):
        there = pl.ds(pl.multiple_of(i * chunk, chunk), chunk)
        number = lax.broadcasted_iota(jnp.int32, (chunk, tokens), 0) + i * chunk
        hit = jnp.where(number == slot_ref[...], 1.0, 0.0).astype(LOW)
        out_ref[there, :] = dot(hit, back_low[...]).astype(LOW)
        return carry

    lax.fori_loop(0, slots // chunk, step, 0)
    xt[...] = x_ref[...].T
    blocks = res.shape[0] // 2
    piece = width // blocks
    half = width // 2
    wide = 3 * half
    for core in range(2):
        there = slice(core * blocks, (core + 1) * blocks)
        for i in range(3):
            cols = slice(core * wide + i * half, core * wide + (i + 1) * half)
            got = dot(xt[...], dmix[:, cols]).astype(LOW)
            res[there, :piece, i * half : (i + 1) * half] = got.reshape(blocks, piece, half)
        got = dot(ctxt_ref[...], low_ref[:, core * half : (core + 1) * half]).astype(LOW)
        res[there, :piece, wide:] = got.reshape(blocks, piece, half)
    back = back_ref[...]
    kind = type_ref[:, :1]
    small[0:1] = jnp.sum(back * (1.0 - kind), axis=0, keepdims=True)
    small[1:2] = jnp.sum(back * kind, axis=0, keepdims=True)
    sources = [(emb, 0)]
    for top, low in ((top0, low0), (top1, low1)):
        sources += [(low, 0), (top, 0)]
    sources += [(emb, 1)]
    for top, low, att in ((top0, low0, att0), (top1, low1, att1)):
        sources += [(att, 0), (att, 1), (low, 2), (low, 1), (top, 2), (top, 1)]
    at = 2
    for ref, row in sources:
        small[at : at + 1] = ref[row : row + 1]
        at += 1
    for bias in (bias0, bias1):
        for i in range(bias.shape[1] // width):
            small[at : at + 1] = bias[:, i * width : (i + 1) * width]
            at += 1
    quarter = at // 4
    group = tokens // blocks // 4
    fill = res.shape[1] - piece
    parts = back.reshape(blocks, 4, group, width)
    for core in range(2):
        pos = jnp.concatenate([parts[:, i, :, core * half : (core + 1) * half] for i in range(4)], axis=2)
        for y in range(2):
            mine = small[(2 * core + y) * quarter : (2 * core + y + 1) * quarter]
            mine = jnp.concatenate([mine, jnp.zeros((fill - group - quarter, width), F32)], axis=0)
            mine = jnp.concatenate([mine, jnp.zeros_like(mine)], axis=1)
            for v in range(blocks // 2):
                block = 2 * v + y
                res[core * blocks + block, piece:, :] = jnp.concatenate([pos[block], mine], axis=0).astype(LOW)
    place(coords_ref, plan, res, keep_ref, send_ref)


def last(plan, coords, length, mixed, lse, gctx, first, n, sp, gains, x, ctxt, low, slot_of, types, sums, w_qkv, slots, blocks, after=()):
    tokens, width = first.shape
    s = jax.ShapeDtypeStruct
    v = pltpu.VMEM
    block = (blocks, width // blocks + 16, 2 * width)
    operands = (coords, length, mixed, lse, gctx, first, n, sp, gains, x, ctxt, low, slot_of, types, *sums, w_qkv)
    return run(
        functools.partial(last_kernel, plan),
        after,
        out_shape=(s((slots, width), LOW), s(block, LOW), s(block, LOW)),
        in_specs=[SM, SM] + [VM] * (len(operands) - 3) + [HBM],
        operands=operands,
        out_specs=(VM,) * 3,
        scratch_shapes=[
            v((width, 3 * width), LOW), v((tokens, 3 * width), LOW), v((width, tokens), LOW),
            v((2 * blocks,) + block[1:], LOW), v((tokens, width), F32), v((tokens, width), LOW),
            v((2, width), F32), v((3, width), F32), v((28, width), F32), pltpu.SemaphoreType.DMA((1,)),
        ],
        cost_estimate=CHEAP,
        vmem=52,
        name="last",
    )


def table_back_kernel(coords_ref, asked_ref, rows_ref, keep_ref, send_ref, total):
    count = total.shape[0]
    chunk = count // 5 if count % 5 == 0 else count

    def step(i, carry):
        at = pl.multiple_of(i * chunk, 8)
        number = lax.broadcasted_iota(jnp.int32, (chunk, rows_ref.shape[0]), 0) + at
        hit = jnp.where(number == asked_ref[...], 1.0, 0.0).astype(LOW)
        total[pl.ds(at, chunk), :] = dot(hit, rows_ref[...])
        return carry

    lax.fori_loop(0, count // chunk, step, 0)
    mine = coords_ref[0]
    half = total.shape[1] // 2

    @pl.when(mine == 0)
    def _():
        keep_ref[...] = total[:, :half].astype(LOW)
        send_ref[...] = total[:, half:].astype(LOW)

    @pl.when(mine == 1)
    def _():
        keep_ref[...] = total[:, half:].astype(LOW)
        send_ref[...] = total[:, :half].astype(LOW)


def table_back(coords, asked, rows, local_rows, after=()):
    width = rows.shape[1]
    half = jax.ShapeDtypeStruct((local_rows, width // 2), LOW)
    return run(
        table_back_kernel,
        after,
        out_shape=(half, half),
        in_specs=[SM, VM, VM],
        operands=(coords, asked, rows),
        out_specs=(VM, VM),
        scratch_shapes=[pltpu.VMEM((local_rows, width), F32)],
        cost_estimate=CHEAP,
        vmem=16,
        name="table_back",
    )


def finish_kernel(coords_ref, *refs):
    five, one = refs[:4], refs[4:8]
    qkv_ref, wout_ref, one_ref, two_ref, pos_ref, small_ref = refs[8:]
    mine_core, mine_y = coords_ref[0] == 0, coords_ref[4] == 0
    half = wout_ref.shape[2] // 2
    wide = 3 * half
    part = wout_ref.shape[1] // 2

    def piece(four, n, core, y):
        own, over_y, over_core, over_both = (ref[n] for ref in four)
        same_y = mine_y if y == 0 else jnp.logical_not(mine_y)
        same_core = mine_core if core == 0 else jnp.logical_not(mine_core)
        here = jnp.where(same_y, own, over_y)
        there = jnp.where(same_y, over_core, over_both)
        return jnp.where(same_core, here, there).astype(F32)

    for layer in range(NL):
        for core in range(2):
            columns = []
            for y in range(2):
                rows = slice(y * part, (y + 1) * part)
                mix = piece(one, 0, core, y) if layer == 0 else piece(five, MIX1, core, y)
                qkv_ref[layer, rows, core * wide : (core + 1) * wide] = mix[:part, :wide]
                wout_ref[layer, rows, core * half : (core + 1) * half] = mix[:part, wide:]
                if layer == 0:
                    for i in range(4):
                        at = (4 * y + i) * 8
                        pos_ref[at : at + 8, core * half : (core + 1) * half] = mix[part : part + 8, i * half : (i + 1) * half]
                    at = (2 * core + y) * 7
                    small_ref[at : at + 7] = mix[part + 8 : part + 15, : 2 * half]
                first = piece(five, ONE0 if layer == 0 else ONE1, core, y)
                one_ref[layer, rows, core * 4 * half : (core + 1) * 4 * half] = first
                second = piece(five, TWO0 if layer == 0 else TWO1, core, y)
                columns += [second[:, i * half : (i + 1) * half] for i in range(4)]
            two_ref[layer, :, core * half : (core + 1) * half] = jnp.concatenate(columns, axis=0).T


MIX1, TWO0, ONE0, TWO1, ONE1 = range(5)


def finish(coords, five, one, width, ff, owners):
    s = jax.ShapeDtypeStruct
    rows = width // owners
    return run(
        finish_kernel,
        (),
        out_shape=(
            s((NL, rows, 3 * width), F32), s((NL, rows, width), F32), s((NL, rows, ff), F32), s((NL, ff // owners, width), F32),
            s((64, width), F32), s((28, width), F32),
        ),
        in_specs=[SM] + [VM] * 8,
        operands=(coords, *five, *one),
        out_specs=(VM,) * 6,
        cost_estimate=CHEAP,
        vmem=24,
        name="finish",
    )


AXES = ("dp", "vocab")
VOCAB_MASK = {"x": 1, "a": 2, "b": 4}


def add(left_op, right_op):
    return (left_op.astype(F32) + right_op.astype(F32)).astype(LOW)


class Cube:
    def __init__(self, dp_size, vocab_size):
        self.dp_size = dp_size
        self.vocab_size = vocab_size
        self.dp_bits = dp_size.bit_length() - 1
        self.vocab_bits = vocab_size.bit_length() - 1
        assert 1 << self.dp_bits == dp_size and 1 << self.vocab_bits == vocab_size
        self.small = self.dp_bits == 2 and self.vocab_bits == 3

    def permute(self, value, dp_mask, vocab_mask):
        count = self.vocab_size
        pairs = [
            (d * count + v, (d ^ dp_mask) * count + (v ^ vocab_mask))
            for d in range(self.dp_size)
            for v in range(count)
        ]
        return lax.ppermute(value, AXES, pairs)

    def core(self, value):
        return self.permute(value, 1, 0)

    def along(self, value, dims):
        return self.permute(
            value, 2 * ("y" in dims) + ("core" in dims), sum(VOCAB_MASK[dim] for dim in dims if dim in VOCAB_MASK)
        )

    def core_is_first(self):
        return (lax.axis_index("dp") & 1) == 0

    def coords(self):
        dp, vocab = lax.axis_index("dp"), lax.axis_index("vocab")
        return jnp.stack([dp & 1, vocab & 1, (vocab >> 1) & 1, (vocab >> 2) & 1, (dp >> 1) & 1])

    def halves(self, matrix):
        mine = lax.axis_index("dp") & 1
        width = matrix.shape[1] // 2
        keep = lax.dynamic_slice_in_dim(matrix, mine * width, width, 1)
        send = lax.dynamic_slice_in_dim(matrix, (1 - mine) * width, width, 1)
        return keep, send

    def ordered(self, first, mine, other, axis):
        return jnp.concatenate(
            [jnp.where(first, mine, other), jnp.where(first, other, mine)], axis=axis
        )

    def join_core(self, share, axis):
        return self.ordered(self.core_is_first(), share, self.core(share), axis).astype(F32)

    def reduce(self, matrix):
        for bit in reversed(range(self.vocab_bits)):
            mine = (lax.axis_index("vocab") >> bit) & 1
            rows = matrix.shape[0] // 2
            keep = lax.dynamic_slice_in_dim(matrix, mine * rows, rows, 0)
            send = lax.dynamic_slice_in_dim(matrix, (1 - mine) * rows, rows, 0)
            matrix = add(keep, self.permute(send, 0, 1 << bit))
        for bit in range(1, self.dp_bits):
            matrix = add(matrix, self.permute(matrix, 1 << bit, 0))
        return matrix


def on_device(
    cube,
    token_ids,
    lengths,
    type_ids,
    word_table,
    pos_table,
    type_table,
    gains,
    shifts,
    w_qkv,
    w_out,
    b_ff1,
    w_ff1,
    w_ff2,
    cotangent,
):
    owners = cube.vocab_size
    local_rows, width = word_table.shape
    assert token_ids.shape[0] == 1
    tokens = token_ids.shape[1]
    slot_count = 2 * tokens // owners
    slots = owners * slot_count
    flat_ids = token_ids.reshape(tokens)
    me = lax.axis_index("vocab")
    coords = cube.coords()

    all_ids = lax.all_to_all(
        jnp.broadcast_to(flat_ids[None, :], (owners, tokens)), "vocab", split_axis=0, concat_axis=0, tiled=True
    )
    local = all_ids - me * local_rows
    here = (local >= 0) & (local < local_rows)
    rank = jnp.cumsum(here.astype(jnp.int32), axis=1) - 1
    slot_hit = (
        jnp.where(here, rank, -1)[:, None, :] == jnp.arange(slot_count, dtype=jnp.int32)[None, :, None]
    )
    asked = jnp.sum(jnp.where(slot_hit, local[:, None, :] + 1, 0), axis=2).reshape(slots) - 1
    row_hit = (asked[:, None] == jnp.arange(local_rows, dtype=jnp.int32)[None, :]).astype(LOW)
    found_rows = dot(row_hit, word_table).astype(LOW)
    replies = lax.all_to_all(
        found_rows.reshape(owners, slot_count, width), "vocab", split_axis=0, concat_axis=0, tiled=True
    ).reshape(slots, width)
    owner_of = flat_ids // local_rows
    chosen = (owner_of[:, None] == jnp.arange(owners, dtype=jnp.int32)[None, :]).astype(jnp.int32)
    before = jnp.cumsum(chosen, axis=0) - chosen
    slot_of = owner_of * slot_count + jnp.sum(before * chosen, axis=1)
    kind = type_ids.reshape(tokens).astype(F32)
    column = lambda row: jnp.broadcast_to(row[:, None], (tokens, 128))
    (n0, s0, hidden), top, layers = forward(
        coords, lengths, replies, column(slot_of), column(kind), pos_table, type_table, gains, shifts, b_ff1.astype(F32),
        cotangent.reshape(tokens, width), w_qkv, w_out, w_ff1, w_ff2,
    )
    norms, saved = [(n0, s0)], []
    for xlow, mixed, lse, ctxt, n1, s1, mlow, gp, act, *end in layers:
        saved.append((mixed, lse, n1, s1, gp) + tuple((own, cube.core(own)) for own in (xlow, ctxt, mlow, act)))
        norms.append(tuple(end))
    hidden_out = hidden.reshape(1, tokens, width)

    gradients = gradients_small if cube.small else gradients_any
    outs = gradients(
        cube, coords, lengths, top, saved, gains, w_qkv, w_out, w_ff1, w_ff2,
        norms, (kind, row_hit, slot_of, asked),
    )
    return (hidden_out,) + outs


def exchange_rows(outgoing, owners):
    shape = outgoing.shape
    return lax.all_to_all(
        outgoing.reshape(owners, -1, shape[1]), "vocab", split_axis=0, concat_axis=0, tiled=True
    ).reshape(shape)


def unpack(pack):
    cores, blocks, _, cols = pack.shape
    pos = pack[:, :, :8].reshape(cores, blocks, 8, 4, cols // 4).transpose(1, 3, 2, 0, 4)
    return pos.reshape(blocks * 32, cols // 2), pack[:, :2, 8:15, : cols // 2].reshape(28, cols // 2)


def small_outs(cube, rows):
    place_of = lax.axis_index("vocab")

    def mine(array):
        size = array.shape[1] // cube.vocab_size
        return lax.dynamic_slice_in_dim(array, place_of * size, size, 1)

    few = mine(rows[:20])
    return few[:2], few[2 : 2 + 2 * NL + 1], few[2 + 2 * NL + 1 :], mine(rows[20:].reshape(NL, -1))


def gradients_any(cube, coords, lengths, top, saved, gains, w_qkv, w_out, w_ff1, w_ff2, norms, embed):
    owners = cube.vocab_size
    width = w_out.shape[1]
    tokens = top[0].shape[0]
    blocks = 8
    half = width // 2
    kind, row_hit, slot_of, asked = embed
    mixed1, lse1, n1_1, s1_1, gp1, x1, ctx1, mid1, act1 = saved[1]
    mixed0, lse0, n1_0, s1_0, gp0, x0, ctx0, mid0, act0 = saved[0]
    e, low, sec_keep, sec_send, top1 = top
    pre_keep, pre_send, bias1, first, _, fst_keep, fst_send, gctx, sums1 = feed(
        1, coords, e, low, n1_1, s1_1, gains, gp1, w_out, w_ff1, w_ff2
    )
    pair = lambda keep, send: (keep, cube.core(send))
    two1, one1 = weights(blocks, (None, None), coords, pair(sec_keep, sec_send), act1, mid1, pair(pre_keep, pre_send))
    fst1 = pair(fst_keep, fst_send)
    (
        mix_keep, mix_send, pre_keep, pre_send, att1, sec_keep, sec_send, top0, bias0, first, low, gctx, sums0
    ) = between(
        1, coords, lengths, mixed1, lse1, gctx, first, *norms[1], n1_0, s1_0, gains, gp0, w_qkv, w_out, w_ff1, w_ff2
    )
    two0, one0, mix1 = weights(
        blocks, (None, None, None), coords, pair(sec_keep, sec_send), act0, mid0, pair(pre_keep, pre_send),
        (x1, pair(mix_keep, mix_send), ctx1, fst1),
    )
    column = jnp.broadcast_to(kind[:, None], (tokens, 128))
    outgoing, first_core, second_core = last(
        None, coords, lengths, mixed0, lse0, gctx, first, *norms[0], gains, x0[0], ctx0[0], low, slot_of[None, :], column,
        (top0, top1, sums0, sums1, att1, bias0, bias1), w_qkv, row_hit.shape[0], 2 * blocks,
    )
    mine = cube.core_is_first()

    def over_cores(first, second):
        return add(jnp.where(mine, first, second), cube.core(jnp.where(mine, second, first)))

    table_part = dot(row_hit, exchange_rows(outgoing, owners), ROWS).astype(LOW)
    table_part = over_cores(table_part[:, :half], table_part[:, half:])
    for bit in range(1, cube.dp_bits):
        table_part = add(table_part, cube.permute(table_part, 1 << bit, 0))
    part = width // blocks // 2
    packs = over_cores(first_core[:, part:], second_core[:, part:])
    other = cube.core(packs)
    pos, small = unpack(jnp.stack([jnp.where(mine, packs, other), jnp.where(mine, other, packs)]))
    pos_out = cube.reduce(pos).astype(F32)
    for bit in range(cube.vocab_bits):
        small = add(small, cube.permute(small, 0, 1 << bit))
    for bit in range(1, cube.dp_bits):
        small = add(small, cube.permute(small, 1 << bit, 0))
    types, gains_out, shifts_out, biases = small_outs(cube, small.astype(F32))
    whole = lambda parts: jnp.concatenate(parts, axis=0)
    one = lambda parts: cube.reduce(whole(parts).reshape(width, -1))
    two = lambda parts: cube.reduce(
        whole(parts).reshape(blocks, 2, width // 16, 4, -1).transpose(0, 4, 1, 3, 2).reshape(-1, half)
    )
    mix0 = over_cores(first_core[:, :part], second_core[:, :part]).reshape(width, -1)
    mixes = jnp.stack([cube.reduce(mix0), one(mix1)])
    wide = 3 * half
    return (
        cube.join_core(table_part, -1), pos_out, types, gains_out, shifts_out,
        cube.join_core(mixes[..., :wide], 2), cube.join_core(mixes[..., wide:], 2), biases,
        cube.join_core(jnp.stack([one(one0), one(one1)]), 2), cube.join_core(jnp.stack([two(two0), two(two1)]), 2),
    )


class Bucket:
    def __init__(self, cube, plan, parts):
        self.cube, self.plan, self.parts = cube, tuple(plan), tuple(parts)

    def start(self):
        turn = self.plan[0]
        if self.plan == (("y",),):
            self.got = (self.parts[0], self.cube.along(self.parts[0], turn))
            return
        self.got = self.parts[:1]
        for n in range(1, len(self.parts)):
            there = [dim for i, dim in enumerate(turn) if (n >> (len(turn) - 1 - i)) & 1]
            self.got += (self.cube.along(self.parts[n], there),)


    def keep(self):
        self.got, self.plan = self.parts, (None,)


def joined(buckets, parts_axis):
    return (tuple(buckets), parts_axis)


def step(groups, after=(), cost=CHEAP):
    groups = [group if isinstance(group, tuple) else ((group,), 0) for group in groups]
    items = []
    for buckets, axis in groups:
        rest = buckets[0].plan[1:]
        assert all(bucket.plan[1:] == rest for bucket in buckets)
        parts = 1 if rest in ((), (("y",),)) else 2 ** len(rest[0])
        items.append((tuple(bucket.got for bucket in buckets), parts, axis))
    for (buckets, _), parts in zip(groups, combine(items, after, cost)):
        buckets[0].plan, buckets[0].parts = buckets[0].plan[1:], tuple(parts)
    return groups[0][0][0].parts[0]


def gradients_small(cube, coords, lengths, top, saved, gains, w_qkv, w_out, w_ff1, w_ff2, norms, embed):
    owners = cube.vocab_size
    width = w_out.shape[1]
    tokens = top[0].shape[0]
    blocks = owners
    half = width // 2
    single = lambda dims: tuple((dim,) for dim in dims)
    plan_two1, plan_one1, plan_mix1 = (("x", "y"), ("a",), ("b",)), single("abxy"), single("ayxb")
    plan_two0, plan_one0, plan_mix0 = single("xayb"), single("yxab"), (("core",), ("y",), ("x", "a"), ("b",))
    kind, row_hit, slot_of, asked = embed
    local_rows = row_hit.shape[1]
    mixed1, lse1, n1_1, s1_1, gp1, x1, ctx1, mid1, act1 = saved[1]
    mixed0, lse0, n1_0, s1_0, gp0, x0, ctx0, mid0, act0 = saved[0]
    pair = lambda keep, send: (keep, cube.core(send))
    e, low, sec_keep, sec_send, top1 = top
    pre_keep, pre_send, bias1, first, _, fst_keep, fst_send, gctx, sums1 = feed(
        1, coords, e, low, n1_1, s1_1, gains, gp1, w_out, w_ff1, w_ff2
    )
    fst1 = pair(fst_keep, fst_send)
    got = weights(
        blocks, (plan_two1, plan_one1), coords, pair(sec_keep, sec_send), act1, mid1, pair(pre_keep, pre_send)
    )
    two1, one1 = Bucket(cube, plan_two1, got[0]), Bucket(cube, plan_one1, got[1])
    two1.start()
    one1.start()
    (
        mix_keep, mix_send, pre_keep, pre_send, att1, sec_keep, sec_send, top0, bias0, first, low, gctx, sums0
    ) = between(
        1, coords, lengths, mixed1, lse1, gctx, first, *norms[1], n1_0, s1_0, gains, gp0, w_qkv, w_out, w_ff1, w_ff2,
        after=got[0][:1],
    )
    mark = step([two1, one1], after=(gctx,), cost=LONG)
    two1.start()
    one1.start()
    got = weights(
        blocks, (plan_two0, plan_one0, plan_mix1), coords, pair(sec_keep, sec_send), act0, mid0, pair(pre_keep, pre_send),
        (x1, pair(mix_keep, mix_send), ctx1, fst1), after=(mark,),
    )
    two0, one0, mix1 = [Bucket(cube, plan, parts) for plan, parts in zip((plan_two0, plan_one0, plan_mix1), got)]
    for bucket in (mix1, two0, one0):
        bucket.start()
    mark = step([two1, one1], after=got[0][:1], cost=LONG)
    two1.start()
    one1.start()
    types = jnp.broadcast_to(kind[:, None], (tokens, 128))
    outgoing, *got = last(
        plan_mix0, coords, lengths, mixed0, lse0, gctx, first, *norms[0], gains, x0[0], ctx0[0], low, slot_of[None, :], types,
        (top0, top1, sums0, sums1, att1, bias0, bias1), w_qkv, row_hit.shape[0], 2 * owners, after=(mark,),
    )
    incoming = exchange_rows(outgoing, owners)
    mix0 = Bucket(cube, plan_mix0, got)
    mix0.start()
    mark = step([two1, one1, mix1, two0, one0], after=got[:1], cost=LONG)
    for bucket in (one1, mix1, two0, one0):
        bucket.start()
    mark = step([mix0], after=(mark,))
    mix0.start()
    mark = step([mix1, two0, one0, one1], after=(mark,), cost=LONG)
    for bucket in (mix1, two0, one0):
        bucket.start()
    folded = (local_rows // 48, 48, half)
    got = table_back(coords, asked[None, :], incoming, local_rows, after=(mark,))
    table = Bucket(cube, single(("core", "y")), [part.reshape(folded) for part in got])
    table.start()
    mark = step([mix0, joined((mix1, two0, one0), 0), table], after=got[:1], cost=LONG)
    mix0.start()
    mix1.start()
    table.start()
    mark = step([mix0], after=(mark,), cost=LONG)
    mix0.start()
    two1.keep()
    mark = step([joined((mix1, two1), 0), table], after=(mark,))
    step([mix0], after=(mark,))
    half_of = lambda n: one1.parts[0][n : n + 1]
    mine_y = (lax.axis_index("dp") >> 1) & 1 == 0
    one1_own = jnp.where(mine_y, half_of(0), half_of(1))
    one1_other = jnp.where(mine_y, half_of(1), half_of(0))
    four = mix1.parts[0]
    own = jnp.concatenate([four, one1_own], axis=0)
    over_y = jnp.concatenate([cube.along(four, ("y",)), one1_other], axis=0)
    last_y = cube.along(mix0.parts[0], ("y",))
    qkv_out, wout_out, one_out, two_out, pos_out, small = finish(
        coords,
        (own, over_y, cube.core(own), cube.core(over_y)),
        (mix0.parts[0], last_y, cube.core(mix0.parts[0]), cube.core(last_y)),
        width, w_ff1.shape[2], owners,
    )
    types, gains, shifts, biases = small_outs(cube, small)
    return (
        cube.join_core(table.parts[0].reshape(local_rows, half), -1), pos_out, types, gains, shifts, qkv_out, wout_out,
        biases, one_out, two_out,
    )


def solution(mesh):
    cube = Cube(mesh.shape["dp"], mesh.shape["vocab"])
    both = ("dp", "vocab")
    in_specs = (
        P(both, None),
        P(both),
        P(both, None),
        P("vocab", None),
        P(),
        P(),
        P(),
        P(),
        P(),
        P(),
        P(),
        P(),
        P(),
        P(both, None, None),
    )
    out_specs = (
        P(both, None, None),
        P("vocab", None),
        P("vocab", None),
        P(None, "vocab"),
        P(None, "vocab"),
        P(None, "vocab"),
        P(None, "vocab", None),
        P(None, "vocab", None),
        P(None, "vocab"),
        P(None, "vocab", None),
        P(None, "vocab", None),
    )
    return jax.shard_map(
        functools.partial(on_device, cube), mesh=mesh, in_specs=in_specs, out_specs=out_specs, check_vma=False
    )
```

```python
import functools
import jax
import jax.numpy as jnp
from jax import lax
from jax.experimental import pallas as pl
from jax.experimental.pallas import tpu as pltpu
from jax.sharding import PartitionSpec as P

HEADS = 12
HEAD_DIM = 64
NL = 2
norm_eps = 1e-12
SCALE = HEAD_DIM ** (-0.5)
ANY = pl.BlockSpec(memory_space=pl.ANY)
HBM = pl.BlockSpec(memory_space=pltpu.HBM)
VM = pl.BlockSpec(memory_space=pltpu.VMEM)
SM = pl.BlockSpec(memory_space=pltpu.SMEM)
F32, LOW = jnp.float32, jnp.bfloat16

CHEAP = pl.CostEstimate(flops=1, bytes_accessed=1, transcendentals=0)
DEAR = pl.CostEstimate(flops=10**10, bytes_accessed=1, transcendentals=0)
LONG = pl.CostEstimate(flops=10**11, bytes_accessed=1, transcendentals=0)


def run(kernel, after, out_shape, in_specs, operands, vmem, **options):
    count = len(operands)

    def body(*refs):
        kernel(*refs[:count], *refs[count + len(after) :])

    return pl.pallas_call(
        body,
        out_shape=out_shape,
        in_specs=list(in_specs) + [ANY] * len(after),
        compiler_params=pltpu.CompilerParams(vmem_limit_bytes=vmem * 1024 * 1024),
        **options,
    )(*operands, *after)


def normalize(inputs):
    centered = inputs - jnp.mean(inputs, axis=-1, keepdims=True)
    spread = lax.rsqrt(jnp.mean(centered * centered, axis=-1, keepdims=True) + norm_eps)
    return (centered * spread, spread)


def norm_back(grad_out, normed, spread, gain_row):
    scaled = grad_out * gain_row
    return spread * (
        scaled
        - jnp.mean(scaled, axis=-1, keepdims=True)
        - normed * jnp.mean(scaled * normed, axis=-1, keepdims=True)
    )


def dot(left_op, right_op, dims=((1,), (0,))):
    return lax.dot_general(left_op, right_op, (dims, ((), ())), preferred_element_type=F32)


ROWS = ((0,), (0,))
COLS = ((1,), (1,))


def gelu_pair(inputs):
    size = jnp.abs(inputs)
    bell = jnp.exp2(inputs * inputs * (-0.5 * 1.4426950408889634))
    t = 1.0 / (1.0 + size * (0.3275911 * 0.7071067811865476))
    tail = t * (
        0.5 * 0.254829592
        + t * (0.5 * -0.284496736 + t * (0.5 * 1.421413741 + t * (0.5 * -1.453152027 + t * (0.5 * 1.061405429))))
    )
    tail = tail * bell
    phi = jnp.where(inputs >= 0.0, 1.0 - tail, tail)
    return inputs * phi, phi + inputs * bell * 0.3989422804014327


def forward_kernel(
    coords_ref, length_ref, replies_ref, slot_ref, kind_ref, pos_ref, type_ref, gains_ref, shifts_ref, ffn_bias_ref,
    grad_ref, wqkv_hbm, wout_hbm, w1_hbm, w2_hbm,
    *refs,
):
    n0_ref, s0_ref, hidden_ref = refs[:3]
    top = refs[3:8]
    outs = [refs[8 + 11 * layer : 19 + 11 * layer] for layer in range(NL)]
    wqkv, wout, w1, w2, sems, xlow, mixed, ctxt, mlow, gp, act, n0, n1, n2, x, osems = refs[6 + 11 * NL :]
    tokens, width = x.shape
    ff = w1.shape[2]
    loads = []
    for layer in range(NL):
        for i, (src, dst) in enumerate([(wqkv_hbm, wqkv), (wout_hbm, wout), (w1_hbm, w1), (w2_hbm, w2)]):
            loads.append(pltpu.make_async_copy(src.at[layer], dst.at[layer], sems.at[4 * layer + i]))
    for load in loads:
        load.start()
    pending, used = {}, [0]

    def emit(name, src, dst, at=None):
        if at is not None:
            src, dst = src.at[:, at], dst.at[:, at]
        copy = pltpu.make_async_copy(src, dst, osems.at[used[0]])
        used[0] += 1
        copy.start()
        pending.setdefault(name, []).append(copy)

    def reuse(name):
        for copy in pending.pop(name, ()):
            copy.wait()

    gains = gains_ref[...].astype(F32)
    shifts = shifts_ref[...].astype(F32)
    number = lax.broadcasted_iota(jnp.int32, (tokens, replies_ref.shape[0]), 1)
    hit = jnp.where(number == slot_ref[:, :1], 1.0, 0.0).astype(LOW)
    types = type_ref[...].astype(F32)
    embedded = dot(hit, replies_ref[...]) + pos_ref[...].astype(F32)
    embedded = embedded + jnp.where(kind_ref[:, :1] > 0.5, types[1:2], types[0:1])
    normed, spread = normalize(embedded)
    n0[...] = normed
    emit("n0", n0, n0_ref)
    s0_ref[...] = jnp.broadcast_to(spread, s0_ref.shape)
    x[...] = normed * gains[0:1] + shifts[0:1]

    key_slot = lax.broadcasted_iota(jnp.int32, (tokens, 128), 0)
    visible = jnp.where(key_slot < length_ref[0], 0.0, -1e30)[:, :1]
    lane = lax.broadcasted_iota(jnp.int32, (tokens, 128), 1)
    chunk = 512

    for layer in range(NL):
        base = 1 + 6 * layer
        xlow_ref, mixed_ref, lse_ref, ctxt_ref, n1_ref, s1_ref, mlow_ref, gp_ref, act_ref = outs[layer][:9]

        reuse("xlow")
        xlow[...] = x[...].astype(LOW)
        emit("xlow", xlow, xlow_ref)
        loads[4 * layer].wait()
        reuse("mixed")
        for i in range(3):
            cols = slice(i * width, (i + 1) * width)
            got = dot(xlow[...], wqkv[layer, :, cols])
            if i != 1:
                row = base + (0 if i == 0 else 1)
                got = got + shifts[row : row + 1]
            mixed[:, cols] = got.astype(LOW)
        emit("mixed", mixed, mixed_ref)
        reuse("ctxt")

        def pair_step(j, carry):
            at = pl.multiple_of(j * 128, 128)
            q = mixed[:, pl.ds(at, 128)] * jnp.asarray(SCALE, LOW)
            k = mixed[:, pl.ds(pl.multiple_of(width + at, 128), 128)]
            v = mixed[:, pl.ds(pl.multiple_of(2 * width + at, 128), 128)]
            vt = v.T
            scores = []
            for h in range(2):
                kh = jnp.where((lane < 64) == (h == 0), k, jnp.zeros_like(k))
                scores.append(dot(kh, q, COLS) + visible)
            for h in range(2):
                top = jnp.max(scores[h], axis=0, keepdims=True)
                weights = jnp.exp(scores[h] - top)
                total = jnp.sum(weights, axis=0, keepdims=True)
                out = dot(vt[h * 64 : (h + 1) * 64], weights.astype(LOW)) * (1.0 / total)
                ctxt[pl.ds(pl.multiple_of(at + h * 64, 64), 64), :] = out.astype(LOW)
                lse_ref[pl.ds(2 * j + h, 1), :] = top + jnp.log(total)
            return carry

        lax.fori_loop(0, HEADS // 2, pair_step, 0)
        emit("ctxt", ctxt, ctxt_ref)
        loads[4 * layer + 1].wait()
        attended = dot(ctxt[...], wout[layer], ROWS) + shifts[base + 2 : base + 3]
        normed, spread = normalize(x[...] + attended)
        reuse("n1")
        n1[...] = normed
        emit("n1", n1, n1_ref)
        s1_ref[...] = jnp.broadcast_to(spread, s1_ref.shape)
        x[...] = normed * gains[1 + 2 * layer : 2 + 2 * layer] + shifts[base + 3 : base + 4]
        reuse("mlow")
        mlow[...] = x[...].astype(LOW)
        emit("mlow", mlow, mlow_ref)
        loads[4 * layer + 2].wait()
        reuse("gp")
        reuse("act")
        for i in range(ff // chunk):
            cols = slice(i * chunk, (i + 1) * chunk)
            pre = dot(mlow[...], w1[layer, :, cols]) + ffn_bias_ref[layer : layer + 1, cols]
            active, slope = gelu_pair(pre)
            gp[:, cols] = slope.astype(LOW)
            act[:, cols] = active.astype(LOW)
            emit("gp", gp, gp_ref, pl.ds(i * chunk, chunk))
            emit("act", act, act_ref, pl.ds(i * chunk, chunk))
        loads[4 * layer + 3].wait()
        normed, spread = normalize(x[...] + shifts[base + 4 : base + 5] + dot(act[...], w2[layer]))
        if layer < NL - 1:
            n2_ref, s2_ref = outs[layer][9:11]
            n2[...] = normed
            emit("n2", n2, n2_ref)
            s2_ref[...] = jnp.broadcast_to(spread, s2_ref.shape)
        else:
            gain = gains[2 * NL : 2 * NL + 1]
            norm_end(coords_ref[0], grad_ref[...].astype(F32), normed, spread, gain, *top)
        x[...] = normed * gains[2 + 2 * layer : 3 + 2 * layer] + shifts[base + 5 : base + 6]
    hidden_ref[...] = x[...].astype(LOW)
    for name in list(pending):
        reuse(name)


def forward(
    coords, length, replies, slot_col, kind_col, pos, types, gains, shifts, ffn_bias, cotangent, w_qkv, w_out, w_ff1, w_ff2
):
    tokens, width = pos.shape
    ff = w_ff1.shape[2]
    s = jax.ShapeDtypeStruct
    v = pltpu.VMEM
    spread = s((tokens, 128), F32)
    wide = s((tokens, width), F32)
    low = s((tokens, width), LOW)
    layer_out = (
        low, s((tokens, 3 * width), LOW), s((HEADS, tokens), F32), s((width, tokens), LOW),
        wide, spread, low, s((tokens, ff), LOW), s((tokens, ff), LOW), wide, spread,
    )
    layer_spec = (ANY, ANY, VM, ANY, ANY, VM, ANY, ANY, ANY, ANY, VM)
    chunks = ff // 512
    end = norm_end_shapes(tokens, width)
    outs = run(
        forward_kernel,
        (),
        out_shape=(wide, spread, low) + end + layer_out * (NL - 1) + layer_out[:9],
        in_specs=[SM, SM] + [VM] * 9 + [HBM] * 4,
        operands=(
            coords, length, replies, slot_col, kind_col, pos, types, gains, shifts, ffn_bias, cotangent, w_qkv, w_out, w_ff1, w_ff2
        ),
        out_specs=(ANY, VM, VM) + (VM,) * 5 + layer_spec * (NL - 1) + layer_spec[:9],
        scratch_shapes=[
            v((NL, width, 3 * width), LOW), v((NL, width, width), LOW), v((NL, width, ff), LOW), v((NL, ff, width), LOW),
            pltpu.SemaphoreType.DMA((4 * NL,)),
            v((tokens, width), LOW), v((tokens, 3 * width), LOW), v((width, tokens), LOW), v((tokens, width), LOW),
            v((tokens, ff), LOW), v((tokens, ff), LOW), v((tokens, width), F32), v((tokens, width), F32),
            v((tokens, width), F32), v((tokens, width), F32), pltpu.SemaphoreType.DMA((1 + NL * (6 + 2 * chunks),)),
        ],
        cost_estimate=CHEAP,
        vmem=60,
        name="forward",
    )
    return outs[:3], outs[3:8], [outs[8 + 11 * layer : 19 + 11 * layer] for layer in range(NL)]


def part(mine, source, keep_to, send_to):
    half = source.shape[1] // 2

    @pl.when(mine == 0)
    def _():
        keep_to[...] = source[:, :half]
        send_to[...] = source[:, half:]

    @pl.when(mine == 1)
    def _():
        keep_to[...] = source[:, half:]
        send_to[...] = source[:, :half]


def norm_end(mine, grad, n, s, gain, back_ref, low_ref, keep_ref, send_ref, sums_ref):
    sums_ref[0:1] = jnp.sum(grad * n, axis=0, keepdims=True)
    sums_ref[1:2] = jnp.sum(grad, axis=0, keepdims=True)
    back = norm_back(grad, n, s, gain)
    sums_ref[2:3] = jnp.sum(back, axis=0, keepdims=True)
    back_ref[...] = back
    low_ref[...] = back.astype(LOW)
    if keep_ref is not None:
        part(mine, low_ref, keep_ref, send_ref)


def norm_end_shapes(tokens, width):
    s = jax.ShapeDtypeStruct
    half = s((tokens, width // 2), LOW)
    return (s((tokens, width), F32), s((tokens, width), LOW), half, half, s((3, width), F32))


def feed_back_body(mine, second, gp, w2, ready, bias_ref, keep, send):
    chunk = 512
    steps = gp.shape[1] // chunk
    for i in range(steps):
        ready(i)
        cols = slice(i * chunk, (i + 1) * chunk)
        grad_pre = dot(second[...], w2[cols, :], COLS) * gp[:, cols].astype(F32)
        bias_ref[:, cols] = jnp.sum(grad_pre, axis=0, keepdims=True)
        side, at = divmod(i, steps // 2)
        there = slice(at * chunk, (at + 1) * chunk)
        low = grad_pre.astype(LOW)

        @pl.when(mine == side)
        def _():
            keep[:, there] = low

        @pl.when(mine != side)
        def _():
            send[:, there] = low


def both_halves(mine, keep, send, weight):
    half = keep.shape[1]
    first = jnp.where(mine == 0, keep[...], send[...])
    second = jnp.where(mine == 0, send[...], keep[...])
    return dot(first, weight[:, :half], COLS) + dot(second, weight[:, half:], COLS)


def attend_back_body(length_ref, mixed_ref, lse_ref, gctx_ref, att_ref, dmix):
    tokens, width = gctx_ref.shape
    key_slot = lax.broadcasted_iota(jnp.int32, (tokens, 128), 0)
    visible = jnp.where(key_slot < length_ref[0], 0.0, -1e30)[:, :1]
    lane = lax.broadcasted_iota(jnp.int32, (tokens, 128), 1)

    def pair_step(j, carry):
        at = pl.multiple_of(j * 128, 128)
        qcols = pl.ds(at, 128)
        kcols = pl.ds(pl.multiple_of(width + at, 128), 128)
        vcols = pl.ds(pl.multiple_of(2 * width + at, 128), 128)
        q = mixed_ref[:, qcols] * jnp.asarray(SCALE, LOW)
        k = mixed_ref[:, kcols]
        v = mixed_ref[:, vcols]
        g = gctx_ref[:, qcols]
        kt = k.T
        grad_v, grad_k, grad_qt = [], [], []
        scores, grad_probs = [], []
        for h in range(2):
            mask = (lane < 64) == (h == 0)
            kh = jnp.where(mask, k, jnp.zeros_like(k))
            vh = jnp.where(mask, v, jnp.zeros_like(v))
            scores.append(dot(kh, q, COLS))
            grad_probs.append(dot(vh, g, COLS))
        for h in range(2):
            probs = jnp.exp(scores[h] + visible - lse_ref[pl.ds(2 * j + h, 1), :])
            weighted = jnp.sum(probs * grad_probs[h], axis=0, keepdims=True)
            grad_scores = (probs * (grad_probs[h] - weighted)).astype(LOW)
            grad_v.append(dot(probs.astype(LOW), g))
            grad_k.append(dot(grad_scores, q))
            grad_qt.append(dot(kt[h * 64 : (h + 1) * 64], grad_scores))
        grad_q = jnp.concatenate(grad_qt, axis=0).T * SCALE
        grad_v = jnp.where(lane < 64, grad_v[0], grad_v[1])
        grad_k = jnp.where(lane < 64, grad_k[0], grad_k[1])
        att_ref[0:1, qcols] = jnp.sum(grad_q, axis=0, keepdims=True)
        att_ref[1:2, qcols] = jnp.sum(grad_v, axis=0, keepdims=True)
        dmix[:, qcols] = grad_q.astype(LOW)
        dmix[:, kcols] = grad_k.astype(LOW)
        dmix[:, vcols] = grad_v.astype(LOW)
        return carry

    lax.fori_loop(0, HEADS // 2, pair_step, 0)


def chunk_loads(sems, at, pairs, chunk=512):
    loads = []
    (w2_src, w2), (gp_src, gp) = pairs
    for i in range(gp.shape[1] // chunk):
        there = pl.ds(i * chunk, chunk)
        loads.append(
            (
                pltpu.make_async_copy(w2_src.at[there], w2.at[there], sems.at[at + 2 * i]),
                pltpu.make_async_copy(gp_src.at[:, there], gp.at[:, there], sems.at[at + 2 * i + 1]),
            )
        )
    return loads


def feed_kernel(
    layer, coords_ref, e_ref, second, n1_ref, s1_ref, gains_ref, gp_hbm, wout_hbm, w1_hbm, w2_hbm,
    keep_ref, send_ref, bias_ref, first_ref, low_ref, fst_keep_ref, fst_send_ref, gctx_ref, sums_ref,
    gp, wout, w1, w2, keep, send, sems,
):
    mine = coords_ref[0]
    loads = chunk_loads(sems, 4, ((w2_hbm.at[layer], w2), (gp_hbm, gp)))
    for pair in loads:
        for load in pair:
            load.start()
    late = [
        pltpu.make_async_copy(w1_hbm.at[layer], w1, sems.at[0]),
        pltpu.make_async_copy(wout_hbm.at[layer], wout, sems.at[1]),
    ]
    for load in late:
        load.start()

    def ready(i):
        for load in loads[i]:
            load.wait()

    feed_back_body(mine, second, gp, w2, ready, bias_ref, keep, send)
    stores = [
        pltpu.make_async_copy(send, send_ref, sems.at[2]),
        pltpu.make_async_copy(keep, keep_ref, sems.at[3]),
    ]
    for store in stores:
        store.start()
    late[0].wait()
    grad = e_ref[...] + both_halves(mine, keep, send, w1)
    gain = gains_ref[...].astype(F32)[1 + 2 * layer : 2 + 2 * layer]
    norm_end(mine, grad, n1_ref[...], s1_ref[:, :1], gain, first_ref, low_ref, fst_keep_ref, fst_send_ref, sums_ref)
    late[1].wait()
    gctx_ref[...] = dot(low_ref[...], wout[...], COLS).astype(LOW)
    for store in stores:
        store.wait()


def feed(layer, coords, e, second, n1, s1, gains, gp, w_out, w_ff1, w_ff2, after=()):
    tokens, width = n1.shape
    ff = gp.shape[1]
    s = jax.ShapeDtypeStruct
    v = pltpu.VMEM
    half = s((tokens, ff // 2), LOW)
    end = norm_end_shapes(tokens, width)
    return run(
        functools.partial(feed_kernel, layer),
        after,
        out_shape=(half, half, s((1, ff), F32)) + end[:4] + (s((tokens, width), LOW), end[4]),
        in_specs=[SM] + [VM] * 5 + [HBM] * 4,
        operands=(coords, e, second, n1, s1, gains, gp, w_out, w_ff1, w_ff2),
        out_specs=(ANY, ANY) + (VM,) * 7,
        scratch_shapes=[
            v((tokens, ff), LOW), v((width, width), LOW), v((width, ff), LOW), v((ff, width), LOW),
            v((tokens, ff // 2), LOW), v((tokens, ff // 2), LOW), pltpu.SemaphoreType.DMA((4 + 2 * (ff // 512),)),
        ],
        cost_estimate=CHEAP,
        vmem=52,
        name="feed",
    )


def between_kernel(
    layer, coords_ref, length_ref, mixed_ref, lse_ref, gctx_in, first_in, n2_ref, s2_ref, n1_ref, s1_ref, gains_ref,
    gp_hbm, wqkv_hbm, wout_hbm, w1_hbm, w2_hbm,
    mix_keep_ref, mix_send_ref, pre_keep_ref, pre_send_ref,
    att_ref, sec_keep_ref, sec_send_ref, top_ref, bias_ref, first_ref, low_ref, gctx_ref, sums_ref,
    gp, wqkv, wout, w1, w2, dmix, mix_keep, mix_send, keep, send, e, second, sems,
):
    mine = coords_ref[0]
    below = layer - 1
    early = pltpu.make_async_copy(wqkv_hbm.at[layer], wqkv, sems.at[0])
    early.start()
    loads = chunk_loads(sems, 7, ((w2_hbm.at[below], w2), (gp_hbm, gp)))
    for pair in loads:
        for load in pair:
            load.start()
    late = [
        pltpu.make_async_copy(w1_hbm.at[below], w1, sems.at[1]),
        pltpu.make_async_copy(wout_hbm.at[below], wout, sems.at[2]),
    ]
    for load in late:
        load.start()
    stores = []

    def emit(src, dst):
        stores.append(pltpu.make_async_copy(src, dst, sems.at[3 + len(stores)]))
        stores[-1].start()

    attend_back_body(length_ref, mixed_ref, lse_ref, gctx_in, att_ref, dmix)
    part(mine, dmix, mix_keep, mix_send)
    emit(mix_send, mix_send_ref)
    emit(mix_keep, mix_keep_ref)
    early.wait()
    grad = first_in[...] + dot(dmix[...], wqkv[...], COLS)
    gains = gains_ref[...].astype(F32)
    norm_end(
        mine, grad, n2_ref[...], s2_ref[:, :1], gains[2 * layer : 2 * layer + 1], e, second, sec_keep_ref, sec_send_ref, top_ref
    )

    def ready(i):
        for load in loads[i]:
            load.wait()

    feed_back_body(mine, second, gp, w2, ready, bias_ref, keep, send)
    emit(send, pre_send_ref)
    emit(keep, pre_keep_ref)
    late[0].wait()
    grad = e[...] + both_halves(mine, keep, send, w1)
    norm_end(
        mine, grad, n1_ref[...], s1_ref[:, :1], gains[1 + 2 * below : 2 + 2 * below], first_ref, low_ref, None, None, sums_ref
    )
    late[1].wait()
    gctx_ref[...] = dot(low_ref[...], wout[...], COLS).astype(LOW)
    for store in stores:
        store.wait()


def between(layer, coords, length, mixed, lse, gctx, first, n2, s2, n1, s1, gains, gp, w_qkv, w_out, w_ff1, w_ff2, after=()):
    tokens, width = first.shape
    ff = gp.shape[1]
    s = jax.ShapeDtypeStruct
    v = pltpu.VMEM
    mix = s((tokens, 3 * width // 2), LOW)
    pre = s((tokens, ff // 2), LOW)
    sec = s((tokens, width // 2), LOW)
    low = s((tokens, width), LOW)
    three = s((3, width), F32)
    return run(
        functools.partial(between_kernel, layer),
        after,
        out_shape=(
            mix, mix, pre, pre, s((2, width), F32), sec, sec, three, s((1, ff), F32), s((tokens, width), F32), low, low, three,
        ),
        in_specs=[SM, SM] + [VM] * 9 + [HBM] * 5,
        operands=(coords, length, mixed, lse, gctx, first, n2, s2, n1, s1, gains, gp, w_qkv, w_out, w_ff1, w_ff2),
        out_specs=(ANY,) * 4 + (VM,) * 9,
        scratch_shapes=[
            v((tokens, ff), LOW), v((width, 3 * width), LOW), v((width, width), LOW), v((width, ff), LOW), v((ff, width), LOW),
            v((tokens, 3 * width), LOW), v(mix.shape, LOW), v(mix.shape, LOW), v(pre.shape, LOW), v(pre.shape, LOW),
            v((tokens, width), F32), v((tokens, width), LOW), pltpu.SemaphoreType.DMA((7 + 2 * (ff // 512),)),
        ],
        cost_estimate=CHEAP,
        vmem=58,
        name="between",
    )


COORDS = ("core", "x", "a", "b", "y")


def place(coords_ref, plan, result, *outs):
    count = result.shape[0]
    size = count // len(outs)
    dims = [] if plan is None else [dim for turn in plan for dim in turn]
    for i in range(count):
        block = i
        if plan is not None:
            bit = {}
            for n, dim in enumerate(dims):
                relative = (i >> (len(dims) - 1 - n)) & 1
                whole = plan[-1] == ("y",) and n == len(dims) - 1
                bit[dim] = relative if whole else coords_ref[COORDS.index(dim)] ^ relative
            block = 16 * bit.get("core", 0) + 8 * bit["b"] + 4 * bit["a"] + 2 * bit["x"] + bit["y"]
        out = outs[i // size]
        out[i % size] = result[block].astype(out.dtype)


def parts_of(plan):
    return 2 if plan is None else 2 ** len(plan[0])


def load_both(pairs, sems):
    loads = []
    for own, oth, dst in pairs:
        for n, src in enumerate((own, oth)):
            size = own.shape[0]
            load = pltpu.make_async_copy(src, dst.at[pl.ds(n * size, size)], sems.at[len(loads)])
            load.start()
            loads.append(load)
    return loads


def weights_kernel(plans, blocks, coords_ref, *refs):
    count = 8 if len(plans) == 2 else 16
    sources, refs = refs[:count], refs[count:]
    outs = []
    for plan in plans:
        outs.append(refs[: parts_of(plan)])
        refs = refs[parts_of(plan) :]
    sec, act, mid, pre, sect, midt, two, one = refs[:8]
    rest, sems = refs[8:-1], refs[-1]
    tokens = sources[0].shape[0]
    loads = []
    targets = [sec, act, mid, pre]
    if rest:
        x, mix, ctxt, fst, xt, mixed = rest
        targets += [x, mix, ctxt, fst]
    for n, target in enumerate(targets):
        for side in range(2):
            there = pl.ds(side * tokens, tokens)
            view = target.at[:, there] if rest and n == 6 else target.at[there]
            loads.append(pltpu.make_async_copy(sources[2 * n + side], view, sems.at[2 * n + side]))
            loads[-1].start()

    def ready(n):
        loads[2 * n].wait()
        loads[2 * n + 1].wait()

    ready(0)
    sect[...] = sec[...].T
    ready(1)
    rows = two.shape[1]
    cols = act.shape[1] // blocks

    def step_two(i, carry):
        got = dot(sect[...], act[:, pl.ds(pl.multiple_of(i * cols, cols), cols)]).astype(LOW)
        for y in range(2):
            for n in range(4):
                at = (4 * y + n) * rows
                two[2 * i + y, :, n * cols : (n + 1) * cols] = got[at : at + rows]
        return carry

    lax.fori_loop(0, blocks, step_two, 0)
    place(coords_ref, plans[0], two, *outs[0])
    ready(2)
    midt[...] = mid[...].T
    ready(3)
    chunk = 512

    def step_one(i, carry):
        there = pl.ds(pl.multiple_of(i * chunk, chunk), chunk)
        one[:, :, there] = dot(midt[...], pre[:, there]).astype(LOW).reshape(one.shape[:2] + (chunk,))
        return carry

    lax.fori_loop(0, pre.shape[1] // chunk, step_one, 0)
    place(coords_ref, plans[1], one, *outs[1])
    if rest:
        ready(4)
        xt[...] = x[...].T
        ready(5)
        width = fst.shape[1]
        shape = mixed.shape[:2] + (width,)
        for i in range(mix.shape[1] // width):
            there = slice(i * width, (i + 1) * width)
            mixed[:, :, there] = dot(xt[...], mix[:, there]).astype(LOW).reshape(shape)
        ready(6)
        ready(7)
        mixed[:, :, mix.shape[1] :] = dot(ctxt[...], fst[...]).astype(LOW).reshape(shape)
        place(coords_ref, plans[2], mixed, *outs[2])


def weights(blocks, plans, coords, sec, act, mid, pre, attention=(), after=()):
    tokens, width = mid[0].shape
    s = jax.ShapeDtypeStruct
    v = pltpu.VMEM
    count = 2 * blocks
    block = (count, width // count, 2 * width)
    outs = sum(((s((count // parts_of(plan),) + block[1:], LOW),) * parts_of(plan) for plan in plans), ())
    pairs = (sec, act, mid, pre) + tuple(attention)
    both = lambda pair: v((2 * tokens, pair[0].shape[1]), LOW)
    scratch = [both(pair) for pair in (sec, act, mid, pre)]
    scratch += [v((sec[0].shape[1], 2 * tokens), LOW), v((width, 2 * tokens), LOW), v(block, LOW), v(block, LOW)]
    if attention:
        x, mix, ctx, fst = attention
        scratch += [both(x), both(mix), v((width, 2 * tokens), LOW), both(fst), v((width, 2 * tokens), LOW), v(block, LOW)]
    got = run(
        functools.partial(weights_kernel, plans, blocks),
        after,
        out_shape=outs,
        in_specs=[SM] + [ANY] * (2 * len(pairs)),
        operands=(coords,) + tuple(array for pair in pairs for array in pair),
        out_specs=(VM,) * len(outs),
        scratch_shapes=scratch + [pltpu.SemaphoreType.DMA((2 * len(pairs),))],
        cost_estimate=CHEAP,
        vmem=52 if attention else 34,
        name="weights",
    )
    parts = []
    for plan in plans:
        parts.append(got[: parts_of(plan)])
        got = got[parts_of(plan) :]
    return parts


def combine_kernel(forms, *refs):
    count = sum(sum(form[0]) for form in forms)
    ins, outs = refs[:count], refs[count:]
    for terms_of, parts, axis in forms:
        results, outs = outs[:parts], outs[parts:]
        at = 0
        for terms in terms_of:
            mine, ins = ins[:terms], ins[terms:]
            size = mine[0].shape[0] // parts
            rows = mine[0].shape[1]
            for part in range(parts):
                for i in range(size):
                    total = mine[0][part * size + i].astype(F32)
                    for term in mine[1:]:
                        total = total + term[part * size + i].astype(F32)
                    if axis == 0:
                        results[part][at + i] = total.astype(LOW)
                    else:
                        results[part][i, at : at + rows] = total.astype(LOW)
            at += size if axis == 0 else rows


def combine(items, after=(), cost=CHEAP):
    forms = tuple((tuple(len(terms) for terms in sums), parts, axis) for sums, parts, axis in items)
    shapes = []
    for sums, parts, axis in items:
        shape = list(sums[0][0].shape)
        shape[axis] = sum(terms[0].shape[axis] for terms in sums)
        shape[0] //= parts
        shapes += [jax.ShapeDtypeStruct(tuple(shape), LOW)] * parts
    operands = tuple(array for sums, _, _ in items for terms in sums for array in terms)
    size = sum(array.size for array in operands)
    outs = run(
        functools.partial(combine_kernel, forms),
        after,
        out_shape=tuple(shapes),
        in_specs=[VM] * len(operands),
        operands=operands,
        out_specs=(VM,) * len(shapes),
        cost_estimate=cost,
        vmem=6 + 4 * size // (1 << 20),
        name="combine",
    )
    got = []
    for _, parts, _ in forms:
        got.append(outs[:parts])
        outs = outs[parts:]
    return got


def last_kernel(
    plan, coords_ref, length_ref, mixed_ref, lse_ref, gctx_ref, first_ref, n_ref, s_ref, gains_ref, x_ref, ctxt_ref, low_ref,
    slot_ref, type_ref, top0, top1, low0, low1, att1, bias0, bias1, wqkv_hbm,
    out_ref, *parts_and_scratch
):
    outs, (wqkv, dmix, xt, res, back_ref, back_low, att0, emb, small, sems) = parts_and_scratch[:-10], parts_and_scratch[-10:]
    tokens, width = back_ref.shape
    load = pltpu.make_async_copy(wqkv_hbm.at[0], wqkv, sems.at[0])
    load.start()
    attend_back_body(length_ref, mixed_ref, lse_ref, gctx_ref, att0, dmix)
    load.wait()
    grad = first_ref[...] + dot(dmix[...], wqkv[...], COLS)
    gain = gains_ref[...].astype(F32)[0:1]
    norm_end(coords_ref[0], grad, n_ref[...], s_ref[:, :1], gain, back_ref, back_low, None, None, emb)
    slots = out_ref.shape[0]
    chunk = 256

    def step(i, carry):
        there = pl.ds(pl.multiple_of(i * chunk, chunk), chunk)
        number = lax.broadcasted_iota(jnp.int32, (chunk, tokens), 0) + i * chunk
        hit = jnp.where(number == slot_ref[...], 1.0, 0.0).astype(LOW)
        out_ref[there, :] = dot(hit, back_low[...]).astype(LOW)
        return carry

    lax.fori_loop(0, slots // chunk, step, 0)
    xt[...] = x_ref[...].T
    blocks = res.shape[0] // 2
    piece = width // blocks
    half = width // 2
    wide = 3 * half
    for core in range(2):
        there = slice(core * blocks, (core + 1) * blocks)
        for i in range(3):
            cols = slice(core * wide + i * half, core * wide + (i + 1) * half)
            got = dot(xt[...], dmix[:, cols]).astype(LOW)
            res[there, :piece, i * half : (i + 1) * half] = got.reshape(blocks, piece, half)
        got = dot(ctxt_ref[...], low_ref[:, core * half : (core + 1) * half]).astype(LOW)
        res[there, :piece, wide:] = got.reshape(blocks, piece, half)
    back = back_ref[...]
    kind = type_ref[:, :1]
    small[0:1] = jnp.sum(back * (1.0 - kind), axis=0, keepdims=True)
    small[1:2] = jnp.sum(back * kind, axis=0, keepdims=True)
    sources = [(emb, 0)]
    for top, low in ((top0, low0), (top1, low1)):
        sources += [(low, 0), (top, 0)]
    sources += [(emb, 1)]
    for top, low, att in ((top0, low0, att0), (top1, low1, att1)):
        sources += [(att, 0), (att, 1), (low, 2), (low, 1), (top, 2), (top, 1)]
    at = 2
    for ref, row in sources:
        small[at : at + 1] = ref[row : row + 1]
        at += 1
    for bias in (bias0, bias1):
        for i in range(bias.shape[1] // width):
            small[at : at + 1] = bias[:, i * width : (i + 1) * width]
            at += 1
    quarter = at // 4
    group = tokens // blocks // 4
    fill = res.shape[1] - piece
    parts = back.reshape(blocks, 4, group, width)
    for core in range(2):
        pos = jnp.concatenate([parts[:, i, :, core * half : (core + 1) * half] for i in range(4)], axis=2)
        for y in range(2):
            mine = small[(2 * core + y) * quarter : (2 * core + y + 1) * quarter]
            mine = jnp.concatenate([mine, jnp.zeros((fill - group - quarter, width), F32)], axis=0)
            mine = jnp.concatenate([mine, jnp.zeros_like(mine)], axis=1)
            for v in range(blocks // 2):
                block = 2 * v + y
                res[core * blocks + block, piece:, :] = jnp.concatenate([pos[block], mine], axis=0).astype(LOW)
    place(coords_ref, plan, res, *outs)


def last(plan, coords, length, mixed, lse, gctx, first, n, sp, gains, x, ctxt, low, slot_of, types, sums, w_qkv, slots, blocks, parts=2, after=()):
    tokens, width = first.shape
    s = jax.ShapeDtypeStruct
    v = pltpu.VMEM
    block = (blocks, width // blocks + 16, 2 * width)
    operands = (coords, length, mixed, lse, gctx, first, n, sp, gains, x, ctxt, low, slot_of, types, *sums, w_qkv)
    return run(
        functools.partial(last_kernel, plan),
        after,
        out_shape=(s((slots, width), LOW),) + (s((2 * blocks // parts,) + block[1:], LOW),) * parts,
        in_specs=[SM, SM] + [VM] * (len(operands) - 3) + [HBM],
        operands=operands,
        out_specs=(VM,) * (1 + parts),
        scratch_shapes=[
            v((width, 3 * width), LOW), v((tokens, 3 * width), LOW), v((width, tokens), LOW),
            v((2 * blocks,) + block[1:], LOW), v((tokens, width), F32), v((tokens, width), LOW),
            v((2, width), F32), v((3, width), F32), v((28, width), F32), pltpu.SemaphoreType.DMA((1,)),
        ],
        cost_estimate=CHEAP,
        vmem=52,
        name="last",
    )


def table_back_kernel(coords_ref, asked_ref, rows_ref, keep_ref, send_ref, total):
    count = total.shape[0]
    chunk = count // 5 if count % 5 == 0 else count

    def step(i, carry):
        at = pl.multiple_of(i * chunk, 8)
        number = lax.broadcasted_iota(jnp.int32, (chunk, rows_ref.shape[0]), 0) + at
        hit = jnp.where(number == asked_ref[...], 1.0, 0.0).astype(LOW)
        total[pl.ds(at, chunk), :] = dot(hit, rows_ref[...])
        return carry

    lax.fori_loop(0, count // chunk, step, 0)
    mine = coords_ref[0]
    half = total.shape[1] // 2

    @pl.when(mine == 0)
    def _():
        keep_ref[...] = total[:, :half].astype(LOW)
        send_ref[...] = total[:, half:].astype(LOW)

    @pl.when(mine == 1)
    def _():
        keep_ref[...] = total[:, half:].astype(LOW)
        send_ref[...] = total[:, :half].astype(LOW)


def table_back(coords, asked, rows, local_rows, after=()):
    width = rows.shape[1]
    half = jax.ShapeDtypeStruct((local_rows, width // 2), LOW)
    return run(
        table_back_kernel,
        after,
        out_shape=(half, half),
        in_specs=[SM, VM, VM],
        operands=(coords, asked, rows),
        out_specs=(VM, VM),
        scratch_shapes=[pltpu.VMEM((local_rows, width), F32)],
        cost_estimate=CHEAP,
        vmem=16,
        name="table_back",
    )


def finish_kernel(coords_ref, *refs):
    five, one = refs[:4], refs[4:8]
    qkv_ref, wout_ref, one_ref, two_ref, pos_ref, small_ref = refs[8:]
    mine_core, mine_y = coords_ref[0] == 0, coords_ref[4] == 0
    half = wout_ref.shape[2] // 2
    wide = 3 * half
    part = wout_ref.shape[1] // 2

    def piece(four, n, core, y):
        own, over_y, over_core, over_both = (ref[n] for ref in four)
        same_y = mine_y if y == 0 else jnp.logical_not(mine_y)
        same_core = mine_core if core == 0 else jnp.logical_not(mine_core)
        here = jnp.where(same_y, own, over_y)
        there = jnp.where(same_y, over_core, over_both)
        return jnp.where(same_core, here, there).astype(F32)

    for layer in range(NL):
        for core in range(2):
            columns = []
            for y in range(2):
                rows = slice(y * part, (y + 1) * part)
                mix = piece(one, 0, core, y) if layer == 0 else piece(five, MIX1, core, y)
                qkv_ref[layer, rows, core * wide : (core + 1) * wide] = mix[:part, :wide]
                wout_ref[layer, rows, core * half : (core + 1) * half] = mix[:part, wide:]
                if layer == 0:
                    for i in range(4):
                        at = (4 * y + i) * 8
                        pos_ref[at : at + 8, core * half : (core + 1) * half] = mix[part : part + 8, i * half : (i + 1) * half]
                    at = (2 * core + y) * 7
                    small_ref[at : at + 7] = mix[part + 8 : part + 15, : 2 * half]
                first = piece(five, ONE0 if layer == 0 else ONE1, core, y)
                one_ref[layer, rows, core * 4 * half : (core + 1) * 4 * half] = first
                second = piece(five, TWO0 if layer == 0 else TWO1, core, y)
                columns += [second[:, i * half : (i + 1) * half] for i in range(4)]
            two_ref[layer, :, core * half : (core + 1) * half] = jnp.concatenate(columns, axis=0).T


MIX1, TWO0, ONE0, TWO1, ONE1 = range(5)


def finish(coords, five, one, width, ff, owners):
    s = jax.ShapeDtypeStruct
    rows = width // owners
    return run(
        finish_kernel,
        (),
        out_shape=(
            s((NL, rows, 3 * width), F32), s((NL, rows, width), F32), s((NL, rows, ff), F32), s((NL, ff // owners, width), F32),
            s((64, width), F32), s((28, width), F32),
        ),
        in_specs=[SM] + [VM] * 8,
        operands=(coords, *five, *one),
        out_specs=(VM,) * 6,
        cost_estimate=CHEAP,
        vmem=24,
        name="finish",
    )


AXES = ("dp", "vocab")
VOCAB_MASK = {"x": 1, "a": 2, "b": 4}


def add(left_op, right_op):
    return (left_op.astype(F32) + right_op.astype(F32)).astype(LOW)


class Cube:
    def __init__(self, dp_size, vocab_size):
        self.dp_size = dp_size
        self.vocab_size = vocab_size
        self.dp_bits = dp_size.bit_length() - 1
        self.vocab_bits = vocab_size.bit_length() - 1
        assert 1 << self.dp_bits == dp_size and 1 << self.vocab_bits == vocab_size
        self.small = self.dp_bits == 2 and self.vocab_bits == 3

    def permute(self, value, dp_mask, vocab_mask):
        count = self.vocab_size
        pairs = [
            (d * count + v, (d ^ dp_mask) * count + (v ^ vocab_mask))
            for d in range(self.dp_size)
            for v in range(count)
        ]
        return lax.ppermute(value, AXES, pairs)

    def core(self, value):
        return self.permute(value, 1, 0)

    def along(self, value, dims):
        return self.permute(
            value, 2 * ("y" in dims) + ("core" in dims), sum(VOCAB_MASK[dim] for dim in dims if dim in VOCAB_MASK)
        )

    def core_is_first(self):
        return (lax.axis_index("dp") & 1) == 0

    def coords(self):
        dp, vocab = lax.axis_index("dp"), lax.axis_index("vocab")
        return jnp.stack([dp & 1, vocab & 1, (vocab >> 1) & 1, (vocab >> 2) & 1, (dp >> 1) & 1])

    def halves(self, matrix):
        mine = lax.axis_index("dp") & 1
        width = matrix.shape[1] // 2
        keep = lax.dynamic_slice_in_dim(matrix, mine * width, width, 1)
        send = lax.dynamic_slice_in_dim(matrix, (1 - mine) * width, width, 1)
        return keep, send

    def ordered(self, first, mine, other, axis):
        return jnp.concatenate(
            [jnp.where(first, mine, other), jnp.where(first, other, mine)], axis=axis
        )

    def join_core(self, share, axis):
        return self.ordered(self.core_is_first(), share, self.core(share), axis).astype(F32)

    def reduce(self, matrix):
        for bit in reversed(range(self.vocab_bits)):
            mine = (lax.axis_index("vocab") >> bit) & 1
            rows = matrix.shape[0] // 2
            keep = lax.dynamic_slice_in_dim(matrix, mine * rows, rows, 0)
            send = lax.dynamic_slice_in_dim(matrix, (1 - mine) * rows, rows, 0)
            matrix = add(keep, self.permute(send, 0, 1 << bit))
        for bit in range(1, self.dp_bits):
            matrix = add(matrix, self.permute(matrix, 1 << bit, 0))
        return matrix


def on_device(
    cube,
    token_ids,
    lengths,
    type_ids,
    word_table,
    pos_table,
    type_table,
    gains,
    shifts,
    w_qkv,
    w_out,
    b_ff1,
    w_ff1,
    w_ff2,
    cotangent,
):
    owners = cube.vocab_size
    local_rows, width = word_table.shape
    assert token_ids.shape[0] == 1
    tokens = token_ids.shape[1]
    slot_count = 2 * tokens // owners
    slots = owners * slot_count
    flat_ids = token_ids.reshape(tokens)
    me = lax.axis_index("vocab")
    coords = cube.coords()

    all_ids = lax.all_to_all(
        jnp.broadcast_to(flat_ids[None, :], (owners, tokens)), "vocab", split_axis=0, concat_axis=0, tiled=True
    )
    local = all_ids - me * local_rows
    here = (local >= 0) & (local < local_rows)
    rank = jnp.cumsum(here.astype(jnp.int32), axis=1) - 1
    slot_hit = (
        jnp.where(here, rank, -1)[:, None, :] == jnp.arange(slot_count, dtype=jnp.int32)[None, :, None]
    )
    asked = jnp.sum(jnp.where(slot_hit, local[:, None, :] + 1, 0), axis=2).reshape(slots) - 1
    row_hit = (asked[:, None] == jnp.arange(local_rows, dtype=jnp.int32)[None, :]).astype(LOW)
    found_rows = dot(row_hit, word_table).astype(LOW)
    replies = lax.all_to_all(
        found_rows.reshape(owners, slot_count, width), "vocab", split_axis=0, concat_axis=0, tiled=True
    ).reshape(slots, width)
    owner_of = flat_ids // local_rows
    chosen = (owner_of[:, None] == jnp.arange(owners, dtype=jnp.int32)[None, :]).astype(jnp.int32)
    before = jnp.cumsum(chosen, axis=0) - chosen
    slot_of = owner_of * slot_count + jnp.sum(before * chosen, axis=1)
    kind = type_ids.reshape(tokens).astype(F32)
    column = lambda row: jnp.broadcast_to(row[:, None], (tokens, 128))
    (n0, s0, hidden), top, layers = forward(
        coords, lengths, replies, column(slot_of), column(kind), pos_table, type_table, gains, shifts, b_ff1.astype(F32),
        cotangent.reshape(tokens, width), w_qkv, w_out, w_ff1, w_ff2,
    )
    norms, saved = [(n0, s0)], []
    for xlow, mixed, lse, ctxt, n1, s1, mlow, gp, act, *end in layers:
        saved.append((mixed, lse, n1, s1, gp) + tuple((own, cube.core(own)) for own in (xlow, ctxt, mlow, act)))
        norms.append(tuple(end))
    hidden_out = hidden.reshape(1, tokens, width)

    gradients = gradients_small if cube.small else gradients_any
    outs = gradients(
        cube, coords, lengths, top, saved, gains, w_qkv, w_out, w_ff1, w_ff2,
        norms, (kind, row_hit, slot_of, asked),
    )
    return (hidden_out,) + outs


def exchange_rows(outgoing, owners):
    shape = outgoing.shape
    return lax.all_to_all(
        outgoing.reshape(owners, -1, shape[1]), "vocab", split_axis=0, concat_axis=0, tiled=True
    ).reshape(shape)


def unpack(pack):
    cores, blocks, _, cols = pack.shape
    pos = pack[:, :, :8].reshape(cores, blocks, 8, 4, cols // 4).transpose(1, 3, 2, 0, 4)
    return pos.reshape(blocks * 32, cols // 2), pack[:, :2, 8:15, : cols // 2].reshape(28, cols // 2)


def small_outs(cube, rows):
    place_of = lax.axis_index("vocab")

    def mine(array):
        size = array.shape[1] // cube.vocab_size
        return lax.dynamic_slice_in_dim(array, place_of * size, size, 1)

    few = mine(rows[:20])
    return few[:2], few[2 : 2 + 2 * NL + 1], few[2 + 2 * NL + 1 :], mine(rows[20:].reshape(NL, -1))


def gradients_any(cube, coords, lengths, top, saved, gains, w_qkv, w_out, w_ff1, w_ff2, norms, embed):
    owners = cube.vocab_size
    width = w_out.shape[1]
    tokens = top[0].shape[0]
    blocks = 8
    half = width // 2
    kind, row_hit, slot_of, asked = embed
    mixed1, lse1, n1_1, s1_1, gp1, x1, ctx1, mid1, act1 = saved[1]
    mixed0, lse0, n1_0, s1_0, gp0, x0, ctx0, mid0, act0 = saved[0]
    e, low, sec_keep, sec_send, top1 = top
    pre_keep, pre_send, bias1, first, _, fst_keep, fst_send, gctx, sums1 = feed(
        1, coords, e, low, n1_1, s1_1, gains, gp1, w_out, w_ff1, w_ff2
    )
    pair = lambda keep, send: (keep, cube.core(send))
    two1, one1 = weights(blocks, (None, None), coords, pair(sec_keep, sec_send), act1, mid1, pair(pre_keep, pre_send))
    fst1 = pair(fst_keep, fst_send)
    (
        mix_keep, mix_send, pre_keep, pre_send, att1, sec_keep, sec_send, top0, bias0, first, low, gctx, sums0
    ) = between(
        1, coords, lengths, mixed1, lse1, gctx, first, *norms[1], n1_0, s1_0, gains, gp0, w_qkv, w_out, w_ff1, w_ff2
    )
    two0, one0, mix1 = weights(
        blocks, (None, None, None), coords, pair(sec_keep, sec_send), act0, mid0, pair(pre_keep, pre_send),
        (x1, pair(mix_keep, mix_send), ctx1, fst1),
    )
    column = jnp.broadcast_to(kind[:, None], (tokens, 128))
    outgoing, first_core, second_core = last(
        None, coords, lengths, mixed0, lse0, gctx, first, *norms[0], gains, x0[0], ctx0[0], low, slot_of[None, :], column,
        (top0, top1, sums0, sums1, att1, bias0, bias1), w_qkv, row_hit.shape[0], 2 * blocks,
    )
    mine = cube.core_is_first()

    def over_cores(first, second):
        return add(jnp.where(mine, first, second), cube.core(jnp.where(mine, second, first)))

    table_part = dot(row_hit, exchange_rows(outgoing, owners), ROWS).astype(LOW)
    table_part = over_cores(table_part[:, :half], table_part[:, half:])
    for bit in range(1, cube.dp_bits):
        table_part = add(table_part, cube.permute(table_part, 1 << bit, 0))
    part = width // blocks // 2
    packs = over_cores(first_core[:, part:], second_core[:, part:])
    other = cube.core(packs)
    pos, small = unpack(jnp.stack([jnp.where(mine, packs, other), jnp.where(mine, other, packs)]))
    pos_out = cube.reduce(pos).astype(F32)
    for bit in range(cube.vocab_bits):
        small = add(small, cube.permute(small, 0, 1 << bit))
    for bit in range(1, cube.dp_bits):
        small = add(small, cube.permute(small, 1 << bit, 0))
    types, gains_out, shifts_out, biases = small_outs(cube, small.astype(F32))
    whole = lambda parts: jnp.concatenate(parts, axis=0)
    one = lambda parts: cube.reduce(whole(parts).reshape(width, -1))
    two = lambda parts: cube.reduce(
        whole(parts).reshape(blocks, 2, width // 16, 4, -1).transpose(0, 4, 1, 3, 2).reshape(-1, half)
    )
    mix0 = over_cores(first_core[:, :part], second_core[:, :part]).reshape(width, -1)
    mixes = jnp.stack([cube.reduce(mix0), one(mix1)])
    wide = 3 * half
    return (
        cube.join_core(table_part, -1), pos_out, types, gains_out, shifts_out,
        cube.join_core(mixes[..., :wide], 2), cube.join_core(mixes[..., wide:], 2), biases,
        cube.join_core(jnp.stack([one(one0), one(one1)]), 2), cube.join_core(jnp.stack([two(two0), two(two1)]), 2),
    )


class Bucket:
    def __init__(self, cube, plan, parts):
        self.cube, self.plan, self.parts = cube, tuple(plan), tuple(parts)

    def start(self):
        turn = self.plan[0]
        if self.plan == (("y",),):
            self.got = (self.parts[0], self.cube.along(self.parts[0], turn))
            return
        self.got = self.parts[:1]
        for n in range(1, len(self.parts)):
            there = [dim for i, dim in enumerate(turn) if (n >> (len(turn) - 1 - i)) & 1]
            self.got += (self.cube.along(self.parts[n], there),)


    def keep(self):
        self.got, self.plan = self.parts, (None,)


def joined(buckets, parts_axis):
    return (tuple(buckets), parts_axis)


def step(groups, after=(), cost=CHEAP):
    groups = [group if isinstance(group, tuple) else ((group,), 0) for group in groups]
    items = []
    for buckets, axis in groups:
        rest = buckets[0].plan[1:]
        assert all(bucket.plan[1:] == rest for bucket in buckets)
        parts = 1 if rest in ((), (("y",),)) else 2 ** len(rest[0])
        items.append((tuple(bucket.got for bucket in buckets), parts, axis))
    for (buckets, _), parts in zip(groups, combine(items, after, cost)):
        buckets[0].plan, buckets[0].parts = buckets[0].plan[1:], tuple(parts)
    return groups[0][0][0].parts[0]


def gradients_small(cube, coords, lengths, top, saved, gains, w_qkv, w_out, w_ff1, w_ff2, norms, embed):
    owners = cube.vocab_size
    width = w_out.shape[1]
    tokens = top[0].shape[0]
    blocks = owners
    half = width // 2
    single = lambda dims: tuple((dim,) for dim in dims)
    plan_two1, plan_one1 = (("x", "y"), ("a",), ("b",)), (("a",), ("x", "y"), ("b",))
    plan_mix1 = single("ayxb")
    plan_two0, plan_one0, plan_mix0 = single("xayb"), single("yxab"), (("core",), ("y",), ("x", "a"), ("b",))
    kind, row_hit, slot_of, asked = embed
    local_rows = row_hit.shape[1]
    mixed1, lse1, n1_1, s1_1, gp1, x1, ctx1, mid1, act1 = saved[1]
    mixed0, lse0, n1_0, s1_0, gp0, x0, ctx0, mid0, act0 = saved[0]
    pair = lambda keep, send: (keep, cube.core(send))
    e, low, sec_keep, sec_send, top1 = top
    pre_keep, pre_send, bias1, first, _, fst_keep, fst_send, gctx, sums1 = feed(
        1, coords, e, low, n1_1, s1_1, gains, gp1, w_out, w_ff1, w_ff2
    )
    fst1 = pair(fst_keep, fst_send)
    got = weights(
        blocks, (plan_two1, plan_one1), coords, pair(sec_keep, sec_send), act1, mid1, pair(pre_keep, pre_send)
    )
    two1, one1 = Bucket(cube, plan_two1, got[0]), Bucket(cube, plan_one1, got[1])
    two1.start()
    one1.start()
    (
        mix_keep, mix_send, pre_keep, pre_send, att1, sec_keep, sec_send, top0, bias0, first, low, gctx, sums0
    ) = between(
        1, coords, lengths, mixed1, lse1, gctx, first, *norms[1], n1_0, s1_0, gains, gp0, w_qkv, w_out, w_ff1, w_ff2,
        after=got[0][:1],
    )
    mark = step([two1, one1], after=(gctx,), cost=LONG)
    two1.start()
    one1.start()
    got = weights(
        blocks, (plan_two0, plan_one0, plan_mix1), coords, pair(sec_keep, sec_send), act0, mid0, pair(pre_keep, pre_send),
        (x1, pair(mix_keep, mix_send), ctx1, fst1), after=(mark,),
    )
    two0, one0, mix1 = [Bucket(cube, plan, parts) for plan, parts in zip((plan_two0, plan_one0, plan_mix1), got)]
    for bucket in (mix1, two0, one0):
        bucket.start()
    mark = step([joined((two1, one1), 0)], after=got[0][:1], cost=LONG)
    two1.start()
    types = jnp.broadcast_to(kind[:, None], (tokens, 128))
    outgoing, *got = last(
        plan_mix0, coords, lengths, mixed0, lse0, gctx, first, *norms[0], gains, x0[0], ctx0[0], low, slot_of[None, :], types,
        (top0, top1, sums0, sums1, att1, bias0, bias1), w_qkv, row_hit.shape[0], 2 * owners, after=(mark,),
    )
    incoming = exchange_rows(outgoing, owners)
    mix0 = Bucket(cube, plan_mix0, got)
    mix0.start()
    mark = step([two1, mix1, two0, one0], after=got[:1], cost=LONG)
    for bucket in (mix1, two0, one0):
        bucket.start()
    mark = step([mix0], after=(mark,))
    mix0.start()
    mark = step([mix1, two0, one0], after=(mark,), cost=LONG)
    for bucket in (mix1, two0, one0):
        bucket.start()
    folded = (local_rows // 48, 48, half)
    got = table_back(coords, asked[None, :], incoming, local_rows, after=(mark,))
    table = Bucket(cube, single(("core", "y")), [part.reshape(folded) for part in got])
    table.start()
    mark = step([mix0, joined((mix1, two0, one0), 0)], after=got[:1], cost=LONG)
    mix0.start()
    mix1.start()
    mark = step([table], after=(mark,))
    table.start()
    mark = step([mix0], after=(mark,), cost=LONG)
    mix0.start()
    two1.keep()
    mark = step([joined((mix1, two1), 0), table], after=(mark,))
    later = Bucket(cube, (), (cube.along(mix1.parts[0], ("y",)),))
    later.keep()
    mark = step([mix0], after=(mark,))
    last_y = Bucket(cube, (), (cube.along(mix0.parts[0], ("y",)),))
    last_y.keep()
    step([last_y], after=(mark,))
    step([later], after=(last_y.parts[0],))
    own = mix1.parts[0]
    over_y, last_y = later.parts[0], last_y.parts[0]
    qkv_out, wout_out, one_out, two_out, pos_out, small = finish(
        coords,
        (own, over_y, cube.core(own), cube.core(over_y)),
        (mix0.parts[0], last_y, cube.core(mix0.parts[0]), cube.core(last_y)),
        width, w_ff1.shape[2], owners,
    )
    types, gains, shifts, biases = small_outs(cube, small)
    return (
        cube.join_core(table.parts[0].reshape(local_rows, half), -1), pos_out, types, gains, shifts, qkv_out, wout_out,
        biases, one_out, two_out,
    )


def solution(mesh):
    cube = Cube(mesh.shape["dp"], mesh.shape["vocab"])
    both = ("dp", "vocab")
    in_specs = (
        P(both, None),
        P(both),
        P(both, None),
        P("vocab", None),
        P(),
        P(),
        P(),
        P(),
        P(),
        P(),
        P(),
        P(),
        P(),
        P(both, None, None),
    )
    out_specs = (
        P(both, None, None),
        P("vocab", None),
        P("vocab", None),
        P(None, "vocab"),
        P(None, "vocab"),
        P(None, "vocab"),
        P(None, "vocab", None),
        P(None, "vocab", None),
        P(None, "vocab"),
        P(None, "vocab", None),
        P(None, "vocab", None),
    )
    return jax.shard_map(
        functools.partial(on_device, cube), mesh=mesh, in_specs=in_specs, out_specs=out_specs, check_vma=False
    )
```

```python
import functools
import jax
import jax.numpy as jnp
from jax import lax
from jax.experimental import pallas as pl
from jax.experimental.pallas import tpu as pltpu
from jax.sharding import PartitionSpec as P

HEADS = 12
HEAD_DIM = 64
NL = 2
norm_eps = 1e-12
SCALE = HEAD_DIM ** (-0.5)
ANY = pl.BlockSpec(memory_space=pl.ANY)
HBM = pl.BlockSpec(memory_space=pltpu.HBM)
VM = pl.BlockSpec(memory_space=pltpu.VMEM)
SM = pl.BlockSpec(memory_space=pltpu.SMEM)
F32, LOW = jnp.float32, jnp.bfloat16

CHEAP = pl.CostEstimate(flops=1, bytes_accessed=1, transcendentals=0)
DEAR = pl.CostEstimate(flops=10**10, bytes_accessed=1, transcendentals=0)
LONG = pl.CostEstimate(flops=10**11, bytes_accessed=1, transcendentals=0)


def run(kernel, after, out_shape, in_specs, operands, vmem, **options):
    count = len(operands)

    def body(*refs):
        kernel(*refs[:count], *refs[count + len(after) :])

    return pl.pallas_call(
        body,
        out_shape=out_shape,
        in_specs=list(in_specs) + [ANY] * len(after),
        compiler_params=pltpu.CompilerParams(vmem_limit_bytes=vmem * 1024 * 1024),
        **options,
    )(*operands, *after)


def normalize(inputs):
    centered = inputs - jnp.mean(inputs, axis=-1, keepdims=True)
    spread = lax.rsqrt(jnp.mean(centered * centered, axis=-1, keepdims=True) + norm_eps)
    return (centered * spread, spread)


def norm_back(grad_out, normed, spread, gain_row):
    scaled = grad_out * gain_row
    return spread * (
        scaled
        - jnp.mean(scaled, axis=-1, keepdims=True)
        - normed * jnp.mean(scaled * normed, axis=-1, keepdims=True)
    )


def dot(left_op, right_op, dims=((1,), (0,))):
    return lax.dot_general(left_op, right_op, (dims, ((), ())), preferred_element_type=F32)


ROWS = ((0,), (0,))
COLS = ((1,), (1,))


def gelu_pair(inputs):
    size = jnp.abs(inputs)
    bell = jnp.exp2(inputs * inputs * (-0.5 * 1.4426950408889634))
    t = 1.0 / (1.0 + size * (0.3275911 * 0.7071067811865476))
    tail = t * (
        0.5 * 0.254829592
        + t * (0.5 * -0.284496736 + t * (0.5 * 1.421413741 + t * (0.5 * -1.453152027 + t * (0.5 * 1.061405429))))
    )
    tail = tail * bell
    phi = jnp.where(inputs >= 0.0, 1.0 - tail, tail)
    return inputs * phi, phi + inputs * bell * 0.3989422804014327


def as_column(row):
    return jnp.broadcast_to(row, (128, row.shape[1])).T[:, :1]


def forward_kernel(
    coords_ref, length_ref, replies_ref, slot_ref, kind_ref, pos_ref, type_ref, gains_ref, shifts_ref, ffn_bias_ref,
    grad_ref, wqkv_hbm, wout_hbm, w1_hbm, w2_hbm,
    *refs,
):
    n0_ref, s0_ref, hidden_ref = refs[:3]
    top = refs[3:8]
    outs = [refs[8 + 11 * layer : 19 + 11 * layer] for layer in range(NL)]
    wqkv, wout, w1, w2, sems, xlow, mixed, ctxt, mlow, gp, act, n0, n1, n2, x, osems = refs[6 + 11 * NL :]
    tokens, width = x.shape
    ff = w1.shape[2]
    loads = []
    for layer in range(NL):
        for i, (src, dst) in enumerate([(wqkv_hbm, wqkv), (wout_hbm, wout), (w1_hbm, w1), (w2_hbm, w2)]):
            loads.append(pltpu.make_async_copy(src.at[layer], dst.at[layer], sems.at[4 * layer + i]))
    for load in loads:
        load.start()
    pending, used = {}, [0]

    def emit(name, src, dst, at=None):
        if at is not None:
            src, dst = src.at[:, at], dst.at[:, at]
        copy = pltpu.make_async_copy(src, dst, osems.at[used[0]])
        used[0] += 1
        copy.start()
        pending.setdefault(name, []).append(copy)

    def reuse(name):
        for copy in pending.pop(name, ()):
            copy.wait()

    gains = gains_ref[...].astype(F32)
    shifts = shifts_ref[...].astype(F32)
    number = lax.broadcasted_iota(jnp.int32, (tokens, replies_ref.shape[0]), 1)
    hit = jnp.where(number == as_column(slot_ref[...].astype(F32)).astype(jnp.int32), 1.0, 0.0).astype(LOW)
    types = type_ref[...].astype(F32)
    embedded = dot(hit, replies_ref[...]) + pos_ref[...].astype(F32)
    embedded = embedded + jnp.where(as_column(kind_ref[...].astype(F32)) > 0.5, types[1:2], types[0:1])
    normed, spread = normalize(embedded)
    n0[...] = normed
    emit("n0", n0, n0_ref)
    s0_ref[...] = jnp.broadcast_to(spread, s0_ref.shape)
    x[...] = normed * gains[0:1] + shifts[0:1]

    key_slot = lax.broadcasted_iota(jnp.int32, (tokens, 128), 0)
    visible = jnp.where(key_slot < length_ref[0], 0.0, -1e30)[:, :1]
    lane = lax.broadcasted_iota(jnp.int32, (tokens, 128), 1)
    chunk = 512

    for layer in range(NL):
        base = 1 + 6 * layer
        xlow_ref, mixed_ref, lse_ref, ctxt_ref, n1_ref, s1_ref, mlow_ref, gp_ref, act_ref = outs[layer][:9]

        reuse("xlow")
        xlow[...] = x[...].astype(LOW)
        emit("xlow", xlow, xlow_ref)
        loads[4 * layer].wait()
        reuse("mixed")
        for i in range(3):
            cols = slice(i * width, (i + 1) * width)
            got = dot(xlow[...], wqkv[layer, :, cols])
            if i != 1:
                row = base + (0 if i == 0 else 1)
                got = got + shifts[row : row + 1]
            mixed[:, cols] = got.astype(LOW)
        emit("mixed", mixed, mixed_ref)
        reuse("ctxt")

        def pair_step(j, carry):
            at = pl.multiple_of(j * 128, 128)
            q = mixed[:, pl.ds(at, 128)] * jnp.asarray(SCALE, LOW)
            k = mixed[:, pl.ds(pl.multiple_of(width + at, 128), 128)]
            v = mixed[:, pl.ds(pl.multiple_of(2 * width + at, 128), 128)]
            vt = v.T
            scores = []
            for h in range(2):
                kh = jnp.where((lane < 64) == (h == 0), k, jnp.zeros_like(k))
                scores.append(dot(kh, q, COLS) + visible)
            for h in range(2):
                top = jnp.max(scores[h], axis=0, keepdims=True)
                weights = jnp.exp(scores[h] - top)
                total = jnp.sum(weights, axis=0, keepdims=True)
                out = dot(vt[h * 64 : (h + 1) * 64], weights.astype(LOW)) * (1.0 / total)
                ctxt[pl.ds(pl.multiple_of(at + h * 64, 64), 64), :] = out.astype(LOW)
                lse_ref[pl.ds(2 * j + h, 1), :] = top + jnp.log(total)
            return carry

        lax.fori_loop(0, HEADS // 2, pair_step, 0)
        emit("ctxt", ctxt, ctxt_ref)
        loads[4 * layer + 1].wait()
        attended = dot(ctxt[...], wout[layer], ROWS) + shifts[base + 2 : base + 3]
        normed, spread = normalize(x[...] + attended)
        reuse("n1")
        n1[...] = normed
        emit("n1", n1, n1_ref)
        s1_ref[...] = jnp.broadcast_to(spread, s1_ref.shape)
        x[...] = normed * gains[1 + 2 * layer : 2 + 2 * layer] + shifts[base + 3 : base + 4]
        reuse("mlow")
        mlow[...] = x[...].astype(LOW)
        emit("mlow", mlow, mlow_ref)
        loads[4 * layer + 2].wait()
        reuse("gp")
        reuse("act")
        for i in range(ff // chunk):
            cols = slice(i * chunk, (i + 1) * chunk)
            pre = dot(mlow[...], w1[layer, :, cols]) + ffn_bias_ref[layer : layer + 1, cols]
            active, slope = gelu_pair(pre)
            gp[:, cols] = slope.astype(LOW)
            act[:, cols] = active.astype(LOW)
            emit("gp", gp, gp_ref, pl.ds(i * chunk, chunk))
            emit("act", act, act_ref, pl.ds(i * chunk, chunk))
        loads[4 * layer + 3].wait()
        normed, spread = normalize(x[...] + shifts[base + 4 : base + 5] + dot(act[...], w2[layer]))
        if layer < NL - 1:
            n2_ref, s2_ref = outs[layer][9:11]
            n2[...] = normed
            emit("n2", n2, n2_ref)
            s2_ref[...] = jnp.broadcast_to(spread, s2_ref.shape)
        else:
            gain = gains[2 * NL : 2 * NL + 1]
            norm_end(coords_ref[0], grad_ref[...].astype(F32), normed, spread, gain, *top)
        x[...] = normed * gains[2 + 2 * layer : 3 + 2 * layer] + shifts[base + 5 : base + 6]
    hidden_ref[...] = x[...].astype(LOW)
    for name in list(pending):
        reuse(name)


def forward(
    coords, length, replies, slot_of, kinds, pos, types, gains, shifts, ffn_bias, cotangent, w_qkv, w_out, w_ff1, w_ff2
):
    tokens, width = pos.shape
    ff = w_ff1.shape[2]
    s = jax.ShapeDtypeStruct
    v = pltpu.VMEM
    spread = s((tokens, 128), F32)
    wide = s((tokens, width), F32)
    low = s((tokens, width), LOW)
    layer_out = (
        low, s((tokens, 3 * width), LOW), s((HEADS, tokens), F32), s((width, tokens), LOW),
        wide, spread, low, s((tokens, ff), LOW), s((tokens, ff), LOW), wide, spread,
    )
    layer_spec = (ANY, ANY, VM, ANY, ANY, VM, ANY, ANY, ANY, ANY, VM)
    chunks = ff // 512
    end = norm_end_shapes(tokens, width)
    outs = run(
        forward_kernel,
        (),
        out_shape=(wide, spread, low) + end + layer_out * (NL - 1) + layer_out[:9],
        in_specs=[SM, SM] + [VM] * 9 + [HBM] * 4,
        operands=(
            coords, length, replies, slot_of, kinds, pos, types, gains, shifts, ffn_bias, cotangent, w_qkv, w_out, w_ff1, w_ff2
        ),
        out_specs=(ANY, VM, VM) + (VM,) * 5 + layer_spec * (NL - 1) + layer_spec[:9],
        scratch_shapes=[
            v((NL, width, 3 * width), LOW), v((NL, width, width), LOW), v((NL, width, ff), LOW), v((NL, ff, width), LOW),
            pltpu.SemaphoreType.DMA((4 * NL,)),
            v((tokens, width), LOW), v((tokens, 3 * width), LOW), v((width, tokens), LOW), v((tokens, width), LOW),
            v((tokens, ff), LOW), v((tokens, ff), LOW), v((tokens, width), F32), v((tokens, width), F32),
            v((tokens, width), F32), v((tokens, width), F32), pltpu.SemaphoreType.DMA((1 + NL * (6 + 2 * chunks),)),
        ],
        cost_estimate=CHEAP,
        vmem=60,
        name="forward",
    )
    return outs[:3], outs[3:8], [outs[8 + 11 * layer : 19 + 11 * layer] for layer in range(NL)]


def part(mine, source, keep_to, send_to):
    half = source.shape[1] // 2

    @pl.when(mine == 0)
    def _():
        keep_to[...] = source[:, :half]
        send_to[...] = source[:, half:]

    @pl.when(mine == 1)
    def _():
        keep_to[...] = source[:, half:]
        send_to[...] = source[:, :half]


def norm_end(mine, grad, n, s, gain, back_ref, low_ref, keep_ref, send_ref, sums_ref):
    sums_ref[0:1] = jnp.sum(grad * n, axis=0, keepdims=True)
    sums_ref[1:2] = jnp.sum(grad, axis=0, keepdims=True)
    back = norm_back(grad, n, s, gain)
    sums_ref[2:3] = jnp.sum(back, axis=0, keepdims=True)
    back_ref[...] = back
    low_ref[...] = back.astype(LOW)
    if keep_ref is not None:
        part(mine, low_ref, keep_ref, send_ref)


def norm_end_shapes(tokens, width):
    s = jax.ShapeDtypeStruct
    half = s((tokens, width // 2), LOW)
    return (s((tokens, width), F32), s((tokens, width), LOW), half, half, s((3, width), F32))


def feed_back_body(mine, second, gp, w2, ready, bias_ref, keep, send):
    chunk = 512
    steps = gp.shape[1] // chunk
    for i in range(steps):
        ready(i)
        cols = slice(i * chunk, (i + 1) * chunk)
        grad_pre = dot(second[...], w2[cols, :], COLS) * gp[:, cols].astype(F32)
        bias_ref[:, cols] = jnp.sum(grad_pre, axis=0, keepdims=True)
        side, at = divmod(i, steps // 2)
        there = slice(at * chunk, (at + 1) * chunk)
        low = grad_pre.astype(LOW)

        @pl.when(mine == side)
        def _():
            keep[:, there] = low

        @pl.when(mine != side)
        def _():
            send[:, there] = low


def both_halves(mine, keep, send, weight):
    half = keep.shape[1]
    first = jnp.where(mine == 0, keep[...], send[...])
    second = jnp.where(mine == 0, send[...], keep[...])
    return dot(first, weight[:, :half], COLS) + dot(second, weight[:, half:], COLS)


def attend_back_body(length_ref, mixed_ref, lse_ref, gctx_ref, att_ref, dmix):
    tokens, width = gctx_ref.shape
    key_slot = lax.broadcasted_iota(jnp.int32, (tokens, 128), 0)
    visible = jnp.where(key_slot < length_ref[0], 0.0, -1e30)[:, :1]
    lane = lax.broadcasted_iota(jnp.int32, (tokens, 128), 1)

    def pair_step(j, carry):
        at = pl.multiple_of(j * 128, 128)
        qcols = pl.ds(at, 128)
        kcols = pl.ds(pl.multiple_of(width + at, 128), 128)
        vcols = pl.ds(pl.multiple_of(2 * width + at, 128), 128)
        q = mixed_ref[:, qcols] * jnp.asarray(SCALE, LOW)
        k = mixed_ref[:, kcols]
        v = mixed_ref[:, vcols]
        g = gctx_ref[:, qcols]
        kt = k.T
        grad_v, grad_k, grad_qt = [], [], []
        scores, grad_probs = [], []
        for h in range(2):
            mask = (lane < 64) == (h == 0)
            kh = jnp.where(mask, k, jnp.zeros_like(k))
            vh = jnp.where(mask, v, jnp.zeros_like(v))
            scores.append(dot(kh, q, COLS))
            grad_probs.append(dot(vh, g, COLS))
        for h in range(2):
            probs = jnp.exp(scores[h] + visible - lse_ref[pl.ds(2 * j + h, 1), :])
            weighted = jnp.sum(probs * grad_probs[h], axis=0, keepdims=True)
            grad_scores = (probs * (grad_probs[h] - weighted)).astype(LOW)
            grad_v.append(dot(probs.astype(LOW), g))
            grad_k.append(dot(grad_scores, q))
            grad_qt.append(dot(kt[h * 64 : (h + 1) * 64], grad_scores))
        grad_q = jnp.concatenate(grad_qt, axis=0).T * SCALE
        grad_v = jnp.where(lane < 64, grad_v[0], grad_v[1])
        grad_k = jnp.where(lane < 64, grad_k[0], grad_k[1])
        att_ref[0:1, qcols] = jnp.sum(grad_q, axis=0, keepdims=True)
        att_ref[1:2, qcols] = jnp.sum(grad_v, axis=0, keepdims=True)
        dmix[:, qcols] = grad_q.astype(LOW)
        dmix[:, kcols] = grad_k.astype(LOW)
        dmix[:, vcols] = grad_v.astype(LOW)
        return carry

    lax.fori_loop(0, HEADS // 2, pair_step, 0)


def chunk_loads(sems, at, pairs, chunk=512):
    loads = []
    (w2_src, w2), (gp_src, gp) = pairs
    for i in range(gp.shape[1] // chunk):
        there = pl.ds(i * chunk, chunk)
        loads.append(
            (
                pltpu.make_async_copy(w2_src.at[there], w2.at[there], sems.at[at + 2 * i]),
                pltpu.make_async_copy(gp_src.at[:, there], gp.at[:, there], sems.at[at + 2 * i + 1]),
            )
        )
    return loads


def feed_kernel(
    layer, coords_ref, e_ref, second, n1_ref, s1_ref, gains_ref, gp_hbm, wout_hbm, w1_hbm, w2_hbm,
    keep_ref, send_ref, bias_ref, first_ref, low_ref, fst_keep_ref, fst_send_ref, gctx_ref, sums_ref,
    gp, wout, w1, w2, keep, send, sems,
):
    mine = coords_ref[0]
    loads = chunk_loads(sems, 4, ((w2_hbm.at[layer], w2), (gp_hbm, gp)))
    for pair in loads:
        for load in pair:
            load.start()
    late = [
        pltpu.make_async_copy(w1_hbm.at[layer], w1, sems.at[0]),
        pltpu.make_async_copy(wout_hbm.at[layer], wout, sems.at[1]),
    ]
    for load in late:
        load.start()

    def ready(i):
        for load in loads[i]:
            load.wait()

    feed_back_body(mine, second, gp, w2, ready, bias_ref, keep, send)
    stores = [
        pltpu.make_async_copy(send, send_ref, sems.at[2]),
        pltpu.make_async_copy(keep, keep_ref, sems.at[3]),
    ]
    for store in stores:
        store.start()
    late[0].wait()
    grad = e_ref[...] + both_halves(mine, keep, send, w1)
    gain = gains_ref[...].astype(F32)[1 + 2 * layer : 2 + 2 * layer]
    norm_end(mine, grad, n1_ref[...], s1_ref[:, :1], gain, first_ref, low_ref, fst_keep_ref, fst_send_ref, sums_ref)
    late[1].wait()
    gctx_ref[...] = dot(low_ref[...], wout[...], COLS).astype(LOW)
    for store in stores:
        store.wait()


def feed(layer, coords, e, second, n1, s1, gains, gp, w_out, w_ff1, w_ff2, after=()):
    tokens, width = n1.shape
    ff = gp.shape[1]
    s = jax.ShapeDtypeStruct
    v = pltpu.VMEM
    half = s((tokens, ff // 2), LOW)
    end = norm_end_shapes(tokens, width)
    return run(
        functools.partial(feed_kernel, layer),
        after,
        out_shape=(half, half, s((1, ff), F32)) + end[:4] + (s((tokens, width), LOW), end[4]),
        in_specs=[SM] + [VM] * 5 + [HBM] * 4,
        operands=(coords, e, second, n1, s1, gains, gp, w_out, w_ff1, w_ff2),
        out_specs=(ANY, ANY) + (VM,) * 7,
        scratch_shapes=[
            v((tokens, ff), LOW), v((width, width), LOW), v((width, ff), LOW), v((ff, width), LOW),
            v((tokens, ff // 2), LOW), v((tokens, ff // 2), LOW), pltpu.SemaphoreType.DMA((4 + 2 * (ff // 512),)),
        ],
        cost_estimate=CHEAP,
        vmem=52,
        name="feed",
    )


def between_kernel(
    layer, coords_ref, length_ref, mixed_ref, lse_ref, gctx_in, first_in, n2_ref, s2_ref, n1_ref, s1_ref, gains_ref,
    gp_hbm, wqkv_hbm, wout_hbm, w1_hbm, w2_hbm,
    mix_keep_ref, mix_send_ref, pre_keep_ref, pre_send_ref,
    att_ref, sec_keep_ref, sec_send_ref, top_ref, bias_ref, first_ref, fst_keep_ref, fst_send_ref, gctx_ref, sums_ref,
    gp, wqkv, wout, w1, w2, dmix, mix_keep, mix_send, keep, send, e, second, low_ref, sems,
):
    mine = coords_ref[0]
    below = layer - 1
    early = pltpu.make_async_copy(wqkv_hbm.at[layer], wqkv, sems.at[0])
    early.start()
    loads = chunk_loads(sems, 7, ((w2_hbm.at[below], w2), (gp_hbm, gp)))
    for pair in loads:
        for load in pair:
            load.start()
    late = [
        pltpu.make_async_copy(w1_hbm.at[below], w1, sems.at[1]),
        pltpu.make_async_copy(wout_hbm.at[below], wout, sems.at[2]),
    ]
    for load in late:
        load.start()
    stores = []

    def emit(src, dst):
        stores.append(pltpu.make_async_copy(src, dst, sems.at[3 + len(stores)]))
        stores[-1].start()

    attend_back_body(length_ref, mixed_ref, lse_ref, gctx_in, att_ref, dmix)
    part(mine, dmix, mix_keep, mix_send)
    emit(mix_send, mix_send_ref)
    emit(mix_keep, mix_keep_ref)
    early.wait()
    grad = first_in[...] + dot(dmix[...], wqkv[...], COLS)
    gains = gains_ref[...].astype(F32)
    norm_end(
        mine, grad, n2_ref[...], s2_ref[:, :1], gains[2 * layer : 2 * layer + 1], e, second, sec_keep_ref, sec_send_ref, top_ref
    )

    def ready(i):
        for load in loads[i]:
            load.wait()

    feed_back_body(mine, second, gp, w2, ready, bias_ref, keep, send)
    emit(send, pre_send_ref)
    emit(keep, pre_keep_ref)
    late[0].wait()
    grad = e[...] + both_halves(mine, keep, send, w1)
    norm_end(
        mine, grad, n1_ref[...], s1_ref[:, :1], gains[1 + 2 * below : 2 + 2 * below], first_ref, low_ref, fst_keep_ref,
        fst_send_ref, sums_ref,
    )
    late[1].wait()
    gctx_ref[...] = dot(low_ref[...], wout[...], COLS).astype(LOW)
    for store in stores:
        store.wait()


def between(layer, coords, length, mixed, lse, gctx, first, n2, s2, n1, s1, gains, gp, w_qkv, w_out, w_ff1, w_ff2, after=()):
    tokens, width = first.shape
    ff = gp.shape[1]
    s = jax.ShapeDtypeStruct
    v = pltpu.VMEM
    mix = s((tokens, 3 * width // 2), LOW)
    pre = s((tokens, ff // 2), LOW)
    sec = s((tokens, width // 2), LOW)
    low = s((tokens, width), LOW)
    three = s((3, width), F32)
    return run(
        functools.partial(between_kernel, layer),
        after,
        out_shape=(
            mix, mix, pre, pre, s((2, width), F32), sec, sec, three, s((1, ff), F32), s((tokens, width), F32), sec, sec, low, three,
        ),
        in_specs=[SM, SM] + [VM] * 9 + [HBM] * 5,
        operands=(coords, length, mixed, lse, gctx, first, n2, s2, n1, s1, gains, gp, w_qkv, w_out, w_ff1, w_ff2),
        out_specs=(ANY,) * 4 + (VM,) * 10,
        scratch_shapes=[
            v((tokens, ff), LOW), v((width, 3 * width), LOW), v((width, width), LOW), v((width, ff), LOW), v((ff, width), LOW),
            v((tokens, 3 * width), LOW), v(mix.shape, LOW), v(mix.shape, LOW), v(pre.shape, LOW), v(pre.shape, LOW),
            v((tokens, width), F32), v((tokens, width), LOW), v((tokens, width), LOW),
            pltpu.SemaphoreType.DMA((7 + 2 * (ff // 512),)),
        ],
        cost_estimate=CHEAP,
        vmem=58,
        name="between",
    )


COORDS = ("core", "x", "a", "b", "y")


def place(coords_ref, plan, result, *outs):
    count = result.shape[0]
    size = count // len(outs)
    dims = [] if plan is None else [dim for turn in plan for dim in turn]
    for i in range(count):
        block = i
        if plan is not None:
            bit = {}
            for n, dim in enumerate(dims):
                relative = (i >> (len(dims) - 1 - n)) & 1
                whole = plan[-1] == ("y",) and n == len(dims) - 1
                bit[dim] = relative if whole else coords_ref[COORDS.index(dim)] ^ relative
            block = 16 * bit.get("core", 0) + 8 * bit["b"] + 4 * bit["a"] + 2 * bit["x"] + bit["y"]
        out = outs[i // size]
        out[i % size] = result[block].astype(out.dtype)


def parts_of(plan):
    return 2 if plan is None else 2 ** len(plan[0])


def load_both(pairs, sems):
    loads = []
    for own, oth, dst in pairs:
        for n, src in enumerate((own, oth)):
            size = own.shape[0]
            load = pltpu.make_async_copy(src, dst.at[pl.ds(n * size, size)], sems.at[len(loads)])
            load.start()
            loads.append(load)
    return loads


def weights_kernel(plans, blocks, coords_ref, *refs):
    count = 8 if len(plans) == 2 else 20
    sources, refs = refs[:count], refs[count:]
    outs = []
    for plan in plans:
        outs.append(refs[: parts_of(plan)])
        refs = refs[parts_of(plan) :]
    sec, act, mid, pre, sect, midt, two, one = refs[:8]
    rest, sems = refs[8:-1], refs[-1]
    tokens = sources[0].shape[0]
    loads = []
    targets = [sec, act, mid, pre]
    if rest:
        x, mix, ctxt, fst, below_ctxt, below_fst, xt, mixed = rest
        targets += [x, mix, ctxt, fst, below_ctxt, below_fst]
    for n, target in enumerate(targets):
        for side in range(2):
            there = pl.ds(side * tokens, tokens)
            view = target.at[:, there] if n in (6, 8) else target.at[there]
            loads.append(pltpu.make_async_copy(sources[2 * n + side], view, sems.at[2 * n + side]))
            loads[-1].start()

    def ready(n):
        loads[2 * n].wait()
        loads[2 * n + 1].wait()

    ready(0)
    sect[...] = sec[...].T
    ready(1)
    rows = two.shape[1]
    cols = act.shape[1] // blocks

    group = 4 if blocks % 4 == 0 else 1

    def step_two(i, carry):
        there = pl.ds(pl.multiple_of(i * group * cols, cols), group * cols)
        got = dot(sect[...], act[:, there]).astype(LOW)
        for v in range(group):
            for y in range(2):
                for n in range(4):
                    at = (4 * y + n) * rows
                    piece = got[at : at + rows, v * cols : (v + 1) * cols]
                    two[2 * (i * group + v) + y, :, n * cols : (n + 1) * cols] = piece
        return carry

    lax.fori_loop(0, blocks // group, step_two, 0)
    place(coords_ref, plans[0], two, *outs[0])
    ready(2)
    midt[...] = mid[...].T
    ready(3)
    chunk = 512
    high = midt.shape[0] // one.shape[0]

    def step_one(i, carry):
        there = pl.ds(pl.multiple_of(i * chunk, chunk), chunk)
        one[:, :high, there] = dot(midt[...], pre[:, there]).astype(LOW).reshape(one.shape[0], high, chunk)
        return carry

    if rest:
        lax.fori_loop(0, pre.shape[1] // chunk, step_one, 0)
        ready(8)
        ready(9)
        part_cols, group_rows = below_fst.shape[1], one.shape[1] - high
        got = dot(below_ctxt[...], below_fst[...]).astype(LOW).reshape(one.shape[0], high, part_cols)
        for n in range(high // group_rows):
            there = slice(n * part_cols, (n + 1) * part_cols)
            one[:, high:, there] = got[:, n * group_rows : (n + 1) * group_rows]
        one[:, high:, high // group_rows * part_cols :] = jnp.zeros((one.shape[0], group_rows, part_cols), LOW)
    else:
        one[...] = dot(midt[...], pre[...]).astype(LOW).reshape(one.shape)
    place(coords_ref, plans[1], one, *outs[1])
    if rest:
        ready(4)
        xt[...] = x[...].T
        ready(5)
        wide = mix.shape[1]
        mixed[:, :, :wide] = dot(xt[...], mix[...]).astype(LOW).reshape(mixed.shape[:2] + (wide,))
        ready(6)
        ready(7)
        mixed[:, :, wide:] = dot(ctxt[...], fst[...]).astype(LOW).reshape(mixed.shape[:2] + (fst.shape[1],))
        place(coords_ref, plans[2], mixed, *outs[2])


def weights(blocks, plans, coords, sec, act, mid, pre, attention=(), after=()):
    tokens, width = mid[0].shape
    s = jax.ShapeDtypeStruct
    v = pltpu.VMEM
    count = 2 * blocks
    block = (count, width // count, 2 * width)
    high = (count, width // count + 16, 2 * width) if attention else block
    sizes = (block, high, block)
    outs = sum(
        ((s((count // parts_of(plan),) + size[1:], LOW),) * parts_of(plan) for plan, size in zip(plans, sizes)), ()
    )
    pairs = (sec, act, mid, pre) + tuple(attention)
    both = lambda pair: v((2 * tokens, pair[0].shape[1]), LOW)
    scratch = [both(pair) for pair in (sec, act, mid, pre)]
    scratch += [v((sec[0].shape[1], 2 * tokens), LOW), v((width, 2 * tokens), LOW), v(block, LOW), v(high, LOW)]
    if attention:
        x, mix, _, fst, _, below_fst = attention
        across = v((width, 2 * tokens), LOW)
        scratch += [both(x), both(mix), across, both(fst), across, both(below_fst), across, v(block, LOW)]
    got = run(
        functools.partial(weights_kernel, plans, blocks),
        after,
        out_shape=outs,
        in_specs=[SM] + [ANY] * (2 * len(pairs)),
        operands=(coords,) + tuple(array for pair in pairs for array in pair),
        out_specs=(VM,) * len(outs),
        scratch_shapes=scratch + [pltpu.SemaphoreType.DMA((2 * len(pairs),))],
        cost_estimate=CHEAP,
        vmem=56 if attention else 34,
        name="weights",
    )
    parts = []
    for plan in plans:
        parts.append(got[: parts_of(plan)])
        got = got[parts_of(plan) :]
    return parts


def combine_kernel(forms, *refs):
    count = sum(sum(form[0]) for form in forms)
    ins, outs = refs[:count], refs[count:]
    for terms_of, parts, axis in forms:
        results, outs = outs[:parts], outs[parts:]
        at = 0
        for terms in terms_of:
            mine, ins = ins[:terms], ins[terms:]
            size = mine[0].shape[0] // parts
            rows = mine[0].shape[1]
            for part in range(parts):
                for i in range(size):
                    total = mine[0][part * size + i].astype(F32)
                    for term in mine[1:]:
                        total = total + term[part * size + i].astype(F32)
                    if axis == 0:
                        results[part][at + i] = total.astype(LOW)
                    else:
                        results[part][i, at : at + rows] = total.astype(LOW)
            at += size if axis == 0 else rows


def combine(items, after=(), cost=CHEAP):
    forms = tuple((tuple(len(terms) for terms in sums), parts, axis) for sums, parts, axis in items)
    shapes = []
    for sums, parts, axis in items:
        shape = list(sums[0][0].shape)
        shape[axis] = sum(terms[0].shape[axis] for terms in sums)
        shape[0] //= parts
        shapes += [jax.ShapeDtypeStruct(tuple(shape), LOW)] * parts
    operands = tuple(array for sums, _, _ in items for terms in sums for array in terms)
    size = sum(array.size for array in operands)
    outs = run(
        functools.partial(combine_kernel, forms),
        after,
        out_shape=tuple(shapes),
        in_specs=[VM] * len(operands),
        operands=operands,
        out_specs=(VM,) * len(shapes),
        cost_estimate=cost,
        vmem=6 + 4 * size // (1 << 20),
        name="combine",
    )
    got = []
    for _, parts, _ in forms:
        got.append(outs[:parts])
        outs = outs[parts:]
    return got


def last_kernel(
    plan, coords_ref, length_ref, mixed_ref, lse_ref, gctx_ref, first_ref, n_ref, s_ref, gains_ref, x_ref,
    slot_ref, type_ref, top0, top1, low0, low1, att1, bias0, bias1, wqkv_hbm,
    out_ref, *parts_and_scratch
):
    outs, (wqkv, dmix, xt, res, back_ref, back_low, att0, emb, small, sems) = parts_and_scratch[:-10], parts_and_scratch[-10:]
    tokens, width = back_ref.shape
    load = pltpu.make_async_copy(wqkv_hbm.at[0], wqkv, sems.at[0])
    load.start()
    attend_back_body(length_ref, mixed_ref, lse_ref, gctx_ref, att0, dmix)
    load.wait()
    grad = first_ref[...] + dot(dmix[...], wqkv[...], COLS)
    gain = gains_ref[...].astype(F32)[0:1]
    norm_end(coords_ref[0], grad, n_ref[...], s_ref[:, :1], gain, back_ref, back_low, None, None, emb)
    slots = out_ref.shape[0]
    chunk = 256

    def step(i, carry):
        there = pl.ds(pl.multiple_of(i * chunk, chunk), chunk)
        number = lax.broadcasted_iota(jnp.int32, (chunk, tokens), 0) + i * chunk
        hit = jnp.where(number == slot_ref[...], 1.0, 0.0).astype(LOW)
        out_ref[there, :] = dot(hit, back_low[...]).astype(LOW)
        return carry

    lax.fori_loop(0, slots // chunk, step, 0)
    xt[...] = x_ref[...].T
    blocks, piece, _ = res.shape
    blocks //= 2
    half = width // 2
    wide = 3 * half
    for core in range(2):
        there = slice(core * blocks, (core + 1) * blocks)
        got = dot(xt[...], dmix[:, core * wide : (core + 1) * wide]).astype(LOW)
        res[there, :, :wide] = got.reshape(blocks, piece, wide)
    back = back_ref[...]
    kind = as_column(type_ref[...].astype(F32))
    small[0:1] = jnp.sum(back * (1.0 - kind), axis=0, keepdims=True)
    small[1:2] = jnp.sum(back * kind, axis=0, keepdims=True)
    sources = [(emb, 0)]
    for top, low in ((top0, low0), (top1, low1)):
        sources += [(low, 0), (top, 0)]
    sources += [(emb, 1)]
    for top, low, att in ((top0, low0, att0), (top1, low1, att1)):
        sources += [(att, 0), (att, 1), (low, 2), (low, 1), (top, 2), (top, 1)]
    at = 2
    for ref, row in sources:
        small[at : at + 1] = ref[row : row + 1]
        at += 1
    for bias in (bias0, bias1):
        for i in range(bias.shape[1] // width):
            small[at : at + 1] = bias[:, i * width : (i + 1) * width]
            at += 1
    quarter = at // 4
    group = tokens // blocks
    positions = back.reshape(blocks, group, width).astype(LOW)
    for core in range(2):
        there = slice(core * blocks, (core + 1) * blocks)
        res[there, :group, wide:] = positions[:, :, core * half : (core + 1) * half]
        for y in range(2):
            mine = small[(2 * core + y) * quarter : (2 * core + y + 1) * quarter]
            rest = jnp.zeros((piece - group - 2 * quarter, half), F32)
            mine = jnp.concatenate([mine[:, :half], mine[:, half:], rest], axis=0).astype(LOW)
            for v in range(blocks // 2):
                res[core * blocks + 2 * v + y, group:, wide:] = mine
    place(coords_ref, plan, res, *outs)


def last(plan, coords, length, mixed, lse, gctx, first, n, sp, gains, x, slot_of, types, sums, w_qkv, slots, blocks, parts=2, after=()):
    tokens, width = first.shape
    s = jax.ShapeDtypeStruct
    v = pltpu.VMEM
    block = (blocks, width // blocks, 2 * width)
    operands = (coords, length, mixed, lse, gctx, first, n, sp, gains, x, slot_of, types, *sums, w_qkv)
    return run(
        functools.partial(last_kernel, plan),
        after,
        out_shape=(s((slots, width), LOW),) + (s((2 * blocks // parts,) + block[1:], LOW),) * parts,
        in_specs=[SM, SM] + [VM] * (len(operands) - 3) + [HBM],
        operands=operands,
        out_specs=(VM,) * (1 + parts),
        scratch_shapes=[
            v((width, 3 * width), LOW), v((tokens, 3 * width), LOW), v((width, tokens), LOW),
            v((2 * blocks,) + block[1:], LOW), v((tokens, width), F32), v((tokens, width), LOW),
            v((2, width), F32), v((3, width), F32), v((28, width), F32), pltpu.SemaphoreType.DMA((1,)),
        ],
        cost_estimate=CHEAP,
        vmem=52,
        name="last",
    )


def table_back_kernel(coords_ref, asked_ref, rows_ref, keep_ref, send_ref, total):
    count = total.shape[0]
    chunk = count // 5 if count % 5 == 0 else count

    def step(i, carry):
        at = pl.multiple_of(i * chunk, 8)
        number = lax.broadcasted_iota(jnp.int32, (chunk, rows_ref.shape[0]), 0) + at
        hit = jnp.where(number == asked_ref[...], 1.0, 0.0).astype(LOW)
        total[pl.ds(at, chunk), :] = dot(hit, rows_ref[...])
        return carry

    lax.fori_loop(0, count // chunk, step, 0)
    mine = coords_ref[0]
    half = total.shape[1] // 2

    @pl.when(mine == 0)
    def _():
        keep_ref[...] = total[:, :half].astype(LOW)
        send_ref[...] = total[:, half:].astype(LOW)

    @pl.when(mine == 1)
    def _():
        keep_ref[...] = total[:, half:].astype(LOW)
        send_ref[...] = total[:, :half].astype(LOW)


def table_back(coords, asked, rows, local_rows, after=()):
    width = rows.shape[1]
    half = jax.ShapeDtypeStruct((local_rows, width // 2), LOW)
    return run(
        table_back_kernel,
        after,
        out_shape=(half, half),
        in_specs=[SM, VM, VM],
        operands=(coords, asked, rows),
        out_specs=(VM, VM),
        scratch_shapes=[pltpu.VMEM((local_rows, width), F32)],
        cost_estimate=CHEAP,
        vmem=16,
        name="table_back",
    )


def finish_kernel(coords_ref, *refs):
    many, few = refs[:4], refs[4:8]
    qkv_ref, wout_ref, one_ref, two_ref, pos_ref, small_ref = refs[8:]
    mine_core, mine_y = coords_ref[0] == 0, coords_ref[4] == 0
    half = wout_ref.shape[2] // 2
    wide = 3 * half
    part = wout_ref.shape[1] // 2

    def piece(four, rows, core, y):
        own, over_y, over_core, over_both = (ref[0, rows] for ref in four)
        same_y = mine_y if y == 0 else jnp.logical_not(mine_y)
        same_core = mine_core if core == 0 else jnp.logical_not(mine_core)
        here = jnp.where(same_y, own, over_y)
        there = jnp.where(same_y, over_core, over_both)
        return jnp.where(same_core, here, there).astype(F32)

    at = lambda n: slice(n * part, (n + 1) * part)
    mix1, two0, one0, two1, one1 = at(0), at(1), at(2), slice(3 * part + 16, 4 * part + 16), slice(4 * part + 16, 5 * part + 16)
    for layer in range(NL):
        for core in range(2):
            columns = []
            mine = slice(core * half, (core + 1) * half)
            for y in range(2):
                rows = slice(y * part, (y + 1) * part)
                mix = piece(few, slice(0, part), core, y) if layer == 0 else piece(many, mix1, core, y)
                qkv_ref[layer, rows, core * wide : (core + 1) * wide] = mix[:, :wide]
                if layer == 0:
                    group = pos_ref.shape[0] // 2
                    pos_ref[y * group : (y + 1) * group, mine] = mix[:group, wide:]
                    first = (2 * core + y) * 7
                    small_ref[first : first + 7, :half] = mix[group : group + 7, wide:]
                    small_ref[first : first + 7, half:] = mix[group + 7 : group + 14, wide:]
                    out = piece(many, slice(3 * part, 3 * part + 16), core, y)
                    for n in range(part // 16):
                        there = slice(y * part + 16 * n, y * part + 16 * (n + 1))
                        wout_ref[layer, there, mine] = out[:, n * half : (n + 1) * half]
                else:
                    wout_ref[layer, rows, mine] = mix[:, wide:]
                one_ref[layer, rows, core * 4 * half : (core + 1) * 4 * half] = piece(many, one0 if layer == 0 else one1, core, y)
                second = piece(many, two0 if layer == 0 else two1, core, y)
                columns += [second[:, i * half : (i + 1) * half] for i in range(4)]
            two_ref[layer, :, mine] = jnp.concatenate(columns, axis=0).T


def finish(coords, many, few, width, ff, owners):
    s = jax.ShapeDtypeStruct
    rows = width // owners
    return run(
        finish_kernel,
        (),
        out_shape=(
            s((NL, rows, 3 * width), F32), s((NL, rows, width), F32), s((NL, rows, ff), F32), s((NL, ff // owners, width), F32),
            s((64, width), F32), s((28, width), F32),
        ),
        in_specs=[SM] + [VM] * 8,
        operands=(coords, *many, *few),
        out_specs=(VM,) * 6,
        cost_estimate=CHEAP,
        vmem=24,
        name="finish",
    )


AXES = ("dp", "vocab")
VOCAB_MASK = {"x": 1, "a": 2, "b": 4}


def add(left_op, right_op):
    return (left_op.astype(F32) + right_op.astype(F32)).astype(LOW)


class Cube:
    def __init__(self, dp_size, vocab_size):
        self.dp_size = dp_size
        self.vocab_size = vocab_size
        self.dp_bits = dp_size.bit_length() - 1
        self.vocab_bits = vocab_size.bit_length() - 1
        assert 1 << self.dp_bits == dp_size and 1 << self.vocab_bits == vocab_size
        self.small = self.dp_bits == 2 and self.vocab_bits == 3

    def permute(self, value, dp_mask, vocab_mask):
        count = self.vocab_size
        pairs = [
            (d * count + v, (d ^ dp_mask) * count + (v ^ vocab_mask))
            for d in range(self.dp_size)
            for v in range(count)
        ]
        return lax.ppermute(value, AXES, pairs)

    def core(self, value):
        return self.permute(value, 1, 0)

    def along(self, value, dims):
        return self.permute(
            value, 2 * ("y" in dims) + ("core" in dims), sum(VOCAB_MASK[dim] for dim in dims if dim in VOCAB_MASK)
        )

    def core_is_first(self):
        return (lax.axis_index("dp") & 1) == 0

    def coords(self):
        dp, vocab = lax.axis_index("dp"), lax.axis_index("vocab")
        return jnp.stack([dp & 1, vocab & 1, (vocab >> 1) & 1, (vocab >> 2) & 1, (dp >> 1) & 1, vocab])

    def halves(self, matrix):
        mine = lax.axis_index("dp") & 1
        width = matrix.shape[1] // 2
        keep = lax.dynamic_slice_in_dim(matrix, mine * width, width, 1)
        send = lax.dynamic_slice_in_dim(matrix, (1 - mine) * width, width, 1)
        return keep, send

    def ordered(self, first, mine, other, axis):
        return jnp.concatenate(
            [jnp.where(first, mine, other), jnp.where(first, other, mine)], axis=axis
        )

    def join_core(self, share, axis):
        return self.ordered(self.core_is_first(), share, self.core(share), axis).astype(F32)

    def reduce(self, matrix):
        for bit in reversed(range(self.vocab_bits)):
            mine = (lax.axis_index("vocab") >> bit) & 1
            rows = matrix.shape[0] // 2
            keep = lax.dynamic_slice_in_dim(matrix, mine * rows, rows, 0)
            send = lax.dynamic_slice_in_dim(matrix, (1 - mine) * rows, rows, 0)
            matrix = add(keep, self.permute(send, 0, 1 << bit))
        for bit in range(1, self.dp_bits):
            matrix = add(matrix, self.permute(matrix, 1 << bit, 0))
        return matrix


def on_device(
    cube,
    token_ids,
    lengths,
    type_ids,
    word_table,
    pos_table,
    type_table,
    gains,
    shifts,
    w_qkv,
    w_out,
    b_ff1,
    w_ff1,
    w_ff2,
    cotangent,
):
    owners = cube.vocab_size
    local_rows, width = word_table.shape
    assert token_ids.shape[0] == 1
    tokens = token_ids.shape[1]
    slot_count = 2 * tokens // owners
    slots = owners * slot_count
    coords = cube.coords()

    all_ids = lax.all_to_all(
        jnp.broadcast_to(token_ids, (owners, tokens)), "vocab", split_axis=0, concat_axis=0, tiled=True
    )
    local = all_ids - lax.axis_index("vocab") * local_rows
    here = (local >= 0) & (local < local_rows)
    rank = jnp.cumsum(here.astype(jnp.int32), axis=1) - 1
    slot_hit = (
        jnp.where(here, rank, -1)[:, None, :] == jnp.arange(slot_count, dtype=jnp.int32)[None, :, None]
    )
    asked = jnp.sum(jnp.where(slot_hit, local[:, None, :] + 1, 0), axis=2).reshape(slots) - 1
    row_hit = (asked[:, None] == jnp.arange(local_rows, dtype=jnp.int32)[None, :]).astype(LOW)
    replies = exchange_rows(dot(row_hit, word_table).astype(LOW), owners)
    number = jnp.arange(owners, dtype=jnp.int32)[:, None]
    chosen = (token_ids >= number * local_rows) & (token_ids < (number + 1) * local_rows)
    own_rank = jnp.cumsum(chosen.astype(jnp.int32), axis=1) - 1
    slot_row = jnp.sum(jnp.where(chosen, number * slot_count + own_rank, 0), axis=0, keepdims=True)
    asked = asked[None, :]
    (n0, s0, hidden), top, layers = forward(
        coords, lengths, replies, slot_row, type_ids, pos_table, type_table, gains, shifts, b_ff1.astype(F32),
        cotangent.reshape(tokens, width), w_qkv, w_out, w_ff1, w_ff2,
    )
    norms, saved = [(n0, s0)], []
    for xlow, mixed, lse, ctxt, n1, s1, mlow, gp, act, *end in layers:
        saved.append((mixed, lse, n1, s1, gp) + tuple((own, cube.core(own)) for own in (xlow, ctxt, mlow, act)))
        norms.append(tuple(end))
    hidden_out = hidden.reshape(1, tokens, width)

    gradients = gradients_small if cube.small else gradients_any
    outs = gradients(
        cube, coords, lengths, top, saved, gains, w_qkv, w_out, w_ff1, w_ff2,
        norms, (type_ids, slot_row, asked, local_rows),
    )
    return (hidden_out,) + outs


def exchange_rows(outgoing, owners):
    shape = outgoing.shape
    return lax.all_to_all(
        outgoing.reshape(owners, -1, shape[1]), "vocab", split_axis=0, concat_axis=0, tiled=True
    ).reshape(shape)


def unpack(pack):
    cores, blocks, _, half = pack.shape
    pos = pack[:, :, :32].transpose(1, 2, 0, 3).reshape(blocks * 32, 2 * half)
    small = pack[:, :2, 32:46].reshape(cores, 2, 2, 7, half).transpose(0, 1, 3, 2, 4)
    return pos, small.reshape(28, 2 * half)


def small_outs(cube, rows):
    place_of = lax.axis_index("vocab")

    def mine(array):
        size = array.shape[1] // cube.vocab_size
        return lax.dynamic_slice_in_dim(array, place_of * size, size, 1)

    few = mine(rows[:20])
    return few[:2], few[2 : 2 + 2 * NL + 1], few[2 + 2 * NL + 1 :], mine(rows[20:].reshape(NL, -1))


def gradients_any(cube, coords, lengths, top, saved, gains, w_qkv, w_out, w_ff1, w_ff2, norms, embed):
    owners = cube.vocab_size
    width = w_out.shape[1]
    tokens = top[0].shape[0]
    blocks = 8
    half = width // 2
    kinds, slot_row, asked, local_rows = embed
    mixed1, lse1, n1_1, s1_1, gp1, x1, ctx1, mid1, act1 = saved[1]
    mixed0, lse0, n1_0, s1_0, gp0, x0, ctx0, mid0, act0 = saved[0]
    e, low, sec_keep, sec_send, top1 = top
    pre_keep, pre_send, bias1, first, _, fst_keep, fst_send, gctx, sums1 = feed(
        1, coords, e, low, n1_1, s1_1, gains, gp1, w_out, w_ff1, w_ff2
    )
    pair = lambda keep, send: (keep, cube.core(send))
    two1, one1 = weights(blocks, (None, None), coords, pair(sec_keep, sec_send), act1, mid1, pair(pre_keep, pre_send))
    fst1 = pair(fst_keep, fst_send)
    (
        mix_keep, mix_send, pre_keep, pre_send, att1, sec_keep, sec_send, top0, bias0, first, fst_keep, fst_send, gctx, sums0
    ) = between(
        1, coords, lengths, mixed1, lse1, gctx, first, *norms[1], n1_0, s1_0, gains, gp0, w_qkv, w_out, w_ff1, w_ff2
    )
    two0, one0, mix1 = weights(
        blocks, (None, None, None), coords, pair(sec_keep, sec_send), act0, mid0, pair(pre_keep, pre_send),
        (x1, pair(mix_keep, mix_send), ctx1, fst1, ctx0, pair(fst_keep, fst_send)),
    )
    outgoing, first_core, second_core = last(
        None, coords, lengths, mixed0, lse0, gctx, first, *norms[0], gains, x0[0], slot_row, kinds,
        (top0, top1, sums0, sums1, att1, bias0, bias1), w_qkv, asked.shape[1], 2 * blocks,
    )
    mine = cube.core_is_first()

    def over_cores(first, second):
        return add(jnp.where(mine, first, second), cube.core(jnp.where(mine, second, first)))

    table_keep, table_send = table_back(coords, asked, exchange_rows(outgoing, owners), local_rows)
    table_part = add(table_keep, cube.core(table_send))
    for bit in range(1, cube.dp_bits):
        table_part = add(table_part, cube.permute(table_part, 1 << bit, 0))
    wide = 3 * half
    sums_last = over_cores(first_core, second_core)
    packs = sums_last[..., wide:]
    other = cube.core(packs)
    pos, small = unpack(jnp.stack([jnp.where(mine, packs, other), jnp.where(mine, other, packs)]))
    pos_out = cube.reduce(pos).astype(F32)
    for bit in range(cube.vocab_bits):
        small = add(small, cube.permute(small, 0, 1 << bit))
    for bit in range(1, cube.dp_bits):
        small = add(small, cube.permute(small, 1 << bit, 0))
    types, gains_out, shifts_out, biases = small_outs(cube, small.astype(F32))
    whole = lambda parts: jnp.concatenate(parts, axis=0)
    part = width // blocks // 2
    one = lambda parts: cube.reduce(whole(parts)[:, :part].reshape(width, -1))
    two = lambda parts: cube.reduce(
        whole(parts).reshape(blocks, 2, width // 16, 4, -1).transpose(0, 4, 1, 3, 2).reshape(-1, half)
    )
    out0 = whole(one0)[:, part:].reshape(2 * blocks, 16, 4, half)[:, :, : part // 16].transpose(0, 2, 1, 3)
    mixes = jnp.stack(
        [
            cube.reduce(jnp.concatenate([sums_last[..., :wide].reshape(width, -1), out0.reshape(width, -1)], axis=1)),
            one(mix1),
        ]
    )
    return (
        cube.join_core(table_part, -1), pos_out, types, gains_out, shifts_out,
        cube.join_core(mixes[..., :wide], 2), cube.join_core(mixes[..., wide:], 2), biases,
        cube.join_core(jnp.stack([one(one0), one(one1)]), 2), cube.join_core(jnp.stack([two(two0), two(two1)]), 2),
    )


class Bucket:
    def __init__(self, cube, plan, parts):
        self.cube, self.plan, self.parts = cube, tuple(plan), tuple(parts)

    def start(self):
        turn = self.plan[0]
        if self.plan == (("y",),):
            self.got = (self.parts[0], self.cube.along(self.parts[0], turn))
            return
        self.got = self.parts[:1]
        for n in range(1, len(self.parts)):
            there = [dim for i, dim in enumerate(turn) if (n >> (len(turn) - 1 - i)) & 1]
            self.got += (self.cube.along(self.parts[n], there),)


    def keep(self):
        self.got, self.plan = self.parts, (None,)


def joined(buckets, parts_axis):
    return (tuple(buckets), parts_axis)


def step(groups, after=(), cost=CHEAP):
    groups = [group if isinstance(group, tuple) else ((group,), 0) for group in groups]
    items = []
    for buckets, axis in groups:
        rest = buckets[0].plan[1:]
        assert all(bucket.plan[1:] == rest for bucket in buckets)
        parts = 1 if rest in ((), (("y",),)) else 2 ** len(rest[0])
        items.append((tuple(bucket.got for bucket in buckets), parts, axis))
    for (buckets, _), parts in zip(groups, combine(items, after, cost)):
        buckets[0].plan, buckets[0].parts = buckets[0].plan[1:], tuple(parts)
    return groups[0][0][0].parts[0]


def gradients_small(cube, coords, lengths, top, saved, gains, w_qkv, w_out, w_ff1, w_ff2, norms, embed):
    owners = cube.vocab_size
    width = w_out.shape[1]
    tokens = top[0].shape[0]
    blocks = owners
    half = width // 2
    single = lambda dims: tuple((dim,) for dim in dims)
    plan_two1, plan_one1 = (("x", "y"), ("a",), ("b",)), (("a",), ("x", "y"), ("b",))
    plan_mix1 = single("ayxb")
    plan_two0, plan_one0, plan_mix0 = single("xayb"), single("yxab"), (("core",), ("y",), ("x", "a"), ("b",))
    kinds, slot_row, asked, local_rows = embed
    mixed1, lse1, n1_1, s1_1, gp1, x1, ctx1, mid1, act1 = saved[1]
    mixed0, lse0, n1_0, s1_0, gp0, x0, ctx0, mid0, act0 = saved[0]
    pair = lambda keep, send: (keep, cube.core(send))
    e, low, sec_keep, sec_send, top1 = top
    pre_keep, pre_send, bias1, first, _, fst_keep, fst_send, gctx, sums1 = feed(
        1, coords, e, low, n1_1, s1_1, gains, gp1, w_out, w_ff1, w_ff2
    )
    fst1 = pair(fst_keep, fst_send)
    got = weights(
        blocks, (plan_two1, plan_one1), coords, pair(sec_keep, sec_send), act1, mid1, pair(pre_keep, pre_send)
    )
    two1, one1 = Bucket(cube, plan_two1, got[0]), Bucket(cube, plan_one1, got[1])
    two1.start()
    one1.start()
    (
        mix_keep, mix_send, pre_keep, pre_send, att1, sec_keep, sec_send, top0, bias0, first, fst_keep, fst_send, gctx, sums0
    ) = between(
        1, coords, lengths, mixed1, lse1, gctx, first, *norms[1], n1_0, s1_0, gains, gp0, w_qkv, w_out, w_ff1, w_ff2,
        after=got[0][:1],
    )
    mark = step([two1, one1], after=(gctx,), cost=LONG)
    two1.start()
    one1.start()
    got = weights(
        blocks, (plan_two0, plan_one0, plan_mix1), coords, pair(sec_keep, sec_send), act0, mid0, pair(pre_keep, pre_send),
        (x1, pair(mix_keep, mix_send), ctx1, fst1, ctx0, pair(fst_keep, fst_send)), after=(mark,),
    )
    two0, one0, mix1 = [Bucket(cube, plan, parts) for plan, parts in zip((plan_two0, plan_one0, plan_mix1), got)]
    for bucket in (mix1, two0, one0):
        bucket.start()
    mark = step([joined((two1, one1), 1)], after=got[0][:1], cost=LONG)
    two1.start()
    outgoing, *got = last(
        plan_mix0, coords, lengths, mixed0, lse0, gctx, first, *norms[0], gains, x0[0], slot_row, kinds,
        (top0, top1, sums0, sums1, att1, bias0, bias1), w_qkv, asked.shape[1], 2 * owners, after=(mark,),
    )
    incoming = exchange_rows(outgoing, owners)
    mix0 = Bucket(cube, plan_mix0, got)
    mix0.start()
    mark = step([two1, mix1, two0, one0], after=got[:1], cost=LONG)
    for bucket in (mix1, two0, one0):
        bucket.start()
    mark = step([mix0], after=(mark,))
    mix0.start()
    mark = step([mix1, two0, one0], after=(mark,), cost=LONG)
    for bucket in (mix1, two0, one0):
        bucket.start()
    folded = (local_rows // 48, 48, half)
    got = table_back(coords, asked, incoming, local_rows, after=(mark,))
    table = Bucket(cube, single(("core", "y")), [part.reshape(folded) for part in got])
    table.start()
    mark = step([mix0, joined((mix1, two0, one0), 1)], after=got[:1], cost=LONG)
    mix0.start()
    mix1.start()
    mark = step([table], after=(mark,))
    table.start()
    mark = step([mix0], after=(mark,), cost=LONG)
    mix0.start()
    two1.keep()
    mark = step([joined((mix1, two1), 1), table], after=(mark,))
    later = Bucket(cube, (), (cube.along(mix1.parts[0], ("y",)),))
    later.keep()
    mark = step([mix0], after=(mark,))
    last_y = Bucket(cube, (), (cube.along(mix0.parts[0], ("y",)),))
    last_y.keep()
    step([last_y], after=(mark,))
    step([later], after=(last_y.parts[0],))
    own = mix1.parts[0]
    over_y, last_y = later.parts[0], last_y.parts[0]
    qkv_out, wout_out, one_out, two_out, pos_out, small = finish(
        coords,
        (own, over_y, cube.core(own), cube.core(over_y)),
        (mix0.parts[0], last_y, cube.core(mix0.parts[0]), cube.core(last_y)),
        width, w_ff1.shape[2], owners,
    )
    types, gains, shifts, biases = small_outs(cube, small)
    return (
        cube.join_core(table.parts[0].reshape(local_rows, half), -1), pos_out, types, gains, shifts, qkv_out, wout_out,
        biases, one_out, two_out,
    )


def solution(mesh):
    cube = Cube(mesh.shape["dp"], mesh.shape["vocab"])
    both = ("dp", "vocab")
    in_specs = (
        P(both, None),
        P(both),
        P(both, None),
        P("vocab", None),
        P(),
        P(),
        P(),
        P(),
        P(),
        P(),
        P(),
        P(),
        P(),
        P(both, None, None),
    )
    out_specs = (
        P(both, None, None),
        P("vocab", None),
        P("vocab", None),
        P(None, "vocab"),
        P(None, "vocab"),
        P(None, "vocab"),
        P(None, "vocab", None),
        P(None, "vocab", None),
        P(None, "vocab"),
        P(None, "vocab", None),
        P(None, "vocab", None),
    )
    return jax.shard_map(
        functools.partial(on_device, cube), mesh=mesh, in_specs=in_specs, out_specs=out_specs, check_vma=False
    )
```

```python
import functools
import jax
import jax.numpy as jnp
from jax import lax
from jax.experimental import pallas as pl
from jax.experimental.pallas import tpu as pltpu
from jax.sharding import PartitionSpec as P

HEADS = 12
HEAD_DIM = 64
NL = 2
norm_eps = 1e-12
SCALE = HEAD_DIM ** (-0.5)
ANY = pl.BlockSpec(memory_space=pl.ANY)
HBM = pl.BlockSpec(memory_space=pltpu.HBM)
VM = pl.BlockSpec(memory_space=pltpu.VMEM)
SM = pl.BlockSpec(memory_space=pltpu.SMEM)
F32, LOW = jnp.float32, jnp.bfloat16

CHEAP = pl.CostEstimate(flops=1, bytes_accessed=1, transcendentals=0)
DEAR = pl.CostEstimate(flops=10**10, bytes_accessed=1, transcendentals=0)
LONG = pl.CostEstimate(flops=10**11, bytes_accessed=1, transcendentals=0)


def run(kernel, after, out_shape, in_specs, operands, vmem, **options):
    count = len(operands)

    def body(*refs):
        kernel(*refs[:count], *refs[count + len(after) :])

    return pl.pallas_call(
        body,
        out_shape=out_shape,
        in_specs=list(in_specs) + [ANY] * len(after),
        compiler_params=pltpu.CompilerParams(vmem_limit_bytes=vmem * 1024 * 1024),
        **options,
    )(*operands, *after)


def normalize(inputs):
    centered = inputs - jnp.mean(inputs, axis=-1, keepdims=True)
    spread = lax.rsqrt(jnp.mean(centered * centered, axis=-1, keepdims=True) + norm_eps)
    return (centered * spread, spread)


def norm_back(grad_out, normed, spread, gain_row):
    scaled = grad_out * gain_row
    return spread * (
        scaled
        - jnp.mean(scaled, axis=-1, keepdims=True)
        - normed * jnp.mean(scaled * normed, axis=-1, keepdims=True)
    )


def dot(left_op, right_op, dims=((1,), (0,))):
    return lax.dot_general(left_op, right_op, (dims, ((), ())), preferred_element_type=F32)


ROWS = ((0,), (0,))
COLS = ((1,), (1,))


def gelu_pair(inputs):
    size = jnp.abs(inputs)
    bell = jnp.exp2(inputs * inputs * (-0.5 * 1.4426950408889634))
    t = 1.0 / (1.0 + size * (0.3275911 * 0.7071067811865476))
    tail = t * (
        0.5 * 0.254829592
        + t * (0.5 * -0.284496736 + t * (0.5 * 1.421413741 + t * (0.5 * -1.453152027 + t * (0.5 * 1.061405429))))
    )
    tail = tail * bell
    phi = jnp.where(inputs >= 0.0, 1.0 - tail, tail)
    return inputs * phi, phi + inputs * bell * 0.3989422804014327


def as_column(row):
    return jnp.broadcast_to(row, (128, row.shape[1])).T[:, :1]


def forward_kernel(
    coords_ref, length_ref, replies_ref, slot_ref, kind_ref, pos_ref, type_ref, gains_ref, shifts_ref, ffn_bias_ref,
    grad_ref, wqkv_hbm, wout_hbm, w1_hbm, w2_hbm,
    *refs,
):
    n0_ref, s0_ref, hidden_ref = refs[:3]
    top = refs[3:8]
    outs = [refs[8 + 11 * layer : 19 + 11 * layer] for layer in range(NL)]
    wqkv, wout, w1, w2, sems, xlow, mixed, ctxt, mlow, gp, act, n0, n1, n2, x, osems = refs[6 + 11 * NL :]
    tokens, width = x.shape
    ff = w1.shape[2]
    loads = []
    for layer in range(NL):
        for i, (src, dst) in enumerate([(wqkv_hbm, wqkv), (wout_hbm, wout), (w1_hbm, w1), (w2_hbm, w2)]):
            loads.append(pltpu.make_async_copy(src.at[layer], dst.at[layer], sems.at[4 * layer + i]))
    for load in loads:
        load.start()
    pending, used = {}, [0]

    def emit(name, src, dst, at=None):
        if at is not None:
            src, dst = src.at[:, at], dst.at[:, at]
        copy = pltpu.make_async_copy(src, dst, osems.at[used[0]])
        used[0] += 1
        copy.start()
        pending.setdefault(name, []).append(copy)

    def reuse(name):
        for copy in pending.pop(name, ()):
            copy.wait()

    gains = gains_ref[...].astype(F32)
    shifts = shifts_ref[...].astype(F32)
    number = lax.broadcasted_iota(jnp.int32, (tokens, replies_ref.shape[0]), 1)
    hit = jnp.where(number == as_column(slot_ref[...].astype(F32)).astype(jnp.int32), 1.0, 0.0).astype(LOW)
    types = type_ref[...].astype(F32)
    embedded = dot(hit, replies_ref[...]) + pos_ref[...].astype(F32)
    embedded = embedded + jnp.where(as_column(kind_ref[...].astype(F32)) > 0.5, types[1:2], types[0:1])
    normed, spread = normalize(embedded)
    n0[...] = normed
    emit("n0", n0, n0_ref)
    s0_ref[...] = jnp.broadcast_to(spread, s0_ref.shape)
    x[...] = normed * gains[0:1] + shifts[0:1]

    key_slot = lax.broadcasted_iota(jnp.int32, (tokens, 128), 0)
    visible = jnp.where(key_slot < length_ref[0], 0.0, -1e30)[:, :1]
    lane = lax.broadcasted_iota(jnp.int32, (tokens, 128), 1)
    chunk = 512

    for layer in range(NL):
        base = 1 + 6 * layer
        xlow_ref, mixed_ref, lse_ref, ctxt_ref, n1_ref, s1_ref, mlow_ref, gp_ref, act_ref = outs[layer][:9]

        reuse("xlow")
        xlow[...] = x[...].astype(LOW)
        emit("xlow", xlow, xlow_ref)
        loads[4 * layer].wait()
        reuse("mixed")
        for i in range(3):
            cols = slice(i * width, (i + 1) * width)
            got = dot(xlow[...], wqkv[layer, :, cols])
            if i != 1:
                row = base + (0 if i == 0 else 1)
                got = got + shifts[row : row + 1]
            mixed[:, cols] = got.astype(LOW)
        emit("mixed", mixed, mixed_ref)
        reuse("ctxt")

        def pair_step(j, carry):
            at = pl.multiple_of(j * 128, 128)
            q = mixed[:, pl.ds(at, 128)] * jnp.asarray(SCALE, LOW)
            k = mixed[:, pl.ds(pl.multiple_of(width + at, 128), 128)]
            v = mixed[:, pl.ds(pl.multiple_of(2 * width + at, 128), 128)]
            vt = v.T
            scores = []
            for h in range(2):
                kh = jnp.where((lane < 64) == (h == 0), k, jnp.zeros_like(k))
                scores.append(dot(kh, q, COLS) + visible)
            for h in range(2):
                top = jnp.max(scores[h], axis=0, keepdims=True)
                weights = jnp.exp(scores[h] - top)
                total = jnp.sum(weights, axis=0, keepdims=True)
                out = dot(vt[h * 64 : (h + 1) * 64], weights.astype(LOW)) * (1.0 / total)
                ctxt[pl.ds(pl.multiple_of(at + h * 64, 64), 64), :] = out.astype(LOW)
                lse_ref[pl.ds(2 * j + h, 1), :] = top + jnp.log(total)
            return carry

        lax.fori_loop(0, HEADS // 2, pair_step, 0)
        emit("ctxt", ctxt, ctxt_ref)
        loads[4 * layer + 1].wait()
        attended = dot(ctxt[...], wout[layer], ROWS) + shifts[base + 2 : base + 3]
        normed, spread = normalize(x[...] + attended)
        reuse("n1")
        n1[...] = normed
        emit("n1", n1, n1_ref)
        s1_ref[...] = jnp.broadcast_to(spread, s1_ref.shape)
        x[...] = normed * gains[1 + 2 * layer : 2 + 2 * layer] + shifts[base + 3 : base + 4]
        reuse("mlow")
        mlow[...] = x[...].astype(LOW)
        emit("mlow", mlow, mlow_ref)
        loads[4 * layer + 2].wait()
        reuse("gp")
        reuse("act")
        for i in range(ff // chunk):
            cols = slice(i * chunk, (i + 1) * chunk)
            pre = dot(mlow[...], w1[layer, :, cols]) + ffn_bias_ref[layer : layer + 1, cols]
            active, slope = gelu_pair(pre)
            gp[:, cols] = slope.astype(LOW)
            act[:, cols] = active.astype(LOW)
            emit("gp", gp, gp_ref, pl.ds(i * chunk, chunk))
            emit("act", act, act_ref, pl.ds(i * chunk, chunk))
        loads[4 * layer + 3].wait()
        normed, spread = normalize(x[...] + shifts[base + 4 : base + 5] + dot(act[...], w2[layer]))
        if layer < NL - 1:
            n2_ref, s2_ref = outs[layer][9:11]
            n2[...] = normed
            emit("n2", n2, n2_ref)
            s2_ref[...] = jnp.broadcast_to(spread, s2_ref.shape)
        else:
            gain = gains[2 * NL : 2 * NL + 1]
            norm_end(coords_ref[0], grad_ref[...].astype(F32), normed, spread, gain, *top)
        x[...] = normed * gains[2 + 2 * layer : 3 + 2 * layer] + shifts[base + 5 : base + 6]
    hidden_ref[...] = x[...].astype(LOW)
    for name in list(pending):
        reuse(name)


def forward(
    coords, length, replies, slot_of, kinds, pos, types, gains, shifts, ffn_bias, cotangent, w_qkv, w_out, w_ff1, w_ff2
):
    tokens, width = pos.shape
    ff = w_ff1.shape[2]
    s = jax.ShapeDtypeStruct
    v = pltpu.VMEM
    spread = s((tokens, 128), F32)
    wide = s((tokens, width), F32)
    low = s((tokens, width), LOW)
    layer_out = (
        low, s((tokens, 3 * width), LOW), s((HEADS, tokens), F32), s((width, tokens), LOW),
        wide, spread, low, s((tokens, ff), LOW), s((tokens, ff), LOW), wide, spread,
    )
    layer_spec = (ANY, ANY, VM, ANY, ANY, VM, ANY, ANY, ANY, ANY, VM)
    chunks = ff // 512
    end = norm_end_shapes(tokens, width)
    outs = run(
        forward_kernel,
        (),
        out_shape=(wide, spread, low) + end + layer_out * (NL - 1) + layer_out[:9],
        in_specs=[SM, SM] + [VM] * 9 + [HBM] * 4,
        operands=(
            coords, length, replies, slot_of, kinds, pos, types, gains, shifts, ffn_bias, cotangent, w_qkv, w_out, w_ff1, w_ff2
        ),
        out_specs=(ANY, VM, VM) + (VM,) * 5 + layer_spec * (NL - 1) + layer_spec[:9],
        scratch_shapes=[
            v((NL, width, 3 * width), LOW), v((NL, width, width), LOW), v((NL, width, ff), LOW), v((NL, ff, width), LOW),
            pltpu.SemaphoreType.DMA((4 * NL,)),
            v((tokens, width), LOW), v((tokens, 3 * width), LOW), v((width, tokens), LOW), v((tokens, width), LOW),
            v((tokens, ff), LOW), v((tokens, ff), LOW), v((tokens, width), F32), v((tokens, width), F32),
            v((tokens, width), F32), v((tokens, width), F32), pltpu.SemaphoreType.DMA((1 + NL * (6 + 2 * chunks),)),
        ],
        cost_estimate=CHEAP,
        vmem=60,
        name="forward",
    )
    return outs[:3], outs[3:8], [outs[8 + 11 * layer : 19 + 11 * layer] for layer in range(NL)]


def part(mine, source, keep_to, send_to):
    half = source.shape[1] // 2

    @pl.when(mine == 0)
    def _():
        keep_to[...] = source[:, :half]
        send_to[...] = source[:, half:]

    @pl.when(mine == 1)
    def _():
        keep_to[...] = source[:, half:]
        send_to[...] = source[:, :half]


def norm_end(mine, grad, n, s, gain, back_ref, low_ref, keep_ref, send_ref, sums_ref):
    sums_ref[0:1] = jnp.sum(grad * n, axis=0, keepdims=True)
    sums_ref[1:2] = jnp.sum(grad, axis=0, keepdims=True)
    back = norm_back(grad, n, s, gain)
    sums_ref[2:3] = jnp.sum(back, axis=0, keepdims=True)
    back_ref[...] = back
    low_ref[...] = back.astype(LOW)
    if keep_ref is not None:
        part(mine, low_ref, keep_ref, send_ref)


def norm_end_shapes(tokens, width):
    s = jax.ShapeDtypeStruct
    half = s((tokens, width // 2), LOW)
    return (s((tokens, width), F32), s((tokens, width), LOW), half, half, s((3, width), F32))


def feed_back_body(mine, second, gp, w2, ready, bias_ref, keep, send):
    chunk = 512
    steps = gp.shape[1] // chunk
    for i in range(steps):
        ready(i)
        cols = slice(i * chunk, (i + 1) * chunk)
        grad_pre = dot(second[...], w2[cols, :], COLS) * gp[:, cols].astype(F32)
        bias_ref[:, cols] = jnp.sum(grad_pre, axis=0, keepdims=True)
        side, at = divmod(i, steps // 2)
        there = slice(at * chunk, (at + 1) * chunk)
        low = grad_pre.astype(LOW)

        @pl.when(mine == side)
        def _():
            keep[:, there] = low

        @pl.when(mine != side)
        def _():
            send[:, there] = low


def both_halves(mine, keep, send, weight):
    half = keep.shape[1]
    first = jnp.where(mine == 0, keep[...], send[...])
    second = jnp.where(mine == 0, send[...], keep[...])
    return dot(first, weight[:, :half], COLS) + dot(second, weight[:, half:], COLS)


def attend_back_body(length_ref, mixed_ref, lse_ref, gctx_ref, att_ref, dmix):
    tokens, width = gctx_ref.shape
    key_slot = lax.broadcasted_iota(jnp.int32, (tokens, 128), 0)
    visible = jnp.where(key_slot < length_ref[0], 0.0, -1e30)[:, :1]
    lane = lax.broadcasted_iota(jnp.int32, (tokens, 128), 1)

    def pair_step(j, carry):
        at = pl.multiple_of(j * 128, 128)
        qcols = pl.ds(at, 128)
        kcols = pl.ds(pl.multiple_of(width + at, 128), 128)
        vcols = pl.ds(pl.multiple_of(2 * width + at, 128), 128)
        q = mixed_ref[:, qcols] * jnp.asarray(SCALE, LOW)
        k = mixed_ref[:, kcols]
        v = mixed_ref[:, vcols]
        g = gctx_ref[:, qcols]
        kt = k.T
        grad_v, grad_k, grad_qt = [], [], []
        scores, grad_probs = [], []
        for h in range(2):
            mask = (lane < 64) == (h == 0)
            kh = jnp.where(mask, k, jnp.zeros_like(k))
            vh = jnp.where(mask, v, jnp.zeros_like(v))
            scores.append(dot(kh, q, COLS))
            grad_probs.append(dot(vh, g, COLS))
        for h in range(2):
            probs = jnp.exp(scores[h] + visible - lse_ref[pl.ds(2 * j + h, 1), :])
            weighted = jnp.sum(probs * grad_probs[h], axis=0, keepdims=True)
            grad_scores = (probs * (grad_probs[h] - weighted)).astype(LOW)
            grad_v.append(dot(probs.astype(LOW), g))
            grad_k.append(dot(grad_scores, q))
            grad_qt.append(dot(kt[h * 64 : (h + 1) * 64], grad_scores))
        grad_q = jnp.concatenate(grad_qt, axis=0).T * SCALE
        grad_v = jnp.where(lane < 64, grad_v[0], grad_v[1])
        grad_k = jnp.where(lane < 64, grad_k[0], grad_k[1])
        att_ref[0:1, qcols] = jnp.sum(grad_q, axis=0, keepdims=True)
        att_ref[1:2, qcols] = jnp.sum(grad_v, axis=0, keepdims=True)
        dmix[:, qcols] = grad_q.astype(LOW)
        dmix[:, kcols] = grad_k.astype(LOW)
        dmix[:, vcols] = grad_v.astype(LOW)
        return carry

    lax.fori_loop(0, HEADS // 2, pair_step, 0)


def chunk_loads(sems, at, pairs, chunk=512):
    loads = []
    (w2_src, w2), (gp_src, gp) = pairs
    for i in range(gp.shape[1] // chunk):
        there = pl.ds(i * chunk, chunk)
        loads.append(
            (
                pltpu.make_async_copy(w2_src.at[there], w2.at[there], sems.at[at + 2 * i]),
                pltpu.make_async_copy(gp_src.at[:, there], gp.at[:, there], sems.at[at + 2 * i + 1]),
            )
        )
    return loads


def feed_kernel(
    layer, coords_ref, e_ref, second, n1_ref, s1_ref, gains_ref, gp_hbm, wout_hbm, w1_hbm, w2_hbm,
    keep_ref, send_ref, bias_ref, first_ref, low_ref, fst_keep_ref, fst_send_ref, gctx_ref, sums_ref,
    gp, wout, w1, w2, keep, send, sems,
):
    mine = coords_ref[0]
    loads = chunk_loads(sems, 4, ((w2_hbm.at[layer], w2), (gp_hbm, gp)))
    for pair in loads:
        for load in pair:
            load.start()
    late = [
        pltpu.make_async_copy(w1_hbm.at[layer], w1, sems.at[0]),
        pltpu.make_async_copy(wout_hbm.at[layer], wout, sems.at[1]),
    ]
    for load in late:
        load.start()

    def ready(i):
        for load in loads[i]:
            load.wait()

    feed_back_body(mine, second, gp, w2, ready, bias_ref, keep, send)
    stores = [
        pltpu.make_async_copy(send, send_ref, sems.at[2]),
        pltpu.make_async_copy(keep, keep_ref, sems.at[3]),
    ]
    for store in stores:
        store.start()
    late[0].wait()
    grad = e_ref[...] + both_halves(mine, keep, send, w1)
    gain = gains_ref[...].astype(F32)[1 + 2 * layer : 2 + 2 * layer]
    norm_end(mine, grad, n1_ref[...], s1_ref[:, :1], gain, first_ref, low_ref, fst_keep_ref, fst_send_ref, sums_ref)
    late[1].wait()
    gctx_ref[...] = dot(low_ref[...], wout[...], COLS).astype(LOW)
    for store in stores:
        store.wait()


def feed(layer, coords, e, second, n1, s1, gains, gp, w_out, w_ff1, w_ff2, after=()):
    tokens, width = n1.shape
    ff = gp.shape[1]
    s = jax.ShapeDtypeStruct
    v = pltpu.VMEM
    half = s((tokens, ff // 2), LOW)
    end = norm_end_shapes(tokens, width)
    return run(
        functools.partial(feed_kernel, layer),
        after,
        out_shape=(half, half, s((1, ff), F32)) + end[:4] + (s((tokens, width), LOW), end[4]),
        in_specs=[SM] + [VM] * 5 + [HBM] * 4,
        operands=(coords, e, second, n1, s1, gains, gp, w_out, w_ff1, w_ff2),
        out_specs=(ANY, ANY) + (VM,) * 7,
        scratch_shapes=[
            v((tokens, ff), LOW), v((width, width), LOW), v((width, ff), LOW), v((ff, width), LOW),
            v((tokens, ff // 2), LOW), v((tokens, ff // 2), LOW), pltpu.SemaphoreType.DMA((4 + 2 * (ff // 512),)),
        ],
        cost_estimate=CHEAP,
        vmem=52,
        name="feed",
    )


def between_kernel(
    layer, coords_ref, length_ref, mixed_ref, lse_ref, gctx_in, first_in, n2_ref, s2_ref, n1_ref, s1_ref, gains_ref,
    gp_hbm, wqkv_hbm, wout_hbm, w1_hbm, w2_hbm,
    mix_keep_ref, mix_send_ref, pre_keep_ref, pre_send_ref,
    att_ref, sec_keep_ref, sec_send_ref, top_ref, bias_ref, first_ref, fst_keep_ref, fst_send_ref, gctx_ref, sums_ref,
    gp, wqkv, wout, w1, w2, dmix, mix_keep, mix_send, keep, send, e, second, low_ref, sems,
):
    mine = coords_ref[0]
    below = layer - 1
    early = pltpu.make_async_copy(wqkv_hbm.at[layer], wqkv, sems.at[0])
    early.start()
    loads = chunk_loads(sems, 7, ((w2_hbm.at[below], w2), (gp_hbm, gp)))
    for pair in loads:
        for load in pair:
            load.start()
    late = [
        pltpu.make_async_copy(w1_hbm.at[below], w1, sems.at[1]),
        pltpu.make_async_copy(wout_hbm.at[below], wout, sems.at[2]),
    ]
    for load in late:
        load.start()
    stores = []

    def emit(src, dst):
        stores.append(pltpu.make_async_copy(src, dst, sems.at[3 + len(stores)]))
        stores[-1].start()

    attend_back_body(length_ref, mixed_ref, lse_ref, gctx_in, att_ref, dmix)
    part(mine, dmix, mix_keep, mix_send)
    emit(mix_send, mix_send_ref)
    emit(mix_keep, mix_keep_ref)
    early.wait()
    grad = first_in[...] + dot(dmix[...], wqkv[...], COLS)
    gains = gains_ref[...].astype(F32)
    norm_end(
        mine, grad, n2_ref[...], s2_ref[:, :1], gains[2 * layer : 2 * layer + 1], e, second, sec_keep_ref, sec_send_ref, top_ref
    )

    def ready(i):
        for load in loads[i]:
            load.wait()

    feed_back_body(mine, second, gp, w2, ready, bias_ref, keep, send)
    emit(send, pre_send_ref)
    emit(keep, pre_keep_ref)
    late[0].wait()
    grad = e[...] + both_halves(mine, keep, send, w1)
    norm_end(
        mine, grad, n1_ref[...], s1_ref[:, :1], gains[1 + 2 * below : 2 + 2 * below], first_ref, low_ref, fst_keep_ref,
        fst_send_ref, sums_ref,
    )
    late[1].wait()
    gctx_ref[...] = dot(low_ref[...], wout[...], COLS).astype(LOW)
    for store in stores:
        store.wait()


def between(layer, coords, length, mixed, lse, gctx, first, n2, s2, n1, s1, gains, gp, w_qkv, w_out, w_ff1, w_ff2, after=()):
    tokens, width = first.shape
    ff = gp.shape[1]
    s = jax.ShapeDtypeStruct
    v = pltpu.VMEM
    mix = s((tokens, 3 * width // 2), LOW)
    pre = s((tokens, ff // 2), LOW)
    sec = s((tokens, width // 2), LOW)
    low = s((tokens, width), LOW)
    three = s((3, width), F32)
    return run(
        functools.partial(between_kernel, layer),
        after,
        out_shape=(
            mix, mix, pre, pre, s((2, width), F32), sec, sec, three, s((1, ff), F32), s((tokens, width), F32), sec, sec, low, three,
        ),
        in_specs=[SM, SM] + [VM] * 9 + [HBM] * 5,
        operands=(coords, length, mixed, lse, gctx, first, n2, s2, n1, s1, gains, gp, w_qkv, w_out, w_ff1, w_ff2),
        out_specs=(ANY,) * 4 + (VM,) * 10,
        scratch_shapes=[
            v((tokens, ff), LOW), v((width, 3 * width), LOW), v((width, width), LOW), v((width, ff), LOW), v((ff, width), LOW),
            v((tokens, 3 * width), LOW), v(mix.shape, LOW), v(mix.shape, LOW), v(pre.shape, LOW), v(pre.shape, LOW),
            v((tokens, width), F32), v((tokens, width), LOW), v((tokens, width), LOW),
            pltpu.SemaphoreType.DMA((7 + 2 * (ff // 512),)),
        ],
        cost_estimate=CHEAP,
        vmem=58,
        name="between",
    )


COORDS = ("core", "x", "a", "b", "y")


def place(coords_ref, plan, result, *outs):
    count = result.shape[0]
    size = count // len(outs)
    dims = [] if plan is None else [dim for turn in plan for dim in turn]
    for i in range(count):
        block = i
        if plan is not None:
            bit = {}
            for n, dim in enumerate(dims):
                relative = (i >> (len(dims) - 1 - n)) & 1
                whole = plan[-1] == ("y",) and n == len(dims) - 1
                bit[dim] = relative if whole else coords_ref[COORDS.index(dim)] ^ relative
            block = 16 * bit.get("core", 0) + 8 * bit["b"] + 4 * bit["a"] + 2 * bit["x"] + bit["y"]
        out = outs[i // size]
        out[i % size] = result[block].astype(out.dtype)


def parts_of(plan):
    return 2 if plan is None else 2 ** len(plan[0])


def load_both(pairs, sems):
    loads = []
    for own, oth, dst in pairs:
        for n, src in enumerate((own, oth)):
            size = own.shape[0]
            load = pltpu.make_async_copy(src, dst.at[pl.ds(n * size, size)], sems.at[len(loads)])
            load.start()
            loads.append(load)
    return loads


def weights_kernel(plans, blocks, coords_ref, *refs):
    count = 8 if len(plans) == 2 else 20
    sources, refs = refs[:count], refs[count:]
    outs = []
    for plan in plans:
        outs.append(refs[: parts_of(plan)])
        refs = refs[parts_of(plan) :]
    sec, act, mid, pre, sect, midt, two, one = refs[:8]
    rest, sems = refs[8:-1], refs[-1]
    tokens = sources[0].shape[0]
    loads = []
    targets = [sec, act, mid, pre]
    if rest:
        x, mix, ctxt, fst, below_ctxt, below_fst, xt, mixed = rest
        targets += [x, mix, ctxt, fst, below_ctxt, below_fst]
    for n, target in enumerate(targets):
        for side in range(2):
            there = pl.ds(side * tokens, tokens)
            view = target.at[:, there] if n in (6, 8) else target.at[there]
            loads.append(pltpu.make_async_copy(sources[2 * n + side], view, sems.at[2 * n + side]))
            loads[-1].start()

    def ready(n):
        loads[2 * n].wait()
        loads[2 * n + 1].wait()

    ready(0)
    sect[...] = sec[...].T
    ready(1)
    rows = two.shape[1]
    cols = act.shape[1] // blocks

    group = 4 if blocks % 4 == 0 else 1

    def step_two(i, carry):
        there = pl.ds(pl.multiple_of(i * group * cols, cols), group * cols)
        got = dot(sect[...], act[:, there]).astype(LOW)
        for v in range(group):
            for y in range(2):
                for n in range(4):
                    at = (4 * y + n) * rows
                    piece = got[at : at + rows, v * cols : (v + 1) * cols]
                    two[2 * (i * group + v) + y, :, n * cols : (n + 1) * cols] = piece
        return carry

    lax.fori_loop(0, blocks // group, step_two, 0)
    place(coords_ref, plans[0], two, *outs[0])
    ready(2)
    midt[...] = mid[...].T
    ready(3)
    chunk = 512
    high = midt.shape[0] // one.shape[0]

    def step_one(i, carry):
        there = pl.ds(pl.multiple_of(i * chunk, chunk), chunk)
        one[:, :high, there] = dot(midt[...], pre[:, there]).astype(LOW).reshape(one.shape[0], high, chunk)
        return carry

    if rest:
        lax.fori_loop(0, pre.shape[1] // chunk, step_one, 0)
        ready(8)
        ready(9)
        part_cols, group_rows = below_fst.shape[1], one.shape[1] - high
        got = dot(below_ctxt[...], below_fst[...]).astype(LOW).reshape(one.shape[0], high, part_cols)
        for n in range(high // group_rows):
            there = slice(n * part_cols, (n + 1) * part_cols)
            one[:, high:, there] = got[:, n * group_rows : (n + 1) * group_rows]
        one[:, high:, high // group_rows * part_cols :] = jnp.zeros((one.shape[0], group_rows, part_cols), LOW)
    else:
        one[...] = dot(midt[...], pre[...]).astype(LOW).reshape(one.shape)
    place(coords_ref, plans[1], one, *outs[1])
    if rest:
        ready(4)
        xt[...] = x[...].T
        ready(5)
        wide = mix.shape[1]
        mixed[:, :, :wide] = dot(xt[...], mix[...]).astype(LOW).reshape(mixed.shape[:2] + (wide,))
        ready(6)
        ready(7)
        mixed[:, :, wide:] = dot(ctxt[...], fst[...]).astype(LOW).reshape(mixed.shape[:2] + (fst.shape[1],))
        place(coords_ref, plans[2], mixed, *outs[2])


def weights(blocks, plans, coords, sec, act, mid, pre, attention=(), after=()):
    tokens, width = mid[0].shape
    s = jax.ShapeDtypeStruct
    v = pltpu.VMEM
    count = 2 * blocks
    block = (count, width // count, 2 * width)
    high = (count, width // count + 16, 2 * width) if attention else block
    sizes = (block, high, block)
    outs = sum(
        ((s((count // parts_of(plan),) + size[1:], LOW),) * parts_of(plan) for plan, size in zip(plans, sizes)), ()
    )
    pairs = (sec, act, mid, pre) + tuple(attention)
    both = lambda pair: v((2 * tokens, pair[0].shape[1]), LOW)
    scratch = [both(pair) for pair in (sec, act, mid, pre)]
    scratch += [v((sec[0].shape[1], 2 * tokens), LOW), v((width, 2 * tokens), LOW), v(block, LOW), v(high, LOW)]
    if attention:
        x, mix, _, fst, _, below_fst = attention
        across = v((width, 2 * tokens), LOW)
        scratch += [both(x), both(mix), across, both(fst), across, both(below_fst), across, v(block, LOW)]
    got = run(
        functools.partial(weights_kernel, plans, blocks),
        after,
        out_shape=outs,
        in_specs=[SM] + [ANY] * (2 * len(pairs)),
        operands=(coords,) + tuple(array for pair in pairs for array in pair),
        out_specs=(VM,) * len(outs),
        scratch_shapes=scratch + [pltpu.SemaphoreType.DMA((2 * len(pairs),))],
        cost_estimate=CHEAP,
        vmem=50 if attention else 34,
        name="weights",
    )
    parts = []
    for plan in plans:
        parts.append(got[: parts_of(plan)])
        got = got[parts_of(plan) :]
    return parts


def combine_kernel(forms, *refs):
    count = sum(sum(form[0]) for form in forms)
    ins, outs = refs[:count], refs[count:]
    for terms_of, parts, axis in forms:
        results, outs = outs[:parts], outs[parts:]
        at = 0
        for terms in terms_of:
            mine, ins = ins[:terms], ins[terms:]
            size = mine[0].shape[0] // parts
            rows = mine[0].shape[1]
            for part in range(parts):
                for i in range(size):
                    total = mine[0][part * size + i].astype(F32)
                    for term in mine[1:]:
                        total = total + term[part * size + i].astype(F32)
                    if axis == 0:
                        results[part][at + i] = total.astype(LOW)
                    else:
                        results[part][i, at : at + rows] = total.astype(LOW)
            at += size if axis == 0 else rows


def combine(items, after=(), cost=CHEAP):
    forms = tuple((tuple(len(terms) for terms in sums), parts, axis) for sums, parts, axis in items)
    shapes = []
    for sums, parts, axis in items:
        shape = list(sums[0][0].shape)
        shape[axis] = sum(terms[0].shape[axis] for terms in sums)
        shape[0] //= parts
        shapes += [jax.ShapeDtypeStruct(tuple(shape), LOW)] * parts
    operands = tuple(array for sums, _, _ in items for terms in sums for array in terms)
    size = sum(array.size for array in operands)
    outs = run(
        functools.partial(combine_kernel, forms),
        after,
        out_shape=tuple(shapes),
        in_specs=[VM] * len(operands),
        operands=operands,
        out_specs=(VM,) * len(shapes),
        cost_estimate=cost,
        vmem=6 + 4 * size // (1 << 20),
        name="combine",
    )
    got = []
    for _, parts, _ in forms:
        got.append(outs[:parts])
        outs = outs[parts:]
    return got


def last_kernel(
    plan, coords_ref, length_ref, mixed_ref, lse_ref, gctx_ref, first_ref, n_ref, s_ref, gains_ref, x_ref,
    slot_ref, type_ref, top0, top1, low0, low1, att1, bias0, bias1, wqkv_hbm,
    out_keep_ref, out_send_ref, *parts_and_scratch
):
    outs, (wqkv, dmix, xt, res, back_ref, back_low, att0, emb, small, sems) = parts_and_scratch[:-10], parts_and_scratch[-10:]
    tokens, width = back_ref.shape
    load = pltpu.make_async_copy(wqkv_hbm.at[0], wqkv, sems.at[0])
    load.start()
    attend_back_body(length_ref, mixed_ref, lse_ref, gctx_ref, att0, dmix)
    load.wait()
    grad = first_ref[...] + dot(dmix[...], wqkv[...], COLS)
    gain = gains_ref[...].astype(F32)[0:1]
    norm_end(coords_ref[0], grad, n_ref[...], s_ref[:, :1], gain, back_ref, back_low, None, None, emb)
    mine = coords_ref[0]
    slots, half = out_keep_ref.shape
    chunk = 256

    def step(i, carry):
        there = pl.ds(pl.multiple_of(i * chunk, chunk), chunk)
        number = lax.broadcasted_iota(jnp.int32, (chunk, tokens), 0) + i * chunk
        hit = jnp.where(number == slot_ref[...], 1.0, 0.0).astype(LOW)
        got = dot(hit, back_low[...]).astype(LOW)

        @pl.when(mine == 0)
        def _():
            out_keep_ref[there, :] = got[:, :half]
            out_send_ref[there, :] = got[:, half:]

        @pl.when(mine == 1)
        def _():
            out_keep_ref[there, :] = got[:, half:]
            out_send_ref[there, :] = got[:, :half]

        return carry

    lax.fori_loop(0, slots // chunk, step, 0)
    xt[...] = x_ref[...].T
    blocks, piece, _ = res.shape
    blocks //= 2
    wide = 3 * half
    for core in range(2):
        there = slice(core * blocks, (core + 1) * blocks)
        got = dot(xt[...], dmix[:, core * wide : (core + 1) * wide]).astype(LOW)
        res[there, :, :wide] = got.reshape(blocks, piece, wide)
    back = back_ref[...]
    kind = as_column(type_ref[...].astype(F32))
    small[0:1] = jnp.sum(back * (1.0 - kind), axis=0, keepdims=True)
    small[1:2] = jnp.sum(back * kind, axis=0, keepdims=True)
    sources = [(emb, 0)]
    for top, low in ((top0, low0), (top1, low1)):
        sources += [(low, 0), (top, 0)]
    sources += [(emb, 1)]
    for top, low, att in ((top0, low0, att0), (top1, low1, att1)):
        sources += [(att, 0), (att, 1), (low, 2), (low, 1), (top, 2), (top, 1)]
    at = 2
    for ref, row in sources:
        small[at : at + 1] = ref[row : row + 1]
        at += 1
    for bias in (bias0, bias1):
        for i in range(bias.shape[1] // width):
            small[at : at + 1] = bias[:, i * width : (i + 1) * width]
            at += 1
    quarter = at // 4
    group = tokens // blocks
    positions = back.reshape(blocks, group, width).astype(LOW)
    for core in range(2):
        there = slice(core * blocks, (core + 1) * blocks)
        res[there, :group, wide:] = positions[:, :, core * half : (core + 1) * half]
        for y in range(2):
            mine = small[(2 * core + y) * quarter : (2 * core + y + 1) * quarter]
            rest = jnp.zeros((piece - group - 2 * quarter, half), F32)
            mine = jnp.concatenate([mine[:, :half], mine[:, half:], rest], axis=0).astype(LOW)
            for v in range(blocks // 2):
                res[core * blocks + 2 * v + y, group:, wide:] = mine
    place(coords_ref, plan, res, *outs)


def last(plan, coords, length, mixed, lse, gctx, first, n, sp, gains, x, slot_of, types, sums, w_qkv, slots, blocks, parts=2, after=()):
    tokens, width = first.shape
    s = jax.ShapeDtypeStruct
    v = pltpu.VMEM
    block = (blocks, width // blocks, 2 * width)
    operands = (coords, length, mixed, lse, gctx, first, n, sp, gains, x, slot_of, types, *sums, w_qkv)
    return run(
        functools.partial(last_kernel, plan),
        after,
        out_shape=(s((slots, width // 2), LOW),) * 2 + (s((2 * blocks // parts,) + block[1:], LOW),) * parts,
        in_specs=[SM, SM] + [VM] * (len(operands) - 3) + [HBM],
        operands=operands,
        out_specs=(VM,) * (2 + parts),
        scratch_shapes=[
            v((width, 3 * width), LOW), v((tokens, 3 * width), LOW), v((width, tokens), LOW),
            v((2 * blocks,) + block[1:], LOW), v((tokens, width), F32), v((tokens, width), LOW),
            v((2, width), F32), v((3, width), F32), v((28, width), F32), pltpu.SemaphoreType.DMA((1,)),
        ],
        cost_estimate=CHEAP,
        vmem=52,
        name="last",
    )


def table_back_kernel(asked_ref, rows_ref, out_ref):
    count = out_ref.shape[0]
    chunk = count // 5 if count % 80 == 0 else count

    def step(i, carry):
        at = pl.multiple_of(i * chunk, 16)
        number = lax.broadcasted_iota(jnp.int32, (chunk, rows_ref.shape[0]), 0) + at
        hit = jnp.where(number == asked_ref[...], 1.0, 0.0).astype(LOW)
        out_ref[pl.ds(at, chunk), :] = dot(hit, rows_ref[...]).astype(LOW)
        return carry

    lax.fori_loop(0, count // chunk, step, 0)


def table_back(asked, rows, local_rows, after=()):
    return run(
        table_back_kernel,
        after,
        out_shape=jax.ShapeDtypeStruct((local_rows, rows.shape[1]), LOW),
        in_specs=[VM, VM],
        operands=(asked, rows),
        out_specs=VM,
        cost_estimate=CHEAP,
        vmem=20,
        name="table_back",
    )


def finish_kernel(coords_ref, *refs):
    many, early, few = refs[:4], refs[4:8], refs[8:12]
    qkv_ref, wout_ref, one_ref, two_ref, pos_ref, type_ref, gain_ref, shift_ref, bias_ref, small_ref = refs[12:]
    mine_core, mine_y = coords_ref[0] == 0, coords_ref[4] == 0
    half = wout_ref.shape[2] // 2
    wide = 3 * half
    part = wout_ref.shape[1] // 2

    def piece(four, rows, core, y):
        own, over_y, over_core, over_both = (ref[0, rows] for ref in four)
        same_y = mine_y if y == 0 else jnp.logical_not(mine_y)
        same_core = mine_core if core == 0 else jnp.logical_not(mine_core)
        here = jnp.where(same_y, own, over_y)
        there = jnp.where(same_y, over_core, over_both)
        return jnp.where(same_core, here, there).astype(F32)

    at = lambda n: slice(n * part, (n + 1) * part)
    for layer in range(NL):
        for core in range(2):
            columns = []
            mine = slice(core * half, (core + 1) * half)
            for y in range(2):
                rows = slice(y * part, (y + 1) * part)
                mix = piece(few, slice(0, part), core, y) if layer == 0 else piece(many, at(0), core, y)
                qkv_ref[layer, rows, core * wide : (core + 1) * wide] = mix[:, :wide]
                if layer == 0:
                    group = pos_ref.shape[0] // 2
                    pos_ref[y * group : (y + 1) * group, mine] = mix[:group, wide:]
                    first = (2 * core + y) * 7
                    small_ref[first : first + 7, :half] = mix[group : group + 7, wide:]
                    small_ref[first : first + 7, half:] = mix[group + 7 : group + 14, wide:]
                    out = piece(many, slice(3 * part, 3 * part + 16), core, y)
                    for n in range(part // 16):
                        there = slice(y * part + 16 * n, y * part + 16 * (n + 1))
                        wout_ref[layer, there, mine] = out[:, n * half : (n + 1) * half]
                else:
                    wout_ref[layer, rows, mine] = mix[:, wide:]
                first = piece(many, at(2), core, y) if layer == 0 else piece(early, at(1), core, y)
                one_ref[layer, rows, core * 4 * half : (core + 1) * 4 * half] = first
                second = piece(many, at(1), core, y) if layer == 0 else piece(early, at(0), core, y)
                columns += [second[:, i * half : (i + 1) * half] for i in range(4)]
            two_ref[layer, :, mine] = jnp.concatenate(columns, axis=0).T
    owners = small_ref.shape[1] // type_ref.shape[1]
    size, long = type_ref.shape[1], bias_ref.shape[1]
    per = long * owners // small_ref.shape[1]
    few_rows = small_ref[:20]
    mine, bias = few_rows[:, :size], [small_ref[20 + n * per : 21 + n * per, :long] for n in range(NL)]
    for owner in range(1, owners):
        chosen = coords_ref[5] == owner
        mine = jnp.where(chosen, few_rows[:, owner * size : (owner + 1) * size], mine)
        row, at_lane = divmod(owner * long, small_ref.shape[1])
        for n in range(NL):
            there = small_ref[20 + n * per + row : 21 + n * per + row, at_lane : at_lane + long]
            bias[n] = jnp.where(chosen, there, bias[n])
    type_ref[...] = mine[:2]
    gain_ref[...] = mine[2 : 2 + 2 * NL + 1]
    shift_ref[...] = mine[2 + 2 * NL + 1 :]
    for n in range(NL):
        bias_ref[n : n + 1] = bias[n]


def finish(coords, many, early, few, width, ff, owners):
    s = jax.ShapeDtypeStruct
    rows = width // owners
    return run(
        finish_kernel,
        (),
        out_shape=(
            s((NL, rows, 3 * width), F32), s((NL, rows, width), F32), s((NL, rows, ff), F32), s((NL, ff // owners, width), F32),
            s((64, width), F32), s((2, rows), F32), s((2 * NL + 1, rows), F32), s((6 * NL + 1, rows), F32), s((NL, ff // owners), F32),
        ),
        in_specs=[SM] + [VM] * 12,
        operands=(coords, *many, *early, *few),
        out_specs=(VM,) * 9,
        scratch_shapes=[pltpu.VMEM((28, width), F32)],
        cost_estimate=CHEAP,
        vmem=24,
        name="finish",
    )


def table_finish_kernel(coords_ref, own_ref, other_ref, out_ref, mark_ref):
    mark_ref[...] = jnp.zeros_like(mark_ref)
    half = own_ref.shape[1]
    first = coords_ref[0] == 0
    out_ref[:, :half] = jnp.where(first, own_ref[...], other_ref[...]).astype(F32)
    out_ref[:, half:] = jnp.where(first, other_ref[...], own_ref[...]).astype(F32)


def table_finish(coords, own, other, after=()):
    return run(
        table_finish_kernel,
        after,
        out_shape=(jax.ShapeDtypeStruct((own.shape[0], 2 * own.shape[1]), F32), jax.ShapeDtypeStruct((8, 128), F32)),
        in_specs=[SM, VM, VM],
        operands=(coords, own, other),
        out_specs=(VM, VM),
        cost_estimate=CHEAP,
        vmem=16,
        name="table_finish",
    )


AXES = ("dp", "vocab")
VOCAB_MASK = {"x": 1, "a": 2, "b": 4}


def add(left_op, right_op):
    return (left_op.astype(F32) + right_op.astype(F32)).astype(LOW)


class Cube:
    def __init__(self, dp_size, vocab_size):
        self.dp_size = dp_size
        self.vocab_size = vocab_size
        self.dp_bits = dp_size.bit_length() - 1
        self.vocab_bits = vocab_size.bit_length() - 1
        assert 1 << self.dp_bits == dp_size and 1 << self.vocab_bits == vocab_size
        self.small = self.dp_bits == 2 and self.vocab_bits == 3

    def permute(self, value, dp_mask, vocab_mask):
        count = self.vocab_size
        pairs = [
            (d * count + v, (d ^ dp_mask) * count + (v ^ vocab_mask))
            for d in range(self.dp_size)
            for v in range(count)
        ]
        return lax.ppermute(value, AXES, pairs)

    def core(self, value):
        return self.permute(value, 1, 0)

    def along(self, value, dims):
        return self.permute(
            value, 2 * ("y" in dims) + ("core" in dims), sum(VOCAB_MASK[dim] for dim in dims if dim in VOCAB_MASK)
        )

    def core_is_first(self):
        return (lax.axis_index("dp") & 1) == 0

    def coords(self):
        dp, vocab = lax.axis_index("dp"), lax.axis_index("vocab")
        return jnp.stack([dp & 1, vocab & 1, (vocab >> 1) & 1, (vocab >> 2) & 1, (dp >> 1) & 1, vocab])

    def halves(self, matrix):
        mine = lax.axis_index("dp") & 1
        width = matrix.shape[1] // 2
        keep = lax.dynamic_slice_in_dim(matrix, mine * width, width, 1)
        send = lax.dynamic_slice_in_dim(matrix, (1 - mine) * width, width, 1)
        return keep, send

    def ordered(self, first, mine, other, axis):
        return jnp.concatenate(
            [jnp.where(first, mine, other), jnp.where(first, other, mine)], axis=axis
        )

    def join_core(self, share, axis):
        return self.ordered(self.core_is_first(), share, self.core(share), axis).astype(F32)

    def reduce(self, matrix):
        for bit in reversed(range(self.vocab_bits)):
            mine = (lax.axis_index("vocab") >> bit) & 1
            rows = matrix.shape[0] // 2
            keep = lax.dynamic_slice_in_dim(matrix, mine * rows, rows, 0)
            send = lax.dynamic_slice_in_dim(matrix, (1 - mine) * rows, rows, 0)
            matrix = add(keep, self.permute(send, 0, 1 << bit))
        for bit in range(1, self.dp_bits):
            matrix = add(matrix, self.permute(matrix, 1 << bit, 0))
        return matrix


def on_device(
    cube,
    token_ids,
    lengths,
    type_ids,
    word_table,
    pos_table,
    type_table,
    gains,
    shifts,
    w_qkv,
    w_out,
    b_ff1,
    w_ff1,
    w_ff2,
    cotangent,
):
    owners = cube.vocab_size
    local_rows, width = word_table.shape
    assert token_ids.shape[0] == 1
    tokens = token_ids.shape[1]
    slot_count = 2 * tokens // owners
    slots = owners * slot_count
    coords = cube.coords()

    all_ids = lax.all_to_all(
        jnp.broadcast_to(token_ids, (owners, tokens)), "vocab", split_axis=0, concat_axis=0, tiled=True
    )
    local = all_ids - lax.axis_index("vocab") * local_rows
    here = (local >= 0) & (local < local_rows)
    rank = jnp.cumsum(here.astype(jnp.int32), axis=1) - 1
    slot_hit = (
        jnp.where(here, rank, -1)[:, None, :] == jnp.arange(slot_count, dtype=jnp.int32)[None, :, None]
    )
    asked = jnp.sum(jnp.where(slot_hit, local[:, None, :] + 1, 0), axis=2).reshape(slots) - 1
    row_hit = (asked[:, None] == jnp.arange(local_rows, dtype=jnp.int32)[None, :]).astype(LOW)
    replies = exchange_rows(dot(row_hit, word_table).astype(LOW), owners)
    number = jnp.arange(owners, dtype=jnp.int32)[:, None]
    chosen = (token_ids >= number * local_rows) & (token_ids < (number + 1) * local_rows)
    own_rank = jnp.cumsum(chosen.astype(jnp.int32), axis=1) - 1
    slot_row = jnp.sum(jnp.where(chosen, number * slot_count + own_rank, 0), axis=0, keepdims=True)
    asked = both_cores(asked[:, None], cube.core(asked[:, None]), owners).reshape(1, -1)
    (n0, s0, hidden), top, layers = forward(
        coords, lengths, replies, slot_row, type_ids, pos_table, type_table, gains, shifts, b_ff1.astype(F32),
        cotangent.reshape(tokens, width), w_qkv, w_out, w_ff1, w_ff2,
    )
    norms, saved = [(n0, s0)], []
    for xlow, mixed, lse, ctxt, n1, s1, mlow, gp, act, *end in layers:
        saved.append((mixed, lse, n1, s1, gp) + tuple((own, cube.core(own)) for own in (xlow, ctxt, mlow, act)))
        norms.append(tuple(end))
    hidden_out = hidden.reshape(1, tokens, width)

    gradients = gradients_small if cube.small else gradients_any
    outs = gradients(
        cube, coords, lengths, top, saved, gains, w_qkv, w_out, w_ff1, w_ff2,
        norms, (type_ids, slot_row, asked, local_rows),
    )
    return (hidden_out,) + outs


def exchange_rows(outgoing, owners):
    shape = outgoing.shape
    return lax.all_to_all(
        outgoing.reshape(owners, -1, shape[1]), "vocab", split_axis=0, concat_axis=0, tiled=True
    ).reshape(shape)


def both_cores(own, other, owners):
    fold = lambda array: array.reshape(owners, 1, -1, array.shape[1])
    return jnp.concatenate([fold(own), fold(other)], axis=1).reshape(-1, own.shape[1])


def unpack(pack):
    cores, blocks, _, half = pack.shape
    pos = pack[:, :, :32].transpose(1, 2, 0, 3).reshape(blocks * 32, 2 * half)
    small = pack[:, :2, 32:46].reshape(cores, 2, 2, 7, half).transpose(0, 1, 3, 2, 4)
    return pos, small.reshape(28, 2 * half)


def small_outs(cube, rows):
    place_of = lax.axis_index("vocab")

    def mine(array):
        size = array.shape[1] // cube.vocab_size
        return lax.dynamic_slice_in_dim(array, place_of * size, size, 1)

    few = mine(rows[:20])
    return few[:2], few[2 : 2 + 2 * NL + 1], few[2 + 2 * NL + 1 :], mine(rows[20:].reshape(NL, -1))


def gradients_any(cube, coords, lengths, top, saved, gains, w_qkv, w_out, w_ff1, w_ff2, norms, embed):
    owners = cube.vocab_size
    width = w_out.shape[1]
    tokens = top[0].shape[0]
    blocks = 8
    half = width // 2
    kinds, slot_row, asked, local_rows = embed
    mixed1, lse1, n1_1, s1_1, gp1, x1, ctx1, mid1, act1 = saved[1]
    mixed0, lse0, n1_0, s1_0, gp0, x0, ctx0, mid0, act0 = saved[0]
    e, low, sec_keep, sec_send, top1 = top
    pre_keep, pre_send, bias1, first, _, fst_keep, fst_send, gctx, sums1 = feed(
        1, coords, e, low, n1_1, s1_1, gains, gp1, w_out, w_ff1, w_ff2
    )
    pair = lambda keep, send: (keep, cube.core(send))
    two1, one1 = weights(blocks, (None, None), coords, pair(sec_keep, sec_send), act1, mid1, pair(pre_keep, pre_send))
    fst1 = pair(fst_keep, fst_send)
    (
        mix_keep, mix_send, pre_keep, pre_send, att1, sec_keep, sec_send, top0, bias0, first, fst_keep, fst_send, gctx, sums0
    ) = between(
        1, coords, lengths, mixed1, lse1, gctx, first, *norms[1], n1_0, s1_0, gains, gp0, w_qkv, w_out, w_ff1, w_ff2
    )
    two0, one0, mix1 = weights(
        blocks, (None, None, None), coords, pair(sec_keep, sec_send), act0, mid0, pair(pre_keep, pre_send),
        (x1, pair(mix_keep, mix_send), ctx1, fst1, ctx0, pair(fst_keep, fst_send)),
    )
    out_keep, out_send, first_core, second_core = last(
        None, coords, lengths, mixed0, lse0, gctx, first, *norms[0], gains, x0[0], slot_row, kinds,
        (top0, top1, sums0, sums1, att1, bias0, bias1), w_qkv, asked.shape[1] // 2, 2 * blocks,
    )
    mine = cube.core_is_first()

    def over_cores(first, second):
        return add(jnp.where(mine, first, second), cube.core(jnp.where(mine, second, first)))

    outgoing = both_cores(out_keep, cube.core(out_send), owners)
    table_part = table_back(asked, exchange_rows(outgoing, owners), local_rows)
    for bit in range(1, cube.dp_bits):
        table_part = add(table_part, cube.permute(table_part, 1 << bit, 0))
    wide = 3 * half
    sums_last = over_cores(first_core, second_core)
    packs = sums_last[..., wide:]
    other = cube.core(packs)
    pos, small = unpack(jnp.stack([jnp.where(mine, packs, other), jnp.where(mine, other, packs)]))
    pos_out = cube.reduce(pos).astype(F32)
    for bit in range(cube.vocab_bits):
        small = add(small, cube.permute(small, 0, 1 << bit))
    for bit in range(1, cube.dp_bits):
        small = add(small, cube.permute(small, 1 << bit, 0))
    types, gains_out, shifts_out, biases = small_outs(cube, small.astype(F32))
    whole = lambda parts: jnp.concatenate(parts, axis=0)
    part = width // blocks // 2
    one = lambda parts: cube.reduce(whole(parts)[:, :part].reshape(width, -1))
    two = lambda parts: cube.reduce(
        whole(parts).reshape(blocks, 2, width // 16, 4, -1).transpose(0, 4, 1, 3, 2).reshape(-1, half)
    )
    out0 = whole(one0)[:, part:].reshape(2 * blocks, 16, 4, half)[:, :, : part // 16].transpose(0, 2, 1, 3)
    mixes = jnp.stack(
        [
            cube.reduce(jnp.concatenate([sums_last[..., :wide].reshape(width, -1), out0.reshape(width, -1)], axis=1)),
            one(mix1),
        ]
    )
    return (
        cube.join_core(table_part, -1), pos_out, types, gains_out, shifts_out,
        cube.join_core(mixes[..., :wide], 2), cube.join_core(mixes[..., wide:], 2), biases,
        cube.join_core(jnp.stack([one(one0), one(one1)]), 2), cube.join_core(jnp.stack([two(two0), two(two1)]), 2),
    )


class Bucket:
    def __init__(self, cube, plan, parts):
        self.cube, self.plan, self.parts = cube, tuple(plan), tuple(parts)

    def start(self):
        turn = self.plan[0]
        if self.plan == (("y",),):
            self.got = (self.parts[0], self.cube.along(self.parts[0], turn))
            return
        self.got = self.parts[:1]
        for n in range(1, len(self.parts)):
            there = [dim for i, dim in enumerate(turn) if (n >> (len(turn) - 1 - i)) & 1]
            self.got += (self.cube.along(self.parts[n], there),)


    def keep(self):
        self.got, self.plan = self.parts, (None,)


def joined(buckets, parts_axis):
    return (tuple(buckets), parts_axis)


def step(groups, after=(), cost=CHEAP):
    groups = [group if isinstance(group, tuple) else ((group,), 0) for group in groups]
    items = []
    for buckets, axis in groups:
        rest = buckets[0].plan[1:]
        assert all(bucket.plan[1:] == rest for bucket in buckets)
        parts = 1 if rest in ((), (("y",),)) else 2 ** len(rest[0])
        items.append((tuple(bucket.got for bucket in buckets), parts, axis))
    for (buckets, _), parts in zip(groups, combine(items, after, cost)):
        buckets[0].plan, buckets[0].parts = buckets[0].plan[1:], tuple(parts)
    return groups[0][0][0].parts[0]


def gradients_small(cube, coords, lengths, top, saved, gains, w_qkv, w_out, w_ff1, w_ff2, norms, embed):
    owners = cube.vocab_size
    width = w_out.shape[1]
    tokens = top[0].shape[0]
    blocks = owners
    half = width // 2
    single = lambda dims: tuple((dim,) for dim in dims)
    plan_two1, plan_one1 = (("x", "y"), ("a",), ("b",)), (("a",), ("x", "y"), ("b",))
    plan_mix1 = single("ayxb")
    plan_two0, plan_one0, plan_mix0 = single("xayb"), single("yxab"), (("core",), ("y",), ("x", "a"), ("b",))
    kinds, slot_row, asked, local_rows = embed
    mixed1, lse1, n1_1, s1_1, gp1, x1, ctx1, mid1, act1 = saved[1]
    mixed0, lse0, n1_0, s1_0, gp0, x0, ctx0, mid0, act0 = saved[0]
    pair = lambda keep, send: (keep, cube.core(send))
    e, low, sec_keep, sec_send, top1 = top
    pre_keep, pre_send, bias1, first, _, fst_keep, fst_send, gctx, sums1 = feed(
        1, coords, e, low, n1_1, s1_1, gains, gp1, w_out, w_ff1, w_ff2
    )
    fst1 = pair(fst_keep, fst_send)
    got = weights(
        blocks, (plan_two1, plan_one1), coords, pair(sec_keep, sec_send), act1, mid1, pair(pre_keep, pre_send)
    )
    two1, one1 = Bucket(cube, plan_two1, got[0]), Bucket(cube, plan_one1, got[1])
    two1.start()
    one1.start()
    (
        mix_keep, mix_send, pre_keep, pre_send, att1, sec_keep, sec_send, top0, bias0, first, fst_keep, fst_send, gctx, sums0
    ) = between(
        1, coords, lengths, mixed1, lse1, gctx, first, *norms[1], n1_0, s1_0, gains, gp0, w_qkv, w_out, w_ff1, w_ff2,
        after=got[0][:1] + (act0[1], mid0[1], ctx0[1], x1[1], ctx1[1]),
    )
    mark = step([two1, one1], after=(gctx,), cost=LONG)
    two1.start()
    one1.start()
    got = weights(
        blocks, (plan_two0, plan_one0, plan_mix1), coords, pair(sec_keep, sec_send), act0, mid0, pair(pre_keep, pre_send),
        (x1, pair(mix_keep, mix_send), ctx1, fst1, ctx0, pair(fst_keep, fst_send)), after=(mark,),
    )
    two0, one0, mix1 = [Bucket(cube, plan, parts) for plan, parts in zip((plan_two0, plan_one0, plan_mix1), got)]
    for bucket in (mix1, two0, one0):
        bucket.start()
    mark = step([joined((two1, one1), 1)], after=got[0][:1], cost=LONG)
    two1.start()
    out_keep, out_send, *got = last(
        plan_mix0, coords, lengths, mixed0, lse0, gctx, first, *norms[0], gains, x0[0], slot_row, kinds,
        (top0, top1, sums0, sums1, att1, bias0, bias1), w_qkv, asked.shape[1] // 2, 2 * owners, after=(mark,),
    )
    incoming = exchange_rows(both_cores(out_keep, cube.core(out_send), owners), owners)
    mix0 = Bucket(cube, plan_mix0, got)
    mix0.start()
    mark = step([two1, mix1, two0, one0], after=got[:1], cost=LONG)
    for bucket in (mix1, two0, one0):
        bucket.start()
    mark = step([mix0], after=(mark,))
    mix0.start()
    mark = step([mix1, two0, one0], after=(mark,), cost=LONG)
    for bucket in (mix1, two0, one0):
        bucket.start()
    folded = (local_rows // 48, 48, half)
    got = table_back(asked, incoming, local_rows, after=(mark,))
    table = Bucket(cube, single("y"), (got.reshape(folded),))
    table.start()
    mark = step([mix0, joined((mix1, two0, one0), 1)], after=(got,), cost=LONG)
    mix0.start()
    mix1.start()
    two1.keep()
    mark = step([table, two1], after=(mark,))
    early = Bucket(cube, (), (cube.along(two1.parts[0], ("y",)),))
    early.keep()
    mark = step([mix0], after=(mark,), cost=LONG)
    mix0.start()
    mark = step([mix1, early], after=(mark,))
    later = Bucket(cube, (), (cube.along(mix1.parts[0], ("y",)),))
    later.keep()
    table_own = table.parts[0].reshape(local_rows, half)
    table_out, mark = table_finish(coords, table_own, cube.core(table_own), after=(mark,))
    others = [Bucket(cube, (), (cube.core(bucket.parts[0]),)) for bucket in (two1, early)]
    for other in others:
        other.keep()
    mark = step([mix0] + others, after=(mark,))
    last_y = Bucket(cube, (), (cube.along(mix0.parts[0], ("y",)),))
    last_y.keep()
    step([last_y], after=(mark,))
    step([later], after=(last_y.parts[0],))
    four = lambda own, over_y: (own, over_y, cube.core(own), cube.core(over_y))
    qkv_out, wout_out, one_out, two_out, pos_out, types, gains, shifts, biases = finish(
        coords, four(mix1.parts[0], later.parts[0]),
        (two1.parts[0], early.parts[0], others[0].parts[0], others[1].parts[0]),
        four(mix0.parts[0], last_y.parts[0]), width, w_ff1.shape[2], owners,
    )
    return (
        table_out, pos_out, types, gains, shifts, qkv_out, wout_out,
        biases, one_out, two_out,
    )


def solution(mesh):
    cube = Cube(mesh.shape["dp"], mesh.shape["vocab"])
    both = ("dp", "vocab")
    in_specs = (
        P(both, None),
        P(both),
        P(both, None),
        P("vocab", None),
        P(),
        P(),
        P(),
        P(),
        P(),
        P(),
        P(),
        P(),
        P(),
        P(both, None, None),
    )
    out_specs = (
        P(both, None, None),
        P("vocab", None),
        P("vocab", None),
        P(None, "vocab"),
        P(None, "vocab"),
        P(None, "vocab"),
        P(None, "vocab", None),
        P(None, "vocab", None),
        P(None, "vocab"),
        P(None, "vocab", None),
        P(None, "vocab", None),
    )
    return jax.shard_map(
        functools.partial(on_device, cube), mesh=mesh, in_specs=in_specs, out_specs=out_specs, check_vma=False
    )
```

```python
import functools
import jax
import jax.numpy as jnp
from jax import lax
from jax.experimental import pallas as pl
from jax.experimental.pallas import tpu as pltpu
from jax.sharding import PartitionSpec as P

HEADS = 12
HEAD_DIM = 64
NL = 2
norm_eps = 1e-12
SCALE = HEAD_DIM ** (-0.5)
ANY = pl.BlockSpec(memory_space=pl.ANY)
HBM = pl.BlockSpec(memory_space=pltpu.HBM)
VM = pl.BlockSpec(memory_space=pltpu.VMEM)
SM = pl.BlockSpec(memory_space=pltpu.SMEM)
F32, LOW = jnp.float32, jnp.bfloat16

CHEAP = pl.CostEstimate(flops=1, bytes_accessed=1, transcendentals=0)
DEAR = pl.CostEstimate(flops=10**10, bytes_accessed=1, transcendentals=0)
LONG = pl.CostEstimate(flops=10**11, bytes_accessed=1, transcendentals=0)


def run(kernel, after, out_shape, in_specs, operands, vmem, **options):
    count = len(operands)

    def body(*refs):
        kernel(*refs[:count], *refs[count + len(after) :])

    return pl.pallas_call(
        body,
        out_shape=out_shape,
        in_specs=list(in_specs) + [ANY] * len(after),
        compiler_params=pltpu.CompilerParams(vmem_limit_bytes=vmem * 1024 * 1024),
        **options,
    )(*operands, *after)


def normalize(inputs):
    centered = inputs - jnp.mean(inputs, axis=-1, keepdims=True)
    spread = lax.rsqrt(jnp.mean(centered * centered, axis=-1, keepdims=True) + norm_eps)
    return (centered * spread, spread)


def norm_back(grad_out, normed, spread, gain_row):
    scaled = grad_out * gain_row
    return spread * (
        scaled
        - jnp.mean(scaled, axis=-1, keepdims=True)
        - normed * jnp.mean(scaled * normed, axis=-1, keepdims=True)
    )


def dot(left_op, right_op, dims=((1,), (0,))):
    return lax.dot_general(left_op, right_op, (dims, ((), ())), preferred_element_type=F32)


ROWS = ((0,), (0,))
COLS = ((1,), (1,))


def gelu_pair(inputs):
    size = jnp.abs(inputs)
    bell = jnp.exp2(inputs * inputs * (-0.5 * 1.4426950408889634))
    t = 1.0 / (1.0 + size * (0.3275911 * 0.7071067811865476))
    tail = t * (
        0.5 * 0.254829592
        + t * (0.5 * -0.284496736 + t * (0.5 * 1.421413741 + t * (0.5 * -1.453152027 + t * (0.5 * 1.061405429))))
    )
    tail = tail * bell
    phi = jnp.where(inputs >= 0.0, 1.0 - tail, tail)
    return inputs * phi, phi + inputs * bell * 0.3989422804014327


def as_column(row):
    return jnp.broadcast_to(row, (128, row.shape[1])).T[:, :1]


def forward_kernel(
    coords_ref, length_ref, replies_ref, slot_ref, kind_ref, pos_ref, type_ref, gains_ref, shifts_ref, ffn_bias_ref,
    grad_ref, wqkv_hbm, wout_hbm, w1_hbm, w2_hbm,
    *refs,
):
    n0_ref, s0_ref, hidden_ref = refs[:3]
    top = refs[3:8]
    outs = [refs[8 + 11 * layer : 19 + 11 * layer] for layer in range(NL)]
    wqkv, wout, w1, w2, sems, xlow, mixed, ctxt, mlow, gp, act, n0, n1, n2, x, osems = refs[6 + 11 * NL :]
    tokens, width = x.shape
    ff = w1.shape[2]
    loads = []
    for layer in range(NL):
        for i, (src, dst) in enumerate([(wqkv_hbm, wqkv), (wout_hbm, wout), (w1_hbm, w1), (w2_hbm, w2)]):
            loads.append(pltpu.make_async_copy(src.at[layer], dst.at[layer], sems.at[4 * layer + i]))
    for load in loads:
        load.start()
    pending, used = {}, [0]

    def emit(name, src, dst, at=None):
        if at is not None:
            src, dst = src.at[:, at], dst.at[:, at]
        copy = pltpu.make_async_copy(src, dst, osems.at[used[0]])
        used[0] += 1
        copy.start()
        pending.setdefault(name, []).append(copy)

    def reuse(name):
        for copy in pending.pop(name, ()):
            copy.wait()

    gains = gains_ref[...].astype(F32)
    shifts = shifts_ref[...].astype(F32)
    number = lax.broadcasted_iota(jnp.int32, (tokens, replies_ref.shape[0]), 1)
    hit = jnp.where(number == as_column(slot_ref[...].astype(F32)).astype(jnp.int32), 1.0, 0.0).astype(LOW)
    types = type_ref[...].astype(F32)
    embedded = dot(hit, replies_ref[...]) + pos_ref[...].astype(F32)
    embedded = embedded + jnp.where(as_column(kind_ref[...].astype(F32)) > 0.5, types[1:2], types[0:1])
    normed, spread = normalize(embedded)
    n0[...] = normed
    emit("n0", n0, n0_ref)
    s0_ref[...] = jnp.broadcast_to(spread, s0_ref.shape)
    x[...] = normed * gains[0:1] + shifts[0:1]

    key_slot = lax.broadcasted_iota(jnp.int32, (tokens, 128), 0)
    visible = jnp.where(key_slot < length_ref[0], 0.0, -1e30)[:, :1]
    lane = lax.broadcasted_iota(jnp.int32, (tokens, 128), 1)
    chunk = 512

    for layer in range(NL):
        base = 1 + 6 * layer
        xlow_ref, mixed_ref, lse_ref, ctxt_ref, n1_ref, s1_ref, mlow_ref, gp_ref, act_ref = outs[layer][:9]

        reuse("xlow")
        xlow[...] = x[...].astype(LOW)
        emit("xlow", xlow, xlow_ref)
        loads[4 * layer].wait()
        reuse("mixed")
        for i in range(3):
            cols = slice(i * width, (i + 1) * width)
            got = dot(xlow[...], wqkv[layer, :, cols])
            if i != 1:
                row = base + (0 if i == 0 else 1)
                got = got + shifts[row : row + 1]
            mixed[:, cols] = got.astype(LOW)
        emit("mixed", mixed, mixed_ref)
        reuse("ctxt")

        def pair_step(j, carry):
            at = pl.multiple_of(j * 128, 128)
            q = mixed[:, pl.ds(at, 128)] * jnp.asarray(SCALE, LOW)
            k = mixed[:, pl.ds(pl.multiple_of(width + at, 128), 128)]
            v = mixed[:, pl.ds(pl.multiple_of(2 * width + at, 128), 128)]
            vt = v.T
            scores = []
            for h in range(2):
                kh = jnp.where((lane < 64) == (h == 0), k, jnp.zeros_like(k))
                scores.append(dot(kh, q, COLS) + visible)
            for h in range(2):
                top = jnp.max(scores[h], axis=0, keepdims=True)
                weights = jnp.exp(scores[h] - top)
                total = jnp.sum(weights, axis=0, keepdims=True)
                out = dot(vt[h * 64 : (h + 1) * 64], weights.astype(LOW)) * (1.0 / total)
                ctxt[pl.ds(pl.multiple_of(at + h * 64, 64), 64), :] = out.astype(LOW)
                lse_ref[pl.ds(2 * j + h, 1), :] = top + jnp.log(total)
            return carry

        lax.fori_loop(0, HEADS // 2, pair_step, 0, unroll=2)
        emit("ctxt", ctxt, ctxt_ref)
        loads[4 * layer + 1].wait()
        attended = dot(ctxt[...], wout[layer], ROWS) + shifts[base + 2 : base + 3]
        normed, spread = normalize(x[...] + attended)
        reuse("n1")
        n1[...] = normed
        emit("n1", n1, n1_ref)
        s1_ref[...] = jnp.broadcast_to(spread, s1_ref.shape)
        x[...] = normed * gains[1 + 2 * layer : 2 + 2 * layer] + shifts[base + 3 : base + 4]
        reuse("mlow")
        mlow[...] = x[...].astype(LOW)
        emit("mlow", mlow, mlow_ref)
        loads[4 * layer + 2].wait()
        reuse("gp")
        reuse("act")
        for i in range(ff // chunk):
            cols = slice(i * chunk, (i + 1) * chunk)
            pre = dot(mlow[...], w1[layer, :, cols]) + ffn_bias_ref[layer : layer + 1, cols]
            active, slope = gelu_pair(pre)
            gp[:, cols] = slope.astype(LOW)
            act[:, cols] = active.astype(LOW)
            emit("gp", gp, gp_ref, pl.ds(i * chunk, chunk))
            emit("act", act, act_ref, pl.ds(i * chunk, chunk))
        loads[4 * layer + 3].wait()
        normed, spread = normalize(x[...] + shifts[base + 4 : base + 5] + dot(act[...], w2[layer]))
        if layer < NL - 1:
            n2_ref, s2_ref = outs[layer][9:11]
            n2[...] = normed
            emit("n2", n2, n2_ref)
            s2_ref[...] = jnp.broadcast_to(spread, s2_ref.shape)
        else:
            gain = gains[2 * NL : 2 * NL + 1]
            norm_end(coords_ref[0], grad_ref[...].astype(F32), normed, spread, gain, *top)
        x[...] = normed * gains[2 + 2 * layer : 3 + 2 * layer] + shifts[base + 5 : base + 6]
    hidden_ref[...] = x[...].astype(LOW)
    for name in list(pending):
        reuse(name)


def forward(
    coords, length, replies, slot_of, kinds, pos, types, gains, shifts, ffn_bias, cotangent, w_qkv, w_out, w_ff1, w_ff2
):
    tokens, width = pos.shape
    ff = w_ff1.shape[2]
    s = jax.ShapeDtypeStruct
    v = pltpu.VMEM
    spread = s((tokens, 128), F32)
    wide = s((tokens, width), F32)
    low = s((tokens, width), LOW)
    layer_out = (
        low, s((tokens, 3 * width), LOW), s((HEADS, tokens), F32), s((width, tokens), LOW),
        wide, spread, low, s((tokens, ff), LOW), s((tokens, ff), LOW), wide, spread,
    )
    layer_spec = (ANY, ANY, VM, ANY, ANY, VM, ANY, ANY, ANY, ANY, VM)
    chunks = ff // 512
    end = norm_end_shapes(tokens, width)
    outs = run(
        forward_kernel,
        (),
        out_shape=(wide, spread, low) + end + layer_out * (NL - 1) + layer_out[:9],
        in_specs=[SM, SM] + [VM] * 9 + [HBM] * 4,
        operands=(
            coords, length, replies, slot_of, kinds, pos, types, gains, shifts, ffn_bias, cotangent, w_qkv, w_out, w_ff1, w_ff2
        ),
        out_specs=(ANY, VM, VM) + (VM,) * 5 + layer_spec * (NL - 1) + layer_spec[:9],
        scratch_shapes=[
            v((NL, width, 3 * width), LOW), v((NL, width, width), LOW), v((NL, width, ff), LOW), v((NL, ff, width), LOW),
            pltpu.SemaphoreType.DMA((4 * NL,)),
            v((tokens, width), LOW), v((tokens, 3 * width), LOW), v((width, tokens), LOW), v((tokens, width), LOW),
            v((tokens, ff), LOW), v((tokens, ff), LOW), v((tokens, width), F32), v((tokens, width), F32),
            v((tokens, width), F32), v((tokens, width), F32), pltpu.SemaphoreType.DMA((1 + NL * (6 + 2 * chunks),)),
        ],
        cost_estimate=CHEAP,
        vmem=60,
        name="forward",
    )
    return outs[:3], outs[3:8], [outs[8 + 11 * layer : 19 + 11 * layer] for layer in range(NL)]


def part(mine, source, keep_to, send_to):
    half = source.shape[1] // 2

    @pl.when(mine == 0)
    def _():
        keep_to[...] = source[:, :half]
        send_to[...] = source[:, half:]

    @pl.when(mine == 1)
    def _():
        keep_to[...] = source[:, half:]
        send_to[...] = source[:, :half]


def norm_end(mine, grad, n, s, gain, back_ref, low_ref, keep_ref, send_ref, sums_ref):
    sums_ref[0:1] = jnp.sum(grad * n, axis=0, keepdims=True)
    sums_ref[1:2] = jnp.sum(grad, axis=0, keepdims=True)
    back = norm_back(grad, n, s, gain)
    sums_ref[2:3] = jnp.sum(back, axis=0, keepdims=True)
    back_ref[...] = back
    low_ref[...] = back.astype(LOW)
    if keep_ref is not None:
        part(mine, low_ref, keep_ref, send_ref)


def norm_end_shapes(tokens, width):
    s = jax.ShapeDtypeStruct
    half = s((tokens, width // 2), LOW)
    return (s((tokens, width), F32), s((tokens, width), LOW), half, half, s((3, width), F32))


def feed_back_body(mine, second, gp, w2, ready, bias_ref, keep, send):
    chunk = 512
    steps = gp.shape[1] // chunk
    for i in range(steps):
        ready(i)
        cols = slice(i * chunk, (i + 1) * chunk)
        grad_pre = dot(second[...], w2[cols, :], COLS) * gp[:, cols].astype(F32)
        bias_ref[:, cols] = jnp.sum(grad_pre, axis=0, keepdims=True)
        side, at = divmod(i, steps // 2)
        there = slice(at * chunk, (at + 1) * chunk)
        low = grad_pre.astype(LOW)

        @pl.when(mine == side)
        def _():
            keep[:, there] = low

        @pl.when(mine != side)
        def _():
            send[:, there] = low


def both_halves(mine, keep, send, weight):
    half = keep.shape[1]
    first = jnp.where(mine == 0, keep[...], send[...])
    second = jnp.where(mine == 0, send[...], keep[...])
    return dot(first, weight[:, :half], COLS) + dot(second, weight[:, half:], COLS)


def attend_back_body(length_ref, mixed_ref, lse_ref, gctx_ref, att_ref, dmix):
    tokens, width = gctx_ref.shape
    key_slot = lax.broadcasted_iota(jnp.int32, (tokens, 128), 0)
    visible = jnp.where(key_slot < length_ref[0], 0.0, -1e30)[:, :1]
    lane = lax.broadcasted_iota(jnp.int32, (tokens, 128), 1)

    def pair_step(j, carry):
        at = pl.multiple_of(j * 128, 128)
        qcols = pl.ds(at, 128)
        kcols = pl.ds(pl.multiple_of(width + at, 128), 128)
        vcols = pl.ds(pl.multiple_of(2 * width + at, 128), 128)
        q = mixed_ref[:, qcols] * jnp.asarray(SCALE, LOW)
        k = mixed_ref[:, kcols]
        v = mixed_ref[:, vcols]
        g = gctx_ref[:, qcols]
        kt = k.T
        grad_v, grad_k, grad_qt = [], [], []
        scores, grad_probs = [], []
        for h in range(2):
            mask = (lane < 64) == (h == 0)
            kh = jnp.where(mask, k, jnp.zeros_like(k))
            vh = jnp.where(mask, v, jnp.zeros_like(v))
            scores.append(dot(kh, q, COLS))
            grad_probs.append(dot(vh, g, COLS))
        for h in range(2):
            probs = jnp.exp(scores[h] + visible - lse_ref[pl.ds(2 * j + h, 1), :])
            weighted = jnp.sum(probs * grad_probs[h], axis=0, keepdims=True)
            grad_scores = (probs * (grad_probs[h] - weighted)).astype(LOW)
            grad_v.append(dot(probs.astype(LOW), g))
            grad_k.append(dot(grad_scores, q))
            grad_qt.append(dot(kt[h * 64 : (h + 1) * 64], grad_scores))
        grad_q = jnp.concatenate(grad_qt, axis=0).T * SCALE
        grad_v = jnp.where(lane < 64, grad_v[0], grad_v[1])
        grad_k = jnp.where(lane < 64, grad_k[0], grad_k[1])
        att_ref[0:1, qcols] = jnp.sum(grad_q, axis=0, keepdims=True)
        att_ref[1:2, qcols] = jnp.sum(grad_v, axis=0, keepdims=True)
        dmix[:, qcols] = grad_q.astype(LOW)
        dmix[:, kcols] = grad_k.astype(LOW)
        dmix[:, vcols] = grad_v.astype(LOW)
        return carry

    lax.fori_loop(0, HEADS // 2, pair_step, 0, unroll=2)


def chunk_loads(sems, at, pairs, chunk=512):
    loads = []
    (w2_src, w2), (gp_src, gp) = pairs
    for i in range(gp.shape[1] // chunk):
        there = pl.ds(i * chunk, chunk)
        loads.append(
            (
                pltpu.make_async_copy(w2_src.at[there], w2.at[there], sems.at[at + 2 * i]),
                pltpu.make_async_copy(gp_src.at[:, there], gp.at[:, there], sems.at[at + 2 * i + 1]),
            )
        )
    return loads


def feed_kernel(
    layer, coords_ref, e_ref, second, n1_ref, s1_ref, gains_ref, gp_hbm, wout_hbm, w1_hbm, w2_hbm,
    keep_ref, send_ref, bias_ref, first_ref, low_ref, fst_keep_ref, fst_send_ref, gctx_ref, sums_ref,
    gp, wout, w1, w2, keep, send, sems,
):
    mine = coords_ref[0]
    loads = chunk_loads(sems, 4, ((w2_hbm.at[layer], w2), (gp_hbm, gp)))
    for pair in loads:
        for load in pair:
            load.start()
    late = [
        pltpu.make_async_copy(w1_hbm.at[layer], w1, sems.at[0]),
        pltpu.make_async_copy(wout_hbm.at[layer], wout, sems.at[1]),
    ]
    for load in late:
        load.start()

    def ready(i):
        for load in loads[i]:
            load.wait()

    feed_back_body(mine, second, gp, w2, ready, bias_ref, keep, send)
    stores = [
        pltpu.make_async_copy(send, send_ref, sems.at[2]),
        pltpu.make_async_copy(keep, keep_ref, sems.at[3]),
    ]
    for store in stores:
        store.start()
    late[0].wait()
    grad = e_ref[...] + both_halves(mine, keep, send, w1)
    gain = gains_ref[...].astype(F32)[1 + 2 * layer : 2 + 2 * layer]
    norm_end(mine, grad, n1_ref[...], s1_ref[:, :1], gain, first_ref, low_ref, fst_keep_ref, fst_send_ref, sums_ref)
    late[1].wait()
    gctx_ref[...] = dot(low_ref[...], wout[...], COLS).astype(LOW)
    for store in stores:
        store.wait()


def feed(layer, coords, e, second, n1, s1, gains, gp, w_out, w_ff1, w_ff2, after=()):
    tokens, width = n1.shape
    ff = gp.shape[1]
    s = jax.ShapeDtypeStruct
    v = pltpu.VMEM
    half = s((tokens, ff // 2), LOW)
    end = norm_end_shapes(tokens, width)
    return run(
        functools.partial(feed_kernel, layer),
        after,
        out_shape=(half, half, s((1, ff), F32)) + end[:4] + (s((tokens, width), LOW), end[4]),
        in_specs=[SM] + [VM] * 5 + [HBM] * 4,
        operands=(coords, e, second, n1, s1, gains, gp, w_out, w_ff1, w_ff2),
        out_specs=(ANY, ANY) + (VM,) * 7,
        scratch_shapes=[
            v((tokens, ff), LOW), v((width, width), LOW), v((width, ff), LOW), v((ff, width), LOW),
            v((tokens, ff // 2), LOW), v((tokens, ff // 2), LOW), pltpu.SemaphoreType.DMA((4 + 2 * (ff // 512),)),
        ],
        cost_estimate=CHEAP,
        vmem=52,
        name="feed",
    )


def between_kernel(
    layer, coords_ref, length_ref, mixed_ref, lse_ref, gctx_in, first_in, n2_ref, s2_ref, n1_ref, s1_ref, gains_ref,
    gp_hbm, wqkv_hbm, wout_hbm, w1_hbm, w2_hbm,
    mix_keep_ref, mix_send_ref, pre_keep_ref, pre_send_ref,
    att_ref, sec_keep_ref, sec_send_ref, top_ref, bias_ref, first_ref, fst_keep_ref, fst_send_ref, gctx_ref, sums_ref,
    gp, wqkv, wout, w1, w2, dmix, mix_keep, mix_send, keep, send, e, second, low_ref, sems,
):
    mine = coords_ref[0]
    below = layer - 1
    early = pltpu.make_async_copy(wqkv_hbm.at[layer], wqkv, sems.at[0])
    early.start()
    loads = chunk_loads(sems, 7, ((w2_hbm.at[below], w2), (gp_hbm, gp)))
    for pair in loads:
        for load in pair:
            load.start()
    late = [
        pltpu.make_async_copy(w1_hbm.at[below], w1, sems.at[1]),
        pltpu.make_async_copy(wout_hbm.at[below], wout, sems.at[2]),
    ]
    for load in late:
        load.start()
    stores = []

    def emit(src, dst):
        stores.append(pltpu.make_async_copy(src, dst, sems.at[3 + len(stores)]))
        stores[-1].start()

    attend_back_body(length_ref, mixed_ref, lse_ref, gctx_in, att_ref, dmix)
    part(mine, dmix, mix_keep, mix_send)
    emit(mix_send, mix_send_ref)
    emit(mix_keep, mix_keep_ref)
    early.wait()
    grad = first_in[...] + dot(dmix[...], wqkv[...], COLS)
    gains = gains_ref[...].astype(F32)
    norm_end(
        mine, grad, n2_ref[...], s2_ref[:, :1], gains[2 * layer : 2 * layer + 1], e, second, sec_keep_ref, sec_send_ref, top_ref
    )

    def ready(i):
        for load in loads[i]:
            load.wait()

    feed_back_body(mine, second, gp, w2, ready, bias_ref, keep, send)
    emit(send, pre_send_ref)
    emit(keep, pre_keep_ref)
    late[0].wait()
    grad = e[...] + both_halves(mine, keep, send, w1)
    norm_end(
        mine, grad, n1_ref[...], s1_ref[:, :1], gains[1 + 2 * below : 2 + 2 * below], first_ref, low_ref, fst_keep_ref,
        fst_send_ref, sums_ref,
    )
    late[1].wait()
    gctx_ref[...] = dot(low_ref[...], wout[...], COLS).astype(LOW)
    for store in stores:
        store.wait()


def between(layer, coords, length, mixed, lse, gctx, first, n2, s2, n1, s1, gains, gp, w_qkv, w_out, w_ff1, w_ff2, after=()):
    tokens, width = first.shape
    ff = gp.shape[1]
    s = jax.ShapeDtypeStruct
    v = pltpu.VMEM
    mix = s((tokens, 3 * width // 2), LOW)
    pre = s((tokens, ff // 2), LOW)
    sec = s((tokens, width // 2), LOW)
    low = s((tokens, width), LOW)
    three = s((3, width), F32)
    return run(
        functools.partial(between_kernel, layer),
        after,
        out_shape=(
            mix, mix, pre, pre, s((2, width), F32), sec, sec, three, s((1, ff), F32), s((tokens, width), F32), sec, sec, low, three,
        ),
        in_specs=[SM, SM] + [VM] * 9 + [HBM] * 5,
        operands=(coords, length, mixed, lse, gctx, first, n2, s2, n1, s1, gains, gp, w_qkv, w_out, w_ff1, w_ff2),
        out_specs=(ANY,) * 4 + (VM,) * 10,
        scratch_shapes=[
            v((tokens, ff), LOW), v((width, 3 * width), LOW), v((width, width), LOW), v((width, ff), LOW), v((ff, width), LOW),
            v((tokens, 3 * width), LOW), v(mix.shape, LOW), v(mix.shape, LOW), v(pre.shape, LOW), v(pre.shape, LOW),
            v((tokens, width), F32), v((tokens, width), LOW), v((tokens, width), LOW),
            pltpu.SemaphoreType.DMA((7 + 2 * (ff // 512),)),
        ],
        cost_estimate=CHEAP,
        vmem=58,
        name="between",
    )


COORDS = ("core", "x", "a", "b", "y")


def place(coords_ref, plan, result, *outs):
    count = result.shape[0]
    size = count // len(outs)
    dims = [] if plan is None else [dim for turn in plan for dim in turn]
    for i in range(count):
        block = i
        if plan is not None:
            bit = {}
            for n, dim in enumerate(dims):
                relative = (i >> (len(dims) - 1 - n)) & 1
                whole = plan[-1] == ("y",) and n == len(dims) - 1
                bit[dim] = relative if whole else coords_ref[COORDS.index(dim)] ^ relative
            block = 16 * bit.get("core", 0) + 8 * bit["b"] + 4 * bit["a"] + 2 * bit["x"] + bit["y"]
        out = outs[i // size]
        out[i % size] = result[block].astype(out.dtype)


def parts_of(plan):
    return 2 if plan is None else 2 ** len(plan[0])


def load_both(pairs, sems):
    loads = []
    for own, oth, dst in pairs:
        for n, src in enumerate((own, oth)):
            size = own.shape[0]
            load = pltpu.make_async_copy(src, dst.at[pl.ds(n * size, size)], sems.at[len(loads)])
            load.start()
            loads.append(load)
    return loads


def weights_kernel(plans, blocks, coords_ref, *refs):
    count = 8 if len(plans) == 2 else 20
    sources, refs = refs[:count], refs[count:]
    outs = []
    for plan in plans:
        outs.append(refs[: parts_of(plan)])
        refs = refs[parts_of(plan) :]
    sec, act, mid, pre, sect, midt, two, one = refs[:8]
    rest, sems = refs[8:-1], refs[-1]
    tokens = sources[0].shape[0]
    loads = []
    targets = [sec, act, mid, pre]
    if rest:
        x, mix, ctxt, fst, below_ctxt, below_fst, xt, mixed = rest
        targets += [x, mix, ctxt, fst, below_ctxt, below_fst]
    for n, target in enumerate(targets):
        for side in range(2):
            there = pl.ds(side * tokens, tokens)
            view = target.at[:, there] if n in (6, 8) else target.at[there]
            loads.append(pltpu.make_async_copy(sources[2 * n + side], view, sems.at[2 * n + side]))
            loads[-1].start()

    def ready(n):
        loads[2 * n].wait()
        loads[2 * n + 1].wait()

    ready(0)
    sect[...] = sec[...].T
    ready(1)
    rows = two.shape[1]
    cols = act.shape[1] // blocks

    group = 4 if blocks % 4 == 0 else 1

    def step_two(i, carry):
        there = pl.ds(pl.multiple_of(i * group * cols, cols), group * cols)
        got = dot(sect[...], act[:, there]).astype(LOW)
        for v in range(group):
            for y in range(2):
                for n in range(4):
                    at = (4 * y + n) * rows
                    piece = got[at : at + rows, v * cols : (v + 1) * cols]
                    two[2 * (i * group + v) + y, :, n * cols : (n + 1) * cols] = piece
        return carry

    lax.fori_loop(0, blocks // group, step_two, 0)
    place(coords_ref, plans[0], two, *outs[0])
    ready(2)
    midt[...] = mid[...].T
    ready(3)
    chunk = 512
    high = midt.shape[0] // one.shape[0]

    def step_one(i, carry):
        there = pl.ds(pl.multiple_of(i * chunk, chunk), chunk)
        one[:, :high, there] = dot(midt[...], pre[:, there]).astype(LOW).reshape(one.shape[0], high, chunk)
        return carry

    if rest:
        lax.fori_loop(0, pre.shape[1] // chunk, step_one, 0)
        ready(8)
        ready(9)
        part_cols, group_rows = below_fst.shape[1], one.shape[1] - high
        got = dot(below_ctxt[...], below_fst[...]).astype(LOW).reshape(one.shape[0], high, part_cols)
        for n in range(high // group_rows):
            there = slice(n * part_cols, (n + 1) * part_cols)
            one[:, high:, there] = got[:, n * group_rows : (n + 1) * group_rows]
        one[:, high:, high // group_rows * part_cols :] = jnp.zeros((one.shape[0], group_rows, part_cols), LOW)
    else:
        one[...] = dot(midt[...], pre[...]).astype(LOW).reshape(one.shape)
    place(coords_ref, plans[1], one, *outs[1])
    if rest:
        ready(4)
        xt[...] = x[...].T
        ready(5)
        wide = mix.shape[1]
        mixed[:, :, :wide] = dot(xt[...], mix[...]).astype(LOW).reshape(mixed.shape[:2] + (wide,))
        ready(6)
        ready(7)
        mixed[:, :, wide:] = dot(ctxt[...], fst[...]).astype(LOW).reshape(mixed.shape[:2] + (fst.shape[1],))
        place(coords_ref, plans[2], mixed, *outs[2])


def weights(blocks, plans, coords, sec, act, mid, pre, attention=(), after=()):
    tokens, width = mid[0].shape
    s = jax.ShapeDtypeStruct
    v = pltpu.VMEM
    count = 2 * blocks
    block = (count, width // count, 2 * width)
    high = (count, width // count + 16, 2 * width) if attention else block
    sizes = (block, high, block)
    outs = sum(
        ((s((count // parts_of(plan),) + size[1:], LOW),) * parts_of(plan) for plan, size in zip(plans, sizes)), ()
    )
    pairs = (sec, act, mid, pre) + tuple(attention)
    both = lambda pair: v((2 * tokens, pair[0].shape[1]), LOW)
    scratch = [both(pair) for pair in (sec, act, mid, pre)]
    scratch += [v((sec[0].shape[1], 2 * tokens), LOW), v((width, 2 * tokens), LOW), v(block, LOW), v(high, LOW)]
    if attention:
        x, mix, _, fst, _, below_fst = attention
        across = v((width, 2 * tokens), LOW)
        scratch += [both(x), both(mix), across, both(fst), across, both(below_fst), across, v(block, LOW)]
    got = run(
        functools.partial(weights_kernel, plans, blocks),
        after,
        out_shape=outs,
        in_specs=[SM] + [ANY] * (2 * len(pairs)),
        operands=(coords,) + tuple(array for pair in pairs for array in pair),
        out_specs=(VM,) * len(outs),
        scratch_shapes=scratch + [pltpu.SemaphoreType.DMA((2 * len(pairs),))],
        cost_estimate=CHEAP,
        vmem=50 if attention else 34,
        name="weights",
    )
    parts = []
    for plan in plans:
        parts.append(got[: parts_of(plan)])
        got = got[parts_of(plan) :]
    return parts


def combine_kernel(forms, *refs):
    count = sum(sum(form[0]) for form in forms)
    ins, outs = refs[:count], refs[count:]
    for terms_of, parts, axis in forms:
        results, outs = outs[:parts], outs[parts:]
        at = 0
        for terms in terms_of:
            mine, ins = ins[:terms], ins[terms:]
            size = mine[0].shape[0] // parts
            rows = mine[0].shape[1]
            for part in range(parts):
                for i in range(size):
                    total = mine[0][part * size + i].astype(F32)
                    for term in mine[1:]:
                        total = total + term[part * size + i].astype(F32)
                    if axis == 0:
                        results[part][at + i] = total.astype(LOW)
                    else:
                        results[part][i, at : at + rows] = total.astype(LOW)
            at += size if axis == 0 else rows


def combine(items, after=(), cost=CHEAP):
    forms = tuple((tuple(len(terms) for terms in sums), parts, axis) for sums, parts, axis in items)
    shapes = []
    for sums, parts, axis in items:
        shape = list(sums[0][0].shape)
        shape[axis] = sum(terms[0].shape[axis] for terms in sums)
        shape[0] //= parts
        shapes += [jax.ShapeDtypeStruct(tuple(shape), LOW)] * parts
    operands = tuple(array for sums, _, _ in items for terms in sums for array in terms)
    size = sum(array.size for array in operands)
    outs = run(
        functools.partial(combine_kernel, forms),
        after,
        out_shape=tuple(shapes),
        in_specs=[VM] * len(operands),
        operands=operands,
        out_specs=(VM,) * len(shapes),
        cost_estimate=cost,
        vmem=6 + 4 * size // (1 << 20),
        name="combine",
    )
    got = []
    for _, parts, _ in forms:
        got.append(outs[:parts])
        outs = outs[parts:]
    return got


def last_kernel(
    plan, coords_ref, length_ref, mixed_ref, lse_ref, gctx_ref, first_ref, n_ref, s_ref, gains_ref, x_ref,
    slot_ref, type_ref, top0, top1, low0, low1, att1, bias0, bias1, wqkv_hbm,
    out_keep_ref, out_send_ref, *parts_and_scratch
):
    outs, (wqkv, dmix, xt, res, back_ref, back_low, att0, emb, small, sems) = parts_and_scratch[:-10], parts_and_scratch[-10:]
    tokens, width = back_ref.shape
    load = pltpu.make_async_copy(wqkv_hbm.at[0], wqkv, sems.at[0])
    load.start()
    attend_back_body(length_ref, mixed_ref, lse_ref, gctx_ref, att0, dmix)
    load.wait()
    grad = first_ref[...] + dot(dmix[...], wqkv[...], COLS)
    gain = gains_ref[...].astype(F32)[0:1]
    norm_end(coords_ref[0], grad, n_ref[...], s_ref[:, :1], gain, back_ref, back_low, None, None, emb)
    mine = coords_ref[0]
    slots, half = out_keep_ref.shape
    chunk = 256

    def step(i, carry):
        there = pl.ds(pl.multiple_of(i * chunk, chunk), chunk)
        number = lax.broadcasted_iota(jnp.int32, (chunk, tokens), 0) + i * chunk
        hit = jnp.where(number == slot_ref[...], 1.0, 0.0).astype(LOW)
        got = dot(hit, back_low[...]).astype(LOW)

        @pl.when(mine == 0)
        def _():
            out_keep_ref[there, :] = got[:, :half]
            out_send_ref[there, :] = got[:, half:]

        @pl.when(mine == 1)
        def _():
            out_keep_ref[there, :] = got[:, half:]
            out_send_ref[there, :] = got[:, :half]

        return carry

    lax.fori_loop(0, slots // chunk, step, 0)
    xt[...] = x_ref[...].T
    blocks, piece, _ = res.shape
    blocks //= 2
    wide = 3 * half
    for core in range(2):
        there = slice(core * blocks, (core + 1) * blocks)
        got = dot(xt[...], dmix[:, core * wide : (core + 1) * wide]).astype(LOW)
        res[there, :, :wide] = got.reshape(blocks, piece, wide)
    back = back_ref[...]
    kind = as_column(type_ref[...].astype(F32))
    small[0:1] = jnp.sum(back * (1.0 - kind), axis=0, keepdims=True)
    small[1:2] = jnp.sum(back * kind, axis=0, keepdims=True)
    sources = [(emb, 0)]
    for top, low in ((top0, low0), (top1, low1)):
        sources += [(low, 0), (top, 0)]
    sources += [(emb, 1)]
    for top, low, att in ((top0, low0, att0), (top1, low1, att1)):
        sources += [(att, 0), (att, 1), (low, 2), (low, 1), (top, 2), (top, 1)]
    at = 2
    for ref, row in sources:
        small[at : at + 1] = ref[row : row + 1]
        at += 1
    for bias in (bias0, bias1):
        for i in range(bias.shape[1] // width):
            small[at : at + 1] = bias[:, i * width : (i + 1) * width]
            at += 1
    quarter = at // 4
    group = tokens // blocks
    positions = back.reshape(blocks, group, width).astype(LOW)
    for core in range(2):
        there = slice(core * blocks, (core + 1) * blocks)
        res[there, :group, wide:] = positions[:, :, core * half : (core + 1) * half]
        for y in range(2):
            mine = small[(2 * core + y) * quarter : (2 * core + y + 1) * quarter]
            rest = jnp.zeros((piece - group - 2 * quarter, half), F32)
            mine = jnp.concatenate([mine[:, :half], mine[:, half:], rest], axis=0).astype(LOW)
            for v in range(blocks // 2):
                res[core * blocks + 2 * v + y, group:, wide:] = mine
    place(coords_ref, plan, res, *outs)


def last(plan, coords, length, mixed, lse, gctx, first, n, sp, gains, x, slot_of, types, sums, w_qkv, slots, blocks, parts=2, after=()):
    tokens, width = first.shape
    s = jax.ShapeDtypeStruct
    v = pltpu.VMEM
    block = (blocks, width // blocks, 2 * width)
    operands = (coords, length, mixed, lse, gctx, first, n, sp, gains, x, slot_of, types, *sums, w_qkv)
    return run(
        functools.partial(last_kernel, plan),
        after,
        out_shape=(s((slots, width // 2), LOW),) * 2 + (s((2 * blocks // parts,) + block[1:], LOW),) * parts,
        in_specs=[SM, SM] + [VM] * (len(operands) - 3) + [HBM],
        operands=operands,
        out_specs=(VM,) * (2 + parts),
        scratch_shapes=[
            v((width, 3 * width), LOW), v((tokens, 3 * width), LOW), v((width, tokens), LOW),
            v((2 * blocks,) + block[1:], LOW), v((tokens, width), F32), v((tokens, width), LOW),
            v((2, width), F32), v((3, width), F32), v((28, width), F32), pltpu.SemaphoreType.DMA((1,)),
        ],
        cost_estimate=CHEAP,
        vmem=52,
        name="last",
    )


def table_back_kernel(asked_ref, rows_ref, out_ref):
    count = out_ref.shape[0]
    chunk = count // 5 if count % 80 == 0 else count

    def step(i, carry):
        at = pl.multiple_of(i * chunk, 16)
        number = lax.broadcasted_iota(jnp.int32, (chunk, rows_ref.shape[0]), 0) + at
        hit = jnp.where(number == asked_ref[...], 1.0, 0.0).astype(LOW)
        out_ref[pl.ds(at, chunk), :] = dot(hit, rows_ref[...]).astype(LOW)
        return carry

    lax.fori_loop(0, count // chunk, step, 0)


def table_back(asked, rows, local_rows, after=()):
    return run(
        table_back_kernel,
        after,
        out_shape=jax.ShapeDtypeStruct((local_rows, rows.shape[1]), LOW),
        in_specs=[VM, VM],
        operands=(asked, rows),
        out_specs=VM,
        cost_estimate=CHEAP,
        vmem=20,
        name="table_back",
    )


def finish_kernel(coords_ref, *refs):
    many, early, few = refs[:4], refs[4:8], refs[8:12]
    qkv_ref, wout_ref, one_ref, two_ref, pos_ref, type_ref, gain_ref, shift_ref, bias_ref, small_ref = refs[12:]
    mine_core, mine_y = coords_ref[0] == 0, coords_ref[4] == 0
    half = wout_ref.shape[2] // 2
    wide = 3 * half
    part = wout_ref.shape[1] // 2

    def piece(four, rows, core, y):
        own, over_y, over_core, over_both = (ref[0, rows] for ref in four)
        same_y = mine_y if y == 0 else jnp.logical_not(mine_y)
        same_core = mine_core if core == 0 else jnp.logical_not(mine_core)
        here = jnp.where(same_y, own, over_y)
        there = jnp.where(same_y, over_core, over_both)
        return jnp.where(same_core, here, there).astype(F32)

    at = lambda n: slice(n * part, (n + 1) * part)
    for layer in range(NL):
        for core in range(2):
            columns = []
            mine = slice(core * half, (core + 1) * half)
            for y in range(2):
                rows = slice(y * part, (y + 1) * part)
                mix = piece(few, slice(0, part), core, y) if layer == 0 else piece(many, at(0), core, y)
                qkv_ref[layer, rows, core * wide : (core + 1) * wide] = mix[:, :wide]
                if layer == 0:
                    group = pos_ref.shape[0] // 2
                    pos_ref[y * group : (y + 1) * group, mine] = mix[:group, wide:]
                    first = (2 * core + y) * 7
                    small_ref[first : first + 7, :half] = mix[group : group + 7, wide:]
                    small_ref[first : first + 7, half:] = mix[group + 7 : group + 14, wide:]
                    out = piece(many, slice(3 * part, 3 * part + 16), core, y)
                    for n in range(part // 16):
                        there = slice(y * part + 16 * n, y * part + 16 * (n + 1))
                        wout_ref[layer, there, mine] = out[:, n * half : (n + 1) * half]
                else:
                    wout_ref[layer, rows, mine] = mix[:, wide:]
                first = piece(many, at(2), core, y) if layer == 0 else piece(early, at(1), core, y)
                one_ref[layer, rows, core * 4 * half : (core + 1) * 4 * half] = first
                second = piece(many, at(1), core, y) if layer == 0 else piece(early, at(0), core, y)
                columns += [second[:, i * half : (i + 1) * half] for i in range(4)]
            two_ref[layer, :, mine] = jnp.concatenate(columns, axis=0).T
    owners = small_ref.shape[1] // type_ref.shape[1]
    size, long = type_ref.shape[1], bias_ref.shape[1]
    per = long * owners // small_ref.shape[1]
    few_rows = small_ref[:20]
    mine, bias = few_rows[:, :size], [small_ref[20 + n * per : 21 + n * per, :long] for n in range(NL)]
    for owner in range(1, owners):
        chosen = coords_ref[5] == owner
        mine = jnp.where(chosen, few_rows[:, owner * size : (owner + 1) * size], mine)
        row, at_lane = divmod(owner * long, small_ref.shape[1])
        for n in range(NL):
            there = small_ref[20 + n * per + row : 21 + n * per + row, at_lane : at_lane + long]
            bias[n] = jnp.where(chosen, there, bias[n])
    type_ref[...] = mine[:2]
    gain_ref[...] = mine[2 : 2 + 2 * NL + 1]
    shift_ref[...] = mine[2 + 2 * NL + 1 :]
    for n in range(NL):
        bias_ref[n : n + 1] = bias[n]


def finish(coords, many, early, few, width, ff, owners):
    s = jax.ShapeDtypeStruct
    rows = width // owners
    return run(
        finish_kernel,
        (),
        out_shape=(
            s((NL, rows, 3 * width), F32), s((NL, rows, width), F32), s((NL, rows, ff), F32), s((NL, ff // owners, width), F32),
            s((64, width), F32), s((2, rows), F32), s((2 * NL + 1, rows), F32), s((6 * NL + 1, rows), F32), s((NL, ff // owners), F32),
        ),
        in_specs=[SM] + [VM] * 12,
        operands=(coords, *many, *early, *few),
        out_specs=(VM,) * 9,
        scratch_shapes=[pltpu.VMEM((28, width), F32)],
        cost_estimate=CHEAP,
        vmem=24,
        name="finish",
    )


def table_finish_kernel(coords_ref, own_ref, other_ref, out_ref, mark_ref):
    mark_ref[...] = jnp.zeros_like(mark_ref)
    half = own_ref.shape[1]
    first = coords_ref[0] == 0
    out_ref[:, :half] = jnp.where(first, own_ref[...], other_ref[...]).astype(F32)
    out_ref[:, half:] = jnp.where(first, other_ref[...], own_ref[...]).astype(F32)


def table_finish(coords, own, other, after=()):
    return run(
        table_finish_kernel,
        after,
        out_shape=(jax.ShapeDtypeStruct((own.shape[0], 2 * own.shape[1]), F32), jax.ShapeDtypeStruct((8, 128), F32)),
        in_specs=[SM, VM, VM],
        operands=(coords, own, other),
        out_specs=(VM, VM),
        cost_estimate=CHEAP,
        vmem=16,
        name="table_finish",
    )


AXES = ("dp", "vocab")
VOCAB_MASK = {"x": 1, "a": 2, "b": 4}


def add(left_op, right_op):
    return (left_op.astype(F32) + right_op.astype(F32)).astype(LOW)


class Cube:
    def __init__(self, dp_size, vocab_size):
        self.dp_size = dp_size
        self.vocab_size = vocab_size
        self.dp_bits = dp_size.bit_length() - 1
        self.vocab_bits = vocab_size.bit_length() - 1
        assert 1 << self.dp_bits == dp_size and 1 << self.vocab_bits == vocab_size
        self.small = self.dp_bits == 2 and self.vocab_bits == 3

    def permute(self, value, dp_mask, vocab_mask):
        count = self.vocab_size
        pairs = [
            (d * count + v, (d ^ dp_mask) * count + (v ^ vocab_mask))
            for d in range(self.dp_size)
            for v in range(count)
        ]
        return lax.ppermute(value, AXES, pairs)

    def core(self, value):
        return self.permute(value, 1, 0)

    def along(self, value, dims):
        return self.permute(
            value, 2 * ("y" in dims) + ("core" in dims), sum(VOCAB_MASK[dim] for dim in dims if dim in VOCAB_MASK)
        )

    def core_is_first(self):
        return (lax.axis_index("dp") & 1) == 0

    def coords(self):
        dp, vocab = lax.axis_index("dp"), lax.axis_index("vocab")
        return jnp.stack([dp & 1, vocab & 1, (vocab >> 1) & 1, (vocab >> 2) & 1, (dp >> 1) & 1, vocab])

    def halves(self, matrix):
        mine = lax.axis_index("dp") & 1
        width = matrix.shape[1] // 2
        keep = lax.dynamic_slice_in_dim(matrix, mine * width, width, 1)
        send = lax.dynamic_slice_in_dim(matrix, (1 - mine) * width, width, 1)
        return keep, send

    def ordered(self, first, mine, other, axis):
        return jnp.concatenate(
            [jnp.where(first, mine, other), jnp.where(first, other, mine)], axis=axis
        )

    def join_core(self, share, axis):
        return self.ordered(self.core_is_first(), share, self.core(share), axis).astype(F32)

    def reduce(self, matrix):
        for bit in reversed(range(self.vocab_bits)):
            mine = (lax.axis_index("vocab") >> bit) & 1
            rows = matrix.shape[0] // 2
            keep = lax.dynamic_slice_in_dim(matrix, mine * rows, rows, 0)
            send = lax.dynamic_slice_in_dim(matrix, (1 - mine) * rows, rows, 0)
            matrix = add(keep, self.permute(send, 0, 1 << bit))
        for bit in range(1, self.dp_bits):
            matrix = add(matrix, self.permute(matrix, 1 << bit, 0))
        return matrix


def on_device(
    cube,
    token_ids,
    lengths,
    type_ids,
    word_table,
    pos_table,
    type_table,
    gains,
    shifts,
    w_qkv,
    w_out,
    b_ff1,
    w_ff1,
    w_ff2,
    cotangent,
):
    owners = cube.vocab_size
    local_rows, width = word_table.shape
    assert token_ids.shape[0] == 1
    tokens = token_ids.shape[1]
    slot_count = 2 * tokens // owners
    slots = owners * slot_count
    coords = cube.coords()

    all_ids = lax.all_to_all(
        jnp.broadcast_to(token_ids, (owners, tokens)), "vocab", split_axis=0, concat_axis=0, tiled=True
    )
    local = all_ids - lax.axis_index("vocab") * local_rows
    here = (local >= 0) & (local < local_rows)
    rank = jnp.cumsum(here.astype(jnp.int32), axis=1) - 1
    slot_hit = (
        jnp.where(here, rank, -1)[:, None, :] == jnp.arange(slot_count, dtype=jnp.int32)[None, :, None]
    )
    asked = jnp.sum(jnp.where(slot_hit, local[:, None, :] + 1, 0), axis=2).reshape(slots) - 1
    row_hit = (asked[:, None] == jnp.arange(local_rows, dtype=jnp.int32)[None, :]).astype(LOW)
    replies = exchange_rows(dot(row_hit, word_table).astype(LOW), owners)
    number = jnp.arange(owners, dtype=jnp.int32)[:, None]
    chosen = (token_ids >= number * local_rows) & (token_ids < (number + 1) * local_rows)
    own_rank = jnp.cumsum(chosen.astype(jnp.int32), axis=1) - 1
    slot_row = jnp.sum(jnp.where(chosen, number * slot_count + own_rank, 0), axis=0, keepdims=True)
    asked = both_cores(asked[:, None], cube.core(asked[:, None]), owners).reshape(1, -1)
    (n0, s0, hidden), top, layers = forward(
        coords, lengths, replies, slot_row, type_ids, pos_table, type_table, gains, shifts, b_ff1.astype(F32),
        cotangent.reshape(tokens, width), w_qkv, w_out, w_ff1, w_ff2,
    )
    norms, saved = [(n0, s0)], []
    for xlow, mixed, lse, ctxt, n1, s1, mlow, gp, act, *end in layers:
        saved.append((mixed, lse, n1, s1, gp) + tuple((own, cube.core(own)) for own in (xlow, ctxt, mlow, act)))
        norms.append(tuple(end))
    hidden_out = hidden.reshape(1, tokens, width)

    gradients = gradients_small if cube.small else gradients_any
    outs = gradients(
        cube, coords, lengths, top, saved, gains, w_qkv, w_out, w_ff1, w_ff2,
        norms, (type_ids, slot_row, asked, local_rows),
    )
    return (hidden_out,) + outs


def exchange_rows(outgoing, owners):
    shape = outgoing.shape
    return lax.all_to_all(
        outgoing.reshape(owners, -1, shape[1]), "vocab", split_axis=0, concat_axis=0, tiled=True
    ).reshape(shape)


def both_cores(own, other, owners):
    fold = lambda array: array.reshape(owners, 1, -1, array.shape[1])
    return jnp.concatenate([fold(own), fold(other)], axis=1).reshape(-1, own.shape[1])


def unpack(pack):
    cores, blocks, _, half = pack.shape
    pos = pack[:, :, :32].transpose(1, 2, 0, 3).reshape(blocks * 32, 2 * half)
    small = pack[:, :2, 32:46].reshape(cores, 2, 2, 7, half).transpose(0, 1, 3, 2, 4)
    return pos, small.reshape(28, 2 * half)


def small_outs(cube, rows):
    place_of = lax.axis_index("vocab")

    def mine(array):
        size = array.shape[1] // cube.vocab_size
        return lax.dynamic_slice_in_dim(array, place_of * size, size, 1)

    few = mine(rows[:20])
    return few[:2], few[2 : 2 + 2 * NL + 1], few[2 + 2 * NL + 1 :], mine(rows[20:].reshape(NL, -1))


def gradients_any(cube, coords, lengths, top, saved, gains, w_qkv, w_out, w_ff1, w_ff2, norms, embed):
    owners = cube.vocab_size
    width = w_out.shape[1]
    tokens = top[0].shape[0]
    blocks = 8
    half = width // 2
    kinds, slot_row, asked, local_rows = embed
    mixed1, lse1, n1_1, s1_1, gp1, x1, ctx1, mid1, act1 = saved[1]
    mixed0, lse0, n1_0, s1_0, gp0, x0, ctx0, mid0, act0 = saved[0]
    e, low, sec_keep, sec_send, top1 = top
    pre_keep, pre_send, bias1, first, _, fst_keep, fst_send, gctx, sums1 = feed(
        1, coords, e, low, n1_1, s1_1, gains, gp1, w_out, w_ff1, w_ff2
    )
    pair = lambda keep, send: (keep, cube.core(send))
    two1, one1 = weights(blocks, (None, None), coords, pair(sec_keep, sec_send), act1, mid1, pair(pre_keep, pre_send))
    fst1 = pair(fst_keep, fst_send)
    (
        mix_keep, mix_send, pre_keep, pre_send, att1, sec_keep, sec_send, top0, bias0, first, fst_keep, fst_send, gctx, sums0
    ) = between(
        1, coords, lengths, mixed1, lse1, gctx, first, *norms[1], n1_0, s1_0, gains, gp0, w_qkv, w_out, w_ff1, w_ff2
    )
    two0, one0, mix1 = weights(
        blocks, (None, None, None), coords, pair(sec_keep, sec_send), act0, mid0, pair(pre_keep, pre_send),
        (x1, pair(mix_keep, mix_send), ctx1, fst1, ctx0, pair(fst_keep, fst_send)),
    )
    out_keep, out_send, first_core, second_core = last(
        None, coords, lengths, mixed0, lse0, gctx, first, *norms[0], gains, x0[0], slot_row, kinds,
        (top0, top1, sums0, sums1, att1, bias0, bias1), w_qkv, asked.shape[1] // 2, 2 * blocks,
    )
    mine = cube.core_is_first()

    def over_cores(first, second):
        return add(jnp.where(mine, first, second), cube.core(jnp.where(mine, second, first)))

    outgoing = both_cores(out_keep, cube.core(out_send), owners)
    table_part = table_back(asked, exchange_rows(outgoing, owners), local_rows)
    for bit in range(1, cube.dp_bits):
        table_part = add(table_part, cube.permute(table_part, 1 << bit, 0))
    wide = 3 * half
    sums_last = over_cores(first_core, second_core)
    packs = sums_last[..., wide:]
    other = cube.core(packs)
    pos, small = unpack(jnp.stack([jnp.where(mine, packs, other), jnp.where(mine, other, packs)]))
    pos_out = cube.reduce(pos).astype(F32)
    for bit in range(cube.vocab_bits):
        small = add(small, cube.permute(small, 0, 1 << bit))
    for bit in range(1, cube.dp_bits):
        small = add(small, cube.permute(small, 1 << bit, 0))
    types, gains_out, shifts_out, biases = small_outs(cube, small.astype(F32))
    whole = lambda parts: jnp.concatenate(parts, axis=0)
    part = width // blocks // 2
    one = lambda parts: cube.reduce(whole(parts)[:, :part].reshape(width, -1))
    two = lambda parts: cube.reduce(
        whole(parts).reshape(blocks, 2, width // 16, 4, -1).transpose(0, 4, 1, 3, 2).reshape(-1, half)
    )
    out0 = whole(one0)[:, part:].reshape(2 * blocks, 16, 4, half)[:, :, : part // 16].transpose(0, 2, 1, 3)
    mixes = jnp.stack(
        [
            cube.reduce(jnp.concatenate([sums_last[..., :wide].reshape(width, -1), out0.reshape(width, -1)], axis=1)),
            one(mix1),
        ]
    )
    return (
        cube.join_core(table_part, -1), pos_out, types, gains_out, shifts_out,
        cube.join_core(mixes[..., :wide], 2), cube.join_core(mixes[..., wide:], 2), biases,
        cube.join_core(jnp.stack([one(one0), one(one1)]), 2), cube.join_core(jnp.stack([two(two0), two(two1)]), 2),
    )


class Bucket:
    def __init__(self, cube, plan, parts):
        self.cube, self.plan, self.parts = cube, tuple(plan), tuple(parts)

    def start(self):
        turn = self.plan[0]
        if self.plan == (("y",),):
            self.got = (self.parts[0], self.cube.along(self.parts[0], turn))
            return
        self.got = self.parts[:1]
        for n in range(1, len(self.parts)):
            there = [dim for i, dim in enumerate(turn) if (n >> (len(turn) - 1 - i)) & 1]
            self.got += (self.cube.along(self.parts[n], there),)


    def keep(self):
        self.got, self.plan = self.parts, (None,)


def joined(buckets, parts_axis):
    return (tuple(buckets), parts_axis)


def step(groups, after=(), cost=CHEAP):
    groups = [group if isinstance(group, tuple) else ((group,), 0) for group in groups]
    items = []
    for buckets, axis in groups:
        rest = buckets[0].plan[1:]
        assert all(bucket.plan[1:] == rest for bucket in buckets)
        parts = 1 if rest in ((), (("y",),)) else 2 ** len(rest[0])
        items.append((tuple(bucket.got for bucket in buckets), parts, axis))
    for (buckets, _), parts in zip(groups, combine(items, after, cost)):
        buckets[0].plan, buckets[0].parts = buckets[0].plan[1:], tuple(parts)
    return groups[0][0][0].parts[0]


def gradients_small(cube, coords, lengths, top, saved, gains, w_qkv, w_out, w_ff1, w_ff2, norms, embed):
    owners = cube.vocab_size
    width = w_out.shape[1]
    tokens = top[0].shape[0]
    blocks = owners
    half = width // 2
    single = lambda dims: tuple((dim,) for dim in dims)
    plan_two1, plan_one1 = (("x", "y"), ("a",), ("b",)), (("a",), ("x", "y"), ("b",))
    plan_mix1 = single("ayxb")
    plan_two0, plan_one0, plan_mix0 = single("xayb"), single("yxab"), (("core",), ("y",), ("x", "a"), ("b",))
    kinds, slot_row, asked, local_rows = embed
    mixed1, lse1, n1_1, s1_1, gp1, x1, ctx1, mid1, act1 = saved[1]
    mixed0, lse0, n1_0, s1_0, gp0, x0, ctx0, mid0, act0 = saved[0]
    pair = lambda keep, send: (keep, cube.core(send))
    e, low, sec_keep, sec_send, top1 = top
    pre_keep, pre_send, bias1, first, _, fst_keep, fst_send, gctx, sums1 = feed(
        1, coords, e, low, n1_1, s1_1, gains, gp1, w_out, w_ff1, w_ff2
    )
    fst1 = pair(fst_keep, fst_send)
    got = weights(
        blocks, (plan_two1, plan_one1), coords, pair(sec_keep, sec_send), act1, mid1, pair(pre_keep, pre_send)
    )
    two1, one1 = Bucket(cube, plan_two1, got[0]), Bucket(cube, plan_one1, got[1])
    two1.start()
    one1.start()
    (
        mix_keep, mix_send, pre_keep, pre_send, att1, sec_keep, sec_send, top0, bias0, first, fst_keep, fst_send, gctx, sums0
    ) = between(
        1, coords, lengths, mixed1, lse1, gctx, first, *norms[1], n1_0, s1_0, gains, gp0, w_qkv, w_out, w_ff1, w_ff2,
        after=got[0][:1] + (act0[1], mid0[1], ctx0[1], x1[1], ctx1[1]),
    )
    mark = step([two1, one1], after=(gctx,), cost=LONG)
    two1.start()
    one1.start()
    got = weights(
        blocks, (plan_two0, plan_one0, plan_mix1), coords, pair(sec_keep, sec_send), act0, mid0, pair(pre_keep, pre_send),
        (x1, pair(mix_keep, mix_send), ctx1, fst1, ctx0, pair(fst_keep, fst_send)), after=(mark,),
    )
    two0, one0, mix1 = [Bucket(cube, plan, parts) for plan, parts in zip((plan_two0, plan_one0, plan_mix1), got)]
    for bucket in (mix1, two0, one0):
        bucket.start()
    mark = step([joined((two1, one1), 1)], after=got[0][:1], cost=LONG)
    two1.start()
    out_keep, out_send, *got = last(
        plan_mix0, coords, lengths, mixed0, lse0, gctx, first, *norms[0], gains, x0[0], slot_row, kinds,
        (top0, top1, sums0, sums1, att1, bias0, bias1), w_qkv, asked.shape[1] // 2, 2 * owners, after=(mark,),
    )
    incoming = exchange_rows(both_cores(out_keep, cube.core(out_send), owners), owners)
    mix0 = Bucket(cube, plan_mix0, got)
    mix0.start()
    mark = step([two1, mix1, two0, one0], after=got[:1], cost=LONG)
    for bucket in (mix1, two0, one0):
        bucket.start()
    mark = step([mix0], after=(mark,))
    mix0.start()
    mark = step([mix1, two0, one0], after=(mark,), cost=LONG)
    for bucket in (mix1, two0, one0):
        bucket.start()
    folded = (local_rows // 48, 48, half)
    got = table_back(asked, incoming, local_rows, after=(mark,))
    table = Bucket(cube, single("y"), (got.reshape(folded),))
    table.start()
    mark = step([mix0, joined((mix1, two0, one0), 1)], after=(got,), cost=LONG)
    mix0.start()
    mix1.start()
    two1.keep()
    mark = step([table, two1], after=(mark,))
    early = Bucket(cube, (), (cube.along(two1.parts[0], ("y",)),))
    early.keep()
    mark = step([mix0, mix1, early], after=(mark,), cost=LONG)
    mix0.start()
    later = Bucket(cube, (), (cube.along(mix1.parts[0], ("y",)),))
    later.keep()
    table_own = table.parts[0].reshape(local_rows, half)
    table_out, mark = table_finish(coords, table_own, cube.core(table_own), after=(mark,))
    others = [Bucket(cube, (), (cube.core(bucket.parts[0]),)) for bucket in (two1, early)]
    for other in others:
        other.keep()
    mark = step([mix0] + others, after=(mark,))
    last_y = Bucket(cube, (), (cube.along(mix0.parts[0], ("y",)),))
    last_y.keep()
    step([last_y], after=(mark,))
    step([later], after=(last_y.parts[0],))
    four = lambda own, over_y: (own, over_y, cube.core(own), cube.core(over_y))
    qkv_out, wout_out, one_out, two_out, pos_out, types, gains, shifts, biases = finish(
        coords, four(mix1.parts[0], later.parts[0]),
        (two1.parts[0], early.parts[0], others[0].parts[0], others[1].parts[0]),
        four(mix0.parts[0], last_y.parts[0]), width, w_ff1.shape[2], owners,
    )
    return (
        table_out, pos_out, types, gains, shifts, qkv_out, wout_out,
        biases, one_out, two_out,
    )


def solution(mesh):
    cube = Cube(mesh.shape["dp"], mesh.shape["vocab"])
    both = ("dp", "vocab")
    in_specs = (
        P(both, None),
        P(both),
        P(both, None),
        P("vocab", None),
        P(),
        P(),
        P(),
        P(),
        P(),
        P(),
        P(),
        P(),
        P(),
        P(both, None, None),
    )
    out_specs = (
        P(both, None, None),
        P("vocab", None),
        P("vocab", None),
        P(None, "vocab"),
        P(None, "vocab"),
        P(None, "vocab"),
        P(None, "vocab", None),
        P(None, "vocab", None),
        P(None, "vocab"),
        P(None, "vocab", None),
        P(None, "vocab", None),
    )
    return jax.shard_map(
        functools.partial(on_device, cube), mesh=mesh, in_specs=in_specs, out_specs=out_specs, check_vma=False
    )
```

```python
import functools
import jax
import jax.numpy as jnp
from jax import lax
from jax.experimental import pallas as pl
from jax.experimental.pallas import tpu as pltpu
from jax.sharding import PartitionSpec as P

HEADS = 12
HEAD_DIM = 64
NL = 2
norm_eps = 1e-12
SCALE = HEAD_DIM ** (-0.5)
ANY = pl.BlockSpec(memory_space=pl.ANY)
HBM = pl.BlockSpec(memory_space=pltpu.HBM)
VM = pl.BlockSpec(memory_space=pltpu.VMEM)
SM = pl.BlockSpec(memory_space=pltpu.SMEM)
F32, LOW = jnp.float32, jnp.bfloat16

CHEAP = pl.CostEstimate(flops=1, bytes_accessed=1, transcendentals=0)
DEAR = pl.CostEstimate(flops=10**10, bytes_accessed=1, transcendentals=0)
LONG = pl.CostEstimate(flops=10**11, bytes_accessed=1, transcendentals=0)


def run(kernel, after, out_shape, in_specs, operands, vmem, **options):
    count = len(operands)

    def body(*refs):
        kernel(*refs[:count], *refs[count + len(after) :])

    return pl.pallas_call(
        body,
        out_shape=out_shape,
        in_specs=list(in_specs) + [ANY] * len(after),
        compiler_params=pltpu.CompilerParams(vmem_limit_bytes=vmem * 1024 * 1024),
        **options,
    )(*operands, *after)


def normalize(inputs):
    centered = inputs - jnp.mean(inputs, axis=-1, keepdims=True)
    spread = lax.rsqrt(jnp.mean(centered * centered, axis=-1, keepdims=True) + norm_eps)
    return (centered * spread, spread)


def norm_back(grad_out, normed, spread, gain_row):
    scaled = grad_out * gain_row
    return spread * (
        scaled
        - jnp.mean(scaled, axis=-1, keepdims=True)
        - normed * jnp.mean(scaled * normed, axis=-1, keepdims=True)
    )


def dot(left_op, right_op, dims=((1,), (0,))):
    return lax.dot_general(left_op, right_op, (dims, ((), ())), preferred_element_type=F32)


ROWS = ((0,), (0,))
COLS = ((1,), (1,))


def gelu_pair(inputs):
    size = jnp.abs(inputs)
    bell = jnp.exp2(inputs * inputs * (-0.5 * 1.4426950408889634))
    t = 1.0 / (1.0 + size * (0.3275911 * 0.7071067811865476))
    tail = t * (
        0.5 * 0.254829592
        + t * (0.5 * -0.284496736 + t * (0.5 * 1.421413741 + t * (0.5 * -1.453152027 + t * (0.5 * 1.061405429))))
    )
    tail = tail * bell
    phi = jnp.where(inputs >= 0.0, 1.0 - tail, tail)
    return inputs * phi, phi + inputs * bell * 0.3989422804014327


def as_column(row):
    return jnp.broadcast_to(row, (128, row.shape[1])).T[:, :1]


def forward_kernel(
    coords_ref, length_ref, replies_ref, slot_ref, kind_ref, pos_ref, type_ref, gains_ref, shifts_ref, ffn_bias_ref,
    grad_ref, wqkv_hbm, wout_hbm, w1_hbm, w2_hbm,
    *refs,
):
    n0_ref, s0_ref, hidden_ref = refs[:3]
    top = refs[3:8]
    outs = [refs[8 + 11 * layer : 19 + 11 * layer] for layer in range(NL)]
    wqkv, wout, w1, w2, sems, xlow, mixed, ctxt, mlow, gp, act, n0, n1, n2, x, osems = refs[6 + 11 * NL :]
    tokens, width = x.shape
    ff = w1.shape[2]
    loads = []
    for layer in range(NL):
        for i, (src, dst) in enumerate([(wqkv_hbm, wqkv), (wout_hbm, wout), (w1_hbm, w1), (w2_hbm, w2)]):
            loads.append(pltpu.make_async_copy(src.at[layer], dst.at[layer], sems.at[4 * layer + i]))
    for load in loads:
        load.start()
    pending, used = {}, [0]

    def emit(name, src, dst, at=None):
        if at is not None:
            src, dst = src.at[:, at], dst.at[:, at]
        copy = pltpu.make_async_copy(src, dst, osems.at[used[0]])
        used[0] += 1
        copy.start()
        pending.setdefault(name, []).append(copy)

    def reuse(name):
        for copy in pending.pop(name, ()):
            copy.wait()

    gains = gains_ref[...].astype(F32)
    shifts = shifts_ref[...].astype(F32)
    number = lax.broadcasted_iota(jnp.int32, (tokens, replies_ref.shape[0]), 1)
    hit = jnp.where(number == as_column(slot_ref[...].astype(F32)).astype(jnp.int32), 1.0, 0.0).astype(LOW)
    types = type_ref[...].astype(F32)
    embedded = dot(hit, replies_ref[...]) + pos_ref[...].astype(F32)
    embedded = embedded + jnp.where(as_column(kind_ref[...].astype(F32)) > 0.5, types[1:2], types[0:1])
    normed, spread = normalize(embedded)
    n0[...] = normed
    emit("n0", n0, n0_ref)
    s0_ref[...] = jnp.broadcast_to(spread, s0_ref.shape)
    x[...] = normed * gains[0:1] + shifts[0:1]

    key_slot = lax.broadcasted_iota(jnp.int32, (tokens, 128), 0)
    visible = jnp.where(key_slot < length_ref[0], 0.0, -1e30)[:, :1]
    lane = lax.broadcasted_iota(jnp.int32, (tokens, 128), 1)
    chunk = 512

    for layer in range(NL):
        base = 1 + 6 * layer
        xlow_ref, mixed_ref, lse_ref, ctxt_ref, n1_ref, s1_ref, mlow_ref, gp_ref, act_ref = outs[layer][:9]

        reuse("xlow")
        xlow[...] = x[...].astype(LOW)
        emit("xlow", xlow, xlow_ref)
        loads[4 * layer].wait()
        reuse("mixed")
        for i in range(3):
            cols = slice(i * width, (i + 1) * width)
            got = dot(xlow[...], wqkv[layer, :, cols])
            if i != 1:
                row = base + (0 if i == 0 else 1)
                got = got + shifts[row : row + 1]
            mixed[:, cols] = got.astype(LOW)
        emit("mixed", mixed, mixed_ref)
        reuse("ctxt")

        def pair_step(j, carry):
            at = pl.multiple_of(j * 128, 128)
            q = mixed[:, pl.ds(at, 128)] * jnp.asarray(SCALE, LOW)
            k = mixed[:, pl.ds(pl.multiple_of(width + at, 128), 128)]
            v = mixed[:, pl.ds(pl.multiple_of(2 * width + at, 128), 128)]
            vt = v.T
            scores = []
            for h in range(2):
                kh = jnp.where((lane < 64) == (h == 0), k, jnp.zeros_like(k))
                scores.append(dot(kh, q, COLS) + visible)
            for h in range(2):
                top = jnp.max(scores[h], axis=0, keepdims=True)
                weights = jnp.exp(scores[h] - top)
                total = jnp.sum(weights, axis=0, keepdims=True)
                out = dot(vt[h * 64 : (h + 1) * 64], weights.astype(LOW)) * (1.0 / total)
                ctxt[pl.ds(pl.multiple_of(at + h * 64, 64), 64), :] = out.astype(LOW)
                lse_ref[pl.ds(2 * j + h, 1), :] = top + jnp.log(total)
            return carry

        lax.fori_loop(0, HEADS // 2, pair_step, 0, unroll=2)
        emit("ctxt", ctxt, ctxt_ref)
        loads[4 * layer + 1].wait()
        attended = dot(ctxt[...], wout[layer], ROWS) + shifts[base + 2 : base + 3]
        normed, spread = normalize(x[...] + attended)
        reuse("n1")
        n1[...] = normed
        emit("n1", n1, n1_ref)
        s1_ref[...] = jnp.broadcast_to(spread, s1_ref.shape)
        x[...] = normed * gains[1 + 2 * layer : 2 + 2 * layer] + shifts[base + 3 : base + 4]
        reuse("mlow")
        mlow[...] = x[...].astype(LOW)
        emit("mlow", mlow, mlow_ref)
        loads[4 * layer + 2].wait()
        reuse("gp")
        reuse("act")
        for i in range(ff // chunk):
            cols = slice(i * chunk, (i + 1) * chunk)
            pre = dot(mlow[...], w1[layer, :, cols]) + ffn_bias_ref[layer : layer + 1, cols]
            active, slope = gelu_pair(pre)
            gp[:, cols] = slope.astype(LOW)
            act[:, cols] = active.astype(LOW)
            emit("gp", gp, gp_ref, pl.ds(i * chunk, chunk))
            emit("act", act, act_ref, pl.ds(i * chunk, chunk))
        loads[4 * layer + 3].wait()
        normed, spread = normalize(x[...] + shifts[base + 4 : base + 5] + dot(act[...], w2[layer]))
        if layer < NL - 1:
            n2_ref, s2_ref = outs[layer][9:11]
            n2[...] = normed
            emit("n2", n2, n2_ref)
            s2_ref[...] = jnp.broadcast_to(spread, s2_ref.shape)
        else:
            gain = gains[2 * NL : 2 * NL + 1]
            norm_end(coords_ref[0], grad_ref[...].astype(F32), normed, spread, gain, *top)
        x[...] = normed * gains[2 + 2 * layer : 3 + 2 * layer] + shifts[base + 5 : base + 6]
    hidden_ref[...] = x[...].astype(LOW)
    for name in list(pending):
        reuse(name)


def forward(
    coords, length, replies, slot_of, kinds, pos, types, gains, shifts, ffn_bias, cotangent, w_qkv, w_out, w_ff1, w_ff2
):
    tokens, width = pos.shape
    ff = w_ff1.shape[2]
    s = jax.ShapeDtypeStruct
    v = pltpu.VMEM
    spread = s((tokens, 128), F32)
    wide = s((tokens, width), F32)
    low = s((tokens, width), LOW)
    layer_out = (
        low, s((tokens, 3 * width), LOW), s((HEADS, tokens), F32), s((width, tokens), LOW),
        wide, spread, low, s((tokens, ff), LOW), s((tokens, ff), LOW), wide, spread,
    )
    layer_spec = (ANY, ANY, VM, ANY, ANY, VM, ANY, ANY, ANY, ANY, VM)
    chunks = ff // 512
    end = norm_end_shapes(tokens, width)
    outs = run(
        forward_kernel,
        (),
        out_shape=(wide, spread, low) + end + layer_out * (NL - 1) + layer_out[:9],
        in_specs=[SM, SM] + [VM] * 9 + [HBM] * 4,
        operands=(
            coords, length, replies, slot_of, kinds, pos, types, gains, shifts, ffn_bias, cotangent, w_qkv, w_out, w_ff1, w_ff2
        ),
        out_specs=(ANY, VM, VM) + (VM,) * 5 + layer_spec * (NL - 1) + layer_spec[:9],
        scratch_shapes=[
            v((NL, width, 3 * width), LOW), v((NL, width, width), LOW), v((NL, width, ff), LOW), v((NL, ff, width), LOW),
            pltpu.SemaphoreType.DMA((4 * NL,)),
            v((tokens, width), LOW), v((tokens, 3 * width), LOW), v((width, tokens), LOW), v((tokens, width), LOW),
            v((tokens, ff), LOW), v((tokens, ff), LOW), v((tokens, width), F32), v((tokens, width), F32),
            v((tokens, width), F32), v((tokens, width), F32), pltpu.SemaphoreType.DMA((1 + NL * (6 + 2 * chunks),)),
        ],
        cost_estimate=CHEAP,
        vmem=57,
        name="forward",
    )
    return outs[:3], outs[3:8], [outs[8 + 11 * layer : 19 + 11 * layer] for layer in range(NL)]


def part(mine, source, keep_to, send_to):
    half = source.shape[1] // 2

    @pl.when(mine == 0)
    def _():
        keep_to[...] = source[:, :half]
        send_to[...] = source[:, half:]

    @pl.when(mine == 1)
    def _():
        keep_to[...] = source[:, half:]
        send_to[...] = source[:, :half]


def norm_end(mine, grad, n, s, gain, back_ref, low_ref, keep_ref, send_ref, sums_ref):
    sums_ref[0:1] = jnp.sum(grad * n, axis=0, keepdims=True)
    sums_ref[1:2] = jnp.sum(grad, axis=0, keepdims=True)
    back = norm_back(grad, n, s, gain)
    sums_ref[2:3] = jnp.sum(back, axis=0, keepdims=True)
    back_ref[...] = back
    low_ref[...] = back.astype(LOW)
    if keep_ref is not None:
        part(mine, low_ref, keep_ref, send_ref)


def norm_end_shapes(tokens, width):
    s = jax.ShapeDtypeStruct
    half = s((tokens, width // 2), LOW)
    return (s((tokens, width), F32), s((tokens, width), LOW), half, half, s((3, width), F32))


def feed_back_body(mine, second, gp, w2, ready, bias_ref, keep, send):
    chunk = 512
    steps = gp.shape[1] // chunk
    for i in range(steps):
        ready(i)
        cols = slice(i * chunk, (i + 1) * chunk)
        grad_pre = dot(second[...], w2[cols, :], COLS) * gp[:, cols].astype(F32)
        bias_ref[:, cols] = jnp.sum(grad_pre, axis=0, keepdims=True)
        side, at = divmod(i, steps // 2)
        there = slice(at * chunk, (at + 1) * chunk)
        low = grad_pre.astype(LOW)

        @pl.when(mine == side)
        def _():
            keep[:, there] = low

        @pl.when(mine != side)
        def _():
            send[:, there] = low


def both_halves(mine, keep, send, weight):
    half = keep.shape[1]
    first = jnp.where(mine == 0, keep[...], send[...])
    second = jnp.where(mine == 0, send[...], keep[...])
    return dot(first, weight[:, :half], COLS) + dot(second, weight[:, half:], COLS)


def attend_back_body(length_ref, mixed_ref, lse_ref, gctx_ref, att_ref, dmix):
    tokens, width = gctx_ref.shape
    key_slot = lax.broadcasted_iota(jnp.int32, (tokens, 128), 0)
    visible = jnp.where(key_slot < length_ref[0], 0.0, -1e30)[:, :1]
    lane = lax.broadcasted_iota(jnp.int32, (tokens, 128), 1)

    def pair_step(j, carry):
        at = pl.multiple_of(j * 128, 128)
        qcols = pl.ds(at, 128)
        kcols = pl.ds(pl.multiple_of(width + at, 128), 128)
        vcols = pl.ds(pl.multiple_of(2 * width + at, 128), 128)
        q = mixed_ref[:, qcols] * jnp.asarray(SCALE, LOW)
        k = mixed_ref[:, kcols]
        v = mixed_ref[:, vcols]
        g = gctx_ref[:, qcols]
        kt = k.T
        grad_v, grad_k, grad_qt = [], [], []
        scores, grad_probs = [], []
        for h in range(2):
            mask = (lane < 64) == (h == 0)
            kh = jnp.where(mask, k, jnp.zeros_like(k))
            vh = jnp.where(mask, v, jnp.zeros_like(v))
            scores.append(dot(kh, q, COLS))
            grad_probs.append(dot(vh, g, COLS))
        for h in range(2):
            probs = jnp.exp(scores[h] + visible - lse_ref[pl.ds(2 * j + h, 1), :])
            weighted = jnp.sum(probs * grad_probs[h], axis=0, keepdims=True)
            grad_scores = (probs * (grad_probs[h] - weighted)).astype(LOW)
            grad_v.append(dot(probs.astype(LOW), g))
            grad_k.append(dot(grad_scores, q))
            grad_qt.append(dot(kt[h * 64 : (h + 1) * 64], grad_scores))
        grad_q = jnp.concatenate(grad_qt, axis=0).T * SCALE
        grad_v = jnp.where(lane < 64, grad_v[0], grad_v[1])
        grad_k = jnp.where(lane < 64, grad_k[0], grad_k[1])
        att_ref[0:1, qcols] = jnp.sum(grad_q, axis=0, keepdims=True)
        att_ref[1:2, qcols] = jnp.sum(grad_v, axis=0, keepdims=True)
        dmix[:, qcols] = grad_q.astype(LOW)
        dmix[:, kcols] = grad_k.astype(LOW)
        dmix[:, vcols] = grad_v.astype(LOW)
        return carry

    lax.fori_loop(0, HEADS // 2, pair_step, 0, unroll=2)


def chunk_loads(sems, at, pairs, chunk=512):
    loads = []
    (w2_src, w2), (gp_src, gp) = pairs
    for i in range(gp.shape[1] // chunk):
        there = pl.ds(i * chunk, chunk)
        loads.append(
            (
                pltpu.make_async_copy(w2_src.at[there], w2.at[there], sems.at[at + 2 * i]),
                pltpu.make_async_copy(gp_src.at[:, there], gp.at[:, there], sems.at[at + 2 * i + 1]),
            )
        )
    return loads


def feed_kernel(
    layer, coords_ref, e_ref, second, n1_ref, s1_ref, gains_ref, gp_hbm, wout_hbm, w1_hbm, w2_hbm,
    keep_ref, send_ref, bias_ref, first_ref, low_ref, fst_keep_ref, fst_send_ref, gctx_ref, sums_ref,
    gp, wout, w1, w2, keep, send, sems,
):
    mine = coords_ref[0]
    loads = chunk_loads(sems, 4, ((w2_hbm.at[layer], w2), (gp_hbm, gp)))
    for pair in loads:
        for load in pair:
            load.start()
    late = [
        pltpu.make_async_copy(w1_hbm.at[layer], w1, sems.at[0]),
        pltpu.make_async_copy(wout_hbm.at[layer], wout, sems.at[1]),
    ]
    for load in late:
        load.start()

    def ready(i):
        for load in loads[i]:
            load.wait()

    feed_back_body(mine, second, gp, w2, ready, bias_ref, keep, send)
    stores = [
        pltpu.make_async_copy(send, send_ref, sems.at[2]),
        pltpu.make_async_copy(keep, keep_ref, sems.at[3]),
    ]
    for store in stores:
        store.start()
    late[0].wait()
    grad = e_ref[...] + both_halves(mine, keep, send, w1)
    gain = gains_ref[...].astype(F32)[1 + 2 * layer : 2 + 2 * layer]
    norm_end(mine, grad, n1_ref[...], s1_ref[:, :1], gain, first_ref, low_ref, fst_keep_ref, fst_send_ref, sums_ref)
    late[1].wait()
    gctx_ref[...] = dot(low_ref[...], wout[...], COLS).astype(LOW)
    for store in stores:
        store.wait()


def feed(layer, coords, e, second, n1, s1, gains, gp, w_out, w_ff1, w_ff2, after=()):
    tokens, width = n1.shape
    ff = gp.shape[1]
    s = jax.ShapeDtypeStruct
    v = pltpu.VMEM
    half = s((tokens, ff // 2), LOW)
    end = norm_end_shapes(tokens, width)
    return run(
        functools.partial(feed_kernel, layer),
        after,
        out_shape=(half, half, s((1, ff), F32)) + end[:4] + (s((tokens, width), LOW), end[4]),
        in_specs=[SM] + [VM] * 5 + [HBM] * 4,
        operands=(coords, e, second, n1, s1, gains, gp, w_out, w_ff1, w_ff2),
        out_specs=(ANY, ANY) + (VM,) * 7,
        scratch_shapes=[
            v((tokens, ff), LOW), v((width, width), LOW), v((width, ff), LOW), v((ff, width), LOW),
            v((tokens, ff // 2), LOW), v((tokens, ff // 2), LOW), pltpu.SemaphoreType.DMA((4 + 2 * (ff // 512),)),
        ],
        cost_estimate=CHEAP,
        vmem=52,
        name="feed",
    )


def between_kernel(
    layer, coords_ref, length_ref, mixed_ref, lse_ref, gctx_in, first_in, n2_ref, s2_ref, n1_ref, s1_ref, gains_ref,
    gp_hbm, wqkv_hbm, wout_hbm, w1_hbm, w2_hbm,
    mix_keep_ref, mix_send_ref, pre_keep_ref, pre_send_ref,
    att_ref, sec_keep_ref, sec_send_ref, top_ref, bias_ref, first_ref, fst_keep_ref, fst_send_ref, gctx_ref, sums_ref,
    gp, wqkv, wout, w1, w2, dmix, mix_keep, mix_send, keep, send, e, second, low_ref, sems,
):
    mine = coords_ref[0]
    below = layer - 1
    early = pltpu.make_async_copy(wqkv_hbm.at[layer], wqkv, sems.at[0])
    early.start()
    loads = chunk_loads(sems, 7, ((w2_hbm.at[below], w2), (gp_hbm, gp)))
    for pair in loads:
        for load in pair:
            load.start()
    late = [
        pltpu.make_async_copy(w1_hbm.at[below], w1, sems.at[1]),
        pltpu.make_async_copy(wout_hbm.at[below], wout, sems.at[2]),
    ]
    for load in late:
        load.start()
    stores = []

    def emit(src, dst):
        stores.append(pltpu.make_async_copy(src, dst, sems.at[3 + len(stores)]))
        stores[-1].start()

    attend_back_body(length_ref, mixed_ref, lse_ref, gctx_in, att_ref, dmix)
    part(mine, dmix, mix_keep, mix_send)
    emit(mix_send, mix_send_ref)
    emit(mix_keep, mix_keep_ref)
    early.wait()
    grad = first_in[...] + dot(dmix[...], wqkv[...], COLS)
    gains = gains_ref[...].astype(F32)
    norm_end(
        mine, grad, n2_ref[...], s2_ref[:, :1], gains[2 * layer : 2 * layer + 1], e, second, sec_keep_ref, sec_send_ref, top_ref
    )

    def ready(i):
        for load in loads[i]:
            load.wait()

    feed_back_body(mine, second, gp, w2, ready, bias_ref, keep, send)
    emit(send, pre_send_ref)
    emit(keep, pre_keep_ref)
    late[0].wait()
    grad = e[...] + both_halves(mine, keep, send, w1)
    norm_end(
        mine, grad, n1_ref[...], s1_ref[:, :1], gains[1 + 2 * below : 2 + 2 * below], first_ref, low_ref, fst_keep_ref,
        fst_send_ref, sums_ref,
    )
    late[1].wait()
    gctx_ref[...] = dot(low_ref[...], wout[...], COLS).astype(LOW)
    for store in stores:
        store.wait()


def between(layer, coords, length, mixed, lse, gctx, first, n2, s2, n1, s1, gains, gp, w_qkv, w_out, w_ff1, w_ff2, after=()):
    tokens, width = first.shape
    ff = gp.shape[1]
    s = jax.ShapeDtypeStruct
    v = pltpu.VMEM
    mix = s((tokens, 3 * width // 2), LOW)
    pre = s((tokens, ff // 2), LOW)
    sec = s((tokens, width // 2), LOW)
    low = s((tokens, width), LOW)
    three = s((3, width), F32)
    return run(
        functools.partial(between_kernel, layer),
        after,
        out_shape=(
            mix, mix, pre, pre, s((2, width), F32), sec, sec, three, s((1, ff), F32), s((tokens, width), F32), sec, sec, low, three,
        ),
        in_specs=[SM, SM] + [VM] * 9 + [HBM] * 5,
        operands=(coords, length, mixed, lse, gctx, first, n2, s2, n1, s1, gains, gp, w_qkv, w_out, w_ff1, w_ff2),
        out_specs=(ANY,) * 4 + (VM,) * 10,
        scratch_shapes=[
            v((tokens, ff), LOW), v((width, 3 * width), LOW), v((width, width), LOW), v((width, ff), LOW), v((ff, width), LOW),
            v((tokens, 3 * width), LOW), v(mix.shape, LOW), v(mix.shape, LOW), v(pre.shape, LOW), v(pre.shape, LOW),
            v((tokens, width), F32), v((tokens, width), LOW), v((tokens, width), LOW),
            pltpu.SemaphoreType.DMA((7 + 2 * (ff // 512),)),
        ],
        cost_estimate=CHEAP,
        vmem=58,
        name="between",
    )


COORDS = ("core", "x", "a", "b", "y")


def place(coords_ref, plan, result, *outs):
    count = result.shape[0]
    size = count // len(outs)
    dims = [] if plan is None else [dim for turn in plan for dim in turn]
    for i in range(count):
        block = i
        if plan is not None:
            bit = {}
            for n, dim in enumerate(dims):
                relative = (i >> (len(dims) - 1 - n)) & 1
                whole = plan[-1] == ("y",) and n == len(dims) - 1
                bit[dim] = relative if whole else coords_ref[COORDS.index(dim)] ^ relative
            block = 16 * bit.get("core", 0) + 8 * bit["b"] + 4 * bit["a"] + 2 * bit["x"] + bit["y"]
        out = outs[i // size]
        out[i % size] = result[block].astype(out.dtype)


def parts_of(plan):
    return 2 if plan is None else 2 ** len(plan[0])


def load_both(pairs, sems):
    loads = []
    for own, oth, dst in pairs:
        for n, src in enumerate((own, oth)):
            size = own.shape[0]
            load = pltpu.make_async_copy(src, dst.at[pl.ds(n * size, size)], sems.at[len(loads)])
            load.start()
            loads.append(load)
    return loads


def weights_kernel(plans, blocks, coords_ref, *refs):
    count = 8 if len(plans) == 2 else 20
    sources, refs = refs[:count], refs[count:]
    outs = []
    for plan in plans:
        outs.append(refs[: parts_of(plan)])
        refs = refs[parts_of(plan) :]
    sec, act, mid, pre, sect, midt, two, one = refs[:8]
    rest, sems = refs[8:-1], refs[-1]
    tokens = sources[0].shape[0]
    loads = []
    targets = [sec, act, mid, pre]
    if rest:
        x, mix, ctxt, fst, below_ctxt, below_fst, xt, mixed = rest
        targets += [x, mix, ctxt, fst, below_ctxt, below_fst]
    for n, target in enumerate(targets):
        for side in range(2):
            there = pl.ds(side * tokens, tokens)
            view = target.at[:, there] if n in (6, 8) else target.at[there]
            loads.append(pltpu.make_async_copy(sources[2 * n + side], view, sems.at[2 * n + side]))
            loads[-1].start()

    def ready(n):
        loads[2 * n].wait()
        loads[2 * n + 1].wait()

    ready(0)
    sect[...] = sec[...].T
    ready(1)
    rows = two.shape[1]
    cols = act.shape[1] // blocks

    group = 4 if blocks % 4 == 0 else 1

    def step_two(i, carry):
        there = pl.ds(pl.multiple_of(i * group * cols, cols), group * cols)
        got = dot(sect[...], act[:, there]).astype(LOW)
        for v in range(group):
            for y in range(2):
                for n in range(4):
                    at = (4 * y + n) * rows
                    piece = got[at : at + rows, v * cols : (v + 1) * cols]
                    two[2 * (i * group + v) + y, :, n * cols : (n + 1) * cols] = piece
        return carry

    lax.fori_loop(0, blocks // group, step_two, 0)
    place(coords_ref, plans[0], two, *outs[0])
    ready(2)
    midt[...] = mid[...].T
    ready(3)
    chunk = 512
    high = midt.shape[0] // one.shape[0]

    def step_one(i, carry):
        there = pl.ds(pl.multiple_of(i * chunk, chunk), chunk)
        one[:, :high, there] = dot(midt[...], pre[:, there]).astype(LOW).reshape(one.shape[0], high, chunk)
        return carry

    if rest:
        lax.fori_loop(0, pre.shape[1] // chunk, step_one, 0)
        ready(8)
        ready(9)
        part_cols, group_rows = below_fst.shape[1], one.shape[1] - high
        got = dot(below_ctxt[...], below_fst[...]).astype(LOW).reshape(one.shape[0], high, part_cols)
        for n in range(high // group_rows):
            there = slice(n * part_cols, (n + 1) * part_cols)
            one[:, high:, there] = got[:, n * group_rows : (n + 1) * group_rows]
        one[:, high:, high // group_rows * part_cols :] = jnp.zeros((one.shape[0], group_rows, part_cols), LOW)
    else:
        one[...] = dot(midt[...], pre[...]).astype(LOW).reshape(one.shape)
    place(coords_ref, plans[1], one, *outs[1])
    if rest:
        ready(4)
        xt[...] = x[...].T
        ready(5)
        wide = mix.shape[1]
        mixed[:, :, :wide] = dot(xt[...], mix[...]).astype(LOW).reshape(mixed.shape[:2] + (wide,))
        ready(6)
        ready(7)
        mixed[:, :, wide:] = dot(ctxt[...], fst[...]).astype(LOW).reshape(mixed.shape[:2] + (fst.shape[1],))
        place(coords_ref, plans[2], mixed, *outs[2])


def weights(blocks, plans, coords, sec, act, mid, pre, attention=(), after=()):
    tokens, width = mid[0].shape
    s = jax.ShapeDtypeStruct
    v = pltpu.VMEM
    count = 2 * blocks
    block = (count, width // count, 2 * width)
    high = (count, width // count + 16, 2 * width) if attention else block
    sizes = (block, high, block)
    outs = sum(
        ((s((count // parts_of(plan),) + size[1:], LOW),) * parts_of(plan) for plan, size in zip(plans, sizes)), ()
    )
    pairs = (sec, act, mid, pre) + tuple(attention)
    both = lambda pair: v((2 * tokens, pair[0].shape[1]), LOW)
    scratch = [both(pair) for pair in (sec, act, mid, pre)]
    scratch += [v((sec[0].shape[1], 2 * tokens), LOW), v((width, 2 * tokens), LOW), v(block, LOW), v(high, LOW)]
    if attention:
        x, mix, _, fst, _, below_fst = attention
        across = v((width, 2 * tokens), LOW)
        scratch += [both(x), both(mix), across, both(fst), across, both(below_fst), across, v(block, LOW)]
    got = run(
        functools.partial(weights_kernel, plans, blocks),
        after,
        out_shape=outs,
        in_specs=[SM] + [ANY] * (2 * len(pairs)),
        operands=(coords,) + tuple(array for pair in pairs for array in pair),
        out_specs=(VM,) * len(outs),
        scratch_shapes=scratch + [pltpu.SemaphoreType.DMA((2 * len(pairs),))],
        cost_estimate=CHEAP,
        vmem=50 if attention else 34,
        name="weights",
    )
    parts = []
    for plan in plans:
        parts.append(got[: parts_of(plan)])
        got = got[parts_of(plan) :]
    return parts


def combine_kernel(forms, *refs):
    count = sum(sum(form[0]) for form in forms)
    ins, outs = refs[:count], refs[count:]
    for terms_of, parts, axis in forms:
        results, outs = outs[:parts], outs[parts:]
        at = 0
        for terms in terms_of:
            mine, ins = ins[:terms], ins[terms:]
            size = mine[0].shape[0] // parts
            rows = mine[0].shape[1]
            for part in range(parts):
                for i in range(size):
                    total = mine[0][part * size + i].astype(F32)
                    for term in mine[1:]:
                        total = total + term[part * size + i].astype(F32)
                    if axis == 0:
                        results[part][at + i] = total.astype(LOW)
                    else:
                        results[part][i, at : at + rows] = total.astype(LOW)
            at += size if axis == 0 else rows


def combine(items, after=(), cost=CHEAP):
    forms = tuple((tuple(len(terms) for terms in sums), parts, axis) for sums, parts, axis in items)
    shapes = []
    for sums, parts, axis in items:
        shape = list(sums[0][0].shape)
        shape[axis] = sum(terms[0].shape[axis] for terms in sums)
        shape[0] //= parts
        shapes += [jax.ShapeDtypeStruct(tuple(shape), LOW)] * parts
    operands = tuple(array for sums, _, _ in items for terms in sums for array in terms)
    size = sum(array.size for array in operands)
    outs = run(
        functools.partial(combine_kernel, forms),
        after,
        out_shape=tuple(shapes),
        in_specs=[VM] * len(operands),
        operands=operands,
        out_specs=(VM,) * len(shapes),
        cost_estimate=cost,
        vmem=6 + 4 * size // (1 << 20),
        name="combine",
    )
    got = []
    for _, parts, _ in forms:
        got.append(outs[:parts])
        outs = outs[parts:]
    return got


def last_kernel(
    plan, coords_ref, length_ref, mixed_ref, lse_ref, gctx_ref, first_ref, n_ref, s_ref, gains_ref, x_ref,
    slot_ref, type_ref, top0, top1, low0, low1, att1, bias0, bias1, wqkv_hbm,
    out_keep_ref, out_send_ref, *parts_and_scratch
):
    outs, (wqkv, dmix, xt, res, back_ref, back_low, att0, emb, small, sems) = parts_and_scratch[:-10], parts_and_scratch[-10:]
    tokens, width = back_ref.shape
    load = pltpu.make_async_copy(wqkv_hbm.at[0], wqkv, sems.at[0])
    load.start()
    attend_back_body(length_ref, mixed_ref, lse_ref, gctx_ref, att0, dmix)
    load.wait()
    grad = first_ref[...] + dot(dmix[...], wqkv[...], COLS)
    gain = gains_ref[...].astype(F32)[0:1]
    norm_end(coords_ref[0], grad, n_ref[...], s_ref[:, :1], gain, back_ref, back_low, None, None, emb)
    mine = coords_ref[0]
    slots, half = out_keep_ref.shape
    chunk = 256

    def step(i, carry):
        there = pl.ds(pl.multiple_of(i * chunk, chunk), chunk)
        number = lax.broadcasted_iota(jnp.int32, (chunk, tokens), 0) + i * chunk
        hit = jnp.where(number == slot_ref[...], 1.0, 0.0).astype(LOW)
        got = dot(hit, back_low[...]).astype(LOW)

        @pl.when(mine == 0)
        def _():
            out_keep_ref[there, :] = got[:, :half]
            out_send_ref[there, :] = got[:, half:]

        @pl.when(mine == 1)
        def _():
            out_keep_ref[there, :] = got[:, half:]
            out_send_ref[there, :] = got[:, :half]

        return carry

    lax.fori_loop(0, slots // chunk, step, 0)
    xt[...] = x_ref[...].T
    blocks, piece, _ = res.shape
    blocks //= 2
    wide = 3 * half
    for core in range(2):
        there = slice(core * blocks, (core + 1) * blocks)
        got = dot(xt[...], dmix[:, core * wide : (core + 1) * wide]).astype(LOW)
        res[there, :, :wide] = got.reshape(blocks, piece, wide)
    back = back_ref[...]
    kind = as_column(type_ref[...].astype(F32))
    small[0:1] = jnp.sum(back * (1.0 - kind), axis=0, keepdims=True)
    small[1:2] = jnp.sum(back * kind, axis=0, keepdims=True)
    sources = [(emb, 0)]
    for top, low in ((top0, low0), (top1, low1)):
        sources += [(low, 0), (top, 0)]
    sources += [(emb, 1)]
    for top, low, att in ((top0, low0, att0), (top1, low1, att1)):
        sources += [(att, 0), (att, 1), (low, 2), (low, 1), (top, 2), (top, 1)]
    at = 2
    for ref, row in sources:
        small[at : at + 1] = ref[row : row + 1]
        at += 1
    for bias in (bias0, bias1):
        for i in range(bias.shape[1] // width):
            small[at : at + 1] = bias[:, i * width : (i + 1) * width]
            at += 1
    quarter = at // 4
    group = tokens // blocks
    positions = back.reshape(blocks, group, width).astype(LOW)
    for core in range(2):
        there = slice(core * blocks, (core + 1) * blocks)
        res[there, :group, wide:] = positions[:, :, core * half : (core + 1) * half]
        for y in range(2):
            mine = small[(2 * core + y) * quarter : (2 * core + y + 1) * quarter]
            rest = jnp.zeros((piece - group - 2 * quarter, half), F32)
            mine = jnp.concatenate([mine[:, :half], mine[:, half:], rest], axis=0).astype(LOW)
            for v in range(blocks // 2):
                res[core * blocks + 2 * v + y, group:, wide:] = mine
    place(coords_ref, plan, res, *outs)


def last(plan, coords, length, mixed, lse, gctx, first, n, sp, gains, x, slot_of, types, sums, w_qkv, slots, blocks, parts=2, after=()):
    tokens, width = first.shape
    s = jax.ShapeDtypeStruct
    v = pltpu.VMEM
    block = (blocks, width // blocks, 2 * width)
    operands = (coords, length, mixed, lse, gctx, first, n, sp, gains, x, slot_of, types, *sums, w_qkv)
    return run(
        functools.partial(last_kernel, plan),
        after,
        out_shape=(s((slots, width // 2), LOW),) * 2 + (s((2 * blocks // parts,) + block[1:], LOW),) * parts,
        in_specs=[SM, SM] + [VM] * (len(operands) - 3) + [HBM],
        operands=operands,
        out_specs=(VM,) * (2 + parts),
        scratch_shapes=[
            v((width, 3 * width), LOW), v((tokens, 3 * width), LOW), v((width, tokens), LOW),
            v((2 * blocks,) + block[1:], LOW), v((tokens, width), F32), v((tokens, width), LOW),
            v((2, width), F32), v((3, width), F32), v((28, width), F32), pltpu.SemaphoreType.DMA((1,)),
        ],
        cost_estimate=CHEAP,
        vmem=52,
        name="last",
    )


def table_back_kernel(asked_ref, rows_ref, out_ref):
    count = out_ref.shape[0]
    chunk = count // 5 if count % 80 == 0 else count

    def step(i, carry):
        at = pl.multiple_of(i * chunk, 16)
        number = lax.broadcasted_iota(jnp.int32, (chunk, rows_ref.shape[0]), 0) + at
        hit = jnp.where(number == asked_ref[...], 1.0, 0.0).astype(LOW)
        out_ref[pl.ds(at, chunk), :] = dot(hit, rows_ref[...]).astype(LOW)
        return carry

    lax.fori_loop(0, count // chunk, step, 0)


def table_back(asked, rows, local_rows, after=()):
    return run(
        table_back_kernel,
        after,
        out_shape=jax.ShapeDtypeStruct((local_rows, rows.shape[1]), LOW),
        in_specs=[VM, VM],
        operands=(asked, rows),
        out_specs=VM,
        cost_estimate=CHEAP,
        vmem=20,
        name="table_back",
    )


def finish_kernel(coords_ref, *refs):
    many, early, few = refs[:4], refs[4:8], refs[8:12]
    qkv_ref, wout_ref, one_ref, two_ref, pos_ref, type_ref, gain_ref, shift_ref, bias_ref, small_ref = refs[12:]
    mine_core, mine_y = coords_ref[0] == 0, coords_ref[4] == 0
    half = wout_ref.shape[2] // 2
    wide = 3 * half
    part = wout_ref.shape[1] // 2

    def piece(four, rows, core, y):
        own, over_y, over_core, over_both = (ref[0, rows] for ref in four)
        same_y = mine_y if y == 0 else jnp.logical_not(mine_y)
        same_core = mine_core if core == 0 else jnp.logical_not(mine_core)
        here = jnp.where(same_y, own, over_y)
        there = jnp.where(same_y, over_core, over_both)
        return jnp.where(same_core, here, there).astype(F32)

    at = lambda n: slice(n * part, (n + 1) * part)
    for layer in range(NL):
        for core in range(2):
            columns = []
            mine = slice(core * half, (core + 1) * half)
            for y in range(2):
                rows = slice(y * part, (y + 1) * part)
                mix = piece(few, slice(0, part), core, y) if layer == 0 else piece(many, at(0), core, y)
                qkv_ref[layer, rows, core * wide : (core + 1) * wide] = mix[:, :wide]
                if layer == 0:
                    group = pos_ref.shape[0] // 2
                    pos_ref[y * group : (y + 1) * group, mine] = mix[:group, wide:]
                    first = (2 * core + y) * 7
                    small_ref[first : first + 7, :half] = mix[group : group + 7, wide:]
                    small_ref[first : first + 7, half:] = mix[group + 7 : group + 14, wide:]
                    out = piece(many, slice(3 * part, 3 * part + 16), core, y)
                    for n in range(part // 16):
                        there = slice(y * part + 16 * n, y * part + 16 * (n + 1))
                        wout_ref[layer, there, mine] = out[:, n * half : (n + 1) * half]
                else:
                    wout_ref[layer, rows, mine] = mix[:, wide:]
                first = piece(many, at(2), core, y) if layer == 0 else piece(early, at(1), core, y)
                one_ref[layer, rows, core * 4 * half : (core + 1) * 4 * half] = first
                second = piece(many, at(1), core, y) if layer == 0 else piece(early, at(0), core, y)
                columns += [second[:, i * half : (i + 1) * half] for i in range(4)]
            two_ref[layer, :, mine] = jnp.concatenate(columns, axis=0).T
    owners = small_ref.shape[1] // type_ref.shape[1]
    size, long = type_ref.shape[1], bias_ref.shape[1]
    per = long * owners // small_ref.shape[1]
    few_rows = small_ref[:20]
    mine, bias = few_rows[:, :size], [small_ref[20 + n * per : 21 + n * per, :long] for n in range(NL)]
    for owner in range(1, owners):
        chosen = coords_ref[5] == owner
        mine = jnp.where(chosen, few_rows[:, owner * size : (owner + 1) * size], mine)
        row, at_lane = divmod(owner * long, small_ref.shape[1])
        for n in range(NL):
            there = small_ref[20 + n * per + row : 21 + n * per + row, at_lane : at_lane + long]
            bias[n] = jnp.where(chosen, there, bias[n])
    type_ref[...] = mine[:2]
    gain_ref[...] = mine[2 : 2 + 2 * NL + 1]
    shift_ref[...] = mine[2 + 2 * NL + 1 :]
    for n in range(NL):
        bias_ref[n : n + 1] = bias[n]


def finish(coords, many, early, few, width, ff, owners):
    s = jax.ShapeDtypeStruct
    rows = width // owners
    return run(
        finish_kernel,
        (),
        out_shape=(
            s((NL, rows, 3 * width), F32), s((NL, rows, width), F32), s((NL, rows, ff), F32), s((NL, ff // owners, width), F32),
            s((64, width), F32), s((2, rows), F32), s((2 * NL + 1, rows), F32), s((6 * NL + 1, rows), F32), s((NL, ff // owners), F32),
        ),
        in_specs=[SM] + [VM] * 12,
        operands=(coords, *many, *early, *few),
        out_specs=(VM,) * 9,
        scratch_shapes=[pltpu.VMEM((28, width), F32)],
        cost_estimate=CHEAP,
        vmem=24,
        name="finish",
    )


def table_finish_kernel(coords_ref, own_ref, other_ref, out_ref, mark_ref):
    mark_ref[...] = jnp.zeros_like(mark_ref)
    half = own_ref.shape[1]
    first = coords_ref[0] == 0
    out_ref[:, :half] = jnp.where(first, own_ref[...], other_ref[...]).astype(F32)
    out_ref[:, half:] = jnp.where(first, other_ref[...], own_ref[...]).astype(F32)


def table_finish(coords, own, other, after=()):
    return run(
        table_finish_kernel,
        after,
        out_shape=(jax.ShapeDtypeStruct((own.shape[0], 2 * own.shape[1]), F32), jax.ShapeDtypeStruct((8, 128), F32)),
        in_specs=[SM, VM, VM],
        operands=(coords, own, other),
        out_specs=(VM, VM),
        cost_estimate=CHEAP,
        vmem=16,
        name="table_finish",
    )


AXES = ("dp", "vocab")
VOCAB_MASK = {"x": 1, "a": 2, "b": 4}


def add(left_op, right_op):
    return (left_op.astype(F32) + right_op.astype(F32)).astype(LOW)


class Cube:
    def __init__(self, dp_size, vocab_size):
        self.dp_size = dp_size
        self.vocab_size = vocab_size
        self.dp_bits = dp_size.bit_length() - 1
        self.vocab_bits = vocab_size.bit_length() - 1
        assert 1 << self.dp_bits == dp_size and 1 << self.vocab_bits == vocab_size
        self.small = self.dp_bits == 2 and self.vocab_bits == 3

    def permute(self, value, dp_mask, vocab_mask):
        count = self.vocab_size
        pairs = [
            (d * count + v, (d ^ dp_mask) * count + (v ^ vocab_mask))
            for d in range(self.dp_size)
            for v in range(count)
        ]
        return lax.ppermute(value, AXES, pairs)

    def core(self, value):
        return self.permute(value, 1, 0)

    def along(self, value, dims):
        return self.permute(
            value, 2 * ("y" in dims) + ("core" in dims), sum(VOCAB_MASK[dim] for dim in dims if dim in VOCAB_MASK)
        )

    def core_is_first(self):
        return (lax.axis_index("dp") & 1) == 0

    def coords(self):
        dp, vocab = lax.axis_index("dp"), lax.axis_index("vocab")
        return jnp.stack([dp & 1, vocab & 1, (vocab >> 1) & 1, (vocab >> 2) & 1, (dp >> 1) & 1, vocab])

    def halves(self, matrix):
        mine = lax.axis_index("dp") & 1
        width = matrix.shape[1] // 2
        keep = lax.dynamic_slice_in_dim(matrix, mine * width, width, 1)
        send = lax.dynamic_slice_in_dim(matrix, (1 - mine) * width, width, 1)
        return keep, send

    def ordered(self, first, mine, other, axis):
        return jnp.concatenate(
            [jnp.where(first, mine, other), jnp.where(first, other, mine)], axis=axis
        )

    def join_core(self, share, axis):
        return self.ordered(self.core_is_first(), share, self.core(share), axis).astype(F32)

    def reduce(self, matrix):
        for bit in reversed(range(self.vocab_bits)):
            mine = (lax.axis_index("vocab") >> bit) & 1
            rows = matrix.shape[0] // 2
            keep = lax.dynamic_slice_in_dim(matrix, mine * rows, rows, 0)
            send = lax.dynamic_slice_in_dim(matrix, (1 - mine) * rows, rows, 0)
            matrix = add(keep, self.permute(send, 0, 1 << bit))
        for bit in range(1, self.dp_bits):
            matrix = add(matrix, self.permute(matrix, 1 << bit, 0))
        return matrix


def on_device(
    cube,
    token_ids,
    lengths,
    type_ids,
    word_table,
    pos_table,
    type_table,
    gains,
    shifts,
    w_qkv,
    w_out,
    b_ff1,
    w_ff1,
    w_ff2,
    cotangent,
):
    owners = cube.vocab_size
    local_rows, width = word_table.shape
    assert token_ids.shape[0] == 1
    tokens = token_ids.shape[1]
    slot_count = 2 * tokens // owners
    slots = owners * slot_count
    coords = cube.coords()

    all_ids = lax.all_to_all(
        jnp.broadcast_to(token_ids, (owners, tokens)), "vocab", split_axis=0, concat_axis=0, tiled=True
    )
    local = all_ids - lax.axis_index("vocab") * local_rows
    here = (local >= 0) & (local < local_rows)
    rank = jnp.cumsum(here.astype(jnp.int32), axis=1) - 1
    slot_hit = (
        jnp.where(here, rank, -1)[:, None, :] == jnp.arange(slot_count, dtype=jnp.int32)[None, :, None]
    )
    asked = jnp.sum(jnp.where(slot_hit, local[:, None, :] + 1, 0), axis=2).reshape(slots) - 1
    row_hit = (asked[:, None] == jnp.arange(local_rows, dtype=jnp.int32)[None, :]).astype(LOW)
    replies = exchange_rows(dot(row_hit, word_table).astype(LOW), owners)
    number = jnp.arange(owners, dtype=jnp.int32)[:, None]
    chosen = (token_ids >= number * local_rows) & (token_ids < (number + 1) * local_rows)
    own_rank = jnp.cumsum(chosen.astype(jnp.int32), axis=1) - 1
    slot_row = jnp.sum(jnp.where(chosen, number * slot_count + own_rank, 0), axis=0, keepdims=True)
    asked = both_cores(asked[:, None], cube.core(asked[:, None]), owners).reshape(1, -1)
    (n0, s0, hidden), top, layers = forward(
        coords, lengths, replies, slot_row, type_ids, pos_table, type_table, gains, shifts, b_ff1.astype(F32),
        cotangent.reshape(tokens, width), w_qkv, w_out, w_ff1, w_ff2,
    )
    norms, saved = [(n0, s0)], []
    for xlow, mixed, lse, ctxt, n1, s1, mlow, gp, act, *end in layers:
        saved.append((mixed, lse, n1, s1, gp) + tuple((own, cube.core(own)) for own in (xlow, ctxt, mlow, act)))
        norms.append(tuple(end))
    hidden_out = hidden.reshape(1, tokens, width)

    gradients = gradients_small if cube.small else gradients_any
    outs = gradients(
        cube, coords, lengths, top, saved, gains, w_qkv, w_out, w_ff1, w_ff2,
        norms, (type_ids, slot_row, asked, local_rows),
    )
    return (hidden_out,) + outs


def exchange_rows(outgoing, owners):
    shape = outgoing.shape
    return lax.all_to_all(
        outgoing.reshape(owners, -1, shape[1]), "vocab", split_axis=0, concat_axis=0, tiled=True
    ).reshape(shape)


def both_cores(own, other, owners):
    fold = lambda array: array.reshape(owners, 1, -1, array.shape[1])
    return jnp.concatenate([fold(own), fold(other)], axis=1).reshape(-1, own.shape[1])


def unpack(pack):
    cores, blocks, _, half = pack.shape
    pos = pack[:, :, :32].transpose(1, 2, 0, 3).reshape(blocks * 32, 2 * half)
    small = pack[:, :2, 32:46].reshape(cores, 2, 2, 7, half).transpose(0, 1, 3, 2, 4)
    return pos, small.reshape(28, 2 * half)


def small_outs(cube, rows):
    place_of = lax.axis_index("vocab")

    def mine(array):
        size = array.shape[1] // cube.vocab_size
        return lax.dynamic_slice_in_dim(array, place_of * size, size, 1)

    few = mine(rows[:20])
    return few[:2], few[2 : 2 + 2 * NL + 1], few[2 + 2 * NL + 1 :], mine(rows[20:].reshape(NL, -1))


def gradients_any(cube, coords, lengths, top, saved, gains, w_qkv, w_out, w_ff1, w_ff2, norms, embed):
    owners = cube.vocab_size
    width = w_out.shape[1]
    tokens = top[0].shape[0]
    blocks = 8
    half = width // 2
    kinds, slot_row, asked, local_rows = embed
    mixed1, lse1, n1_1, s1_1, gp1, x1, ctx1, mid1, act1 = saved[1]
    mixed0, lse0, n1_0, s1_0, gp0, x0, ctx0, mid0, act0 = saved[0]
    e, low, sec_keep, sec_send, top1 = top
    pre_keep, pre_send, bias1, first, _, fst_keep, fst_send, gctx, sums1 = feed(
        1, coords, e, low, n1_1, s1_1, gains, gp1, w_out, w_ff1, w_ff2
    )
    pair = lambda keep, send: (keep, cube.core(send))
    two1, one1 = weights(blocks, (None, None), coords, pair(sec_keep, sec_send), act1, mid1, pair(pre_keep, pre_send))
    fst1 = pair(fst_keep, fst_send)
    (
        mix_keep, mix_send, pre_keep, pre_send, att1, sec_keep, sec_send, top0, bias0, first, fst_keep, fst_send, gctx, sums0
    ) = between(
        1, coords, lengths, mixed1, lse1, gctx, first, *norms[1], n1_0, s1_0, gains, gp0, w_qkv, w_out, w_ff1, w_ff2
    )
    two0, one0, mix1 = weights(
        blocks, (None, None, None), coords, pair(sec_keep, sec_send), act0, mid0, pair(pre_keep, pre_send),
        (x1, pair(mix_keep, mix_send), ctx1, fst1, ctx0, pair(fst_keep, fst_send)),
    )
    out_keep, out_send, first_core, second_core = last(
        None, coords, lengths, mixed0, lse0, gctx, first, *norms[0], gains, x0[0], slot_row, kinds,
        (top0, top1, sums0, sums1, att1, bias0, bias1), w_qkv, asked.shape[1] // 2, 2 * blocks,
    )
    mine = cube.core_is_first()

    def over_cores(first, second):
        return add(jnp.where(mine, first, second), cube.core(jnp.where(mine, second, first)))

    outgoing = both_cores(out_keep, cube.core(out_send), owners)
    table_part = table_back(asked, exchange_rows(outgoing, owners), local_rows)
    for bit in range(1, cube.dp_bits):
        table_part = add(table_part, cube.permute(table_part, 1 << bit, 0))
    wide = 3 * half
    sums_last = over_cores(first_core, second_core)
    packs = sums_last[..., wide:]
    other = cube.core(packs)
    pos, small = unpack(jnp.stack([jnp.where(mine, packs, other), jnp.where(mine, other, packs)]))
    pos_out = cube.reduce(pos).astype(F32)
    for bit in range(cube.vocab_bits):
        small = add(small, cube.permute(small, 0, 1 << bit))
    for bit in range(1, cube.dp_bits):
        small = add(small, cube.permute(small, 1 << bit, 0))
    types, gains_out, shifts_out, biases = small_outs(cube, small.astype(F32))
    whole = lambda parts: jnp.concatenate(parts, axis=0)
    part = width // blocks // 2
    one = lambda parts: cube.reduce(whole(parts)[:, :part].reshape(width, -1))
    two = lambda parts: cube.reduce(
        whole(parts).reshape(blocks, 2, width // 16, 4, -1).transpose(0, 4, 1, 3, 2).reshape(-1, half)
    )
    out0 = whole(one0)[:, part:].reshape(2 * blocks, 16, 4, half)[:, :, : part // 16].transpose(0, 2, 1, 3)
    mixes = jnp.stack(
        [
            cube.reduce(jnp.concatenate([sums_last[..., :wide].reshape(width, -1), out0.reshape(width, -1)], axis=1)),
            one(mix1),
        ]
    )
    return (
        cube.join_core(table_part, -1), pos_out, types, gains_out, shifts_out,
        cube.join_core(mixes[..., :wide], 2), cube.join_core(mixes[..., wide:], 2), biases,
        cube.join_core(jnp.stack([one(one0), one(one1)]), 2), cube.join_core(jnp.stack([two(two0), two(two1)]), 2),
    )


class Bucket:
    def __init__(self, cube, plan, parts):
        self.cube, self.plan, self.parts = cube, tuple(plan), tuple(parts)

    def start(self):
        turn = self.plan[0]
        if self.plan == (("y",),):
            self.got = (self.parts[0], self.cube.along(self.parts[0], turn))
            return
        self.got = self.parts[:1]
        for n in range(1, len(self.parts)):
            there = [dim for i, dim in enumerate(turn) if (n >> (len(turn) - 1 - i)) & 1]
            self.got += (self.cube.along(self.parts[n], there),)


    def keep(self):
        self.got, self.plan = self.parts, (None,)


def joined(buckets, parts_axis):
    return (tuple(buckets), parts_axis)


def step(groups, after=(), cost=CHEAP):
    groups = [group if isinstance(group, tuple) else ((group,), 0) for group in groups]
    items = []
    for buckets, axis in groups:
        rest = buckets[0].plan[1:]
        assert all(bucket.plan[1:] == rest for bucket in buckets)
        parts = 1 if rest in ((), (("y",),)) else 2 ** len(rest[0])
        items.append((tuple(bucket.got for bucket in buckets), parts, axis))
    for (buckets, _), parts in zip(groups, combine(items, after, cost)):
        buckets[0].plan, buckets[0].parts = buckets[0].plan[1:], tuple(parts)
    return groups[0][0][0].parts[0]


def gradients_small(cube, coords, lengths, top, saved, gains, w_qkv, w_out, w_ff1, w_ff2, norms, embed):
    owners = cube.vocab_size
    width = w_out.shape[1]
    tokens = top[0].shape[0]
    blocks = owners
    half = width // 2
    single = lambda dims: tuple((dim,) for dim in dims)
    plan_two1, plan_one1 = (("x", "y"), ("a",), ("b",)), (("a",), ("x", "y"), ("b",))
    plan_mix1 = single("ayxb")
    plan_two0, plan_one0, plan_mix0 = single("xayb"), single("yxab"), (("core",), ("y",), ("x", "a"), ("b",))
    kinds, slot_row, asked, local_rows = embed
    mixed1, lse1, n1_1, s1_1, gp1, x1, ctx1, mid1, act1 = saved[1]
    mixed0, lse0, n1_0, s1_0, gp0, x0, ctx0, mid0, act0 = saved[0]
    pair = lambda keep, send: (keep, cube.core(send))
    e, low, sec_keep, sec_send, top1 = top
    pre_keep, pre_send, bias1, first, _, fst_keep, fst_send, gctx, sums1 = feed(
        1, coords, e, low, n1_1, s1_1, gains, gp1, w_out, w_ff1, w_ff2
    )
    fst1 = pair(fst_keep, fst_send)
    got = weights(
        blocks, (plan_two1, plan_one1), coords, pair(sec_keep, sec_send), act1, mid1, pair(pre_keep, pre_send)
    )
    two1, one1 = Bucket(cube, plan_two1, got[0]), Bucket(cube, plan_one1, got[1])
    two1.start()
    one1.start()
    (
        mix_keep, mix_send, pre_keep, pre_send, att1, sec_keep, sec_send, top0, bias0, first, fst_keep, fst_send, gctx, sums0
    ) = between(
        1, coords, lengths, mixed1, lse1, gctx, first, *norms[1], n1_0, s1_0, gains, gp0, w_qkv, w_out, w_ff1, w_ff2,
        after=got[0][:1] + (act0[1], mid0[1], ctx0[1], x1[1], ctx1[1]),
    )
    mark = step([two1, one1], after=(gctx,), cost=LONG)
    two1.start()
    one1.start()
    got = weights(
        blocks, (plan_two0, plan_one0, plan_mix1), coords, pair(sec_keep, sec_send), act0, mid0, pair(pre_keep, pre_send),
        (x1, pair(mix_keep, mix_send), ctx1, fst1, ctx0, pair(fst_keep, fst_send)), after=(mark,),
    )
    two0, one0, mix1 = [Bucket(cube, plan, parts) for plan, parts in zip((plan_two0, plan_one0, plan_mix1), got)]
    for bucket in (mix1, two0, one0):
        bucket.start()
    mark = step([joined((two1, one1), 1)], after=got[0][:1], cost=LONG)
    two1.start()
    out_keep, out_send, *got = last(
        plan_mix0, coords, lengths, mixed0, lse0, gctx, first, *norms[0], gains, x0[0], slot_row, kinds,
        (top0, top1, sums0, sums1, att1, bias0, bias1), w_qkv, asked.shape[1] // 2, 2 * owners, after=(mark,),
    )
    incoming = exchange_rows(both_cores(out_keep, cube.core(out_send), owners), owners)
    mix0 = Bucket(cube, plan_mix0, got)
    mix0.start()
    mark = step([two1, mix1, two0, one0], after=got[:1], cost=LONG)
    for bucket in (mix1, two0, one0):
        bucket.start()
    mark = step([mix0], after=(mark,))
    mix0.start()
    mark = step([mix1, two0, one0], after=(mark,), cost=LONG)
    for bucket in (mix1, two0, one0):
        bucket.start()
    folded = (local_rows // 48, 48, half)
    got = table_back(asked, incoming, local_rows, after=(mark,))
    table = Bucket(cube, single("y"), (got.reshape(folded),))
    table.start()
    mark = step([mix0, joined((mix1, two0, one0), 1)], after=(got,), cost=LONG)
    mix0.start()
    mix1.start()
    two1.keep()
    mark = step([table, two1], after=(mark,))
    early = Bucket(cube, (), (cube.along(two1.parts[0], ("y",)),))
    early.keep()
    mark = step([mix0, mix1, early], after=(mark,), cost=LONG)
    mix0.start()
    later = Bucket(cube, (), (cube.along(mix1.parts[0], ("y",)),))
    later.keep()
    table_own = table.parts[0].reshape(local_rows, half)
    table_out, mark = table_finish(coords, table_own, cube.core(table_own), after=(mark,))
    others = [Bucket(cube, (), (cube.core(bucket.parts[0]),)) for bucket in (two1, early)]
    for other in others:
        other.keep()
    mark = step([mix0] + others, after=(mark,))
    last_y = Bucket(cube, (), (cube.along(mix0.parts[0], ("y",)),))
    last_y.keep()
    step([last_y], after=(mark,))
    step([later], after=(last_y.parts[0],))
    four = lambda own, over_y: (own, over_y, cube.core(own), cube.core(over_y))
    qkv_out, wout_out, one_out, two_out, pos_out, types, gains, shifts, biases = finish(
        coords, four(mix1.parts[0], later.parts[0]),
        (two1.parts[0], early.parts[0], others[0].parts[0], others[1].parts[0]),
        four(mix0.parts[0], last_y.parts[0]), width, w_ff1.shape[2], owners,
    )
    return (
        table_out, pos_out, types, gains, shifts, qkv_out, wout_out,
        biases, one_out, two_out,
    )


def solution(mesh):
    cube = Cube(mesh.shape["dp"], mesh.shape["vocab"])
    both = ("dp", "vocab")
    in_specs = (
        P(both, None),
        P(both),
        P(both, None),
        P("vocab", None),
        P(),
        P(),
        P(),
        P(),
        P(),
        P(),
        P(),
        P(),
        P(),
        P(both, None, None),
    )
    out_specs = (
        P(both, None, None),
        P("vocab", None),
        P("vocab", None),
        P(None, "vocab"),
        P(None, "vocab"),
        P(None, "vocab"),
        P(None, "vocab", None),
        P(None, "vocab", None),
        P(None, "vocab"),
        P(None, "vocab", None),
        P(None, "vocab", None),
    )
    return jax.shard_map(
        functools.partial(on_device, cube), mesh=mesh, in_specs=in_specs, out_specs=out_specs, check_vma=False
    )
```
